32 devices in a mesh: fsdp: 8 (over z, x), seq: 4 (over y, core).
Axes of the slice: x: 2, y: 2, z: 4, core: 2. Of those that a mesh axis runs over, the one named last changes fastest.
Arguments:
- hidden: bfloat16 [2, 8, 512, 576], P(None, 'fsdp', 'seq'), may hold values from -6 to 6
- w_qkv: bfloat16 [576, 960], P('fsdp'), may hold values from -0.25 to 0.25
- b_qkv: bfloat16 [960], P('fsdp'), may hold values from -3 to 3
- w_out: bfloat16 [576, 576], P('fsdp'), may hold values from -1 to 1
- w_gate_up: bfloat16 [576, 3072], P('fsdp'), may hold values from -0.25 to 0.25
- w_down: bfloat16 [1536, 576], P('fsdp'), may hold values from -0.15625 to 0.15625
- norm_gains: bfloat16 [2, 576], P(None, 'fsdp'), may hold values from 0.5 to 1.5
- segment_ids: int32 [2, 8, 512], P(None, 'fsdp', 'seq'), may hold values from 0 to 3, as said below
- token_counts: int32 [2], replicated, may hold values from 2048 to 4096
- cotangent: bfloat16 [2, 8, 512, 576], P(None, 'fsdp', 'seq'), may hold values from -6 to 6
Outputs:
- block_out: bfloat16 [2, 8, 512, 576], P(None, 'fsdp', 'seq')
- hidden_grad: float32 [2, 8, 512, 576], P(None, 'fsdp', 'seq')
- w_qkv_grad: float32 [576, 960], P('fsdp')
- b_qk_grad: float32 [768], P('fsdp')
- b_v_grad: float32 [192], P('fsdp')
- w_out_grad: float32 [576, 576], P('fsdp')
- w_gate_up_grad: float32 [576, 3072], P('fsdp')
- w_down_grad: float32 [1536, 576], P('fsdp')
- norm_gains_grad: float32 [2, 576], P(None, 'fsdp')
The draws below stay inside these ranges and needn't reach their ends.
Inputs may be any that keep to these rules, and one draw needn't show every extreme that they name: `segment_ids`: in each sequence the ids start at 0 and never fall; equal ids mark one document of 200 to 2000 tokens, which the sequence's ends may cut.
All inputs are finite; a program needn't handle non-finite values.
Results may differ from the reference program's by a relative error of at most 0.017.
Values may be sent and summed in bfloat16 or wider, within the bound.
No kernel may reach another device: no remote copies, remote signals or barrier semaphores. Data moves between devices by JAX's collectives and lax.ppermute only.
A program may use at most 128 MiB of HBM per device.

```python
import jax
import jax.numpy as jnp
from jax import lax

D = 576
FF = 1536
HEADS = 9
KV_HEADS = 3
HEAD_DIM = 64
SEQ_LEN = 512
SEQ_DEV = 1
MICRO = 2
DOC_MIN = 200
DOC_MAX = 2000
SEQS = 8
QW = 576
QKW = 768
QKV = 960
TOKENS_MB = 4096


def draw_segment_ids(key, part):
    key = jax.random.fold_in(key, 7)
    key_len, key_off, key_pick = jax.random.split(key, 3)
    pieces = SEQ_LEN // DOC_MIN + 2
    doc_lengths = jax.random.randint(key_len, (MICRO, SEQS, pieces), DOC_MIN, DOC_MAX + 1)
    offsets = jax.random.randint(key_off, (MICRO, SEQS), 0, doc_lengths[:, :, 0])
    chosen = jax.random.randint(key_pick, (SEQS // SEQ_DEV,), 0, MICRO * SEQ_DEV)
    slot_index = jnp.arange(MICRO)[:, None] * SEQ_DEV + jnp.arange(SEQS)[None, :] % SEQ_DEV
    group_index = jnp.arange(SEQS) // SEQ_DEV
    spanning = slot_index == chosen[group_index][None, :]
    dense_slot = (chosen[0] + 1) % (MICRO * SEQ_DEV)
    dense = (slot_index == dense_slot) & (group_index[None, :] == 0)
    piece_index = jnp.arange(pieces)[None, None, :]
    doc_lengths = jnp.where(dense[:, :, None] & (piece_index >= 1), DOC_MIN, doc_lengths)
    offsets = jnp.where(dense, doc_lengths[:, :, 0] - 1, offsets)
    doc_ends = jnp.cumsum(doc_lengths, axis=-1) - offsets[:, :, None]
    places = jnp.arange(SEQ_LEN, dtype=jnp.int32)
    segments = jnp.sum((places[None, None, :, None] >= doc_ends[:, :, None, :]).astype(jnp.int32), axis=-1)
    return jnp.where(spanning[:, :, None], 0, segments).astype(jnp.int32)


def with_spikes(values, own_key, source, target, blocks, factor):
    owner, partner = [(jnp.arange(values.shape[position]) // (values.shape[position] // blocks)).reshape([-1 if axis == position else 1 for axis in range(values.ndim)]) for position in (source, target)]
    chosen = jax.random.permutation(own_key, blocks)[partner]
    strong = (owner == chosen) | (owner == (partner + blocks // 2) % blocks)
    return jnp.where(strong, factor * values, values)


def level_of(key, shape, cuts, smallest, top_value):
    factor_of, own = 1.0, jax.random.fold_in(key, 6)
    for dim, parts in cuts:
        heights = jnp.exp(jax.random.uniform(jax.random.fold_in(own, dim), (parts,), jnp.float32, smallest / len(cuts), top_value / len(cuts)))
        factor_of = factor_of * jnp.repeat(heights, shape[dim] // parts).reshape([-1 if axis == dim else 1 for axis in range(len(shape))])
    return factor_of


def normal_values(key, extent, scale, most, cuts=(), kind=jnp.bfloat16):
    loudness = level_of(key, extent, cuts, -0.22, 0.18) if cuts else 1.0
    entries = jax.random.normal(key, extent, jnp.float32) * scale * loudness
    return jnp.minimum(jnp.maximum(entries, -most), most).astype(kind)


def gaussian_with(own_key, extent, deviation, limit, cuts, heavy, kind=jnp.bfloat16):
    array = deviation * jax.random.normal(own_key, extent, jnp.float32)
    if cuts:
        array = array * level_of(own_key, extent, cuts, -0.22, 0.18)
    return jnp.clip(with_spikes(array, jax.random.fold_in(own_key, 3), *heavy), -limit, limit).astype(kind)


def setup_inputs(seed: int = 0) -> dict:
    key_of = jax.random.split(jax.random.key(seed), 11)
    return {
        "hidden": gaussian_with(key_of[0], (MICRO, SEQS, SEQ_LEN, D), 1.0, 6.0, ((1, 8), (2, 4)), (1, 3, 8, 2.0)),
        "w_qkv": normal_values(key_of[1], (D, QKV), D ** -0.5, 0.25, ((0, 8),)),
        "b_qkv": normal_values(key_of[2], (QKV,), 0.5, 3.0, ((0, 8),)),
        "w_out": normal_values(key_of[3], (QW, D), (QW // 16) ** -0.5, 1.0, ((0, 8),)),
        "w_gate_up": normal_values(key_of[4], (D, 2 * FF), D ** -0.5, 0.25, ((0, 8),)),
        "w_down": normal_values(key_of[5], (FF, D), FF ** -0.5, 0.15625, ((0, 8),)),
        "norm_gains": jnp.clip(1.0 + 0.1 * jax.random.normal(key_of[6], (2, D), jnp.float32), 0.5, 1.5).astype(jnp.bfloat16),
        "segment_ids": draw_segment_ids(jax.random.fold_in(key_of[10], 71), 0),
        "token_counts": jax.random.randint(key_of[8], (MICRO,), TOKENS_MB // 2, TOKENS_MB + 1).astype(jnp.int32),
        "cotangent": normal_values(key_of[9], (MICRO, SEQS, SEQ_LEN, D), 1.0, 6.0, ((1, 8), (2, 4))),
    }


@jax.custom_vjp
def low(v):
    return lax.optimization_barrier(v.astype(jnp.bfloat16)).astype(jnp.float32)

@jax.custom_vjp
def low_back(v):
    return v

def low_keep(v):
    return (low(v), None)

def low_pass(kept, grad):
    return (grad,)

def back_keep(v):
    return (v, None)

def back_low(kept, grad):
    return (low(grad),)
low.defvjp(low_keep, low_pass)
low_back.defvjp(back_keep, back_low)
epsilon = 1e-05
rope_base = 100000.0
masked_value = -1000000000.0
highest = lax.Precision.HIGHEST

def frequencies():
    steps_half = jnp.arange(HEAD_DIM // 2, dtype=jnp.float32)
    return jnp.power(rope_base, -2.0 * steps_half / HEAD_DIM)

def rotary(values, angles):
    half_dim = values.shape[-1] // 2
    cosine = jnp.cos(angles)[:, :, None, :]
    sine_part = jnp.sin(angles)[:, :, None, :]
    leading = values[..., :half_dim]
    trailing = values[..., half_dim:]
    return jnp.concatenate([leading * cosine - trailing * sine_part, trailing * cosine + leading * sine_part], axis=-1)

def rms_norm(values, gain):
    factor = lax.rsqrt(lax.optimization_barrier(jnp.mean(values * values, axis=-1, keepdims=True)) + epsilon)
    return values * factor * gain

def forward_block(hidden, params, segments):
    w_qkv, b_qkv, w_out, w_gate_up, w_down, gains = params
    batch, length = (hidden.shape[0], hidden.shape[1])
    q_width = HEADS * HEAD_DIM
    k_width = KV_HEADS * HEAD_DIM
    group = HEADS // KV_HEADS
    normed = low(rms_norm(hidden, gains[0]))
    joined = low_back(jnp.einsum('bld,de->ble', normed, w_qkv, precision=highest) + b_qkv)
    angles = jnp.arange(length, dtype=jnp.float32)[:, None] * frequencies()[None, :]
    angles = jnp.broadcast_to(angles[None], (batch, length, HEAD_DIM // 2))
    queries = low(rotary(joined[..., :q_width].reshape(batch, length, HEADS, HEAD_DIM), angles))
    keys = low(rotary(joined[..., q_width:q_width + k_width].reshape(batch, length, KV_HEADS, HEAD_DIM), angles))
    values = low(joined[..., q_width + k_width:].reshape(batch, length, KV_HEADS, HEAD_DIM))
    grouped = queries.reshape(batch, length, KV_HEADS, group, HEAD_DIM)
    scores = jnp.einsum('bigrd,bjgd->bgrij', grouped, keys, precision=highest) * HEAD_DIM ** (-0.5)
    places = jnp.arange(length)
    allowed = (segments[:, :, None] == segments[:, None, :]) & (places[None, :, None] >= places[None, None, :])
    scores = low_back(jnp.where(allowed[:, None, None, :, :], scores, masked_value))
    top = lax.optimization_barrier(jnp.max(scores, axis=-1, keepdims=True))
    total = jnp.log(lax.optimization_barrier(jnp.sum(jnp.exp(scores - top), axis=-1, keepdims=True))) + top
    probs = low(jnp.exp(scores - total))
    attended = jnp.einsum('bgrij,bjgd->bigrd', probs, values, precision=highest).reshape(batch, length, q_width)
    attended = low(low_back(attended))
    branch = low_back(jnp.einsum('ble,ed->bld', attended, w_out, precision=highest))
    middle = hidden + branch
    normed_mid = low(rms_norm(middle, gains[1]))
    gate_up = low_back(jnp.einsum('bld,df->blf', normed_mid, w_gate_up, precision=highest))
    product = low(jax.nn.silu(gate_up[..., :FF]) * gate_up[..., FF:])
    feed = low_back(jnp.einsum('blf,fd->bld', product, w_down, precision=highest))
    return middle + feed

def reference(hidden, w_qkv, b_qkv, w_out, w_gate_up, w_down, norm_gains, segment_ids, token_counts, cotangent):
    params = tuple((entry.astype(jnp.float32) for entry in (w_qkv, b_qkv, w_out, w_gate_up, w_down, norm_gains)))
    group_size = 8 if SEQS % 8 == 0 else 1
    blocks = SEQS // group_size
    loss_weight = TOKENS_MB / token_counts.astype(jnp.float32)
    shape_in = (MICRO * blocks, group_size, SEQ_LEN, D)
    items = (hidden.reshape(shape_in), segment_ids.reshape(MICRO * blocks, group_size, SEQ_LEN), cotangent.reshape(shape_in), jnp.repeat(loss_weight, blocks))

    def visit(totals, item):
        block_rows, block_segments, block_cot, weight = item

        def forward_rows(rows_in, params_in):
            return forward_block(rows_in, params_in, block_segments)
        result, pullback = jax.vjp(forward_rows, block_rows.astype(jnp.float32), params)
        rows_grad, params_grad = pullback(block_cot.astype(jnp.float32) * weight)
        return (jax.tree.map(jnp.add, totals, params_grad), (result.astype(jnp.bfloat16), rows_grad))
    initial = tuple((jnp.zeros_like(entry) for entry in params))
    totals, (outputs, rows_grads) = lax.scan(visit, initial, items)
    shape_out = (MICRO, SEQS, SEQ_LEN, D)
    bias_total = totals[1]
    return (outputs.reshape(shape_out), rows_grads.reshape(shape_out), totals[0], bias_total[:QKW], bias_total[QKW:], totals[2], totals[3], totals[4], totals[5])
```

```python
import jax
import jax.numpy as jnp
import numpy as np
from jax import lax
from jax.sharding import PartitionSpec as P

HEADS = 9
KV_HEADS = 3
HEAD_DIM = 64
GROUP = HEADS // KV_HEADS
QW = HEADS * HEAD_DIM
KW = KV_HEADS * HEAD_DIM
EPS = 1e-05
ROPE_BASE = 100000.0
MASKED = -1000000000.0
BF = jnp.bfloat16
F32 = jnp.float32


def dot(a, b, ca, cb):
    return lax.dot_general(a, b, (((ca,), (cb,)), ((), ())), preferred_element_type=F32)


def rotary(values, cosine, sine):
    half = values.shape[-1] // 2
    a, b = values[..., :half], values[..., half:]
    return jnp.concatenate([a * cosine - b * sine, b * cosine + a * sine], axis=-1)


def norm_parts(values):
    factor = lax.rsqrt(jnp.mean(values * values, axis=-1, keepdims=True) + EPS)
    return factor, values * factor


def norm_back(grad_in, gain, factor, normed):
    scaled = grad_in * gain
    return factor * (scaled - normed * jnp.mean(scaled * normed, axis=-1, keepdims=True))


class Net:
    def __init__(self, n_fsdp, n_seq):
        self.n_fsdp, self.n_seq = n_fsdp, n_seq
        self.total = n_fsdp * n_seq
        f, s = lax.axis_index("fsdp"), lax.axis_index("seq")
        self.index = f * n_seq + s
        self.seq_bits = [1 << b for b in range(n_seq.bit_length() - 1)]
        self.fsdp_bits = [n_seq << b for b in range(n_fsdp.bit_length() - 1)]

    def swap(self, value, mask):
        pairs = [(i, i ^ mask) for i in range(self.total)]
        return lax.ppermute(value, ("fsdp", "seq"), pairs)

    def bit(self, mask):
        return (self.index & mask) != 0

    def both(self, mine, mask, axis):
        other = self.swap(mine, mask)
        high = self.bit(mask)
        return jnp.stack([jnp.where(high, other, mine), jnp.where(high, mine, other)], axis=axis)

    def half(self, value, mask, axis):
        return lax.dynamic_index_in_dim(
            value, self.bit(mask).astype(jnp.int32), axis, keepdims=False
        )

    def add_half(self, value, mask, axis):
        mine = self.bit(mask).astype(jnp.int32)
        keep = lax.dynamic_index_in_dim(value, mine, axis, keepdims=False)
        give = lax.dynamic_index_in_dim(value, 1 - mine, axis, keepdims=False)
        got = self.swap(give, mask)
        return (keep.astype(F32) + got.astype(F32)).astype(value.dtype)

    def gather_fsdp(self, value):
        for step, mask in enumerate(reversed(self.fsdp_bits)):
            value = self.both(value, mask, step)
        return value

    def scatter_fsdp(self, value, first_axis=0):
        count = len(self.fsdp_bits)
        for step, mask in enumerate(self.fsdp_bits):
            value = self.add_half(value, mask, first_axis + count - 1 - step)
        return value


def on_device(
    hidden, w_qkv, b_qkv, w_out, w_gate_up, w_down, norm_gains, segment_ids, token_counts, cotangent,
    n_fsdp, n_seq,
):
    net = Net(n_fsdp, n_seq)
    micro, batch, length, width = hidden.shape
    full_length = length * n_seq
    tokens_micro = batch * n_fsdp * full_length
    scale = HEAD_DIM ** (-0.5)
    rows = micro * batch * length
    d_rows = w_qkv.shape[0]
    ff_rows = w_down.shape[0]
    units = w_gate_up.shape[1] // 2
    qkv_w = w_qkv.shape[1]
    core = net.seq_bits[0]
    f_lead = (2,) * len(net.fsdp_bits)

    ids = segment_ids.reshape(rows, 1).astype(BF)
    block = jnp.concatenate(
        [hidden.reshape(rows, width), jnp.broadcast_to(ids, (rows, 64))], axis=1
    )
    blocks = block[None]
    for mask in reversed(net.seq_bits):
        blocks = jnp.concatenate([blocks, net.swap(blocks, mask)], axis=0)
    order = [0]
    for mask in reversed(net.seq_bits):
        order = order + [o ^ mask for o in order]
    seq_index = lax.axis_index("seq")
    block_ids = [seq_index ^ o for o in order]

    pad_rows = -(d_rows + 1) % 16 + 1
    extra = jnp.zeros((pad_rows, qkv_w), BF)
    small = jnp.concatenate([b_qkv, norm_gains.reshape(-1)])
    extra = extra.at[0, : small.shape[0]].set(small)
    shard_a = jnp.concatenate([w_qkv, extra], axis=0).reshape(2, -1, qkv_w)
    got_a = net.gather_fsdp(net.half(shard_a, core, 0))
    full_a = net.both(got_a, core, len(f_lead)).reshape(n_fsdp, d_rows + pad_rows, qkv_w)
    wf_qkv = full_a[:, :d_rows].reshape(n_fsdp * d_rows, qkv_w)
    smalls = full_a[:, d_rows]
    n_bias = b_qkv.shape[0]
    bias = smalls[:, :n_bias].reshape(-1).astype(F32)
    gains = smalls[:, n_bias : n_bias + 2 * d_rows].reshape(n_fsdp, 2, d_rows).astype(F32)
    gain_one = gains[:, 0].reshape(-1)
    gain_two = gains[:, 1].reshape(-1)

    pad_b = -(d_rows + ff_rows) % 16
    shard_b = jnp.concatenate([w_out, w_down, jnp.zeros((pad_b, width), BF)], axis=0)
    shard_b = shard_b.reshape(2, -1, width)
    got_b = net.gather_fsdp(net.half(shard_b, core, 0))

    parts = n_seq
    shard_c = w_gate_up.reshape(d_rows, parts, -1)
    got_c = net.gather_fsdp(lax.dynamic_index_in_dim(shard_c, seq_index, 1, keepdims=False))
    full_b = net.both(got_b, core, len(f_lead)).reshape(n_fsdp, -1, width)
    wf_out = full_b[:, :d_rows].reshape(n_fsdp * d_rows, width)
    wf_down = full_b[:, d_rows : d_rows + ff_rows].reshape(n_fsdp * ff_rows, width)
    got_c = got_c.reshape(n_fsdp * d_rows, -1)
    for mask in reversed(net.seq_bits):
        got_c = net.both(got_c, mask, got_c.ndim - 1)
    wf_gate_up = got_c.reshape(n_fsdp * d_rows, 2 * units)

    places = np.arange(full_length, dtype=np.float32)
    speeds = np.power(ROPE_BASE, -2.0 * np.arange(HEAD_DIM // 2, dtype=np.float32) / HEAD_DIM)
    angles = places[:, None] * speeds.astype(np.float32)[None, :]
    cos_all = jnp.asarray(np.cos(angles).reshape(n_seq, length, -1))
    sin_all = jnp.asarray(np.sin(angles).reshape(n_seq, length, -1))
    cos_b = jnp.stack([lax.dynamic_index_in_dim(cos_all, b, 0, keepdims=False) for b in block_ids])
    sin_b = jnp.stack([lax.dynamic_index_in_dim(sin_all, b, 0, keepdims=False) for b in block_ids])

    seqs = micro * batch
    all_rows = blocks[..., :width].reshape(n_seq * rows, width)
    source_all = all_rows.astype(F32)
    scale_all, normed_all = norm_parts(source_all)
    first_all = (normed_all * gain_one).astype(BF)
    source, scale_one, normed_one = source_all[:rows], scale_all[:rows], normed_all[:rows]
    first_own = first_all[:rows]
    joined_q = dot(first_own, wf_qkv[:, :QW], 1, 0) + bias[:QW]
    joined_kv = dot(first_all, wf_qkv[:, QW:], 1, 0) + bias[QW:]
    queries = rotary(
        joined_q.reshape(seqs, length, HEADS, HEAD_DIM), cos_b[0][:, None], sin_b[0][:, None]
    ).astype(BF)
    keys = rotary(
        joined_kv[:, :KW].reshape(n_seq, seqs, length, KV_HEADS, HEAD_DIM),
        cos_b[:, None, :, None],
        sin_b[:, None, :, None],
    ).astype(BF)
    values = joined_kv[:, KW:].reshape(n_seq, seqs, length, KV_HEADS, HEAD_DIM).astype(BF)
    seg_all = blocks[..., width].reshape(n_seq, seqs, length)
    seg_own = seg_all[0]
    own_places = seq_index * length + jnp.arange(length, dtype=jnp.int32)
    key_places = jnp.stack(block_ids)[:, None] * length + jnp.arange(length, dtype=jnp.int32)
    allowed = (seg_own[:, :, None, None] == seg_all.transpose(1, 0, 2)[:, None]) & (
        own_places[None, :, None, None] >= key_places[None, None]
    )
    allowed = allowed.reshape(seqs, 1, 1, length, full_length)
    grouped = queries.reshape(seqs, length, KV_HEADS, GROUP, HEAD_DIM)
    keys_s = keys.transpose(1, 0, 2, 3, 4).reshape(seqs, full_length, KV_HEADS, HEAD_DIM)
    values_s = values.transpose(1, 0, 2, 3, 4).reshape(seqs, full_length, KV_HEADS, HEAD_DIM)
    raw = jnp.einsum("bigrd,bjgd->bgrij", grouped, keys_s, preferred_element_type=F32) * scale
    scores = jnp.where(allowed, raw, MASKED)
    top = jnp.max(scores, axis=-1, keepdims=True)
    total = jnp.log(jnp.sum(jnp.exp(scores - top), axis=-1, keepdims=True)) + top
    probs_full = jnp.exp(scores - total)
    probs = probs_full.astype(BF)
    attended = jnp.einsum("bgrij,bjgd->bigrd", probs, values_s, preferred_element_type=F32)
    attended = attended.reshape(rows, QW).astype(BF)

    middle = source + dot(attended, wf_out, 1, 0)
    scale_two, normed_two = norm_parts(middle)
    second_in = (normed_two * gain_two).astype(BF)
    gate_up = dot(second_in, wf_gate_up, 1, 0)
    gate, up_part = gate_up[:, :units], gate_up[:, units:]
    sig = jax.nn.sigmoid(gate)
    activated = gate * sig
    product = (activated * up_part).astype(BF)
    feed = dot(product, wf_down, 1, 0)
    block_out = (middle + feed).astype(BF).reshape(hidden.shape)

    weight = tokens_micro / token_counts.astype(F32)
    out_grad = (cotangent.astype(F32) * weight[:, None, None, None]).reshape(rows, width)
    feed_grad = out_grad.astype(BF)
    down_grad = dot(product, feed_grad, 0, 0).astype(BF)
    product_grad = dot(feed_grad, wf_down, 1, 1)
    gate_grad = product_grad * up_part * (sig * (1.0 + gate * (1.0 - sig)))
    up_grad = product_grad * activated
    gate_up_grad = jnp.concatenate([gate_grad, up_grad], axis=-1).astype(BF)
    gate_up_wgrad = dot(second_in, gate_up_grad, 0, 0).astype(BF)
    second_grad = dot(gate_up_grad, wf_gate_up, 1, 1)
    gain_two_grad = jnp.sum(second_grad * normed_two, axis=0)
    middle_grad = out_grad + norm_back(second_grad, gain_two, scale_two, normed_two)
    branch_grad = middle_grad.astype(BF)
    out_wgrad = dot(attended, branch_grad, 0, 0).astype(BF)
    attended_grad = dot(branch_grad, wf_out, 1, 1).astype(BF)

    def seq_axes(value, axis, masks):
        for mask in masks:
            value = net.add_half(value, mask, axis)
        return value

    quarter = (2,) * len(net.seq_bits)
    n_f = len(f_lead)
    red_down = down_grad.reshape(f_lead + quarter + (ff_rows // n_seq, width))
    for step, mask in enumerate(net.seq_bits):
        red_down = net.add_half(red_down, mask, n_f + len(quarter) - 1 - step)
    red_down = net.scatter_fsdp(red_down)

    red_gate = gate_up_wgrad.reshape(f_lead + (d_rows,) + quarter + (2 * units // n_seq,))
    red_gate = net.add_half(red_gate, core, n_f + len(quarter))
    red_gate = net.add_half(red_gate, net.fsdp_bits[0], n_f - 1)
    for step, mask in enumerate(net.seq_bits[1:]):
        red_gate = net.add_half(red_gate, mask, n_f - 1 + len(quarter) - 1 - step)
    for step, mask in enumerate(net.fsdp_bits[1:]):
        red_gate = net.add_half(red_gate, mask, n_f - 2 - step)

    agrad = attended_grad.reshape(seqs, length, KV_HEADS, GROUP, HEAD_DIM)
    value_grad = jnp.einsum("bgrij,bigrd->bjgd", probs, agrad, preferred_element_type=F32)
    prob_grad = jnp.einsum("bigrd,bjgd->bgrij", agrad, values_s, preferred_element_type=F32)
    inner = jnp.sum(probs_full * prob_grad, axis=-1, keepdims=True)
    score_grad = (probs_full * (prob_grad - inner)).astype(BF)
    query_grad = (
        jnp.einsum("bgrij,bjgd->bigrd", score_grad, keys_s, preferred_element_type=F32) * scale
    )
    key_grad = (
        jnp.einsum("bgrij,bigrd->bjgd", score_grad, grouped, preferred_element_type=F32) * scale
    )
    query_back = rotary(
        query_grad.reshape(seqs, length, HEADS, HEAD_DIM), cos_b[0][:, None], -sin_b[0][:, None]
    )
    query_back = query_back.reshape(rows, QW).astype(BF)
    key_part = key_grad.reshape(seqs, n_seq, length, KV_HEADS, HEAD_DIM).transpose(1, 0, 2, 3, 4)
    key_back = rotary(key_part, cos_b[:, None, :, None], -sin_b[:, None, :, None])
    value_part = value_grad.reshape(seqs, n_seq, length, KV_HEADS, HEAD_DIM).transpose(1, 0, 2, 3, 4)
    kv_part = jnp.concatenate(
        [key_back.reshape(n_seq, rows, KW), value_part.reshape(n_seq, rows, KW)], axis=-1
    ).astype(BF)
    kv_sum = kv_part[0].astype(F32)
    for place, mask in enumerate(order):
        if mask:
            kv_sum = kv_sum + net.swap(kv_part[place], mask).astype(F32)
    kv_own = kv_sum.astype(BF)

    kv_flat = kv_part.reshape(n_seq * rows, 2 * KW)
    q_wgrad = dot(first_own, query_back, 0, 0)
    kv_wgrad = dot(first_all, kv_flat, 0, 0)
    bias_grad = jnp.concatenate(
        [jnp.sum(query_back.astype(F32), axis=0), jnp.sum(kv_flat.astype(F32), axis=0)]
    )
    joined_grad = jnp.concatenate([query_back, kv_own], axis=-1)
    first_grad = dot(joined_grad, wf_qkv, 1, 1)
    gain_one_grad = jnp.sum(first_grad * normed_one, axis=0)
    hidden_grad = middle_grad + norm_back(first_grad, gain_one, scale_one, normed_one)
    hidden_grad = hidden_grad.reshape(hidden.shape)

    qk_rows, v_rows = (QW + KW) // n_fsdp, KW // n_fsdp
    small_grads = jnp.concatenate(
        [
            bias_grad[: QW + KW].reshape(n_fsdp, qk_rows),
            bias_grad[QW + KW :].reshape(n_fsdp, v_rows),
            gain_one_grad.reshape(n_fsdp, d_rows),
            gain_two_grad.reshape(n_fsdp, d_rows),
        ],
        axis=1,
    ).astype(BF)
    wide = qkv_w + width
    small_pad = jnp.zeros((n_fsdp, pad_rows, wide), BF)
    small_pad = small_pad.at[:, 0, : small_grads.shape[1]].set(small_grads)
    rest = jnp.concatenate([q_wgrad.astype(BF), kv_wgrad.astype(BF), out_wgrad], axis=1)
    rest = jnp.concatenate([rest.reshape(n_fsdp, d_rows, wide), small_pad], axis=1)
    rest = rest.reshape(f_lead + (d_rows + pad_rows,) + quarter + (wide // n_seq,))
    for step, mask in enumerate(net.seq_bits):
        rest = net.add_half(rest, mask, n_f + 1 + len(quarter) - 1 - step)
    rest = net.scatter_fsdp(rest)

    def seq_back(value, axis):
        for step, mask in enumerate(reversed(net.seq_bits)):
            value = net.both(value, mask, axis + step)
        return value

    out_down = seq_back(red_down, 0).reshape(ff_rows, width).astype(F32)
    out_gate = seq_back(red_gate, 1).reshape(d_rows, 2 * units).astype(F32)
    out_rest = seq_back(rest, 1).reshape(d_rows + pad_rows, wide).astype(F32)
    line = out_rest[d_rows]
    edge = qk_rows + v_rows
    return (
        block_out,
        hidden_grad,
        out_rest[:d_rows, :qkv_w],
        line[:qk_rows],
        line[qk_rows:edge],
        out_rest[:d_rows, qkv_w:],
        out_gate,
        out_down,
        line[edge : edge + 2 * d_rows].reshape(2, d_rows),
    )


def solution(mesh):
    n_fsdp, n_seq = mesh.shape["fsdp"], mesh.shape["seq"]
    in_specs = (
        P(None, "fsdp", "seq", None),
        P("fsdp", None),
        P("fsdp"),
        P("fsdp", None),
        P("fsdp", None),
        P("fsdp", None),
        P(None, "fsdp"),
        P(None, "fsdp", "seq"),
        P(),
        P(None, "fsdp", "seq", None),
    )
    out_specs = (
        P(None, "fsdp", "seq", None),
        P(None, "fsdp", "seq", None),
        P("fsdp", None),
        P("fsdp"),
        P("fsdp"),
        P("fsdp", None),
        P("fsdp", None),
        P("fsdp", None),
        P(None, "fsdp"),
    )

    def local(*args):
        return on_device(*args, n_fsdp=n_fsdp, n_seq=n_seq)

    return jax.shard_map(local, mesh=mesh, in_specs=in_specs, out_specs=out_specs, check_vma=False)
```

```python
import functools

import jax
import jax.numpy as jnp
import numpy as np
from jax import lax
from jax.experimental import pallas as pl
from jax.experimental.pallas import tpu as pltpu
from jax.sharding import PartitionSpec as P

HEADS = 9
KV_HEADS = 3
HEAD_DIM = 64
GROUP = HEADS // KV_HEADS
QW = HEADS * HEAD_DIM
KW = KV_HEADS * HEAD_DIM
EPS = 1e-05
ROPE_BASE = 100000.0
MASKED = -1000000000.0
BF = jnp.bfloat16
F32 = jnp.float32


def dot(a, b, ca, cb):
    return lax.dot_general(a, b, (((ca,), (cb,)), ((), ())), preferred_element_type=F32)


def rotary(values, cosine, sine):
    half = values.shape[-1] // 2
    a, b = values[..., :half], values[..., half:]
    return jnp.concatenate([a * cosine - b * sine, b * cosine + a * sine], axis=-1)


def norm_parts(values):
    factor = lax.rsqrt(jnp.mean(values * values, axis=-1, keepdims=True) + EPS)
    return factor, values * factor


def norm_back(grad_in, gain, factor, normed):
    scaled = grad_in * gain
    return factor * (scaled - normed * jnp.mean(scaled * normed, axis=-1, keepdims=True))


def whole(*shape_dtypes):
    return [pl.BlockSpec(memory_space=pltpu.VMEM) for _ in shape_dtypes]


def call(kernel, scalars, arrays, outs, flops):
    specs = [pl.BlockSpec(memory_space=pltpu.SMEM)] * len(scalars) + whole(*arrays)
    moved = sum(a.size * a.dtype.itemsize for a in arrays) + sum(
        int(np.prod(o.shape)) * o.dtype.itemsize for o in outs
    )
    return pl.pallas_call(
        kernel,
        out_shape=outs,
        in_specs=specs,
        out_specs=whole(*outs),
        compiler_params=pltpu.CompilerParams(vmem_limit_bytes=52 * 1024 * 1024),
        cost_estimate=pl.CostEstimate(flops=flops, bytes_accessed=moved, transcendentals=0),
    )(*scalars, *arrays)


def sds(shape, dtype):
    return jax.ShapeDtypeStruct(shape, dtype)


def turn(x, cosine, sine):
    tiles = []
    low = lax.broadcasted_iota(jnp.int32, (1, 128), 1) % HEAD_DIM < HEAD_DIM // 2
    for t in range(x.shape[1] // 128):
        part = x[:, 128 * t : 128 * t + 128]
        other = jnp.where(low, pltpu.roll(part, 96, 1), pltpu.roll(part, 32, 1))
        tiles.append(part * cosine + other * sine)
    return tiles


def turn_kv(x, cosine, sine):
    lane = lax.broadcasted_iota(jnp.int32, (1, 128), 1)
    first, second = turn(x[:, :256], cosine, sine)
    second = jnp.where(lane < KW - 128, second, x[:, 128:256])
    return jnp.concatenate([first, second, x[:, 256:]], axis=1)


def tables(seq, order, cos_ref, sin_ref):
    cosine = jnp.concatenate([cos_ref[seq ^ o] for o in order], axis=0)
    sine = jnp.concatenate([sin_ref[seq ^ o] for o in order], axis=0)
    return cosine, sine


def heads_to_rows(x, g):
    return jnp.concatenate(
        [x[:, HEAD_DIM * h : HEAD_DIM * (h + 1)] for h in range(GROUP * g, GROUP * (g + 1))], axis=0
    )


def rows_to_heads(parts, length):
    return jnp.concatenate(
        [p[length * r : length * (r + 1)] for p in parts for r in range(GROUP)], axis=1
    )


def attention_forward(order, length, seq_ref, blocks, wq, wkv, bq, bkv, gain, cos, sin, mask,
                      att_o, q_o, k_o, v_o, lse_o):
    seq = seq_ref[0]
    cosine, sine = tables(seq, order, cos, sin)
    width = gain.shape[1]
    for b in range(blocks.shape[1] // length):
        x = blocks[:, b * length : (b + 1) * length, :width].astype(F32)
        x = x.reshape(len(order) * length, width)
        first = (norm_parts(x)[1] * gain[...]).astype(BF)
        kv = dot(first, wkv[...], 1, 0) + bkv[...]
        q = dot(first[:length], wq[...], 1, 0) + bq[...]
        q = jnp.concatenate(turn(q, cosine[:length], sine[:length]), axis=1).astype(BF)
        q = q * jnp.asarray(HEAD_DIM ** (-0.5), BF)
        kv = turn_kv(kv, cosine, sine).astype(BF)
        allowed = jnp.concatenate([mask[b]] * GROUP, axis=0) > 0.0
        parts = []
        for g in range(KV_HEADS):
            qg = heads_to_rows(q, g)
            kg = kv[:, HEAD_DIM * g : HEAD_DIM * (g + 1)]
            vg = kv[:, KW + HEAD_DIM * g : KW + HEAD_DIM * (g + 1)]
            q_o[b, g] = qg
            k_o[b, g] = kg
            v_o[b, g] = vg
            scores = jnp.where(allowed, dot(qg, kg, 1, 1), MASKED)
            top = jnp.max(scores, axis=-1, keepdims=True)
            e = jnp.exp(scores - top)
            total = jnp.sum(e, axis=-1, keepdims=True)
            lse_o[b, g] = jnp.log(total) + top
            probs = (e * (1.0 / total)).astype(BF)
            parts.append(dot(probs, vg, 1, 0))
        att_o[b * length : (b + 1) * length, :] = rows_to_heads(parts, length).astype(BF)


def feed_forward(attended, source, wo, wgu, wd, gain, cot, weight,
                 out_o, down_o, gu_o, mid_o, wout_o, attg_o, gain_o):
    units = wd.shape[0]
    step = units // 3
    att = attended[...]
    middle = source[...].astype(F32) + dot(att, wo[...], 1, 0)
    scale_two, normed = norm_parts(middle)
    g2 = gain[...]
    second = (normed * g2).astype(BF)
    out_grad = cot[...].astype(F32) * weight[...]
    feed_grad = out_grad.astype(BF)
    feed = None
    back = None
    for j in range(0, units, step):
        wg = wgu[:, j : j + step]
        wu = wgu[:, units + j : units + j + step]
        wdj = wd[j : j + step, :]
        gate = dot(second, wg, 1, 0)
        up = dot(second, wu, 1, 0)
        sig = jax.nn.sigmoid(gate)
        act = gate * sig
        product = (act * up).astype(BF)
        part = dot(product, wdj, 1, 0)
        feed = part if feed is None else feed + part
        down_o[j : j + step, :] = dot(product, feed_grad, 0, 0).astype(BF)
        pgrad = dot(feed_grad, wdj, 1, 1)
        ggrad = (pgrad * up * (sig * (1.0 + gate * (1.0 - sig)))).astype(BF)
        ugrad = (pgrad * act).astype(BF)
        gu_o[:, j : j + step] = dot(second, ggrad, 0, 0).astype(BF)
        gu_o[:, units + j : units + j + step] = dot(second, ugrad, 0, 0).astype(BF)
        part = dot(ggrad, wg, 1, 1) + dot(ugrad, wu, 1, 1)
        back = part if back is None else back + part
    out_o[...] = (middle + feed).astype(BF)
    gain_o[...] = jnp.sum(back * normed, axis=0, keepdims=True)
    middle_grad = out_grad + norm_back(back, g2, scale_two, normed)
    mid_o[...] = middle_grad
    branch = middle_grad.astype(BF)
    wout_o[...] = dot(att, branch, 0, 0).astype(BF)
    attg_o[...] = dot(branch, wo[...], 1, 1).astype(BF)


def attention_backward(order, length, seq_ref, blocks, wq, wkv, gain, cos, sin, mask, q_i, k_i, v_i,
                       lse, attg, dq_o, dkv_o, wgrad_o, bias_o, gain_o):
    seq = seq_ref[0]
    cosine, sine = tables(seq, order, cos, sin)
    width = gain.shape[1]
    q_wgrad = kv_wgrad = bias_q = bias_kv = gain_sum = None
    for b in range(blocks.shape[1] // length):
        x = blocks[:, b * length : (b + 1) * length, :width].astype(F32)
        x = x.reshape(len(order) * length, width)
        normed = norm_parts(x)[1]
        first = (normed * gain[...]).astype(BF)
        allowed = jnp.concatenate([mask[b]] * GROUP, axis=0) > 0.0
        ag = attg[b * length : (b + 1) * length, :]
        dqs, dks, dvs = [], [], []
        for g in range(KV_HEADS):
            qg, kg, vg = q_i[b, g], k_i[b, g], v_i[b, g]
            agg = heads_to_rows(ag, g)
            p = jnp.exp(jnp.where(allowed, dot(qg, kg, 1, 1), MASKED) - lse[b, g])
            dvs.append(dot(p.astype(BF), agg, 0, 0))
            pg = dot(agg, vg, 1, 1)
            inner = jnp.sum(p * pg, axis=-1, keepdims=True)
            ds = (p * (pg - inner)).astype(BF)
            dqs.append(dot(ds, kg, 1, 0) * HEAD_DIM ** (-0.5))
            dks.append(dot(ds, qg, 0, 0))
        dq = rows_to_heads(dqs, length)
        dq = jnp.concatenate([dq, jnp.zeros((length, 64), F32)], axis=1)
        dq = jnp.concatenate(turn(dq, cosine[:length], -sine[:length]), axis=1).astype(BF)
        dkv = jnp.concatenate(dks + dvs, axis=1)
        dkv = turn_kv(dkv, cosine, -sine).astype(BF)
        dq_o[b * length : (b + 1) * length, :] = dq
        for r in range(len(order)):
            dkv_o[r, b * length : (b + 1) * length, :] = dkv[r * length : (r + 1) * length, :]
        wq_part = dot(first[:length], dq, 0, 0)
        wkv_part = dot(first, dkv, 0, 0)
        bq_part = jnp.sum(dq.astype(F32), axis=0, keepdims=True)
        bkv_part = jnp.sum(dkv.astype(F32), axis=0, keepdims=True)
        e_kv = dot(dkv, wkv[...], 1, 1) * normed
        e_q = dot(dq[:, :QW], wq[:, :QW], 1, 1) * normed[:length]
        g_part = jnp.sum(e_kv, axis=0, keepdims=True) + jnp.sum(e_q, axis=0, keepdims=True)
        if q_wgrad is None:
            q_wgrad, kv_wgrad, bias_q, bias_kv, gain_sum = wq_part, wkv_part, bq_part, bkv_part, g_part
        else:
            q_wgrad, kv_wgrad = q_wgrad + wq_part, kv_wgrad + wkv_part
            bias_q, bias_kv, gain_sum = bias_q + bq_part, bias_kv + bkv_part, gain_sum + g_part
    wgrad_o[...] = jnp.concatenate([q_wgrad[:, :QW], kv_wgrad], axis=1).astype(BF)
    bias_o[...] = jnp.concatenate([bias_q[:, :QW], bias_kv], axis=1)
    gain_o[...] = gain_sum


def input_gradient(dq, own, a, b, c, source, mid, wq, wkv, gain, out_o):
    kv = own[...].astype(F32) + a[...].astype(F32) + b[...].astype(F32) + c[...].astype(F32)
    first_grad = dot(dq[:, :QW], wq[:, :QW], 1, 1) + dot(kv.astype(BF), wkv[...], 1, 1)
    scale_one, normed = norm_parts(source[...].astype(F32))
    out_o[...] = mid[...] + norm_back(first_grad, gain[...], scale_one, normed)


class Net:
    def __init__(self, n_fsdp, n_seq):
        self.n_fsdp, self.n_seq = n_fsdp, n_seq
        self.total = n_fsdp * n_seq
        f, s = lax.axis_index("fsdp"), lax.axis_index("seq")
        self.index = f * n_seq + s
        self.seq_bits = [1 << b for b in range(n_seq.bit_length() - 1)]
        self.fsdp_bits = [n_seq << b for b in range(n_fsdp.bit_length() - 1)]

    def swap(self, value, mask):
        pairs = [(i, i ^ mask) for i in range(self.total)]
        return lax.ppermute(value, ("fsdp", "seq"), pairs)

    def bit(self, mask):
        return (self.index & mask) != 0

    def both(self, mine, mask, axis):
        other = self.swap(mine, mask)
        high = self.bit(mask)
        return jnp.stack([jnp.where(high, other, mine), jnp.where(high, mine, other)], axis=axis)

    def half(self, value, mask, axis):
        return lax.dynamic_index_in_dim(
            value, self.bit(mask).astype(jnp.int32), axis, keepdims=False
        )

    def add_half(self, value, mask, axis):
        mine = self.bit(mask).astype(jnp.int32)
        keep = lax.dynamic_index_in_dim(value, mine, axis, keepdims=False)
        give = lax.dynamic_index_in_dim(value, 1 - mine, axis, keepdims=False)
        got = self.swap(give, mask)
        return (keep.astype(F32) + got.astype(F32)).astype(value.dtype)

    def gather_fsdp(self, value):
        for step, mask in enumerate(reversed(self.fsdp_bits)):
            value = self.both(value, mask, step)
        return value

    def scatter_fsdp(self, value, first_axis=0):
        count = len(self.fsdp_bits)
        for step, mask in enumerate(self.fsdp_bits):
            value = self.add_half(value, mask, first_axis + count - 1 - step)
        return value


def on_device(
    hidden, w_qkv, b_qkv, w_out, w_gate_up, w_down, norm_gains, segment_ids, token_counts, cotangent,
    n_fsdp, n_seq,
):
    net = Net(n_fsdp, n_seq)
    micro, batch, length, width = hidden.shape
    full_length = length * n_seq
    tokens_micro = batch * n_fsdp * full_length
    scale = HEAD_DIM ** (-0.5)
    rows = micro * batch * length
    d_rows = w_qkv.shape[0]
    ff_rows = w_down.shape[0]
    units = w_gate_up.shape[1] // 2
    qkv_w = w_qkv.shape[1]
    core = net.seq_bits[0]
    f_lead = (2,) * len(net.fsdp_bits)

    ids = segment_ids.reshape(rows, 1).astype(BF)
    block = jnp.concatenate(
        [hidden.reshape(rows, width), jnp.broadcast_to(ids, (rows, 64))], axis=1
    )
    blocks = block[None]
    for mask in reversed(net.seq_bits):
        blocks = jnp.concatenate([blocks, net.swap(blocks, mask)], axis=0)
    order = [0]
    for mask in reversed(net.seq_bits):
        order = order + [o ^ mask for o in order]
    seq_index = lax.axis_index("seq")
    block_ids = [seq_index ^ o for o in order]

    pad_rows = -(d_rows + 1) % 16 + 1
    extra = jnp.zeros((pad_rows, qkv_w), BF)
    small = jnp.concatenate([b_qkv, norm_gains.reshape(-1)])
    extra = extra.at[0, : small.shape[0]].set(small)
    shard_a = jnp.concatenate([w_qkv, extra], axis=0).reshape(2, -1, qkv_w)
    got_a = net.gather_fsdp(net.half(shard_a, core, 0))
    full_a = net.both(got_a, core, len(f_lead)).reshape(n_fsdp, d_rows + pad_rows, qkv_w)
    wf_qkv = full_a[:, :d_rows].reshape(n_fsdp * d_rows, qkv_w)
    smalls = full_a[:, d_rows]
    n_bias = b_qkv.shape[0]
    bias = smalls[:, :n_bias].reshape(-1).astype(F32)
    gains = smalls[:, n_bias : n_bias + 2 * d_rows].reshape(n_fsdp, 2, d_rows).astype(F32)
    gain_one = gains[:, 0].reshape(-1)
    gain_two = gains[:, 1].reshape(-1)

    pad_b = -(d_rows + ff_rows) % 16
    shard_b = jnp.concatenate([w_out, w_down, jnp.zeros((pad_b, width), BF)], axis=0)
    shard_b = shard_b.reshape(2, -1, width)
    got_b = net.gather_fsdp(net.half(shard_b, core, 0))

    parts = n_seq
    shard_c = w_gate_up.reshape(d_rows, parts, -1)
    got_c = net.gather_fsdp(lax.dynamic_index_in_dim(shard_c, seq_index, 1, keepdims=False))
    full_b = net.both(got_b, core, len(f_lead)).reshape(n_fsdp, -1, width)
    wf_out = full_b[:, :d_rows].reshape(n_fsdp * d_rows, width)
    wf_down = full_b[:, d_rows : d_rows + ff_rows].reshape(n_fsdp * ff_rows, width)
    got_c = got_c.reshape(n_fsdp * d_rows, -1)
    for mask in reversed(net.seq_bits):
        got_c = net.both(got_c, mask, got_c.ndim - 1)
    wf_gate_up = got_c.reshape(n_fsdp * d_rows, 2 * units)

    places = np.arange(full_length, dtype=np.float32)
    speeds = np.power(ROPE_BASE, -2.0 * np.arange(HEAD_DIM // 2, dtype=np.float32) / HEAD_DIM)
    angles = places[:, None] * speeds.astype(np.float32)[None, :]
    cos_t = np.tile(np.cos(angles), (1, 4)).reshape(n_seq, length, 128)
    sin_t = np.concatenate([-np.sin(angles), np.sin(angles)] * 2, axis=1).reshape(n_seq, length, 128)
    cos_t, sin_t = jnp.asarray(cos_t, F32), jnp.asarray(sin_t, F32)
    seqs = micro * batch
    seg_all = blocks[..., width].reshape(n_seq, seqs, length).transpose(1, 0, 2)
    own_places = seq_index * length + jnp.arange(length, dtype=jnp.int32)
    key_places = jnp.stack(block_ids)[:, None] * length + jnp.arange(length, dtype=jnp.int32)
    allowed = (seg_all[:, 0, :, None] == seg_all.reshape(seqs, 1, -1)) & (
        own_places[None, :, None] >= key_places.reshape(1, 1, -1)
    )
    allowed = allowed.astype(F32)
    seq_scalar = seq_index.astype(jnp.int32).reshape(1)
    wq, wkv = wf_qkv[:, : QW + 64], wf_qkv[:, QW:]
    gain_one, gain_two = gain_one[None], gain_two[None]
    source = hidden.reshape(rows, width)
    n_all = n_seq * rows
    attended, q_s, k_s, v_s, lse = call(
        functools.partial(attention_forward, order, length),
        [seq_scalar],
        [blocks, wq, wkv, bias[None, : QW + 64], bias[None, QW:], gain_one, cos_t, sin_t, allowed],
        [
            sds((rows, QW), BF),
            sds((seqs, KV_HEADS, GROUP * length, HEAD_DIM), BF),
            sds((seqs, KV_HEADS, full_length, HEAD_DIM), BF),
            sds((seqs, KV_HEADS, full_length, HEAD_DIM), BF),
            sds((seqs, KV_HEADS, GROUP * length, 1), F32),
        ],
        2 * n_all * width * 2 * KW + 2 * rows * width * QW + 4 * rows * full_length * QW,
    )

    weight = tokens_micro / token_counts.astype(F32)
    weight = jnp.repeat(weight, batch * length)[:, None]
    block_out, down_grad, gate_up_wgrad, middle_grad, out_wgrad, attended_grad, gain_two_grad = call(
        feed_forward,
        [],
        [attended, source, wf_out, wf_gate_up, wf_down, gain_two, cotangent.reshape(rows, width), weight],
        [
            sds((rows, width), BF),
            sds((units, width), BF),
            sds((width, 2 * units), BF),
            sds((rows, width), F32),
            sds((QW, width), BF),
            sds((rows, QW), BF),
            sds((1, width), F32),
        ],
        6 * rows * width * 3 * units + 6 * rows * width * QW,
    )
    block_out = block_out.reshape(hidden.shape)

    def seq_axes(value, axis, masks):
        for mask in masks:
            value = net.add_half(value, mask, axis)
        return value

    quarter = (2,) * len(net.seq_bits)
    n_f = len(f_lead)
    red_down = down_grad.reshape(f_lead + quarter + (ff_rows // n_seq, width))
    for step, mask in enumerate(net.seq_bits):
        red_down = net.add_half(red_down, mask, n_f + len(quarter) - 1 - step)
    red_down = net.scatter_fsdp(red_down)

    red_gate = gate_up_wgrad.reshape(f_lead + (d_rows,) + quarter + (2 * units // n_seq,))
    red_gate = net.add_half(red_gate, core, n_f + len(quarter))
    red_gate = net.add_half(red_gate, net.fsdp_bits[0], n_f - 1)
    for step, mask in enumerate(net.seq_bits[1:]):
        red_gate = net.add_half(red_gate, mask, n_f - 1 + len(quarter) - 1 - step)
    for step, mask in enumerate(net.fsdp_bits[1:]):
        red_gate = net.add_half(red_gate, mask, n_f - 2 - step)

    dq, dkv, qkv_wgrad, bias_grad, gain_one_grad = call(
        functools.partial(attention_backward, order, length),
        [seq_scalar],
        [blocks, wq, wkv, gain_one, cos_t, sin_t, allowed, q_s, k_s, v_s, lse, attended_grad],
        [
            sds((rows, QW + 64), BF),
            sds((n_seq, rows, 2 * KW), BF),
            sds((width, qkv_w), BF),
            sds((1, qkv_w), F32),
            sds((1, width), F32),
        ],
        4 * n_all * width * 2 * KW + 4 * rows * width * QW + 10 * rows * full_length * QW,
    )
    kv_parts = [dkv[0]]
    for place, mask_bits in enumerate(order):
        if mask_bits:
            kv_parts.append(net.swap(dkv[place], mask_bits))
    (hidden_grad,) = call(
        input_gradient,
        [],
        [dq, *kv_parts, source, middle_grad, wq, wkv, gain_one],
        [sds((rows, width), F32)],
        2 * rows * width * qkv_w,
    )
    hidden_grad = hidden_grad.reshape(hidden.shape)
    bias_grad, gain_one_grad, gain_two_grad = bias_grad[0], gain_one_grad[0], gain_two_grad[0]

    qk_rows, v_rows = (QW + KW) // n_fsdp, KW // n_fsdp
    small_grads = jnp.concatenate(
        [
            bias_grad[: QW + KW].reshape(n_fsdp, qk_rows),
            bias_grad[QW + KW :].reshape(n_fsdp, v_rows),
            gain_one_grad.reshape(n_fsdp, d_rows),
            gain_two_grad.reshape(n_fsdp, d_rows),
        ],
        axis=1,
    ).astype(BF)
    wide = qkv_w + width
    small_pad = jnp.zeros((n_fsdp, pad_rows, wide), BF)
    small_pad = small_pad.at[:, 0, : small_grads.shape[1]].set(small_grads)
    rest = jnp.concatenate([qkv_wgrad, out_wgrad], axis=1)
    rest = jnp.concatenate([rest.reshape(n_fsdp, d_rows, wide), small_pad], axis=1)
    rest = rest.reshape(f_lead + (d_rows + pad_rows,) + quarter + (wide // n_seq,))
    for step, mask in enumerate(net.seq_bits):
        rest = net.add_half(rest, mask, n_f + 1 + len(quarter) - 1 - step)
    rest = net.scatter_fsdp(rest)

    def seq_back(value, axis):
        for step, mask in enumerate(reversed(net.seq_bits)):
            value = net.both(value, mask, axis + step)
        return value

    out_down = seq_back(red_down, 0).reshape(ff_rows, width).astype(F32)
    out_gate = seq_back(red_gate, 1).reshape(d_rows, 2 * units).astype(F32)
    out_rest = seq_back(rest, 1).reshape(d_rows + pad_rows, wide).astype(F32)
    line = out_rest[d_rows]
    edge = qk_rows + v_rows
    return (
        block_out,
        hidden_grad,
        out_rest[:d_rows, :qkv_w],
        line[:qk_rows],
        line[qk_rows:edge],
        out_rest[:d_rows, qkv_w:],
        out_gate,
        out_down,
        line[edge : edge + 2 * d_rows].reshape(2, d_rows),
    )


def solution(mesh):
    n_fsdp, n_seq = mesh.shape["fsdp"], mesh.shape["seq"]
    in_specs = (
        P(None, "fsdp", "seq", None),
        P("fsdp", None),
        P("fsdp"),
        P("fsdp", None),
        P("fsdp", None),
        P("fsdp", None),
        P(None, "fsdp"),
        P(None, "fsdp", "seq"),
        P(),
        P(None, "fsdp", "seq", None),
    )
    out_specs = (
        P(None, "fsdp", "seq", None),
        P(None, "fsdp", "seq", None),
        P("fsdp", None),
        P("fsdp"),
        P("fsdp"),
        P("fsdp", None),
        P("fsdp", None),
        P("fsdp", None),
        P(None, "fsdp"),
    )

    def local(*args):
        return on_device(*args, n_fsdp=n_fsdp, n_seq=n_seq)

    return jax.shard_map(local, mesh=mesh, in_specs=in_specs, out_specs=out_specs, check_vma=False)
```

```python
import functools

import jax
import jax.numpy as jnp
import numpy as np
from jax import lax
from jax.experimental import pallas as pl
from jax.experimental.pallas import tpu as pltpu
from jax.sharding import PartitionSpec as P

HEADS = 9
KV_HEADS = 3
HEAD_DIM = 64
GROUP = HEADS // KV_HEADS
QW = HEADS * HEAD_DIM
KW = KV_HEADS * HEAD_DIM
EPS = 1e-05
ROPE_BASE = 100000.0
MASKED = -1000000000.0
BF = jnp.bfloat16
F32 = jnp.float32


def dot(a, b, ca, cb):
    return lax.dot_general(a, b, (((ca,), (cb,)), ((), ())), preferred_element_type=F32)


def rotary(values, cosine, sine):
    half = values.shape[-1] // 2
    a, b = values[..., :half], values[..., half:]
    return jnp.concatenate([a * cosine - b * sine, b * cosine + a * sine], axis=-1)


def norm_parts(values):
    factor = lax.rsqrt(jnp.mean(values * values, axis=-1, keepdims=True) + EPS)
    return factor, values * factor


def norm_back(grad_in, gain, factor, normed):
    scaled = grad_in * gain
    return factor * (scaled - normed * jnp.mean(scaled * normed, axis=-1, keepdims=True))


def whole(*shape_dtypes):
    return [pl.BlockSpec(memory_space=pltpu.VMEM) for _ in shape_dtypes]


def call(kernel, scalars, arrays, outs, flops, scratch=()):
    specs = [pl.BlockSpec(memory_space=pltpu.SMEM)] * len(scalars) + whole(*arrays)
    moved = sum(a.size * a.dtype.itemsize for a in arrays) + sum(
        int(np.prod(o.shape)) * o.dtype.itemsize for o in outs
    )
    return pl.pallas_call(
        kernel,
        out_shape=outs,
        in_specs=specs,
        out_specs=whole(*outs),
        scratch_shapes=[pltpu.VMEM(shape, F32) for shape in scratch],
        compiler_params=pltpu.CompilerParams(vmem_limit_bytes=52 * 1024 * 1024),
        cost_estimate=pl.CostEstimate(flops=flops, bytes_accessed=moved, transcendentals=0),
    )(*scalars, *arrays)


def sds(shape, dtype):
    return jax.ShapeDtypeStruct(shape, dtype)


def turn(x, cosine, sine):
    tiles = []
    low = lax.broadcasted_iota(jnp.int32, (1, 128), 1) % HEAD_DIM < HEAD_DIM // 2
    for t in range(x.shape[1] // 128):
        part = x[:, 128 * t : 128 * t + 128]
        other = jnp.where(low, pltpu.roll(part, 96, 1), pltpu.roll(part, 32, 1))
        tiles.append(part * cosine + other * sine)
    return tiles


def turn_kv(x, cosine, sine):
    lane = lax.broadcasted_iota(jnp.int32, (1, 128), 1)
    first, second = turn(x[:, :256], cosine, sine)
    second = jnp.where(lane < KW - 128, second, x[:, 128:256])
    return jnp.concatenate([first, second, x[:, 256:]], axis=1)


def tables(seq, order, cos_ref, sin_ref):
    cosine = jnp.concatenate([cos_ref[seq ^ o] for o in order], axis=0)
    sine = jnp.concatenate([sin_ref[seq ^ o] for o in order], axis=0)
    return cosine, sine


def heads_to_rows(x, g):
    return jnp.concatenate(
        [x[:, HEAD_DIM * h : HEAD_DIM * (h + 1)] for h in range(GROUP * g, GROUP * (g + 1))], axis=0
    )


def rows_to_heads(parts, length):
    return jnp.concatenate(
        [p[length * r : length * (r + 1)] for p in parts for r in range(GROUP)], axis=1
    )


def attention_forward(order, length, seq_ref, blocks, wq, wkv, bq, bkv, gain, cos, sin, mask,
                      att_o, q_o, k_o, v_o, lse_o):
    seq = seq_ref[0]
    cosine, sine = tables(seq, order, cos, sin)
    width = gain.shape[1]
    for b in range(blocks.shape[1] // length):
        x = blocks[:, b * length : (b + 1) * length, :width].astype(F32)
        x = x.reshape(len(order) * length, width)
        first = (norm_parts(x)[1] * gain[...]).astype(BF)
        kv = dot(first, wkv[...], 1, 0) + bkv[...]
        q = dot(first[:length], wq[...], 1, 0) + bq[...]
        q = jnp.concatenate(turn(q, cosine[:length], sine[:length]), axis=1).astype(BF)
        q = q * jnp.asarray(HEAD_DIM ** (-0.5), BF)
        kv = turn_kv(kv, cosine, sine).astype(BF)
        allowed = jnp.concatenate([mask[b]] * GROUP, axis=0) > 0.0
        parts = []
        for g in range(KV_HEADS):
            qg = heads_to_rows(q, g)
            kg = kv[:, HEAD_DIM * g : HEAD_DIM * (g + 1)]
            vg = kv[:, KW + HEAD_DIM * g : KW + HEAD_DIM * (g + 1)]
            q_o[b, g] = qg
            k_o[b, g] = kg
            v_o[b, g] = vg
            scores = jnp.where(allowed, dot(qg, kg, 1, 1), MASKED)
            top = jnp.max(scores, axis=-1, keepdims=True)
            e = jnp.exp(scores - top)
            total = jnp.sum(e, axis=-1, keepdims=True)
            lse_o[b, g] = jnp.log(total) + top
            probs = (e * (1.0 / total)).astype(BF)
            parts.append(dot(probs, vg, 1, 0))
        att_o[b * length : (b + 1) * length, :] = rows_to_heads(parts, length).astype(BF)


def feed_forward(attended, source, wo, wgu, wd, gain, cot, weight,
                 out_o, down_o, gu_o, mid_o, wout_o, attg_o, gain_o):
    units = wd.shape[0]
    step = units // 3
    att = attended[...]
    middle = source[...].astype(F32) + dot(att, wo[...], 1, 0)
    scale_two, normed = norm_parts(middle)
    g2 = gain[...]
    second = (normed * g2).astype(BF)
    out_grad = cot[...].astype(F32) * weight[...]
    feed_grad = out_grad.astype(BF)
    feed = None
    back = None
    for j in range(0, units, step):
        wg = wgu[:, j : j + step]
        wu = wgu[:, units + j : units + j + step]
        wdj = wd[j : j + step, :]
        gate = dot(second, wg, 1, 0)
        up = dot(second, wu, 1, 0)
        sig = jax.nn.sigmoid(gate)
        act = gate * sig
        product = (act * up).astype(BF)
        part = dot(product, wdj, 1, 0)
        feed = part if feed is None else feed + part
        down_o[j : j + step, :] = dot(product, feed_grad, 0, 0).astype(BF)
        pgrad = dot(feed_grad, wdj, 1, 1)
        ggrad = (pgrad * up * (sig * (1.0 + gate * (1.0 - sig)))).astype(BF)
        ugrad = (pgrad * act).astype(BF)
        gu_o[:, j : j + step] = dot(second, ggrad, 0, 0).astype(BF)
        gu_o[:, units + j : units + j + step] = dot(second, ugrad, 0, 0).astype(BF)
        part = dot(ggrad, wg, 1, 1) + dot(ugrad, wu, 1, 1)
        back = part if back is None else back + part
    out_o[...] = (middle + feed).astype(BF)
    gain_o[...] = jnp.sum(back * normed, axis=0, keepdims=True)
    middle_grad = out_grad + norm_back(back, g2, scale_two, normed)
    mid_o[...] = middle_grad
    branch = middle_grad.astype(BF)
    wout_o[...] = dot(att, branch, 0, 0).astype(BF)
    attg_o[...] = dot(branch, wo[...], 1, 1).astype(BF)


def attention_backward(order, length, seq_ref, blocks, wq, wkv, gain, cos, sin, mask, q_i, k_i, v_i,
                       lse, attg, dq_o, dkv_o, wgrad_o, bias_o, gain_o):
    seq = seq_ref[0]
    cosine, sine = tables(seq, order, cos, sin)
    width = gain.shape[1]
    q_wgrad = kv_wgrad = bias_q = bias_kv = gain_sum = None
    for b in range(blocks.shape[1] // length):
        x = blocks[:, b * length : (b + 1) * length, :width].astype(F32)
        x = x.reshape(len(order) * length, width)
        normed = norm_parts(x)[1]
        first = (normed * gain[...]).astype(BF)
        allowed = jnp.concatenate([mask[b]] * GROUP, axis=0) > 0.0
        ag = attg[b * length : (b + 1) * length, :]
        dqs, dks, dvs = [], [], []
        for g in range(KV_HEADS):
            qg, kg, vg = q_i[b, g], k_i[b, g], v_i[b, g]
            agg = heads_to_rows(ag, g)
            p = jnp.exp(jnp.where(allowed, dot(qg, kg, 1, 1), MASKED) - lse[b, g])
            dvs.append(dot(p.astype(BF), agg, 0, 0))
            pg = dot(agg, vg, 1, 1)
            inner = jnp.sum(p * pg, axis=-1, keepdims=True)
            ds = (p * (pg - inner)).astype(BF)
            dqs.append(dot(ds, kg, 1, 0) * HEAD_DIM ** (-0.5))
            dks.append(dot(ds, qg, 0, 0))
        dq = rows_to_heads(dqs, length)
        dq = jnp.concatenate([dq, jnp.zeros((length, 64), F32)], axis=1)
        dq = jnp.concatenate(turn(dq, cosine[:length], -sine[:length]), axis=1).astype(BF)
        dkv = jnp.concatenate(dks + dvs, axis=1)
        dkv = turn_kv(dkv, cosine, -sine).astype(BF)
        dq_o[b * length : (b + 1) * length, :] = dq
        for r in range(len(order)):
            dkv_o[r, b * length : (b + 1) * length, :] = dkv[r * length : (r + 1) * length, :]
        wq_part = dot(first[:length], dq, 0, 0)
        wkv_part = dot(first, dkv, 0, 0)
        bq_part = jnp.sum(dq.astype(F32), axis=0, keepdims=True)
        bkv_part = jnp.sum(dkv.astype(F32), axis=0, keepdims=True)
        e_kv = dot(dkv, wkv[...], 1, 1) * normed
        e_q = dot(dq[:, :QW], wq[:, :QW], 1, 1) * normed[:length]
        g_part = jnp.sum(e_kv, axis=0, keepdims=True) + jnp.sum(e_q, axis=0, keepdims=True)
        if q_wgrad is None:
            q_wgrad, kv_wgrad, bias_q, bias_kv, gain_sum = wq_part, wkv_part, bq_part, bkv_part, g_part
        else:
            q_wgrad, kv_wgrad = q_wgrad + wq_part, kv_wgrad + wkv_part
            bias_q, bias_kv, gain_sum = bias_q + bq_part, bias_kv + bkv_part, gain_sum + g_part
    wgrad_o[...] = jnp.concatenate([q_wgrad[:, :QW], kv_wgrad], axis=1).astype(BF)
    bias_o[...] = jnp.concatenate([bias_q[:, :QW], bias_kv], axis=1)
    gain_o[...] = gain_sum


def input_gradient(dq, own, a, b, c, source, mid, wq, wkv, gain, out_o):
    kv = own[...].astype(F32) + a[...].astype(F32) + b[...].astype(F32) + c[...].astype(F32)
    first_grad = dot(dq[:, :QW], wq[:, :QW], 1, 1) + dot(kv.astype(BF), wkv[...], 1, 1)
    scale_one, normed = norm_parts(source[...].astype(F32))
    out_o[...] = mid[...] + norm_back(first_grad, gain[...], scale_one, normed)

def chosen(flag, a, b):
    return jnp.where(flag != 0, b, a)


def first_forward(order, length, d_rows, n_bias, meta, blocks, am, ao, cos, sin, mask,
                  att_o, q_o, k_o, v_o, lse_o, w_o, gain_o, w_s, b_s):
    core = meta[0] & 1
    cut = am.shape[1]
    bias, gains = [], [[], []]
    for f in range(am.shape[0]):
        mine, other = am[f].astype(F32), ao[f].astype(F32)
        low, high = chosen(core, mine, other), chosen(core, other, mine)
        w_s[d_rows * f : d_rows * f + cut, :] = low
        w_s[d_rows * f + cut : d_rows * (f + 1), :] = high[: d_rows - cut]
        line = high[d_rows - cut : d_rows - cut + 1]
        bias.append(line[:, :n_bias])
        for i in range(2):
            gains[i].append(line[:, n_bias + d_rows * i : n_bias + d_rows * (i + 1)])
    w_o[...] = w_s[...].astype(BF)
    b_s[...] = jnp.concatenate(bias, axis=1)
    for i in range(2):
        gain_o[i : i + 1, :] = jnp.concatenate(gains[i], axis=1)
    wide = QW + 64
    attention_forward(order, length, meta, blocks, w_o[:, :wide], w_o[:, QW:], b_s[:, :wide], b_s[:, QW:],
                      gain_o[0:1, :], cos, sin, mask, att_o, q_o, k_o, v_o, lse_o)


def rel(meta, f):
    r = f ^ meta[1]
    return r & 1, (r >> 1) & 1, (r >> 2) & 1


def feed_forward_pieces(d_rows, ff_rows, meta, attended, source, bm, bo, c00, c10, c01, c11, gains, cot, weight,
                        out_o, gk_o, gg_o, dk_o, dg_o, mid_o, attg_o, gain_o, down_s, wout_s):
    core, y = meta[0] & 1, (meta[0] >> 1) & 1
    n_f = bm.shape[0]
    hf = n_f // 2
    part_d = ff_rows // 4
    part_o = d_rows // 3
    cut = bm.shape[1] - ff_rows // 2
    wo = []
    for f in range(n_f):
        mine, other = bm[f, ff_rows // 2 :, :].astype(F32), bo[f, ff_rows // 2 :, :].astype(F32)
        wo.append(chosen(core, mine, other))
        wo.append(chosen(core, other, mine)[: d_rows - cut])
    wo = jnp.concatenate(wo, axis=0).astype(BF)
    att = attended[...]
    middle = source[...].astype(F32) + dot(att, wo, 1, 0)
    scale_two, normed = norm_parts(middle)
    g2 = gains[1:2, :]
    second = (normed * g2).astype(BF)
    out_grad = cot[...].astype(F32) * weight[...]
    feed_grad = out_grad.astype(BF)
    feed = back = None
    for c_rel in (1, 0):
        first_q, second_q = (c01, c11) if c_rel else (c00, c10)
        wg = chosen(y, first_q[...], second_q[...])
        wu = chosen(y, second_q[...], first_q[...])
        h = core ^ c_rel
        wd = []
        for i in range(hf):
            mine, other = bm[hf * h + i, : ff_rows // 2, :], bo[hf * h + i, : ff_rows // 2, :]
            wd += [chosen(core, mine, other), chosen(core, other, mine)]
        wd = jnp.concatenate(wd, axis=0)
        gate = dot(second, wg, 1, 0)
        up = dot(second, wu, 1, 0)
        sig = jax.nn.sigmoid(gate)
        act = gate * sig
        product = (act * up).astype(BF)
        part = dot(product, wd, 1, 0)
        feed = part if feed is None else feed + part
        down_s[...] = dot(product, feed_grad, 0, 0)
        pgrad = dot(feed_grad, wd, 1, 1)
        ggrad = (pgrad * up * (sig * (1.0 + gate * (1.0 - sig)))).astype(BF)
        ugrad = (pgrad * act).astype(BF)
        part = dot(ggrad, wg, 1, 1) + dot(ugrad, wu, 1, 1)
        back = part if back is None else back + part
        for i in range(hf):
            x, z0, z1 = rel(meta, hf * h + i)
            for yy in range(2):
                for c_to, to in ((0, dk_o), (1, dg_o)):
                    at = pl.multiple_of(i * ff_rows + (yy * 2 + (core ^ c_to)) * part_d, 16)
                    to[y ^ yy, x, z0, z1, :part_d, :] = down_s[pl.ds(at, part_d), :].astype(BF)
        to = gg_o if c_rel else gk_o
        for yy, grad in ((0, ggrad), (1, ugrad)):
            wgrad = dot(second, grad, 0, 0)
            for f in range(n_f):
                x, z0, z1 = rel(meta, f)
                to[x, y ^ yy, z0, z1] = wgrad[d_rows * f : d_rows * (f + 1), :].astype(BF)
    out_o[...] = (middle + feed).astype(BF)
    gain_o[...] = jnp.sum(back * normed, axis=0, keepdims=True)
    middle_grad = out_grad + norm_back(back, g2, scale_two, normed)
    mid_o[...] = middle_grad
    branch = middle_grad.astype(BF)
    attg_o[...] = dot(branch, wo, 1, 1).astype(BF)
    wout = dot(att, branch, 0, 0)
    for f in range(n_f):
        wout_s[f, :d_rows, :] = wout[d_rows * f : d_rows * (f + 1), :]
        wout_s[f, d_rows:, :] = jnp.zeros((part_o, wout.shape[1]), F32)
    for f in range(n_f):
        x, z0, z1 = rel(meta, f)
        for yy in range(2):
            for c_to, to in ((0, dk_o), (1, dg_o)):
                at = pl.multiple_of((yy * 2 + (core ^ c_to)) * part_o, 8)
                to[y ^ yy, x, z0, z1, part_d:, :] = wout_s[f, pl.ds(at, part_o), :].astype(BF)


def attention_backward_pieces(order, length, d_rows, meta, blocks, w, gains, cos, sin, mask, q_i, k_i, v_i,
                              lse, attg, gain_two, dq_o, dk_o, dg_o, rk_o, rg_o, w_s, bias_s, gain_s, small_s):
    class Rows:
        def __init__(self, ref, base):
            self.ref, self.base = ref, base

        def __setitem__(self, key, value):
            if key is not Ellipsis:
                self.ref[(key[0] - self.base,) + key[1:]] = value

    half = len(order) // 2

    class Blocks:
        def __setitem__(self, key, value):
            ref = dk_o if key[0] < half else dg_o
            ref[(key[0] % half,) + key[1:]] = value

    class Wgrad:
        def __setitem__(self, key, value):
            w_s[:, : 2 * KW] = value[:, QW:].astype(F32)
            w_s[:, 2 * KW : 2 * KW + QW] = value[:, :QW].astype(F32)
            w_s[:, 2 * KW + QW :] = jnp.zeros((value.shape[0], 64), F32)

    wide = QW + 64
    attention_backward(order, length, meta, blocks, w[:, :wide], w[:, QW:], gains[0:1, :], cos, sin, mask,
                       q_i, k_i, v_i, lse, attg, dq_o, Blocks(), Wgrad(), bias_s, gain_s)
    n_f = small_s.shape[0]
    qk, v = (QW + KW) // n_f, KW // n_f
    bias, g1, g2 = bias_s[...], gain_s[...], gain_two[...]
    for f in range(n_f):
        line = jnp.concatenate(
            [
                bias[:, qk * f : qk * (f + 1)],
                bias[:, QW + KW + v * f : QW + KW + v * (f + 1)],
                g1[:, d_rows * f : d_rows * (f + 1)],
                jnp.zeros((1, 256 - qk - v - d_rows), F32),
                g2[:, d_rows * f : d_rows * (f + 1)],
                jnp.zeros((1, 768 - d_rows), F32),
            ],
            axis=1,
        )
        small_s[f] = jnp.broadcast_to(line, (8, 1024))
    core, y = meta[0] & 1, (meta[0] >> 1) & 1
    for f in range(n_f):
        x, z0, z1 = rel(meta, f)
        for yy in range(2):
            for c_to, to in ((0, rk_o), (1, rg_o)):
                at = pl.multiple_of((yy * 2 + (core ^ c_to)) * 256, 256)
                block = [w_s[d_rows * f : d_rows * (f + 1), pl.ds(at, 256)], small_s[f, :, pl.ds(at, 256)]]
                to[x, y ^ yy, z0, z1] = jnp.concatenate(block, axis=0).astype(BF)


def input_gradient_two(dq, own, other, source, mid, w, gains, out_o):
    kv = (own[...].astype(F32) + other[...].astype(F32)).astype(BF)
    first_grad = dot(dq[:, :QW], w[:, :QW], 1, 1) + dot(kv, w[:, QW:], 1, 1)
    scale_one, normed = norm_parts(source[...].astype(F32))
    out_o[...] = mid[...] + norm_back(first_grad, gains[0:1, :], scale_one, normed)


def place_gate(meta, p00, p10, pc, out_o):
    seq = meta[0]
    n = p00.shape[1]
    for piece, o in ((p00[...], 0), (p10[...], 2), (pc[0], 1), (pc[1], 3)):
        out_o[:, pl.ds(pl.multiple_of((seq ^ o) * n, 128), n)] = piece.astype(F32)


def place_down(part_d, meta, p00, p10, pc, out_o, wout_o):
    seq = meta[0]
    part_o = p00.shape[0] - part_d
    for piece, o in ((p00[...], 0), (p10[...], 2), (pc[0], 1), (pc[1], 3)):
        piece = piece.astype(F32)
        to = seq ^ o
        out_o[pl.ds(pl.multiple_of(to * part_d, 16), part_d), :] = piece[:part_d]

        @pl.when(to < 3)
        def _():
            wout_o[pl.ds(pl.multiple_of(to * part_o, 8), part_o), :] = piece[part_d:]


def place_qkv(qk, v, meta, p00, p10, pc, w_o, bqk_o, bv_o, gains_o, all_s):
    seq = meta[0]
    n = p00.shape[1]
    for piece, o in ((p00[...], 0), (p10[...], 2), (pc[0], 1), (pc[1], 3)):
        all_s[:, pl.ds(pl.multiple_of((seq ^ o) * n, 128), n)] = piece.astype(F32)
    d_rows = w_o.shape[0]
    w_o[:, :QW] = all_s[:d_rows, 2 * KW : 2 * KW + QW]
    w_o[:, QW:] = all_s[:d_rows, : 2 * KW]
    line = all_s[d_rows : d_rows + 1, :]
    bqk_o[...] = line[:, :qk]
    bv_o[...] = line[:, qk : qk + v]
    gains_o[0:1, :] = line[:, qk + v : qk + v + d_rows]
    gains_o[1:2, :] = line[:, 256 : 256 + d_rows]


class Net:
    def __init__(self, n_fsdp, n_seq):
        self.n_fsdp, self.n_seq = n_fsdp, n_seq
        self.total = n_fsdp * n_seq
        f, s = lax.axis_index("fsdp"), lax.axis_index("seq")
        self.index = f * n_seq + s
        self.seq_bits = [1 << b for b in range(n_seq.bit_length() - 1)]
        self.fsdp_bits = [n_seq << b for b in range(n_fsdp.bit_length() - 1)]

    def swap(self, value, mask):
        pairs = [(i, i ^ mask) for i in range(self.total)]
        return lax.ppermute(value, ("fsdp", "seq"), pairs)

    def bit(self, mask):
        return (self.index & mask) != 0

    def both(self, mine, mask, axis):
        other = self.swap(mine, mask)
        high = self.bit(mask)
        return jnp.stack([jnp.where(high, other, mine), jnp.where(high, mine, other)], axis=axis)

    def half(self, value, mask, axis):
        return lax.dynamic_index_in_dim(
            value, self.bit(mask).astype(jnp.int32), axis, keepdims=False
        )

    def add_half(self, value, mask, axis):
        mine = self.bit(mask).astype(jnp.int32)
        keep = lax.dynamic_index_in_dim(value, mine, axis, keepdims=False)
        give = lax.dynamic_index_in_dim(value, 1 - mine, axis, keepdims=False)
        got = self.swap(give, mask)
        return (keep.astype(F32) + got.astype(F32)).astype(value.dtype)

    def gather_fsdp(self, value):
        for step, mask in enumerate(reversed(self.fsdp_bits)):
            value = self.both(value, mask, step)
        return value

    def scatter_fsdp(self, value, first_axis=0):
        count = len(self.fsdp_bits)
        for step, mask in enumerate(self.fsdp_bits):
            value = self.add_half(value, mask, first_axis + count - 1 - step)
        return value


def on_device(
    hidden, w_qkv, b_qkv, w_out, w_gate_up, w_down, norm_gains, segment_ids, token_counts, cotangent,
    n_fsdp, n_seq,
):
    net = Net(n_fsdp, n_seq)
    micro, batch, length, width = hidden.shape
    full_length = length * n_seq
    tokens_micro = batch * n_fsdp * full_length
    scale = HEAD_DIM ** (-0.5)
    rows = micro * batch * length
    d_rows = w_qkv.shape[0]
    ff_rows = w_down.shape[0]
    units = w_gate_up.shape[1] // 2
    qkv_w = w_qkv.shape[1]
    core = net.seq_bits[0]
    f_lead = (2,) * len(net.fsdp_bits)

    ids = segment_ids.reshape(rows, 1).astype(BF)
    block = jnp.concatenate(
        [hidden.reshape(rows, width), jnp.broadcast_to(ids, (rows, 64))], axis=1
    )
    blocks = block[None]
    for mask in reversed(net.seq_bits):
        blocks = jnp.concatenate([blocks, net.swap(blocks, mask)], axis=0)
    order = [0]
    for mask in reversed(net.seq_bits):
        order = order + [o ^ mask for o in order]
    seq_index = lax.axis_index("seq")
    block_ids = [seq_index ^ o for o in order]

    pad_rows = -(d_rows + 1) % 16 + 1
    extra = jnp.zeros((pad_rows, qkv_w), BF)
    small = jnp.concatenate([b_qkv, norm_gains.reshape(-1)])
    extra = extra.at[0, : small.shape[0]].set(small)
    shard_a = jnp.concatenate([w_qkv, extra], axis=0).reshape(2, -1, qkv_w)
    got_a = net.gather_fsdp(net.half(shard_a, core, 0))
    full_a = net.both(got_a, core, len(f_lead)).reshape(n_fsdp, d_rows + pad_rows, qkv_w)
    wf_qkv = full_a[:, :d_rows].reshape(n_fsdp * d_rows, qkv_w)
    smalls = full_a[:, d_rows]
    n_bias = b_qkv.shape[0]
    bias = smalls[:, :n_bias].reshape(-1).astype(F32)
    gains = smalls[:, n_bias : n_bias + 2 * d_rows].reshape(n_fsdp, 2, d_rows).astype(F32)
    gain_one = gains[:, 0].reshape(-1)
    gain_two = gains[:, 1].reshape(-1)

    pad_b = -(d_rows + ff_rows) % 16
    shard_b = jnp.concatenate([w_out, w_down, jnp.zeros((pad_b, width), BF)], axis=0)
    shard_b = shard_b.reshape(2, -1, width)
    got_b = net.gather_fsdp(net.half(shard_b, core, 0))

    parts = n_seq
    shard_c = w_gate_up.reshape(d_rows, parts, -1)
    got_c = net.gather_fsdp(lax.dynamic_index_in_dim(shard_c, seq_index, 1, keepdims=False))
    full_b = net.both(got_b, core, len(f_lead)).reshape(n_fsdp, -1, width)
    wf_out = full_b[:, :d_rows].reshape(n_fsdp * d_rows, width)
    wf_down = full_b[:, d_rows : d_rows + ff_rows].reshape(n_fsdp * ff_rows, width)
    got_c = got_c.reshape(n_fsdp * d_rows, -1)
    for mask in reversed(net.seq_bits):
        got_c = net.both(got_c, mask, got_c.ndim - 1)
    wf_gate_up = got_c.reshape(n_fsdp * d_rows, 2 * units)

    places = np.arange(full_length, dtype=np.float32)
    speeds = np.power(ROPE_BASE, -2.0 * np.arange(HEAD_DIM // 2, dtype=np.float32) / HEAD_DIM)
    angles = places[:, None] * speeds.astype(np.float32)[None, :]
    cos_t = np.tile(np.cos(angles), (1, 4)).reshape(n_seq, length, 128)
    sin_t = np.concatenate([-np.sin(angles), np.sin(angles)] * 2, axis=1).reshape(n_seq, length, 128)
    cos_t, sin_t = jnp.asarray(cos_t, F32), jnp.asarray(sin_t, F32)
    seqs = micro * batch
    seg_all = blocks[..., width].reshape(n_seq, seqs, length).transpose(1, 0, 2)
    own_places = seq_index * length + jnp.arange(length, dtype=jnp.int32)
    key_places = jnp.stack(block_ids)[:, None] * length + jnp.arange(length, dtype=jnp.int32)
    allowed = (seg_all[:, 0, :, None] == seg_all.reshape(seqs, 1, -1)) & (
        own_places[None, :, None] >= key_places.reshape(1, 1, -1)
    )
    allowed = allowed.astype(F32)
    seq_scalar = seq_index.astype(jnp.int32).reshape(1)
    wq, wkv = wf_qkv[:, : QW + 64], wf_qkv[:, QW:]
    gain_one, gain_two = gain_one[None], gain_two[None]
    source = hidden.reshape(rows, width)
    n_all = n_seq * rows
    attended, q_s, k_s, v_s, lse = call(
        functools.partial(attention_forward, order, length),
        [seq_scalar],
        [blocks, wq, wkv, bias[None, : QW + 64], bias[None, QW:], gain_one, cos_t, sin_t, allowed],
        [
            sds((rows, QW), BF),
            sds((seqs, KV_HEADS, GROUP * length, HEAD_DIM), BF),
            sds((seqs, KV_HEADS, full_length, HEAD_DIM), BF),
            sds((seqs, KV_HEADS, full_length, HEAD_DIM), BF),
            sds((seqs, KV_HEADS, GROUP * length, 1), F32),
        ],
        2 * n_all * width * 2 * KW + 2 * rows * width * QW + 4 * rows * full_length * QW,
    )

    weight = tokens_micro / token_counts.astype(F32)
    weight = jnp.repeat(weight, batch * length)[:, None]
    block_out, down_grad, gate_up_wgrad, middle_grad, out_wgrad, attended_grad, gain_two_grad = call(
        feed_forward,
        [],
        [attended, source, wf_out, wf_gate_up, wf_down, gain_two, cotangent.reshape(rows, width), weight],
        [
            sds((rows, width), BF),
            sds((units, width), BF),
            sds((width, 2 * units), BF),
            sds((rows, width), F32),
            sds((QW, width), BF),
            sds((rows, QW), BF),
            sds((1, width), F32),
        ],
        6 * rows * width * 3 * units + 6 * rows * width * QW,
    )
    block_out = block_out.reshape(hidden.shape)

    def seq_axes(value, axis, masks):
        for mask in masks:
            value = net.add_half(value, mask, axis)
        return value

    quarter = (2,) * len(net.seq_bits)
    n_f = len(f_lead)
    red_down = down_grad.reshape(f_lead + quarter + (ff_rows // n_seq, width))
    for step, mask in enumerate(net.seq_bits):
        red_down = net.add_half(red_down, mask, n_f + len(quarter) - 1 - step)
    red_down = net.scatter_fsdp(red_down)

    red_gate = gate_up_wgrad.reshape(f_lead + (d_rows,) + quarter + (2 * units // n_seq,))
    red_gate = net.add_half(red_gate, core, n_f + len(quarter))
    red_gate = net.add_half(red_gate, net.fsdp_bits[0], n_f - 1)
    for step, mask in enumerate(net.seq_bits[1:]):
        red_gate = net.add_half(red_gate, mask, n_f - 1 + len(quarter) - 1 - step)
    for step, mask in enumerate(net.fsdp_bits[1:]):
        red_gate = net.add_half(red_gate, mask, n_f - 2 - step)

    dq, dkv, qkv_wgrad, bias_grad, gain_one_grad = call(
        functools.partial(attention_backward, order, length),
        [seq_scalar],
        [blocks, wq, wkv, gain_one, cos_t, sin_t, allowed, q_s, k_s, v_s, lse, attended_grad],
        [
            sds((rows, QW + 64), BF),
            sds((n_seq, rows, 2 * KW), BF),
            sds((width, qkv_w), BF),
            sds((1, qkv_w), F32),
            sds((1, width), F32),
        ],
        4 * n_all * width * 2 * KW + 4 * rows * width * QW + 10 * rows * full_length * QW,
    )
    kv_parts = [dkv[0]]
    for place, mask_bits in enumerate(order):
        if mask_bits:
            kv_parts.append(net.swap(dkv[place], mask_bits))
    (hidden_grad,) = call(
        input_gradient,
        [],
        [dq, *kv_parts, source, middle_grad, wq, wkv, gain_one],
        [sds((rows, width), F32)],
        2 * rows * width * qkv_w,
    )
    hidden_grad = hidden_grad.reshape(hidden.shape)
    bias_grad, gain_one_grad, gain_two_grad = bias_grad[0], gain_one_grad[0], gain_two_grad[0]

    qk_rows, v_rows = (QW + KW) // n_fsdp, KW // n_fsdp
    small_grads = jnp.concatenate(
        [
            bias_grad[: QW + KW].reshape(n_fsdp, qk_rows),
            bias_grad[QW + KW :].reshape(n_fsdp, v_rows),
            gain_one_grad.reshape(n_fsdp, d_rows),
            gain_two_grad.reshape(n_fsdp, d_rows),
        ],
        axis=1,
    ).astype(BF)
    wide = qkv_w + width
    small_pad = jnp.zeros((n_fsdp, pad_rows, wide), BF)
    small_pad = small_pad.at[:, 0, : small_grads.shape[1]].set(small_grads)
    rest = jnp.concatenate([qkv_wgrad, out_wgrad], axis=1)
    rest = jnp.concatenate([rest.reshape(n_fsdp, d_rows, wide), small_pad], axis=1)
    rest = rest.reshape(f_lead + (d_rows + pad_rows,) + quarter + (wide // n_seq,))
    for step, mask in enumerate(net.seq_bits):
        rest = net.add_half(rest, mask, n_f + 1 + len(quarter) - 1 - step)
    rest = net.scatter_fsdp(rest)

    def seq_back(value, axis):
        for step, mask in enumerate(reversed(net.seq_bits)):
            value = net.both(value, mask, axis + step)
        return value

    out_down = seq_back(red_down, 0).reshape(ff_rows, width).astype(F32)
    out_gate = seq_back(red_gate, 1).reshape(d_rows, 2 * units).astype(F32)
    out_rest = seq_back(rest, 1).reshape(d_rows + pad_rows, wide).astype(F32)
    line = out_rest[d_rows]
    edge = qk_rows + v_rows
    return (
        block_out,
        hidden_grad,
        out_rest[:d_rows, :qkv_w],
        line[:qk_rows],
        line[qk_rows:edge],
        out_rest[:d_rows, qkv_w:],
        out_gate,
        out_down,
        line[edge : edge + 2 * d_rows].reshape(2, d_rows),
    )


def after(value, *others):
    return lax.optimization_barrier((value, *others))[0]


def rope_tables(full_length, n_seq):
    places = np.arange(full_length, dtype=np.float32)
    speeds = np.power(ROPE_BASE, -2.0 * np.arange(HEAD_DIM // 2, dtype=np.float32) / HEAD_DIM)
    angles = places[:, None] * speeds.astype(np.float32)[None, :]
    cos_t = np.tile(np.cos(angles), (1, 4)).reshape(n_seq, -1, 128)
    sin_t = np.concatenate([-np.sin(angles), np.sin(angles)] * 2, axis=1).reshape(n_seq, -1, 128)
    return jnp.asarray(cos_t, F32), jnp.asarray(sin_t, F32)


def on_device_tiled(
    hidden, w_qkv, b_qkv, w_out, w_gate_up, w_down, norm_gains, segment_ids, token_counts, cotangent,
    n_fsdp, n_seq,
):
    net = Net(n_fsdp, n_seq)
    micro, batch, length, width = hidden.shape
    full_length = length * n_seq
    tokens_micro = batch * n_fsdp * full_length
    rows = micro * batch * length
    seqs = micro * batch
    d_rows, qkv_w = w_qkv.shape
    ff_rows = w_down.shape[0]
    units = w_gate_up.shape[1] // 2
    n_bias = b_qkv.shape[0]
    core, ybit = net.seq_bits
    xbit, znear, zfar = net.fsdp_bits
    order = [0, 2, 1, 3]
    seq_index = lax.axis_index("seq")
    meta = jnp.stack([seq_index, lax.axis_index("fsdp")]).astype(jnp.int32)
    source = hidden.reshape(rows, width)

    small = jnp.concatenate([b_qkv, norm_gains.reshape(-1)])
    extra = jnp.zeros((8, qkv_w), BF).at[:, : small.shape[0]].set(small[None])
    shard_a = jnp.concatenate([w_qkv, extra], axis=0).reshape(2, -1, qkv_w)
    a = net.half(shard_a, core, 0)
    a = net.both(a, zfar, 0)

    ids = segment_ids.reshape(rows, 1).astype(BF)
    block = jnp.concatenate([source, jnp.broadcast_to(ids, (rows, 64))], axis=1)
    blocks = jnp.stack([block, net.swap(block, ybit)])
    blocks = jnp.concatenate([blocks, net.swap(blocks, core)], axis=0)

    gu = lax.dynamic_slice_in_dim(
        w_gate_up, seq_index * (2 * units // n_seq), 2 * units // n_seq, axis=1
    )
    gu = after(gu, a)
    half_b = jnp.concatenate(
        [
            w_down.reshape(2, ff_rows // 2, width),
            jnp.concatenate([w_out, jnp.zeros((8, width), BF)], axis=0).reshape(2, -1, width),
        ],
        axis=1,
    )
    b = after(net.half(half_b, core, 0), a)
    gu = net.both(gu, zfar, 0)
    b = net.both(b, zfar, 0)
    a = net.both(a, znear, 1)
    a = net.both(a, xbit, 2).reshape(n_fsdp, -1, qkv_w)
    gu = net.both(gu, znear, 1)
    b = net.both(b, znear, 1)
    a_other = net.swap(a, core)
    gu = net.both(gu, xbit, 2).reshape(n_fsdp * d_rows, -1)
    b = net.both(b, xbit, 2).reshape(n_fsdp, -1, width)
    gu_c = net.swap(gu, core)
    gu_y = net.swap(gu, ybit)
    b_other = net.swap(b, core)
    gu_yc = net.swap(gu_y, core)

    cos_t, sin_t = rope_tables(full_length, n_seq)
    block_ids = [seq_index ^ o for o in order]
    seg_all = blocks[..., width].reshape(n_seq, seqs, length).transpose(1, 0, 2)
    own_places = seq_index * length + jnp.arange(length, dtype=jnp.int32)
    key_places = jnp.stack(block_ids)[:, None] * length + jnp.arange(length, dtype=jnp.int32)
    allowed = (seg_all[:, 0, :, None] == seg_all.reshape(seqs, 1, -1)) & (
        own_places[None, :, None] >= key_places.reshape(1, 1, -1)
    )
    allowed = allowed.astype(F32)
    n_all = n_seq * rows
    attended, q_s, k_s, v_s, lse, wf, gains = call(
        functools.partial(first_forward, order, length, d_rows, n_bias),
        [meta],
        [blocks, a, a_other, cos_t, sin_t, allowed],
        [
            sds((rows, QW), BF),
            sds((seqs, KV_HEADS, GROUP * length, HEAD_DIM), BF),
            sds((seqs, KV_HEADS, full_length, HEAD_DIM), BF),
            sds((seqs, KV_HEADS, full_length, HEAD_DIM), BF),
            sds((seqs, KV_HEADS, GROUP * length, 1), F32),
            sds((width, qkv_w), BF),
            sds((2, width), F32),
        ],
        2 * n_all * width * 2 * KW + 2 * rows * width * QW + 4 * rows * full_length * QW,
        [(width, qkv_w), (1, qkv_w)],
    )

    weight = tokens_micro / token_counts.astype(F32)
    weight = jnp.repeat(weight, batch * length)[:, None]
    lead = (2, 2, 2, 2)
    block_out, gate_keep, gate_give, down_keep, down_give, middle_grad, attended_grad, gain_two = call(
        functools.partial(feed_forward_pieces, d_rows, ff_rows),
        [meta],
        [attended, source, b, b_other, gu, gu_y, gu_c, gu_yc, gains, cotangent.reshape(rows, width), weight],
        [
            sds((rows, width), BF),
            sds(lead + (d_rows, units // 2), BF),
            sds(lead + (d_rows, units // 2), BF),
            sds(lead + (ff_rows // 4 + d_rows // 3, width), BF),
            sds(lead + (ff_rows // 4 + d_rows // 3, width), BF),
            sds((rows, width), F32),
            sds((rows, QW), BF),
            sds((1, width), F32),
        ],
        6 * rows * width * 3 * units + 6 * rows * width * QW,
        [(units // 2, width), (n_fsdp, d_rows + d_rows // 3, width)],
    )
    block_out = block_out.reshape(hidden.shape)

    def add(keep, got):
        return (keep.astype(F32) + got.astype(F32)).astype(BF)

    gate = add(gate_keep, net.swap(gate_give, core))
    down = add(down_keep, net.swap(down_give, core))
    attended_grad = after(attended_grad, gate, down)
    gate_got = net.swap(gate[1], xbit)
    down_got = net.swap(down[1], ybit)

    dq, dkv_keep, dkv_give, rest_keep, rest_give = call(
        functools.partial(attention_backward_pieces, order, length, d_rows),
        [meta],
        [blocks, wf, gains, cos_t, sin_t, allowed, q_s, k_s, v_s, lse, attended_grad, gain_two],
        [
            sds((rows, QW + 64), BF),
            sds((2, rows, 2 * KW), BF),
            sds((2, rows, 2 * KW), BF),
            sds(lead + (d_rows + 8, 256), BF),
            sds(lead + (d_rows + 8, 256), BF),
        ],
        4 * n_all * width * 2 * KW + 4 * rows * width * QW + 10 * rows * full_length * QW,
        [(width, 1024), (1, qkv_w), (1, width), (n_fsdp, 8, 1024)],
    )
    rest = add(rest_keep, net.swap(rest_give, core))
    dkv = add(dkv_keep, net.swap(dkv_give, core))
    rest_got = net.swap(rest[1], xbit)
    dkv_got = net.swap(dkv[1], ybit)

    gate = add(gate[0], gate_got)
    down = add(down[0], down_got)
    gate_got = net.swap(gate[1], ybit)
    down_got = net.swap(down[1], xbit)
    rest = add(rest[0], rest_got)
    rest_got = net.swap(rest[1], ybit)
    (hidden_grad,) = call(
        input_gradient_two,
        [],
        [dq, dkv[0], dkv_got, source, middle_grad, wf, gains],
        [sds((rows, width), F32)],
        2 * rows * width * qkv_w,
    )
    hidden_grad = hidden_grad.reshape(hidden.shape)
    gate = add(gate[0], gate_got)
    down = add(down[0], down_got)
    rest = add(rest[0], rest_got)
    for mask in (znear, zfar):
        gots = [net.swap(part[1], mask) for part in (gate, down, rest)]
        gate, down, rest = [add(part[0], got) for part, got in zip((gate, down, rest), gots)]

    def spread(part):
        other = net.swap(part, ybit)
        return [part, other, net.swap(jnp.stack([part, other]), core)]

    (out_gate,) = call(place_gate, [meta], spread(gate), [sds((d_rows, 2 * units), F32)], 0)
    out_down, out_wout = call(
        functools.partial(place_down, ff_rows // 4),
        [meta],
        spread(down),
        [sds((ff_rows, width), F32), sds((d_rows, width), F32)],
        0,
    )
    qk, v = (QW + KW) // n_fsdp, KW // n_fsdp
    out_qkv, b_qk, b_v, out_gains = call(
        functools.partial(place_qkv, qk, v),
        [meta],
        spread(rest),
        [sds((d_rows, qkv_w), F32), sds((1, qk), F32), sds((1, v), F32), sds((2, d_rows), F32)],
        0,
        [(d_rows + 8, 1024)],
    )
    return (
        block_out,
        hidden_grad,
        out_qkv,
        b_qk.reshape(qk),
        b_v.reshape(v),
        out_wout,
        out_gate,
        out_down,
        out_gains,
    )


def solution(mesh):
    n_fsdp, n_seq = mesh.shape["fsdp"], mesh.shape["seq"]
    in_specs = (
        P(None, "fsdp", "seq", None),
        P("fsdp", None),
        P("fsdp"),
        P("fsdp", None),
        P("fsdp", None),
        P("fsdp", None),
        P(None, "fsdp"),
        P(None, "fsdp", "seq"),
        P(),
        P(None, "fsdp", "seq", None),
    )
    out_specs = (
        P(None, "fsdp", "seq", None),
        P(None, "fsdp", "seq", None),
        P("fsdp", None),
        P("fsdp"),
        P("fsdp"),
        P("fsdp", None),
        P("fsdp", None),
        P("fsdp", None),
        P(None, "fsdp"),
    )

    def local(*args):
        body = on_device_tiled if (n_fsdp, n_seq) == (8, 4) else on_device
        return body(*args, n_fsdp=n_fsdp, n_seq=n_seq)

    return jax.shard_map(local, mesh=mesh, in_specs=in_specs, out_specs=out_specs, check_vma=False)
```

```python
import functools

import jax
import jax.numpy as jnp
import numpy as np
from jax import lax
from jax.experimental import pallas as pl
from jax.experimental.pallas import tpu as pltpu
from jax.sharding import PartitionSpec as P

HEADS = 9
KV_HEADS = 3
HEAD_DIM = 64
GROUP = HEADS // KV_HEADS
QW = HEADS * HEAD_DIM
KW = KV_HEADS * HEAD_DIM
EPS = 1e-05
ROPE_BASE = 100000.0
MASKED = -1000000000.0
BF = jnp.bfloat16
F32 = jnp.float32


def dot(a, b, ca, cb):
    return lax.dot_general(a, b, (((ca,), (cb,)), ((), ())), preferred_element_type=F32)


def rotary(values, cosine, sine):
    half = values.shape[-1] // 2
    a, b = values[..., :half], values[..., half:]
    return jnp.concatenate([a * cosine - b * sine, b * cosine + a * sine], axis=-1)


def norm_parts(values):
    factor = lax.rsqrt(jnp.mean(values * values, axis=-1, keepdims=True) + EPS)
    return factor, values * factor


def norm_back(grad_in, gain, factor, normed):
    scaled = grad_in * gain
    return factor * (scaled - normed * jnp.mean(scaled * normed, axis=-1, keepdims=True))


def whole(*shape_dtypes):
    return [pl.BlockSpec(memory_space=pltpu.VMEM) for _ in shape_dtypes]


def call(kernel, scalars, arrays, outs, flops, scratch=()):
    specs = [pl.BlockSpec(memory_space=pltpu.SMEM)] * len(scalars) + whole(*arrays)
    moved = sum(a.size * a.dtype.itemsize for a in arrays) + sum(
        int(np.prod(o.shape)) * o.dtype.itemsize for o in outs
    )
    return pl.pallas_call(
        kernel,
        out_shape=outs,
        in_specs=specs,
        out_specs=whole(*outs),
        scratch_shapes=[pltpu.VMEM(shape, F32) for shape in scratch],
        compiler_params=pltpu.CompilerParams(vmem_limit_bytes=52 * 1024 * 1024),
        cost_estimate=pl.CostEstimate(flops=int(flops), bytes_accessed=moved, transcendentals=0),
    )(*scalars, *arrays)


def sds(shape, dtype):
    return jax.ShapeDtypeStruct(shape, dtype)


def turn(x, cosine, sine):
    tiles = []
    low = lax.broadcasted_iota(jnp.int32, (1, 128), 1) % HEAD_DIM < HEAD_DIM // 2
    for t in range(x.shape[1] // 128):
        part = x[:, 128 * t : 128 * t + 128]
        other = jnp.where(low, pltpu.roll(part, 96, 1), pltpu.roll(part, 32, 1))
        tiles.append(part * cosine + other * sine)
    return tiles


def turn_kv(x, cosine, sine):
    lane = lax.broadcasted_iota(jnp.int32, (1, 128), 1)
    first, second = turn(x[:, :256], cosine, sine)
    second = jnp.where(lane < KW - 128, second, x[:, 128:256])
    return jnp.concatenate([first, second, x[:, 256:]], axis=1)


def tables(seq, order, cos_ref, sin_ref):
    cosine = jnp.concatenate([cos_ref[seq ^ o] for o in order], axis=0)
    sine = jnp.concatenate([sin_ref[seq ^ o] for o in order], axis=0)
    return cosine, sine


def heads_to_rows(x, g):
    return jnp.concatenate(
        [x[:, HEAD_DIM * h : HEAD_DIM * (h + 1)] for h in range(GROUP * g, GROUP * (g + 1))], axis=0
    )


def rows_to_heads(parts, length):
    return jnp.concatenate(
        [p[length * r : length * (r + 1)] for p in parts for r in range(GROUP)], axis=1
    )


def attention_forward(order, length, seq_ref, blocks, wq, wkv, bq, bkv, gain, cos, sin, mask,
                      att_o, q_o, k_o, v_o, lse_o):
    seq = seq_ref[0]
    cosine, sine = tables(seq, order, cos, sin)
    width = gain.shape[1]
    for b in range(blocks.shape[1] // length):
        x = blocks[:, b * length : (b + 1) * length, :width].astype(F32)
        x = x.reshape(len(order) * length, width)
        first = (norm_parts(x)[1] * gain[...]).astype(BF)
        kv = dot(first, wkv[...], 1, 0) + bkv[...]
        q = dot(first[:length], wq[...], 1, 0) + bq[...]
        q = jnp.concatenate(turn(q, cosine[:length], sine[:length]), axis=1).astype(BF)
        q = q * jnp.asarray(HEAD_DIM ** (-0.5), BF)
        kv = turn_kv(kv, cosine, sine).astype(BF)
        allowed = jnp.concatenate([mask[b]] * GROUP, axis=0) > 0.0
        parts = []
        for g in range(KV_HEADS):
            qg = heads_to_rows(q, g)
            kg = kv[:, HEAD_DIM * g : HEAD_DIM * (g + 1)]
            vg = kv[:, KW + HEAD_DIM * g : KW + HEAD_DIM * (g + 1)]
            q_o[b, g] = qg
            k_o[b, g] = kg
            v_o[b, g] = vg
            scores = jnp.where(allowed, dot(qg, kg, 1, 1), MASKED)
            top = jnp.max(scores, axis=-1, keepdims=True)
            e = jnp.exp(scores - top)
            total = jnp.sum(e, axis=-1, keepdims=True)
            lse_o[b, g] = jnp.log(total) + top
            probs = (e * (1.0 / total)).astype(BF)
            parts.append(dot(probs, vg, 1, 0))
        att_o[b * length : (b + 1) * length, :] = rows_to_heads(parts, length).astype(BF)


def feed_forward(attended, source, wo, wgu, wd, gain, cot, weight,
                 out_o, down_o, gu_o, mid_o, wout_o, attg_o, gain_o):
    units = wd.shape[0]
    step = units // 3
    att = attended[...]
    middle = source[...].astype(F32) + dot(att, wo[...], 1, 0)
    scale_two, normed = norm_parts(middle)
    g2 = gain[...]
    second = (normed * g2).astype(BF)
    out_grad = cot[...].astype(F32) * weight[...]
    feed_grad = out_grad.astype(BF)
    feed = None
    back = None
    for j in range(0, units, step):
        wg = wgu[:, j : j + step]
        wu = wgu[:, units + j : units + j + step]
        wdj = wd[j : j + step, :]
        gate = dot(second, wg, 1, 0)
        up = dot(second, wu, 1, 0)
        sig = jax.nn.sigmoid(gate)
        act = gate * sig
        product = (act * up).astype(BF)
        part = dot(product, wdj, 1, 0)
        feed = part if feed is None else feed + part
        down_o[j : j + step, :] = dot(product, feed_grad, 0, 0).astype(BF)
        pgrad = dot(feed_grad, wdj, 1, 1)
        ggrad = (pgrad * up * (sig * (1.0 + gate * (1.0 - sig)))).astype(BF)
        ugrad = (pgrad * act).astype(BF)
        gu_o[:, j : j + step] = dot(second, ggrad, 0, 0).astype(BF)
        gu_o[:, units + j : units + j + step] = dot(second, ugrad, 0, 0).astype(BF)
        part = dot(ggrad, wg, 1, 1) + dot(ugrad, wu, 1, 1)
        back = part if back is None else back + part
    out_o[...] = (middle + feed).astype(BF)
    gain_o[...] = jnp.sum(back * normed, axis=0, keepdims=True)
    middle_grad = out_grad + norm_back(back, g2, scale_two, normed)
    mid_o[...] = middle_grad
    branch = middle_grad.astype(BF)
    wout_o[...] = dot(att, branch, 0, 0).astype(BF)
    attg_o[...] = dot(branch, wo[...], 1, 1).astype(BF)


def attention_backward(order, length, seq_ref, blocks, wq, wkv, gain, cos, sin, mask, q_i, k_i, v_i,
                       lse, attg, dq_o, dkv_o, wgrad_o, bias_o, gain_o):
    seq = seq_ref[0]
    cosine, sine = tables(seq, order, cos, sin)
    width = gain.shape[1]
    q_wgrad = kv_wgrad = bias_q = bias_kv = gain_sum = None
    for b in range(blocks.shape[1] // length):
        x = blocks[:, b * length : (b + 1) * length, :width].astype(F32)
        x = x.reshape(len(order) * length, width)
        normed = norm_parts(x)[1]
        first = (normed * gain[...]).astype(BF)
        allowed = jnp.concatenate([mask[b]] * GROUP, axis=0) > 0.0
        ag = attg[b * length : (b + 1) * length, :]
        dqs, dks, dvs = [], [], []
        for g in range(KV_HEADS):
            qg, kg, vg = q_i[b, g], k_i[b, g], v_i[b, g]
            agg = heads_to_rows(ag, g)
            p = jnp.exp(jnp.where(allowed, dot(qg, kg, 1, 1), MASKED) - lse[b, g])
            dvs.append(dot(p.astype(BF), agg, 0, 0))
            pg = dot(agg, vg, 1, 1)
            inner = jnp.sum(p * pg, axis=-1, keepdims=True)
            ds = (p * (pg - inner)).astype(BF)
            dqs.append(dot(ds, kg, 1, 0) * HEAD_DIM ** (-0.5))
            dks.append(dot(ds, qg, 0, 0))
        dq = rows_to_heads(dqs, length)
        dq = jnp.concatenate([dq, jnp.zeros((length, 64), F32)], axis=1)
        dq = jnp.concatenate(turn(dq, cosine[:length], -sine[:length]), axis=1).astype(BF)
        dkv = jnp.concatenate(dks + dvs, axis=1)
        dkv = turn_kv(dkv, cosine, -sine).astype(BF)
        dq_o[b * length : (b + 1) * length, :] = dq
        for r in range(len(order)):
            dkv_o[r, b * length : (b + 1) * length, :] = dkv[r * length : (r + 1) * length, :]
        wq_part = dot(first[:length], dq, 0, 0)
        wkv_part = dot(first, dkv, 0, 0)
        bq_part = jnp.sum(dq.astype(F32), axis=0, keepdims=True)
        bkv_part = jnp.sum(dkv.astype(F32), axis=0, keepdims=True)
        e_kv = dot(dkv, wkv[...], 1, 1) * normed
        e_q = dot(dq[:, :QW], wq[:, :QW], 1, 1) * normed[:length]
        g_part = jnp.sum(e_kv, axis=0, keepdims=True) + jnp.sum(e_q, axis=0, keepdims=True)
        if q_wgrad is None:
            q_wgrad, kv_wgrad, bias_q, bias_kv, gain_sum = wq_part, wkv_part, bq_part, bkv_part, g_part
        else:
            q_wgrad, kv_wgrad = q_wgrad + wq_part, kv_wgrad + wkv_part
            bias_q, bias_kv, gain_sum = bias_q + bq_part, bias_kv + bkv_part, gain_sum + g_part
    wgrad_o[...] = jnp.concatenate([q_wgrad[:, :QW], kv_wgrad], axis=1).astype(BF)
    bias_o[...] = jnp.concatenate([bias_q[:, :QW], bias_kv], axis=1)
    gain_o[...] = gain_sum


def input_gradient(dq, own, a, b, c, source, mid, wq, wkv, gain, out_o):
    kv = own[...].astype(F32) + a[...].astype(F32) + b[...].astype(F32) + c[...].astype(F32)
    first_grad = dot(dq[:, :QW], wq[:, :QW], 1, 1) + dot(kv.astype(BF), wkv[...], 1, 1)
    scale_one, normed = norm_parts(source[...].astype(F32))
    out_o[...] = mid[...] + norm_back(first_grad, gain[...], scale_one, normed)

def chosen(flag, a, b):
    return jnp.where(flag != 0, b, a)


class Blocks:
    def __init__(self, *refs):
        self.refs = refs
        self.shape = (len(refs),) + refs[0].shape

    def __getitem__(self, key):
        return jnp.stack([ref[key[1:]] for ref in self.refs])


def cut_qkv(core_bit, meta, w, bias, gains, out_o, all_s):
    rows = w.shape[0]
    n = bias.shape[1]
    all_s[:rows, :] = w[...].astype(F32)
    all_s[rows:, :] = jnp.zeros((8, w.shape[1]), F32)
    all_s[rows : rows + 1, :n] = bias[...].astype(F32)
    for i in range(2):
        all_s[rows : rows + 1, n + rows * i : n + rows * (i + 1)] = gains[i : i + 1, :].astype(F32)
    half = out_o.shape[0]
    at = pl.multiple_of((meta[0] & core_bit) * half, 8)
    out_o[...] = all_s[pl.ds(at, half), :].astype(BF)


def first_forward(order, length, d_rows, n_bias, meta, b0, b1, b2, b3, a00, a10, a01, a11, cos, sin, mask,
                  att_o, q_o, k_o, v_o, lse_o, w_o, gain_o, w_s, b_s):
    blocks = Blocks(b0, b1, b2, b3)
    core, x = meta[0] & 1, meta[1] & 1
    cut = a00.shape[2]
    for x_rel, c_rel, piece in ((0, 0, a00), (1, 0, a10), (0, 1, a01), (1, 1, a11)):
        for z0 in range(2):
            for z1 in range(2):
                at = (z1 * 4 + z0 * 2 + (x ^ x_rel)) * 2 * cut + (core ^ c_rel) * cut
                w_s[pl.ds(pl.multiple_of(at, 8), cut), :] = piece[z0, z1].astype(F32)
    n_f = w_s.shape[0] // (2 * cut)
    starts = [2 * cut * f for f in range(n_f)]
    w_o[...] = jnp.concatenate([w_s[at : at + d_rows, :] for at in starts], axis=0).astype(BF)
    lines = [w_s[at + d_rows : at + d_rows + 1, :] for at in starts]
    b_s[...] = jnp.concatenate([line[:, :n_bias] for line in lines], axis=1)
    for i in range(2):
        at = n_bias + d_rows * i
        gain_o[i : i + 1, :] = jnp.concatenate([line[:, at : at + d_rows] for line in lines], axis=1)
    wide = QW + 64
    attention_forward(order, length, meta, blocks, w_o[:, :wide], w_o[:, QW:], b_s[:, :wide], b_s[:, QW:],
                      gain_o[0:1, :], cos, sin, mask, att_o, q_o, k_o, v_o, lse_o)


def turned(out, value):
    length = out.shape[2]
    for b in range(out.shape[0]):
        out[b] = value[length * b : length * (b + 1)].T.astype(out.dtype)


def rel(meta, f):
    r = f ^ meta[1]
    return r & 1, (r >> 1) & 1, (r >> 2) & 1


def feed_forward_pieces(d_rows, ff_rows, meta, attended, source, b00, b10, b01, b11,
                        g000, g100, g010, g110, g001, g101, g011, g111, gains, cot, weight,
                        out_o, gk_o, gg_o, dk_o, dg_o, mid_o, attg_o, gain_o, down_s, wout_s):
    core, y, x_own = meta[0] & 1, (meta[0] >> 1) & 1, meta[1] & 1
    n_f = 8
    hf = n_f // 2
    part_d = ff_rows // 4
    part_o = d_rows // 3
    cut = b00.shape[2] - ff_rows // 2

    def b_rows(z0, z1, x, c, rows):
        low = chosen(x_own ^ x, b00[z0, z1, rows, :], b10[z0, z1, rows, :])
        high = chosen(x_own ^ x, b01[z0, z1, rows, :], b11[z0, z1, rows, :])
        return chosen(core ^ c, low, high)

    def quarter(near, far):
        parts = []
        for f in range(n_f):
            z1, z0, x = f >> 2, (f >> 1) & 1, f & 1
            mine, other = near[z0, z1].astype(F32), far[z0, z1].astype(F32)
            parts.append(chosen(x_own ^ x, mine, other))
        return jnp.concatenate(parts, axis=0).astype(BF)

    wo = []
    for f in range(n_f):
        z1, z0, x = f >> 2, (f >> 1) & 1, f & 1
        wo.append(b_rows(z0, z1, x, 0, slice(ff_rows // 2, None)).astype(F32))
        wo.append(b_rows(z0, z1, x, 1, slice(ff_rows // 2, None)).astype(F32)[: d_rows - cut])
    wo = jnp.concatenate(wo, axis=0).astype(BF)
    att = attended[...]
    middle = source[...].astype(F32) + dot(att, wo, 1, 0)
    scale_two, normed = norm_parts(middle)
    g2 = gains[1:2, :]
    second = (normed * g2).astype(BF)
    out_grad = cot[...].astype(F32) * weight[...]
    feed_grad = out_grad.astype(BF)
    feed = back = None
    for c_rel in (1, 0):
        first_q = quarter(g001, g101) if c_rel else quarter(g000, g100)
        second_q = quarter(g011, g111) if c_rel else quarter(g010, g110)
        wg = chosen(y, first_q, second_q)
        wu = chosen(y, second_q, first_q)
        h = core ^ c_rel
        wd = []
        for i in range(hf):
            for c in range(2):
                wd.append(b_rows(i >> 1, h, i & 1, c, slice(0, ff_rows // 2)))
        wd = jnp.concatenate(wd, axis=0)
        gate = dot(second, wg, 1, 0)
        up = dot(second, wu, 1, 0)
        sig = jax.nn.sigmoid(gate)
        act = gate * sig
        product = (act * up).astype(BF)
        part = dot(product, wd, 1, 0)
        feed = part if feed is None else feed + part
        down_s[...] = dot(product, feed_grad, 0, 0)
        pgrad = dot(feed_grad, wd, 1, 1)
        ggrad = (pgrad * up * (sig * (1.0 + gate * (1.0 - sig)))).astype(BF)
        ugrad = (pgrad * act).astype(BF)
        part = dot(ggrad, wg, 1, 1) + dot(ugrad, wu, 1, 1)
        back = part if back is None else back + part
        for i in range(hf):
            x, z0, z1 = rel(meta, hf * h + i)
            for yy in range(2):
                for c_to, to in ((0, dk_o), (1, dg_o)):
                    at = pl.multiple_of(i * ff_rows + (yy * 2 + (core ^ c_to)) * part_d, 16)
                    to[y ^ yy, x, z0, z1, :part_d, :] = down_s[pl.ds(at, part_d), :].astype(BF)
        to = gg_o if c_rel else gk_o
        for yy, grad in ((0, ggrad), (1, ugrad)):
            wgrad = dot(second, grad, 0, 0)
            for f in range(n_f):
                x, z0, z1 = rel(meta, f)
                to[x, y ^ yy, z0, z1] = wgrad[d_rows * f : d_rows * (f + 1), :].astype(BF)
    turned(out_o, middle + feed)
    gain_o[...] = jnp.sum(back * normed, axis=0, keepdims=True)
    middle_grad = out_grad + norm_back(back, g2, scale_two, normed)
    mid_o[...] = middle_grad
    branch = middle_grad.astype(BF)
    attg_o[...] = dot(branch, wo, 1, 1).astype(BF)
    wout = dot(att, branch, 0, 0)
    for f in range(n_f):
        wout_s[f, :d_rows, :] = wout[d_rows * f : d_rows * (f + 1), :]
        wout_s[f, d_rows:, :] = jnp.zeros((part_o, wout.shape[1]), F32)
    for f in range(n_f):
        x, z0, z1 = rel(meta, f)
        for yy in range(2):
            for c_to, to in ((0, dk_o), (1, dg_o)):
                at = pl.multiple_of((yy * 2 + (core ^ c_to)) * part_o, 8)
                to[y ^ yy, x, z0, z1, part_d:, :] = wout_s[f, pl.ds(at, part_o), :].astype(BF)


def attention_backward_pieces(order, length, d_rows, meta, b0, b1, b2, b3, w, gains, cos, sin, mask, q_i, k_i, v_i,
                              lse, attg, gain_two, dq_o, dk_o, dg_o, rk_o, rg_o, w_s, bias_s, gain_s, small_s):
    blocks = Blocks(b0, b1, b2, b3)
    half = len(order) // 2

    class Pieces:
        def __setitem__(self, key, value):
            ref = dk_o if key[0] < half else dg_o
            ref[(key[0] % half,) + key[1:]] = value

    class Wgrad:
        def __setitem__(self, key, value):
            w_s[:, : 2 * KW] = value[:, QW:].astype(F32)
            w_s[:, 2 * KW : 2 * KW + QW] = value[:, :QW].astype(F32)
            w_s[:, 2 * KW + QW :] = jnp.zeros((value.shape[0], 64), F32)

    wide = QW + 64
    attention_backward(order, length, meta, blocks, w[:, :wide], w[:, QW:], gains[0:1, :], cos, sin, mask,
                       q_i, k_i, v_i, lse, attg, dq_o, Pieces(), Wgrad(), bias_s, gain_s)
    n_f = small_s.shape[0]
    qk, v = (QW + KW) // n_f, KW // n_f
    bias, g1, g2 = bias_s[...], gain_s[...], gain_two[...]
    for f in range(n_f):
        line = jnp.concatenate(
            [
                bias[:, qk * f : qk * (f + 1)],
                bias[:, QW + KW + v * f : QW + KW + v * (f + 1)],
                g1[:, d_rows * f : d_rows * (f + 1)],
                jnp.zeros((1, 256 - qk - v - d_rows), F32),
                g2[:, d_rows * f : d_rows * (f + 1)],
                jnp.zeros((1, 768 - d_rows), F32),
            ],
            axis=1,
        )
        small_s[f] = jnp.broadcast_to(line, (8, 1024))
    core, y = meta[0] & 1, (meta[0] >> 1) & 1
    for f in range(n_f):
        x, z0, z1 = rel(meta, f)
        for yy in range(2):
            for c_to, to in ((0, rk_o), (1, rg_o)):
                at = pl.multiple_of((yy * 2 + (core ^ c_to)) * 256, 256)
                block = [w_s[d_rows * f : d_rows * (f + 1), pl.ds(at, 256)], small_s[f, :, pl.ds(at, 256)]]
                to[x, y ^ yy, z0, z1] = jnp.concatenate(block, axis=0).astype(BF)


def input_gradient_two(dq, own, other, source, mid, w, gains, out_o):
    kv = (own[...].astype(F32) + other[...].astype(F32)).astype(BF)
    first_grad = dot(dq[:, :QW], w[:, :QW], 1, 1) + dot(kv, w[:, QW:], 1, 1)
    scale_one, normed = norm_parts(source[...].astype(F32))
    turned(out_o, mid[...] + norm_back(first_grad, gains[0:1, :], scale_one, normed))


def place_gate(meta, p00, p10, p01, p11, out_o):
    seq = meta[0]
    n = p00.shape[1]
    for piece, o in ((p00[...], 0), (p10[...], 2), (p01[...], 1), (p11[...], 3)):
        out_o[:, pl.ds(pl.multiple_of((seq ^ o) * n, 128), n)] = piece.astype(F32)


def place_down(part_d, meta, p00, p10, p01, p11, out_o, wout_o):
    seq = meta[0]
    part_o = p00.shape[0] - part_d
    for piece, o in ((p00[...], 0), (p10[...], 2), (p01[...], 1), (p11[...], 3)):
        piece = piece.astype(F32)
        to = seq ^ o
        out_o[pl.ds(pl.multiple_of(to * part_d, 16), part_d), :] = piece[:part_d]

        @pl.when(to < 3)
        def _():
            wout_o[pl.ds(pl.multiple_of(to * part_o, 8), part_o), :] = piece[part_d:]


def place_qkv(qk, v, meta, p00, p10, p01, p11, w_o, bqk_o, bv_o, gains_o, all_s):
    seq = meta[0]
    n = p00.shape[1]
    for piece, o in ((p00[...], 0), (p10[...], 2), (p01[...], 1), (p11[...], 3)):
        all_s[:, pl.ds(pl.multiple_of((seq ^ o) * n, 128), n)] = piece.astype(F32)
    d_rows = w_o.shape[0]
    w_o[:, :QW] = all_s[:d_rows, 2 * KW : 2 * KW + QW]
    w_o[:, QW:] = all_s[:d_rows, : 2 * KW]
    line = all_s[d_rows : d_rows + 1, :]
    bqk_o[...] = line[:, :qk]
    bv_o[...] = line[:, qk : qk + v]
    gains_o[0:1, :] = line[:, qk + v : qk + v + d_rows]
    gains_o[1:2, :] = line[:, 256 : 256 + d_rows]


class Net:
    def __init__(self, n_fsdp, n_seq):
        self.n_fsdp, self.n_seq = n_fsdp, n_seq
        self.total = n_fsdp * n_seq
        f, s = lax.axis_index("fsdp"), lax.axis_index("seq")
        self.index = f * n_seq + s
        self.seq_bits = [1 << b for b in range(n_seq.bit_length() - 1)]
        self.fsdp_bits = [n_seq << b for b in range(n_fsdp.bit_length() - 1)]

    def swap(self, value, mask):
        pairs = [(i, i ^ mask) for i in range(self.total)]
        return lax.ppermute(value, ("fsdp", "seq"), pairs)

    def bit(self, mask):
        return (self.index & mask) != 0

    def both(self, mine, mask, axis, other=None):
        other = self.swap(mine, mask) if other is None else other
        high = self.bit(mask)
        return jnp.stack([jnp.where(high, other, mine), jnp.where(high, mine, other)], axis=axis)

    def half(self, value, mask, axis):
        return lax.dynamic_index_in_dim(
            value, self.bit(mask).astype(jnp.int32), axis, keepdims=False
        )

    def add_half(self, value, mask, axis):
        mine = self.bit(mask).astype(jnp.int32)
        keep = lax.dynamic_index_in_dim(value, mine, axis, keepdims=False)
        give = lax.dynamic_index_in_dim(value, 1 - mine, axis, keepdims=False)
        got = self.swap(give, mask)
        return (keep.astype(F32) + got.astype(F32)).astype(value.dtype)

    def gather_fsdp(self, value):
        for step, mask in enumerate(reversed(self.fsdp_bits)):
            value = self.both(value, mask, step)
        return value

    def scatter_fsdp(self, value, first_axis=0):
        count = len(self.fsdp_bits)
        for step, mask in enumerate(self.fsdp_bits):
            value = self.add_half(value, mask, first_axis + count - 1 - step)
        return value


def on_device(
    hidden, w_qkv, b_qkv, w_out, w_gate_up, w_down, norm_gains, segment_ids, token_counts, cotangent,
    n_fsdp, n_seq,
):
    net = Net(n_fsdp, n_seq)
    micro, batch, length, width = hidden.shape
    full_length = length * n_seq
    tokens_micro = batch * n_fsdp * full_length
    scale = HEAD_DIM ** (-0.5)
    rows = micro * batch * length
    d_rows = w_qkv.shape[0]
    ff_rows = w_down.shape[0]
    units = w_gate_up.shape[1] // 2
    qkv_w = w_qkv.shape[1]
    core = net.seq_bits[0]
    f_lead = (2,) * len(net.fsdp_bits)

    ids = segment_ids.reshape(rows, 1).astype(BF)
    block = jnp.concatenate(
        [hidden.reshape(rows, width), jnp.broadcast_to(ids, (rows, 64))], axis=1
    )
    blocks = block[None]
    for mask in reversed(net.seq_bits):
        blocks = jnp.concatenate([blocks, net.swap(blocks, mask)], axis=0)
    order = [0]
    for mask in reversed(net.seq_bits):
        order = order + [o ^ mask for o in order]
    seq_index = lax.axis_index("seq")
    block_ids = [seq_index ^ o for o in order]

    pad_rows = -(d_rows + 1) % 16 + 1
    extra = jnp.zeros((pad_rows, qkv_w), BF)
    small = jnp.concatenate([b_qkv, norm_gains.reshape(-1)])
    extra = extra.at[0, : small.shape[0]].set(small)
    shard_a = jnp.concatenate([w_qkv, extra], axis=0).reshape(2, -1, qkv_w)
    got_a = net.gather_fsdp(net.half(shard_a, core, 0))
    full_a = net.both(got_a, core, len(f_lead)).reshape(n_fsdp, d_rows + pad_rows, qkv_w)
    wf_qkv = full_a[:, :d_rows].reshape(n_fsdp * d_rows, qkv_w)
    smalls = full_a[:, d_rows]
    n_bias = b_qkv.shape[0]
    bias = smalls[:, :n_bias].reshape(-1).astype(F32)
    gains = smalls[:, n_bias : n_bias + 2 * d_rows].reshape(n_fsdp, 2, d_rows).astype(F32)
    gain_one = gains[:, 0].reshape(-1)
    gain_two = gains[:, 1].reshape(-1)

    pad_b = -(d_rows + ff_rows) % 16
    shard_b = jnp.concatenate([w_out, w_down, jnp.zeros((pad_b, width), BF)], axis=0)
    shard_b = shard_b.reshape(2, -1, width)
    got_b = net.gather_fsdp(net.half(shard_b, core, 0))

    parts = n_seq
    shard_c = w_gate_up.reshape(d_rows, parts, -1)
    got_c = net.gather_fsdp(lax.dynamic_index_in_dim(shard_c, seq_index, 1, keepdims=False))
    full_b = net.both(got_b, core, len(f_lead)).reshape(n_fsdp, -1, width)
    wf_out = full_b[:, :d_rows].reshape(n_fsdp * d_rows, width)
    wf_down = full_b[:, d_rows : d_rows + ff_rows].reshape(n_fsdp * ff_rows, width)
    got_c = got_c.reshape(n_fsdp * d_rows, -1)
    for mask in reversed(net.seq_bits):
        got_c = net.both(got_c, mask, got_c.ndim - 1)
    wf_gate_up = got_c.reshape(n_fsdp * d_rows, 2 * units)

    places = np.arange(full_length, dtype=np.float32)
    speeds = np.power(ROPE_BASE, -2.0 * np.arange(HEAD_DIM // 2, dtype=np.float32) / HEAD_DIM)
    angles = places[:, None] * speeds.astype(np.float32)[None, :]
    cos_t = np.tile(np.cos(angles), (1, 4)).reshape(n_seq, length, 128)
    sin_t = np.concatenate([-np.sin(angles), np.sin(angles)] * 2, axis=1).reshape(n_seq, length, 128)
    cos_t, sin_t = jnp.asarray(cos_t, F32), jnp.asarray(sin_t, F32)
    seqs = micro * batch
    seg_all = blocks[..., width].reshape(n_seq, seqs, length).transpose(1, 0, 2)
    own_places = seq_index * length + jnp.arange(length, dtype=jnp.int32)
    key_places = jnp.stack(block_ids)[:, None] * length + jnp.arange(length, dtype=jnp.int32)
    allowed = (seg_all[:, 0, :, None] == seg_all.reshape(seqs, 1, -1)) & (
        own_places[None, :, None] >= key_places.reshape(1, 1, -1)
    )
    allowed = allowed.astype(F32)
    seq_scalar = seq_index.astype(jnp.int32).reshape(1)
    wq, wkv = wf_qkv[:, : QW + 64], wf_qkv[:, QW:]
    gain_one, gain_two = gain_one[None], gain_two[None]
    source = hidden.reshape(rows, width)
    n_all = n_seq * rows
    attended, q_s, k_s, v_s, lse = call(
        functools.partial(attention_forward, order, length),
        [seq_scalar],
        [blocks, wq, wkv, bias[None, : QW + 64], bias[None, QW:], gain_one, cos_t, sin_t, allowed],
        [
            sds((rows, QW), BF),
            sds((seqs, KV_HEADS, GROUP * length, HEAD_DIM), BF),
            sds((seqs, KV_HEADS, full_length, HEAD_DIM), BF),
            sds((seqs, KV_HEADS, full_length, HEAD_DIM), BF),
            sds((seqs, KV_HEADS, GROUP * length, 1), F32),
        ],
        2 * n_all * width * 2 * KW + 2 * rows * width * QW + 4 * rows * full_length * QW,
    )

    weight = tokens_micro / token_counts.astype(F32)
    weight = jnp.repeat(weight, batch * length)[:, None]
    block_out, down_grad, gate_up_wgrad, middle_grad, out_wgrad, attended_grad, gain_two_grad = call(
        feed_forward,
        [],
        [attended, source, wf_out, wf_gate_up, wf_down, gain_two, cotangent.reshape(rows, width), weight],
        [
            sds((rows, width), BF),
            sds((units, width), BF),
            sds((width, 2 * units), BF),
            sds((rows, width), F32),
            sds((QW, width), BF),
            sds((rows, QW), BF),
            sds((1, width), F32),
        ],
        6 * rows * width * 3 * units + 6 * rows * width * QW,
    )
    block_out = block_out.reshape(hidden.shape)

    def seq_axes(value, axis, masks):
        for mask in masks:
            value = net.add_half(value, mask, axis)
        return value

    quarter = (2,) * len(net.seq_bits)
    n_f = len(f_lead)
    red_down = down_grad.reshape(f_lead + quarter + (ff_rows // n_seq, width))
    for step, mask in enumerate(net.seq_bits):
        red_down = net.add_half(red_down, mask, n_f + len(quarter) - 1 - step)
    red_down = net.scatter_fsdp(red_down)

    red_gate = gate_up_wgrad.reshape(f_lead + (d_rows,) + quarter + (2 * units // n_seq,))
    red_gate = net.add_half(red_gate, core, n_f + len(quarter))
    red_gate = net.add_half(red_gate, net.fsdp_bits[0], n_f - 1)
    for step, mask in enumerate(net.seq_bits[1:]):
        red_gate = net.add_half(red_gate, mask, n_f - 1 + len(quarter) - 1 - step)
    for step, mask in enumerate(net.fsdp_bits[1:]):
        red_gate = net.add_half(red_gate, mask, n_f - 2 - step)

    dq, dkv, qkv_wgrad, bias_grad, gain_one_grad = call(
        functools.partial(attention_backward, order, length),
        [seq_scalar],
        [blocks, wq, wkv, gain_one, cos_t, sin_t, allowed, q_s, k_s, v_s, lse, attended_grad],
        [
            sds((rows, QW + 64), BF),
            sds((n_seq, rows, 2 * KW), BF),
            sds((width, qkv_w), BF),
            sds((1, qkv_w), F32),
            sds((1, width), F32),
        ],
        4 * n_all * width * 2 * KW + 4 * rows * width * QW + 10 * rows * full_length * QW,
    )
    kv_parts = [dkv[0]]
    for place, mask_bits in enumerate(order):
        if mask_bits:
            kv_parts.append(net.swap(dkv[place], mask_bits))
    (hidden_grad,) = call(
        input_gradient,
        [],
        [dq, *kv_parts, source, middle_grad, wq, wkv, gain_one],
        [sds((rows, width), F32)],
        2 * rows * width * qkv_w,
    )
    hidden_grad = hidden_grad.reshape(hidden.shape)
    bias_grad, gain_one_grad, gain_two_grad = bias_grad[0], gain_one_grad[0], gain_two_grad[0]

    qk_rows, v_rows = (QW + KW) // n_fsdp, KW // n_fsdp
    small_grads = jnp.concatenate(
        [
            bias_grad[: QW + KW].reshape(n_fsdp, qk_rows),
            bias_grad[QW + KW :].reshape(n_fsdp, v_rows),
            gain_one_grad.reshape(n_fsdp, d_rows),
            gain_two_grad.reshape(n_fsdp, d_rows),
        ],
        axis=1,
    ).astype(BF)
    wide = qkv_w + width
    small_pad = jnp.zeros((n_fsdp, pad_rows, wide), BF)
    small_pad = small_pad.at[:, 0, : small_grads.shape[1]].set(small_grads)
    rest = jnp.concatenate([qkv_wgrad, out_wgrad], axis=1)
    rest = jnp.concatenate([rest.reshape(n_fsdp, d_rows, wide), small_pad], axis=1)
    rest = rest.reshape(f_lead + (d_rows + pad_rows,) + quarter + (wide // n_seq,))
    for step, mask in enumerate(net.seq_bits):
        rest = net.add_half(rest, mask, n_f + 1 + len(quarter) - 1 - step)
    rest = net.scatter_fsdp(rest)

    def seq_back(value, axis):
        for step, mask in enumerate(reversed(net.seq_bits)):
            value = net.both(value, mask, axis + step)
        return value

    out_down = seq_back(red_down, 0).reshape(ff_rows, width).astype(F32)
    out_gate = seq_back(red_gate, 1).reshape(d_rows, 2 * units).astype(F32)
    out_rest = seq_back(rest, 1).reshape(d_rows + pad_rows, wide).astype(F32)
    line = out_rest[d_rows]
    edge = qk_rows + v_rows
    return (
        block_out,
        hidden_grad,
        out_rest[:d_rows, :qkv_w],
        line[:qk_rows],
        line[qk_rows:edge],
        out_rest[:d_rows, qkv_w:],
        out_gate,
        out_down,
        line[edge : edge + 2 * d_rows].reshape(2, d_rows),
    )


def after(value, *others):
    return lax.optimization_barrier((value, *others))[0]


def rope_tables(full_length, n_seq):
    places = np.arange(full_length, dtype=np.float32)
    speeds = np.power(ROPE_BASE, -2.0 * np.arange(HEAD_DIM // 2, dtype=np.float32) / HEAD_DIM)
    angles = places[:, None] * speeds.astype(np.float32)[None, :]
    cos_t = np.tile(np.cos(angles), (1, 4)).reshape(n_seq, -1, 128)
    sin_t = np.concatenate([-np.sin(angles), np.sin(angles)] * 2, axis=1).reshape(n_seq, -1, 128)
    return jnp.asarray(cos_t, F32), jnp.asarray(sin_t, F32)


def on_device_tiled(
    hidden, w_qkv, b_qkv, w_out, w_gate_up, w_down, norm_gains, segment_ids, token_counts, cotangent,
    n_fsdp, n_seq,
):
    net = Net(n_fsdp, n_seq)
    micro, batch, length, width = hidden.shape
    full_length = length * n_seq
    tokens_micro = batch * n_fsdp * full_length
    rows = micro * batch * length
    seqs = micro * batch
    d_rows, qkv_w = w_qkv.shape
    ff_rows = w_down.shape[0]
    units = w_gate_up.shape[1] // 2
    n_bias = b_qkv.shape[0]
    core, ybit = net.seq_bits
    xbit, znear, zfar = net.fsdp_bits
    order = [0, 2, 1, 3]
    seq_index = lax.axis_index("seq")
    meta = jnp.stack([seq_index, lax.axis_index("fsdp")]).astype(jnp.int32)
    source = hidden.reshape(rows, width)

    (a0,) = call(
        functools.partial(cut_qkv, core),
        [meta],
        [w_qkv, b_qkv[None], norm_gains],
        [sds(((d_rows + 8) // 2, qkv_w), BF)],
        1e8,
        [(d_rows + 8, qkv_w)],
    )
    a1 = net.both(a0, zfar, 0)

    ids = segment_ids.reshape(rows, 1).astype(BF)
    block = jnp.concatenate([source, jnp.broadcast_to(ids, (rows, 64))], axis=1)
    block = after(block, a0)
    block_y = net.swap(block, ybit)
    block_c = net.swap(block, core)

    quarter = 2 * units // n_seq
    gu0 = lax.dynamic_slice_in_dim(after(w_gate_up, a0), seq_index * quarter, quarter, axis=1)
    half_b = jnp.concatenate(
        [
            w_down.reshape(2, ff_rows // 2, width),
            jnp.concatenate([w_out, jnp.zeros((8, width), BF)], axis=0).reshape(2, -1, width),
        ],
        axis=1,
    )
    b0 = net.half(after(half_b, a0), core, 0)
    a2 = net.both(a1, znear, 0)
    a_x = net.swap(a2, xbit)
    a_c = net.swap(a2, core)
    gu1 = net.both(gu0, zfar, 0)
    b1 = net.both(b0, zfar, 0)
    gu2 = net.both(after(gu1, a2), znear, 0)
    b2 = net.both(after(b1, a2), znear, 0)
    block_yc = net.swap(block_y, core)
    a_xc = net.swap(a_x, core)
    gu2 = after(gu2, a_x)
    b2 = after(b2, a_x)
    gu_x = net.swap(gu2, xbit)
    gu_y = net.swap(gu2, ybit)
    b_x = net.swap(b2, xbit)
    gu_c = net.swap(gu2, core)
    b_c = net.swap(b2, core)
    a_xc = after(a_xc, gu2, b2)

    cos_t, sin_t = rope_tables(full_length, n_seq)
    block_ids = [seq_index ^ o for o in order]
    blocks = [block, block_y, block_c, block_yc]
    seg_all = jnp.stack([b[:, width].reshape(seqs, length) for b in blocks], axis=1)
    own_places = seq_index * length + jnp.arange(length, dtype=jnp.int32)
    key_places = jnp.stack(block_ids)[:, None] * length + jnp.arange(length, dtype=jnp.int32)
    allowed = (seg_all[:, 0, :, None] == seg_all.reshape(seqs, 1, -1)) & (
        own_places[None, :, None] >= key_places.reshape(1, 1, -1)
    )
    allowed = allowed.astype(F32)
    attended, q_s, k_s, v_s, lse, wf, gains = call(
        functools.partial(first_forward, order, length, d_rows, n_bias),
        [meta],
        [*blocks, a2, a_x, a_c, a_xc, cos_t, sin_t, allowed],
        [
            sds((rows, QW), BF),
            sds((seqs, KV_HEADS, GROUP * length, HEAD_DIM), BF),
            sds((seqs, KV_HEADS, full_length, HEAD_DIM), BF),
            sds((seqs, KV_HEADS, full_length, HEAD_DIM), BF),
            sds((seqs, KV_HEADS, GROUP * length, 1), F32),
            sds((width, qkv_w), BF),
            sds((2, width), F32),
        ],
        1.2e10,
        [(n_fsdp * (d_rows + 8), qkv_w), (1, qkv_w)],
    )
    gu_x, gu_y, b_x = after(gu_x, attended), after(gu_y, attended), after(b_x, attended)
    gu_xy = net.swap(gu_x, ybit)
    gu_yc = net.swap(gu_y, core)
    gu_xc = net.swap(gu_x, core)
    b_xc = net.swap(b_x, core)
    gu_xyc = net.swap(gu_xy, core)
    gate_up = [gu2, gu_x, gu_y, gu_xy, gu_c, gu_xc, gu_yc, gu_xyc]

    weight = tokens_micro / token_counts.astype(F32)
    weight = jnp.repeat(weight, batch * length)[:, None]
    lead = (2, 2, 2, 2)
    block_out, gate_keep, gate_give, down_keep, down_give, middle_grad, attended_grad, gain_two = call(
        functools.partial(feed_forward_pieces, d_rows, ff_rows),
        [meta],
        [attended, source, b2, b_x, b_c, b_xc, *gate_up, gains, cotangent.reshape(rows, width), weight],
        [
            sds((seqs, width, length), BF),
            sds(lead + (d_rows, units // 2), BF),
            sds(lead + (d_rows, units // 2), BF),
            sds(lead + (ff_rows // 4 + d_rows // 3, width), BF),
            sds(lead + (ff_rows // 4 + d_rows // 3, width), BF),
            sds((rows, width), F32),
            sds((rows, QW), BF),
            sds((1, width), F32),
        ],
        1.4e10,
        [(units // 2, width), (n_fsdp, d_rows + d_rows // 3, width)],
    )
    block_out = block_out.reshape(micro, batch, width, length).swapaxes(2, 3)

    def add(keep, got):
        return (keep.astype(F32) + got.astype(F32)).astype(BF)

    def halves(keep, got):
        return add(keep[0], got[0]), add(keep[1], got[1])

    gate, gate_give = halves(gate_keep, net.swap(gate_give, core))
    down, down_give = halves(down_keep, net.swap(down_give, core))
    attended_grad = after(attended_grad, gate_give, down_give)
    gate_got = net.swap(gate_give, xbit)
    down_got = net.swap(down_give, ybit)

    dq, dkv_keep, dkv_give, rest_keep, rest_give = call(
        functools.partial(attention_backward_pieces, order, length, d_rows),
        [meta],
        [*blocks, wf, gains, cos_t, sin_t, allowed, q_s, k_s, v_s, lse, attended_grad, gain_two],
        [
            sds((rows, QW + 64), BF),
            sds((2, rows, 2 * KW), BF),
            sds((2, rows, 2 * KW), BF),
            sds(lead + (d_rows + 8, 256), BF),
            sds(lead + (d_rows + 8, 256), BF),
        ],
        1.4e10,
        [(width, 1024), (1, qkv_w), (1, width), (n_fsdp, 8, 1024)],
    )
    dkv, dkv_give = halves(dkv_keep, net.swap(dkv_give, core))
    rest, rest_give = halves(rest_keep, after(net.swap(rest_give, core), gate_got))
    dkv_got = net.swap(dkv_give, ybit)
    rest_got = net.swap(rest_give, xbit)
    down, down_give = halves(down, down_got)
    down_got = net.swap(down_give, xbit)
    gate, gate_give = halves(gate, gate_got)
    gate_got = net.swap(gate_give, ybit)
    (hidden_grad,) = call(
        input_gradient_two,
        [],
        [dq, dkv, dkv_got, source, middle_grad, wf, gains],
        [sds((seqs, width, length), F32)],
        3e9,
    )
    rest_got = after(rest_got, hidden_grad)
    hidden_grad = hidden_grad.reshape(micro, batch, width, length).swapaxes(2, 3)
    rest, rest_give = halves(rest, rest_got)
    rest_got = net.swap(rest_give, ybit)
    parts, gots = [gate, down, rest], [gate_got, down_got, rest_got]
    for mask in (znear, zfar):
        pairs = [halves(part, got) for part, got in zip(parts, gots)]
        parts, gots = [keep for keep, _ in pairs], [net.swap(give, mask) for _, give in pairs]
    gate, down, rest = [add(part, got) for part, got in zip(parts, gots)]

    def spread(part):
        other = net.swap(part, ybit)
        return [part, other, net.swap(part, core), net.swap(other, core)]

    (out_gate,) = call(place_gate, [meta], spread(gate), [sds((d_rows, 2 * units), F32)], 0)
    out_down, out_wout = call(
        functools.partial(place_down, ff_rows // 4),
        [meta],
        spread(down),
        [sds((ff_rows, width), F32), sds((d_rows, width), F32)],
        0,
    )
    qk, v = (QW + KW) // n_fsdp, KW // n_fsdp
    out_qkv, b_qk, b_v, out_gains = call(
        functools.partial(place_qkv, qk, v),
        [meta],
        spread(rest),
        [sds((d_rows, qkv_w), F32), sds((1, qk), F32), sds((1, v), F32), sds((2, d_rows), F32)],
        0,
        [(d_rows + 8, 1024)],
    )
    return (
        block_out,
        hidden_grad,
        out_qkv,
        b_qk.reshape(qk),
        b_v.reshape(v),
        out_wout,
        out_gate,
        out_down,
        out_gains,
    )


def solution(mesh):
    n_fsdp, n_seq = mesh.shape["fsdp"], mesh.shape["seq"]
    in_specs = (
        P(None, "fsdp", "seq", None),
        P("fsdp", None),
        P("fsdp"),
        P("fsdp", None),
        P("fsdp", None),
        P("fsdp", None),
        P(None, "fsdp"),
        P(None, "fsdp", "seq"),
        P(),
        P(None, "fsdp", "seq", None),
    )
    out_specs = (
        P(None, "fsdp", "seq", None),
        P(None, "fsdp", "seq", None),
        P("fsdp", None),
        P("fsdp"),
        P("fsdp"),
        P("fsdp", None),
        P("fsdp", None),
        P("fsdp", None),
        P(None, "fsdp"),
    )

    def local(*args):
        body = on_device_tiled if (n_fsdp, n_seq) == (8, 4) else on_device
        return body(*args, n_fsdp=n_fsdp, n_seq=n_seq)

    return jax.shard_map(local, mesh=mesh, in_specs=in_specs, out_specs=out_specs, check_vma=False)
```

```python
import functools

import jax
import jax.numpy as jnp
import numpy as np
from jax import lax
from jax.experimental import pallas as pl
from jax.experimental.pallas import tpu as pltpu
from jax.sharding import PartitionSpec as P

HEADS = 9
KV_HEADS = 3
HEAD_DIM = 64
GROUP = HEADS // KV_HEADS
QW = HEADS * HEAD_DIM
KW = KV_HEADS * HEAD_DIM
EPS = 1e-05
ROPE_BASE = 100000.0
MASKED = -1000000000.0
BF = jnp.bfloat16
F32 = jnp.float32


def dot(a, b, ca, cb):
    return lax.dot_general(a, b, (((ca,), (cb,)), ((), ())), preferred_element_type=F32)


def rotary(values, cosine, sine):
    half = values.shape[-1] // 2
    a, b = values[..., :half], values[..., half:]
    return jnp.concatenate([a * cosine - b * sine, b * cosine + a * sine], axis=-1)


def norm_parts(values):
    factor = lax.rsqrt(jnp.mean(values * values, axis=-1, keepdims=True) + EPS)
    return factor, values * factor


def norm_back(grad_in, gain, factor, normed):
    scaled = grad_in * gain
    return factor * (scaled - normed * jnp.mean(scaled * normed, axis=-1, keepdims=True))


def whole(*shape_dtypes):
    return [pl.BlockSpec(memory_space=pltpu.VMEM) for _ in shape_dtypes]


def call(kernel, scalars, arrays, outs, flops, scratch=()):
    specs = [pl.BlockSpec(memory_space=pltpu.SMEM)] * len(scalars) + whole(*arrays)
    moved = sum(a.size * a.dtype.itemsize for a in arrays) + sum(
        int(np.prod(o.shape)) * o.dtype.itemsize for o in outs
    )
    return pl.pallas_call(
        kernel,
        out_shape=outs,
        in_specs=specs,
        out_specs=whole(*outs),
        scratch_shapes=[pltpu.VMEM(shape, F32) for shape in scratch],
        compiler_params=pltpu.CompilerParams(vmem_limit_bytes=52 * 1024 * 1024),
        cost_estimate=pl.CostEstimate(flops=int(flops), bytes_accessed=moved, transcendentals=0),
    )(*scalars, *arrays)


def sds(shape, dtype):
    return jax.ShapeDtypeStruct(shape, dtype)


def turn(x, cosine, sine):
    tiles = []
    low = lax.broadcasted_iota(jnp.int32, (1, 128), 1) % HEAD_DIM < HEAD_DIM // 2
    for t in range(x.shape[1] // 128):
        part = x[:, 128 * t : 128 * t + 128]
        other = jnp.where(low, pltpu.roll(part, 96, 1), pltpu.roll(part, 32, 1))
        tiles.append(part * cosine + other * sine)
    return tiles


def turn_kv(x, cosine, sine):
    lane = lax.broadcasted_iota(jnp.int32, (1, 128), 1)
    first, second = turn(x[:, :256], cosine, sine)
    second = jnp.where(lane < KW - 128, second, x[:, 128:256])
    return jnp.concatenate([first, second, x[:, 256:]], axis=1)


def tables(seq, order, cos_ref, sin_ref):
    cosine = jnp.concatenate([cos_ref[seq ^ o] for o in order], axis=0)
    sine = jnp.concatenate([sin_ref[seq ^ o] for o in order], axis=0)
    return cosine, sine


def heads_to_rows(x, g):
    return jnp.concatenate(
        [x[:, HEAD_DIM * h : HEAD_DIM * (h + 1)] for h in range(GROUP * g, GROUP * (g + 1))], axis=0
    )


def rows_to_heads(parts, length):
    return jnp.concatenate(
        [p[length * r : length * (r + 1)] for p in parts for r in range(GROUP)], axis=1
    )


def attention_forward(order, length, seq_ref, blocks, wq, wkv, bq, bkv, gain, cos, sin, mask,
                      att_o, q_o, k_o, v_o, lse_o):
    seq = seq_ref[0]
    cosine, sine = tables(seq, order, cos, sin)
    width = gain.shape[1]
    for b in range(blocks.shape[1] // length):
        x = blocks[:, b * length : (b + 1) * length, :width].astype(F32)
        x = x.reshape(len(order) * length, width)
        first = (norm_parts(x)[1] * gain[...]).astype(BF)
        kv = dot(first, wkv[...], 1, 0) + bkv[...]
        q = dot(first[:length], wq[...], 1, 0) + bq[...]
        q = jnp.concatenate(turn(q, cosine[:length], sine[:length]), axis=1).astype(BF)
        q = q * jnp.asarray(HEAD_DIM ** (-0.5), BF)
        kv = turn_kv(kv, cosine, sine).astype(BF)
        allowed = jnp.concatenate([mask[b]] * GROUP, axis=0) > 0.0
        parts = []
        for g in range(KV_HEADS):
            qg = heads_to_rows(q, g)
            kg = kv[:, HEAD_DIM * g : HEAD_DIM * (g + 1)]
            vg = kv[:, KW + HEAD_DIM * g : KW + HEAD_DIM * (g + 1)]
            q_o[b, g] = qg
            k_o[b, g] = kg
            v_o[b, g] = vg
            scores = jnp.where(allowed, dot(qg, kg, 1, 1), MASKED)
            top = jnp.max(scores, axis=-1, keepdims=True)
            e = jnp.exp(scores - top)
            total = jnp.sum(e, axis=-1, keepdims=True)
            lse_o[b, g] = jnp.log(total) + top
            probs = (e * (1.0 / total)).astype(BF)
            parts.append(dot(probs, vg, 1, 0))
        att_o[b * length : (b + 1) * length, :] = rows_to_heads(parts, length).astype(BF)


def feed_forward(attended, source, wo, wgu, wd, gain, cot, weight,
                 out_o, down_o, gu_o, mid_o, wout_o, attg_o, gain_o):
    units = wd.shape[0]
    step = units // 3
    att = attended[...]
    middle = source[...].astype(F32) + dot(att, wo[...], 1, 0)
    scale_two, normed = norm_parts(middle)
    g2 = gain[...]
    second = (normed * g2).astype(BF)
    out_grad = cot[...].astype(F32) * weight[...]
    feed_grad = out_grad.astype(BF)
    feed = None
    back = None
    for j in range(0, units, step):
        wg = wgu[:, j : j + step]
        wu = wgu[:, units + j : units + j + step]
        wdj = wd[j : j + step, :]
        gate = dot(second, wg, 1, 0)
        up = dot(second, wu, 1, 0)
        sig = jax.nn.sigmoid(gate)
        act = gate * sig
        product = (act * up).astype(BF)
        part = dot(product, wdj, 1, 0)
        feed = part if feed is None else feed + part
        down_o[j : j + step, :] = dot(product, feed_grad, 0, 0).astype(BF)
        pgrad = dot(feed_grad, wdj, 1, 1)
        ggrad = (pgrad * up * (sig * (1.0 + gate * (1.0 - sig)))).astype(BF)
        ugrad = (pgrad * act).astype(BF)
        gu_o[:, j : j + step] = dot(second, ggrad, 0, 0).astype(BF)
        gu_o[:, units + j : units + j + step] = dot(second, ugrad, 0, 0).astype(BF)
        part = dot(ggrad, wg, 1, 1) + dot(ugrad, wu, 1, 1)
        back = part if back is None else back + part
    out_o[...] = (middle + feed).astype(BF)
    gain_o[...] = jnp.sum(back * normed, axis=0, keepdims=True)
    middle_grad = out_grad + norm_back(back, g2, scale_two, normed)
    mid_o[...] = middle_grad
    branch = middle_grad.astype(BF)
    wout_o[...] = dot(att, branch, 0, 0).astype(BF)
    attg_o[...] = dot(branch, wo[...], 1, 1).astype(BF)


def attention_backward(order, length, seq_ref, blocks, wq, wkv, gain, cos, sin, mask, q_i, k_i, v_i,
                       lse, attg, dq_o, dkv_o, wgrad_o, bias_o, gain_o):
    seq = seq_ref[0]
    cosine, sine = tables(seq, order, cos, sin)
    width = gain.shape[1]
    q_wgrad = kv_wgrad = bias_q = bias_kv = gain_sum = None
    for b in range(blocks.shape[1] // length):
        x = blocks[:, b * length : (b + 1) * length, :width].astype(F32)
        x = x.reshape(len(order) * length, width)
        normed = norm_parts(x)[1]
        first = (normed * gain[...]).astype(BF)
        allowed = jnp.concatenate([mask[b]] * GROUP, axis=0) > 0.0
        ag = attg[b * length : (b + 1) * length, :]
        dqs, dks, dvs = [], [], []
        for g in range(KV_HEADS):
            qg, kg, vg = q_i[b, g], k_i[b, g], v_i[b, g]
            agg = heads_to_rows(ag, g)
            p = jnp.exp(jnp.where(allowed, dot(qg, kg, 1, 1), MASKED) - lse[b, g])
            dvs.append(dot(p.astype(BF), agg, 0, 0))
            pg = dot(agg, vg, 1, 1)
            inner = jnp.sum(p * pg, axis=-1, keepdims=True)
            ds = (p * (pg - inner)).astype(BF)
            dqs.append(dot(ds, kg, 1, 0) * HEAD_DIM ** (-0.5))
            dks.append(dot(ds, qg, 0, 0))
        dq = rows_to_heads(dqs, length)
        dq = jnp.concatenate([dq, jnp.zeros((length, 64), F32)], axis=1)
        dq = jnp.concatenate(turn(dq, cosine[:length], -sine[:length]), axis=1).astype(BF)
        dkv = jnp.concatenate(dks + dvs, axis=1)
        dkv = turn_kv(dkv, cosine, -sine).astype(BF)
        dq_o[b * length : (b + 1) * length, :] = dq
        for r in range(len(order)):
            dkv_o[r, b * length : (b + 1) * length, :] = dkv[r * length : (r + 1) * length, :]
        wq_part = dot(first[:length], dq, 0, 0)
        wkv_part = dot(first, dkv, 0, 0)
        bq_part = jnp.sum(dq.astype(F32), axis=0, keepdims=True)
        bkv_part = jnp.sum(dkv.astype(F32), axis=0, keepdims=True)
        e_kv = dot(dkv, wkv[...], 1, 1) * normed
        e_q = dot(dq[:, :QW], wq[:, :QW], 1, 1) * normed[:length]
        g_part = jnp.sum(e_kv, axis=0, keepdims=True) + jnp.sum(e_q, axis=0, keepdims=True)
        if q_wgrad is None:
            q_wgrad, kv_wgrad, bias_q, bias_kv, gain_sum = wq_part, wkv_part, bq_part, bkv_part, g_part
        else:
            q_wgrad, kv_wgrad = q_wgrad + wq_part, kv_wgrad + wkv_part
            bias_q, bias_kv, gain_sum = bias_q + bq_part, bias_kv + bkv_part, gain_sum + g_part
    wgrad_o[...] = jnp.concatenate([q_wgrad[:, :QW], kv_wgrad], axis=1).astype(BF)
    bias_o[...] = jnp.concatenate([bias_q[:, :QW], bias_kv], axis=1)
    gain_o[...] = gain_sum


def input_gradient(dq, own, a, b, c, source, mid, wq, wkv, gain, out_o):
    kv = own[...].astype(F32) + a[...].astype(F32) + b[...].astype(F32) + c[...].astype(F32)
    first_grad = dot(dq[:, :QW], wq[:, :QW], 1, 1) + dot(kv.astype(BF), wkv[...], 1, 1)
    scale_one, normed = norm_parts(source[...].astype(F32))
    out_o[...] = mid[...] + norm_back(first_grad, gain[...], scale_one, normed)

def chosen(flag, a, b):
    return jnp.where(flag != 0, b, a)


class Blocks:
    def __init__(self, *refs):
        self.refs = refs
        self.shape = (len(refs),) + refs[0].shape

    def __getitem__(self, key):
        return jnp.stack([ref[key[1:]] for ref in self.refs])


def cut_qkv(core_bit, meta, w, bias, gains, out_o, all_s):
    rows = w.shape[0]
    n = bias.shape[1]
    all_s[:rows, :] = w[...].astype(F32)
    all_s[rows:, :] = jnp.zeros((8, w.shape[1]), F32)
    all_s[rows : rows + 1, :n] = bias[...].astype(F32)
    for i in range(2):
        all_s[rows : rows + 1, n + rows * i : n + rows * (i + 1)] = gains[i : i + 1, :].astype(F32)
    half = out_o.shape[0]
    at = pl.multiple_of((meta[0] & core_bit) * half, 8)
    out_o[...] = all_s[pl.ds(at, half), :].astype(BF)


def first_forward(order, length, d_rows, n_bias, meta, b0, b1, b2, b3, a00, a10, a01, a11, cos, sin, mask,
                  att_o, q_o, k_o, v_o, lse_o, w_o, gain_o, w_s, b_s):
    blocks = Blocks(b0, b1, b2, b3)
    core, x = meta[0] & 1, meta[1] & 1
    cut = a00.shape[2]
    for x_rel, c_rel, piece in ((0, 0, a00), (1, 0, a10), (0, 1, a01), (1, 1, a11)):
        for z0 in range(2):
            for z1 in range(2):
                at = (z1 * 4 + z0 * 2 + (x ^ x_rel)) * 2 * cut + (core ^ c_rel) * cut
                w_s[pl.ds(pl.multiple_of(at, 8), cut), :] = piece[z0, z1].astype(F32)
    n_f = w_s.shape[0] // (2 * cut)
    starts = [2 * cut * f for f in range(n_f)]
    w_o[...] = jnp.concatenate([w_s[at : at + d_rows, :] for at in starts], axis=0).astype(BF)
    lines = [w_s[at + d_rows : at + d_rows + 1, :] for at in starts]
    b_s[...] = jnp.concatenate([line[:, :n_bias] for line in lines], axis=1)
    for i in range(2):
        at = n_bias + d_rows * i
        gain_o[i : i + 1, :] = jnp.concatenate([line[:, at : at + d_rows] for line in lines], axis=1)
    wide = QW + 64
    attention_forward(order, length, meta, blocks, w_o[:, :wide], w_o[:, QW:], b_s[:, :wide], b_s[:, QW:],
                      gain_o[0:1, :], cos, sin, mask, att_o, q_o, k_o, v_o, lse_o)


def turned(out, value):
    length = out.shape[2]
    for b in range(out.shape[0]):
        out[b] = value[length * b : length * (b + 1)].T.astype(out.dtype)


def rel(meta, f):
    r = f ^ meta[1]
    return r & 1, (r >> 1) & 1, (r >> 2) & 1


def feed_forward_pieces(d_rows, ff_rows, meta, attended, source, b00, b10, b01, b11,
                        g000, g100, g010, g110, g001, g101, g011, g111, gains, cot, weight,
                        out_o, gk_o, gg_o, dk_o, dg_o, mid_o, attg_o, gain_o, down_s, wout_s):
    core, y, x_own = meta[0] & 1, (meta[0] >> 1) & 1, meta[1] & 1
    n_f = 8
    hf = n_f // 2
    part_d = ff_rows // 4
    part_o = d_rows // 3
    cut = b00.shape[2] - ff_rows // 2

    def b_rows(z0, z1, x, c, rows):
        low = chosen(x_own ^ x, b00[z0, z1, rows, :], b10[z0, z1, rows, :])
        high = chosen(x_own ^ x, b01[z0, z1, rows, :], b11[z0, z1, rows, :])
        return chosen(core ^ c, low, high)

    def quarter(near, far):
        parts = []
        for f in range(n_f):
            z1, z0, x = f >> 2, (f >> 1) & 1, f & 1
            mine, other = near[z0, z1].astype(F32), far[z0, z1].astype(F32)
            parts.append(chosen(x_own ^ x, mine, other))
        return jnp.concatenate(parts, axis=0).astype(BF)

    wo = []
    for f in range(n_f):
        z1, z0, x = f >> 2, (f >> 1) & 1, f & 1
        wo.append(b_rows(z0, z1, x, 0, slice(ff_rows // 2, None)).astype(F32))
        wo.append(b_rows(z0, z1, x, 1, slice(ff_rows // 2, None)).astype(F32)[: d_rows - cut])
    wo = jnp.concatenate(wo, axis=0).astype(BF)
    att = attended[...]
    middle = source[...].astype(F32) + dot(att, wo, 1, 0)
    scale_two, normed = norm_parts(middle)
    g2 = gains[1:2, :]
    second = (normed * g2).astype(BF)
    out_grad = cot[...].astype(F32) * weight[...]
    feed_grad = out_grad.astype(BF)
    feed = back = None
    for c_rel in (1, 0):
        first_q = quarter(g001, g101) if c_rel else quarter(g000, g100)
        second_q = quarter(g011, g111) if c_rel else quarter(g010, g110)
        wg = chosen(y, first_q, second_q)
        wu = chosen(y, second_q, first_q)
        h = core ^ c_rel
        wd = []
        for i in range(hf):
            for c in range(2):
                wd.append(b_rows(i >> 1, h, i & 1, c, slice(0, ff_rows // 2)))
        wd = jnp.concatenate(wd, axis=0)
        gate = dot(second, wg, 1, 0)
        up = dot(second, wu, 1, 0)
        sig = jax.nn.sigmoid(gate)
        act = gate * sig
        product = (act * up).astype(BF)
        part = dot(product, wd, 1, 0)
        feed = part if feed is None else feed + part
        down_s[...] = dot(product, feed_grad, 0, 0)
        pgrad = dot(feed_grad, wd, 1, 1)
        ggrad = (pgrad * up * (sig * (1.0 + gate * (1.0 - sig)))).astype(BF)
        ugrad = (pgrad * act).astype(BF)
        part = dot(ggrad, wg, 1, 1) + dot(ugrad, wu, 1, 1)
        back = part if back is None else back + part
        for i in range(hf):
            x, z0, z1 = rel(meta, hf * h + i)
            for yy in range(2):
                for c_to, to in ((0, dk_o), (1, dg_o)):
                    at = pl.multiple_of(i * ff_rows + (yy * 2 + (core ^ c_to)) * part_d, 16)
                    to[y ^ yy, x, z0, z1, :part_d, :] = down_s[pl.ds(at, part_d), :].astype(BF)
        to = gg_o if c_rel else gk_o
        for yy, grad in ((0, ggrad), (1, ugrad)):
            wgrad = dot(second, grad, 0, 0)
            for f in range(n_f):
                x, z0, z1 = rel(meta, f)
                to[x, z0, z1, yy] = wgrad[d_rows * f : d_rows * (f + 1), :].astype(BF)
    turned(out_o, middle + feed)
    gain_o[...] = jnp.sum(back * normed, axis=0, keepdims=True)
    middle_grad = out_grad + norm_back(back, g2, scale_two, normed)
    mid_o[...] = middle_grad
    branch = middle_grad.astype(BF)
    attg_o[...] = dot(branch, wo, 1, 1).astype(BF)
    wout = dot(att, branch, 0, 0)
    for f in range(n_f):
        wout_s[f, :d_rows, :] = wout[d_rows * f : d_rows * (f + 1), :]
        wout_s[f, d_rows:, :] = jnp.zeros((part_o, wout.shape[1]), F32)
    for f in range(n_f):
        x, z0, z1 = rel(meta, f)
        for yy in range(2):
            for c_to, to in ((0, dk_o), (1, dg_o)):
                at = pl.multiple_of((yy * 2 + (core ^ c_to)) * part_o, 8)
                to[y ^ yy, x, z0, z1, part_d:, :] = wout_s[f, pl.ds(at, part_o), :].astype(BF)


def attention_backward_pieces(order, length, d_rows, meta, b0, b1, b2, b3, w, gains, cos, sin, mask, q_i, k_i, v_i,
                              lse, attg, gain_two, dq_o, dk_o, dg_o, rk_o, rg_o, w_s, bias_s, gain_s, small_s):
    blocks = Blocks(b0, b1, b2, b3)
    half = len(order) // 2

    class Pieces:
        def __setitem__(self, key, value):
            ref = dk_o if key[0] < half else dg_o
            ref[(key[0] % half,) + key[1:]] = value

    class Wgrad:
        def __setitem__(self, key, value):
            w_s[:, : 2 * KW] = value[:, QW:].astype(F32)
            w_s[:, 2 * KW : 2 * KW + QW] = value[:, :QW].astype(F32)
            w_s[:, 2 * KW + QW :] = jnp.zeros((value.shape[0], 64), F32)

    wide = QW + 64
    attention_backward(order, length, meta, blocks, w[:, :wide], w[:, QW:], gains[0:1, :], cos, sin, mask,
                       q_i, k_i, v_i, lse, attg, dq_o, Pieces(), Wgrad(), bias_s, gain_s)
    n_f = small_s.shape[0]
    qk, v = (QW + KW) // n_f, KW // n_f
    bias, g1, g2 = bias_s[...], gain_s[...], gain_two[...]
    for f in range(n_f):
        line = jnp.concatenate(
            [
                bias[:, qk * f : qk * (f + 1)],
                bias[:, QW + KW + v * f : QW + KW + v * (f + 1)],
                g1[:, d_rows * f : d_rows * (f + 1)],
                jnp.zeros((1, 256 - qk - v - d_rows), F32),
                g2[:, d_rows * f : d_rows * (f + 1)],
                jnp.zeros((1, 768 - d_rows), F32),
            ],
            axis=1,
        )
        small_s[f] = jnp.broadcast_to(line, (8, 1024))
    core, y = meta[0] & 1, (meta[0] >> 1) & 1
    for f in range(n_f):
        x, z0, z1 = rel(meta, f)
        for yy in range(2):
            for c_to, to in ((0, rk_o), (1, rg_o)):
                at = pl.multiple_of((yy * 2 + (core ^ c_to)) * 256, 256)
                block = [w_s[d_rows * f : d_rows * (f + 1), pl.ds(at, 256)], small_s[f, :, pl.ds(at, 256)]]
                to[y ^ yy, x, z0, z1] = jnp.concatenate(block, axis=0).astype(BF)


def input_gradient_two(dq, own, other, source, mid, w, gains, out_o):
    kv = (own[...].astype(F32) + other[...].astype(F32)).astype(BF)
    first_grad = dot(dq[:, :QW], w[:, :QW], 1, 1) + dot(kv, w[:, QW:], 1, 1)
    scale_one, normed = norm_parts(source[...].astype(F32))
    turned(out_o, mid[...] + norm_back(first_grad, gains[0:1, :], scale_one, normed))


def place_gate(meta, near, far, out_o):
    core = meta[0] & 1
    n = near.shape[2]
    for pieces, c_rel in ((near, 0), (far, 1)):
        for yy in range(2):
            at = pl.multiple_of((yy * 2 + (core ^ c_rel)) * n, 128)
            out_o[:, pl.ds(at, n)] = pieces[yy].astype(F32)


def place_down(part_d, meta, p00, p10, p01, p11, out_o, wout_o):
    seq = meta[0]
    part_o = p00.shape[0] - part_d
    for piece, o in ((p00[...], 0), (p10[...], 2), (p01[...], 1), (p11[...], 3)):
        piece = piece.astype(F32)
        to = seq ^ o
        out_o[pl.ds(pl.multiple_of(to * part_d, 16), part_d), :] = piece[:part_d]

        @pl.when(to < 3)
        def _():
            wout_o[pl.ds(pl.multiple_of(to * part_o, 8), part_o), :] = piece[part_d:]


def place_qkv(qk, v, meta, p00, p10, p01, p11, w_o, bqk_o, bv_o, gains_o, all_s):
    seq = meta[0]
    n = p00.shape[1]
    for piece, o in ((p00[...], 0), (p10[...], 2), (p01[...], 1), (p11[...], 3)):
        all_s[:, pl.ds(pl.multiple_of((seq ^ o) * n, 128), n)] = piece.astype(F32)
    d_rows = w_o.shape[0]
    w_o[:, :QW] = all_s[:d_rows, 2 * KW : 2 * KW + QW]
    w_o[:, QW:] = all_s[:d_rows, : 2 * KW]
    line = all_s[d_rows : d_rows + 1, :]
    bqk_o[...] = line[:, :qk]
    bv_o[...] = line[:, qk : qk + v]
    gains_o[0:1, :] = line[:, qk + v : qk + v + d_rows]
    gains_o[1:2, :] = line[:, 256 : 256 + d_rows]


def place_all(part_d, qk, v, meta, near, far, d0, d1, d2, d3, r0, r1, r2, r3,
              gate_o, down_o, wout_o, w_o, bqk_o, bv_o, gains_o, all_s):
    place_gate(meta, near, far, gate_o)
    place_down(part_d, meta, d0, d1, d2, d3, down_o, wout_o)
    place_qkv(qk, v, meta, r0, r1, r2, r3, w_o, bqk_o, bv_o, gains_o, all_s)


class Net:
    def __init__(self, n_fsdp, n_seq):
        self.n_fsdp, self.n_seq = n_fsdp, n_seq
        self.total = n_fsdp * n_seq
        f, s = lax.axis_index("fsdp"), lax.axis_index("seq")
        self.index = f * n_seq + s
        self.seq_bits = [1 << b for b in range(n_seq.bit_length() - 1)]
        self.fsdp_bits = [n_seq << b for b in range(n_fsdp.bit_length() - 1)]

    def swap(self, value, mask):
        pairs = [(i, i ^ mask) for i in range(self.total)]
        return lax.ppermute(value, ("fsdp", "seq"), pairs)

    def bit(self, mask):
        return (self.index & mask) != 0

    def both(self, mine, mask, axis, other=None):
        other = self.swap(mine, mask) if other is None else other
        high = self.bit(mask)
        return jnp.stack([jnp.where(high, other, mine), jnp.where(high, mine, other)], axis=axis)

    def half(self, value, mask, axis):
        return lax.dynamic_index_in_dim(
            value, self.bit(mask).astype(jnp.int32), axis, keepdims=False
        )

    def add_half(self, value, mask, axis):
        mine = self.bit(mask).astype(jnp.int32)
        keep = lax.dynamic_index_in_dim(value, mine, axis, keepdims=False)
        give = lax.dynamic_index_in_dim(value, 1 - mine, axis, keepdims=False)
        got = self.swap(give, mask)
        return (keep.astype(F32) + got.astype(F32)).astype(value.dtype)

    def gather_fsdp(self, value):
        for step, mask in enumerate(reversed(self.fsdp_bits)):
            value = self.both(value, mask, step)
        return value

    def scatter_fsdp(self, value, first_axis=0):
        count = len(self.fsdp_bits)
        for step, mask in enumerate(self.fsdp_bits):
            value = self.add_half(value, mask, first_axis + count - 1 - step)
        return value


def on_device(
    hidden, w_qkv, b_qkv, w_out, w_gate_up, w_down, norm_gains, segment_ids, token_counts, cotangent,
    n_fsdp, n_seq,
):
    net = Net(n_fsdp, n_seq)
    micro, batch, length, width = hidden.shape
    full_length = length * n_seq
    tokens_micro = batch * n_fsdp * full_length
    scale = HEAD_DIM ** (-0.5)
    rows = micro * batch * length
    d_rows = w_qkv.shape[0]
    ff_rows = w_down.shape[0]
    units = w_gate_up.shape[1] // 2
    qkv_w = w_qkv.shape[1]
    core = net.seq_bits[0]
    f_lead = (2,) * len(net.fsdp_bits)

    ids = segment_ids.reshape(rows, 1).astype(BF)
    block = jnp.concatenate(
        [hidden.reshape(rows, width), jnp.broadcast_to(ids, (rows, 64))], axis=1
    )
    blocks = block[None]
    for mask in reversed(net.seq_bits):
        blocks = jnp.concatenate([blocks, net.swap(blocks, mask)], axis=0)
    order = [0]
    for mask in reversed(net.seq_bits):
        order = order + [o ^ mask for o in order]
    seq_index = lax.axis_index("seq")
    block_ids = [seq_index ^ o for o in order]

    pad_rows = -(d_rows + 1) % 16 + 1
    extra = jnp.zeros((pad_rows, qkv_w), BF)
    small = jnp.concatenate([b_qkv, norm_gains.reshape(-1)])
    extra = extra.at[0, : small.shape[0]].set(small)
    shard_a = jnp.concatenate([w_qkv, extra], axis=0).reshape(2, -1, qkv_w)
    got_a = net.gather_fsdp(net.half(shard_a, core, 0))
    full_a = net.both(got_a, core, len(f_lead)).reshape(n_fsdp, d_rows + pad_rows, qkv_w)
    wf_qkv = full_a[:, :d_rows].reshape(n_fsdp * d_rows, qkv_w)
    smalls = full_a[:, d_rows]
    n_bias = b_qkv.shape[0]
    bias = smalls[:, :n_bias].reshape(-1).astype(F32)
    gains = smalls[:, n_bias : n_bias + 2 * d_rows].reshape(n_fsdp, 2, d_rows).astype(F32)
    gain_one = gains[:, 0].reshape(-1)
    gain_two = gains[:, 1].reshape(-1)

    pad_b = -(d_rows + ff_rows) % 16
    shard_b = jnp.concatenate([w_out, w_down, jnp.zeros((pad_b, width), BF)], axis=0)
    shard_b = shard_b.reshape(2, -1, width)
    got_b = net.gather_fsdp(net.half(shard_b, core, 0))

    parts = n_seq
    shard_c = w_gate_up.reshape(d_rows, parts, -1)
    got_c = net.gather_fsdp(lax.dynamic_index_in_dim(shard_c, seq_index, 1, keepdims=False))
    full_b = net.both(got_b, core, len(f_lead)).reshape(n_fsdp, -1, width)
    wf_out = full_b[:, :d_rows].reshape(n_fsdp * d_rows, width)
    wf_down = full_b[:, d_rows : d_rows + ff_rows].reshape(n_fsdp * ff_rows, width)
    got_c = got_c.reshape(n_fsdp * d_rows, -1)
    for mask in reversed(net.seq_bits):
        got_c = net.both(got_c, mask, got_c.ndim - 1)
    wf_gate_up = got_c.reshape(n_fsdp * d_rows, 2 * units)

    places = np.arange(full_length, dtype=np.float32)
    speeds = np.power(ROPE_BASE, -2.0 * np.arange(HEAD_DIM // 2, dtype=np.float32) / HEAD_DIM)
    angles = places[:, None] * speeds.astype(np.float32)[None, :]
    cos_t = np.tile(np.cos(angles), (1, 4)).reshape(n_seq, length, 128)
    sin_t = np.concatenate([-np.sin(angles), np.sin(angles)] * 2, axis=1).reshape(n_seq, length, 128)
    cos_t, sin_t = jnp.asarray(cos_t, F32), jnp.asarray(sin_t, F32)
    seqs = micro * batch
    seg_all = blocks[..., width].reshape(n_seq, seqs, length).transpose(1, 0, 2)
    own_places = seq_index * length + jnp.arange(length, dtype=jnp.int32)
    key_places = jnp.stack(block_ids)[:, None] * length + jnp.arange(length, dtype=jnp.int32)
    allowed = (seg_all[:, 0, :, None] == seg_all.reshape(seqs, 1, -1)) & (
        own_places[None, :, None] >= key_places.reshape(1, 1, -1)
    )
    allowed = allowed.astype(F32)
    seq_scalar = seq_index.astype(jnp.int32).reshape(1)
    wq, wkv = wf_qkv[:, : QW + 64], wf_qkv[:, QW:]
    gain_one, gain_two = gain_one[None], gain_two[None]
    source = hidden.reshape(rows, width)
    n_all = n_seq * rows
    attended, q_s, k_s, v_s, lse = call(
        functools.partial(attention_forward, order, length),
        [seq_scalar],
        [blocks, wq, wkv, bias[None, : QW + 64], bias[None, QW:], gain_one, cos_t, sin_t, allowed],
        [
            sds((rows, QW), BF),
            sds((seqs, KV_HEADS, GROUP * length, HEAD_DIM), BF),
            sds((seqs, KV_HEADS, full_length, HEAD_DIM), BF),
            sds((seqs, KV_HEADS, full_length, HEAD_DIM), BF),
            sds((seqs, KV_HEADS, GROUP * length, 1), F32),
        ],
        2 * n_all * width * 2 * KW + 2 * rows * width * QW + 4 * rows * full_length * QW,
    )

    weight = tokens_micro / token_counts.astype(F32)
    weight = jnp.repeat(weight, batch * length)[:, None]
    block_out, down_grad, gate_up_wgrad, middle_grad, out_wgrad, attended_grad, gain_two_grad = call(
        feed_forward,
        [],
        [attended, source, wf_out, wf_gate_up, wf_down, gain_two, cotangent.reshape(rows, width), weight],
        [
            sds((rows, width), BF),
            sds((units, width), BF),
            sds((width, 2 * units), BF),
            sds((rows, width), F32),
            sds((QW, width), BF),
            sds((rows, QW), BF),
            sds((1, width), F32),
        ],
        6 * rows * width * 3 * units + 6 * rows * width * QW,
    )
    block_out = block_out.reshape(hidden.shape)

    def seq_axes(value, axis, masks):
        for mask in masks:
            value = net.add_half(value, mask, axis)
        return value

    quarter = (2,) * len(net.seq_bits)
    n_f = len(f_lead)
    red_down = down_grad.reshape(f_lead + quarter + (ff_rows // n_seq, width))
    for step, mask in enumerate(net.seq_bits):
        red_down = net.add_half(red_down, mask, n_f + len(quarter) - 1 - step)
    red_down = net.scatter_fsdp(red_down)

    red_gate = gate_up_wgrad.reshape(f_lead + (d_rows,) + quarter + (2 * units // n_seq,))
    red_gate = net.add_half(red_gate, core, n_f + len(quarter))
    red_gate = net.add_half(red_gate, net.fsdp_bits[0], n_f - 1)
    for step, mask in enumerate(net.seq_bits[1:]):
        red_gate = net.add_half(red_gate, mask, n_f - 1 + len(quarter) - 1 - step)
    for step, mask in enumerate(net.fsdp_bits[1:]):
        red_gate = net.add_half(red_gate, mask, n_f - 2 - step)

    dq, dkv, qkv_wgrad, bias_grad, gain_one_grad = call(
        functools.partial(attention_backward, order, length),
        [seq_scalar],
        [blocks, wq, wkv, gain_one, cos_t, sin_t, allowed, q_s, k_s, v_s, lse, attended_grad],
        [
            sds((rows, QW + 64), BF),
            sds((n_seq, rows, 2 * KW), BF),
            sds((width, qkv_w), BF),
            sds((1, qkv_w), F32),
            sds((1, width), F32),
        ],
        4 * n_all * width * 2 * KW + 4 * rows * width * QW + 10 * rows * full_length * QW,
    )
    kv_parts = [dkv[0]]
    for place, mask_bits in enumerate(order):
        if mask_bits:
            kv_parts.append(net.swap(dkv[place], mask_bits))
    (hidden_grad,) = call(
        input_gradient,
        [],
        [dq, *kv_parts, source, middle_grad, wq, wkv, gain_one],
        [sds((rows, width), F32)],
        2 * rows * width * qkv_w,
    )
    hidden_grad = hidden_grad.reshape(hidden.shape)
    bias_grad, gain_one_grad, gain_two_grad = bias_grad[0], gain_one_grad[0], gain_two_grad[0]

    qk_rows, v_rows = (QW + KW) // n_fsdp, KW // n_fsdp
    small_grads = jnp.concatenate(
        [
            bias_grad[: QW + KW].reshape(n_fsdp, qk_rows),
            bias_grad[QW + KW :].reshape(n_fsdp, v_rows),
            gain_one_grad.reshape(n_fsdp, d_rows),
            gain_two_grad.reshape(n_fsdp, d_rows),
        ],
        axis=1,
    ).astype(BF)
    wide = qkv_w + width
    small_pad = jnp.zeros((n_fsdp, pad_rows, wide), BF)
    small_pad = small_pad.at[:, 0, : small_grads.shape[1]].set(small_grads)
    rest = jnp.concatenate([qkv_wgrad, out_wgrad], axis=1)
    rest = jnp.concatenate([rest.reshape(n_fsdp, d_rows, wide), small_pad], axis=1)
    rest = rest.reshape(f_lead + (d_rows + pad_rows,) + quarter + (wide // n_seq,))
    for step, mask in enumerate(net.seq_bits):
        rest = net.add_half(rest, mask, n_f + 1 + len(quarter) - 1 - step)
    rest = net.scatter_fsdp(rest)

    def seq_back(value, axis):
        for step, mask in enumerate(reversed(net.seq_bits)):
            value = net.both(value, mask, axis + step)
        return value

    out_down = seq_back(red_down, 0).reshape(ff_rows, width).astype(F32)
    out_gate = seq_back(red_gate, 1).reshape(d_rows, 2 * units).astype(F32)
    out_rest = seq_back(rest, 1).reshape(d_rows + pad_rows, wide).astype(F32)
    line = out_rest[d_rows]
    edge = qk_rows + v_rows
    return (
        block_out,
        hidden_grad,
        out_rest[:d_rows, :qkv_w],
        line[:qk_rows],
        line[qk_rows:edge],
        out_rest[:d_rows, qkv_w:],
        out_gate,
        out_down,
        line[edge : edge + 2 * d_rows].reshape(2, d_rows),
    )


def after(value, *others):
    return lax.optimization_barrier((value, *others))[0]


def rope_tables(full_length, n_seq):
    places = np.arange(full_length, dtype=np.float32)
    speeds = np.power(ROPE_BASE, -2.0 * np.arange(HEAD_DIM // 2, dtype=np.float32) / HEAD_DIM)
    angles = places[:, None] * speeds.astype(np.float32)[None, :]
    cos_t = np.tile(np.cos(angles), (1, 4)).reshape(n_seq, -1, 128)
    sin_t = np.concatenate([-np.sin(angles), np.sin(angles)] * 2, axis=1).reshape(n_seq, -1, 128)
    return jnp.asarray(cos_t, F32), jnp.asarray(sin_t, F32)


def on_device_tiled(
    hidden, w_qkv, b_qkv, w_out, w_gate_up, w_down, norm_gains, segment_ids, token_counts, cotangent,
    n_fsdp, n_seq,
):
    net = Net(n_fsdp, n_seq)
    micro, batch, length, width = hidden.shape
    full_length = length * n_seq
    tokens_micro = batch * n_fsdp * full_length
    rows = micro * batch * length
    seqs = micro * batch
    d_rows, qkv_w = w_qkv.shape
    ff_rows = w_down.shape[0]
    units = w_gate_up.shape[1] // 2
    n_bias = b_qkv.shape[0]
    core, ybit = net.seq_bits
    xbit, znear, zfar = net.fsdp_bits
    order = [0, 2, 1, 3]
    seq_index = lax.axis_index("seq")
    meta = jnp.stack([seq_index, lax.axis_index("fsdp")]).astype(jnp.int32)
    source = hidden.reshape(rows, width)

    (a0,) = call(
        functools.partial(cut_qkv, core),
        [meta],
        [w_qkv, b_qkv[None], norm_gains],
        [sds(((d_rows + 8) // 2, qkv_w), BF)],
        1e8,
        [(d_rows + 8, qkv_w)],
    )
    a1 = net.both(a0, zfar, 0)

    ids = segment_ids.reshape(rows, 1).astype(BF)
    block = jnp.concatenate([source, jnp.broadcast_to(ids, (rows, 64))], axis=1)
    block = after(block, a0)
    block_y = net.swap(block, ybit)
    block_c = net.swap(block, core)

    quarter = 2 * units // n_seq
    gu0 = lax.dynamic_slice_in_dim(after(w_gate_up, a0), seq_index * quarter, quarter, axis=1)
    half_b = jnp.concatenate(
        [
            w_down.reshape(2, ff_rows // 2, width),
            jnp.concatenate([w_out, jnp.zeros((8, width), BF)], axis=0).reshape(2, -1, width),
        ],
        axis=1,
    )
    a2 = net.both(a1, znear, 0)
    b0 = net.half(after(half_b, a2), core, 0)
    a_x = net.swap(a2, xbit)
    a_c = net.swap(a2, core)
    gu1 = net.both(gu0, zfar, 0)
    b1 = net.both(b0, zfar, 0)
    gu2 = net.both(after(gu1, a2), znear, 0)
    b2 = net.both(after(b1, a2), znear, 0)
    block_yc = net.swap(block_y, core)
    a_xc = net.swap(a_x, core)
    gu2 = after(gu2, a_x)
    b2 = after(b2, a_x)
    gu_x = net.swap(gu2, xbit)
    gu_y = net.swap(gu2, ybit)
    b_x = net.swap(b2, xbit)
    gu_c = net.swap(gu2, core)
    b_c = net.swap(b2, core)
    a_xc = after(a_xc, gu2, b2)

    cos_t, sin_t = rope_tables(full_length, n_seq)
    block_ids = [seq_index ^ o for o in order]
    blocks = [block, block_y, block_c, block_yc]
    seg_all = jnp.stack([b[:, width].reshape(seqs, length) for b in blocks], axis=1)
    own_places = seq_index * length + jnp.arange(length, dtype=jnp.int32)
    key_places = jnp.stack(block_ids)[:, None] * length + jnp.arange(length, dtype=jnp.int32)
    allowed = (seg_all[:, 0, :, None] == seg_all.reshape(seqs, 1, -1)) & (
        own_places[None, :, None] >= key_places.reshape(1, 1, -1)
    )
    allowed = allowed.astype(F32)
    attended, q_s, k_s, v_s, lse, wf, gains = call(
        functools.partial(first_forward, order, length, d_rows, n_bias),
        [meta],
        [*blocks, a2, a_x, a_c, a_xc, cos_t, sin_t, allowed],
        [
            sds((rows, QW), BF),
            sds((seqs, KV_HEADS, GROUP * length, HEAD_DIM), BF),
            sds((seqs, KV_HEADS, full_length, HEAD_DIM), BF),
            sds((seqs, KV_HEADS, full_length, HEAD_DIM), BF),
            sds((seqs, KV_HEADS, GROUP * length, 1), F32),
            sds((width, qkv_w), BF),
            sds((2, width), F32),
        ],
        1.2e10,
        [(n_fsdp * (d_rows + 8), qkv_w), (1, qkv_w)],
    )
    gu_x, gu_y, b_x = after(gu_x, attended), after(gu_y, attended), after(b_x, attended)
    gu_xy = net.swap(gu_x, ybit)
    gu_yc = net.swap(gu_y, core)
    gu_xc = net.swap(gu_x, core)
    b_xc = net.swap(b_x, core)
    gu_xyc = net.swap(gu_xy, core)
    gate_up = [gu2, gu_x, gu_y, gu_xy, gu_c, gu_xc, gu_yc, gu_xyc]

    weight = tokens_micro / token_counts.astype(F32)
    weight = jnp.repeat(weight, batch * length)[:, None]
    lead = (2, 2, 2, 2)
    block_out, gate_keep, gate_give, down_keep, down_give, middle_grad, attended_grad, gain_two = call(
        functools.partial(feed_forward_pieces, d_rows, ff_rows),
        [meta],
        [attended, source, b2, b_x, b_c, b_xc, *gate_up, gains, cotangent.reshape(rows, width), weight],
        [
            sds((seqs, width, length), BF),
            sds(lead + (d_rows, units // 2), BF),
            sds(lead + (d_rows, units // 2), BF),
            sds(lead + (ff_rows // 4 + d_rows // 3, width), BF),
            sds(lead + (ff_rows // 4 + d_rows // 3, width), BF),
            sds((rows, width), F32),
            sds((rows, QW), BF),
            sds((1, width), F32),
        ],
        1.4e10,
        [(units // 2, width), (n_fsdp, d_rows + d_rows // 3, width)],
    )
    block_out = block_out.reshape(micro, batch, width, length).swapaxes(2, 3)

    def add(keep, got):
        return (keep.astype(F32) + got.astype(F32)).astype(BF)

    def halves(keep, got):
        return add(keep[0], got[0]), add(keep[1], got[1])

    gate, gate_give = halves(gate_keep, net.swap(gate_give, core))
    down, down_give = halves(down_keep, net.swap(down_give, core))
    attended_grad = after(attended_grad, gate_give, down_give)
    gate_got = net.swap(gate_give, xbit)
    down_got = net.swap(down_give, ybit)

    dq, dkv_keep, dkv_give, rest_keep, rest_give = call(
        functools.partial(attention_backward_pieces, order, length, d_rows),
        [meta],
        [*blocks, wf, gains, cos_t, sin_t, allowed, q_s, k_s, v_s, lse, attended_grad, gain_two],
        [
            sds((rows, QW + 64), BF),
            sds((2, rows, 2 * KW), BF),
            sds((2, rows, 2 * KW), BF),
            sds(lead + (d_rows + 8, 256), BF),
            sds(lead + (d_rows + 8, 256), BF),
        ],
        1.4e10,
        [(width, 1024), (1, qkv_w), (1, width), (n_fsdp, 8, 1024)],
    )
    gate, gate_give = halves(gate, after(gate_got, dq))
    gate_got = net.swap(gate_give, znear)
    dkv, dkv_give = halves(dkv_keep, after(net.swap(dkv_give, core), gate_give))
    rest, rest_give = halves(rest_keep, after(net.swap(rest_give, core), gate_give))
    down, down_give = halves(down, after(down_got, gate_give))
    dkv_got = net.swap(dkv_give, ybit)
    rest_got = net.swap(rest_give, ybit)
    down_got = net.swap(down_give, xbit)
    (hidden_grad,) = call(
        input_gradient_two,
        [],
        [dq, dkv, dkv_got, source, middle_grad, wf, gains],
        [sds((seqs, width, length), F32)],
        3e9,
    )
    rest_got = after(rest_got, hidden_grad)
    hidden_grad = hidden_grad.reshape(micro, batch, width, length).swapaxes(2, 3)
    rest, rest_give = halves(rest, rest_got)
    rest_got = net.swap(rest_give, xbit)
    gate, gate_give = halves(gate, gate_got)
    gate_got = net.swap(gate_give, zfar)
    down, down_give = halves(down, down_got)
    down_got = net.swap(down_give, znear)
    rest, rest_give = halves(rest, rest_got)
    rest_got = net.swap(rest_give, znear)
    gate = add(gate, gate_got)
    gate_got = net.swap(gate, ybit)
    down, down_give = halves(down, down_got)
    down_got = net.swap(down_give, zfar)
    rest, rest_give = halves(rest, rest_got)
    rest_got = net.swap(rest_give, zfar)
    down = add(down, down_got)
    rest = add(rest, rest_got)

    def spread(part):
        other = net.swap(part, ybit)
        return [part, other, net.swap(part, core), net.swap(other, core)]

    gate = add(gate, gate_got)
    gate = [gate, net.swap(gate, core)]
    qk, v = (QW + KW) // n_fsdp, KW // n_fsdp
    out_gate, out_down, out_wout, out_qkv, b_qk, b_v, out_gains = call(
        functools.partial(place_all, ff_rows // 4, qk, v),
        [meta],
        [*gate, *spread(down), *spread(rest)],
        [
            sds((d_rows, 2 * units), F32),
            sds((ff_rows, width), F32),
            sds((d_rows, width), F32),
            sds((d_rows, qkv_w), F32),
            sds((1, qk), F32),
            sds((1, v), F32),
            sds((2, d_rows), F32),
        ],
        3e9,
        [(d_rows + 8, 1024)],
    )
    return (
        block_out,
        hidden_grad,
        out_qkv,
        b_qk.reshape(qk),
        b_v.reshape(v),
        out_wout,
        out_gate,
        out_down,
        out_gains,
    )


def solution(mesh):
    n_fsdp, n_seq = mesh.shape["fsdp"], mesh.shape["seq"]
    in_specs = (
        P(None, "fsdp", "seq", None),
        P("fsdp", None),
        P("fsdp"),
        P("fsdp", None),
        P("fsdp", None),
        P("fsdp", None),
        P(None, "fsdp"),
        P(None, "fsdp", "seq"),
        P(),
        P(None, "fsdp", "seq", None),
    )
    out_specs = (
        P(None, "fsdp", "seq", None),
        P(None, "fsdp", "seq", None),
        P("fsdp", None),
        P("fsdp"),
        P("fsdp"),
        P("fsdp", None),
        P("fsdp", None),
        P("fsdp", None),
        P(None, "fsdp"),
    )

    def local(*args):
        body = on_device_tiled if (n_fsdp, n_seq) == (8, 4) else on_device
        return body(*args, n_fsdp=n_fsdp, n_seq=n_seq)

    return jax.shard_map(local, mesh=mesh, in_specs=in_specs, out_specs=out_specs, check_vma=False)
```

```python
import functools

import jax
import jax.numpy as jnp
import numpy as np
from jax import lax
from jax.experimental import pallas as pl
from jax.experimental.pallas import tpu as pltpu
from jax.sharding import PartitionSpec as P

HEADS = 9
KV_HEADS = 3
HEAD_DIM = 64
GROUP = HEADS // KV_HEADS
QW = HEADS * HEAD_DIM
KW = KV_HEADS * HEAD_DIM
EPS = 1e-05
ROPE_BASE = 100000.0
MASKED = -1000000000.0
BF = jnp.bfloat16
F32 = jnp.float32


def dot(a, b, ca, cb):
    return lax.dot_general(a, b, (((ca,), (cb,)), ((), ())), preferred_element_type=F32)


def rotary(values, cosine, sine):
    half = values.shape[-1] // 2
    a, b = values[..., :half], values[..., half:]
    return jnp.concatenate([a * cosine - b * sine, b * cosine + a * sine], axis=-1)


def norm_parts(values):
    factor = lax.rsqrt(jnp.mean(values * values, axis=-1, keepdims=True) + EPS)
    return factor, values * factor


def norm_back(grad_in, gain, factor, normed):
    scaled = grad_in * gain
    return factor * (scaled - normed * jnp.mean(scaled * normed, axis=-1, keepdims=True))


def whole(*shape_dtypes):
    return [pl.BlockSpec(memory_space=pltpu.VMEM) for _ in shape_dtypes]


def call(kernel, scalars, arrays, outs, flops, scratch=(), mib=52):
    specs = [pl.BlockSpec(memory_space=pltpu.SMEM)] * len(scalars) + whole(*arrays)
    moved = sum(a.size * a.dtype.itemsize for a in arrays) + sum(
        int(np.prod(o.shape)) * o.dtype.itemsize for o in outs
    )
    return pl.pallas_call(
        kernel,
        out_shape=outs,
        in_specs=specs,
        out_specs=whole(*outs),
        scratch_shapes=[pltpu.VMEM(shape, F32) for shape in scratch],
        compiler_params=pltpu.CompilerParams(vmem_limit_bytes=mib * 1024 * 1024),
        cost_estimate=pl.CostEstimate(flops=int(flops), bytes_accessed=moved, transcendentals=0),
    )(*scalars, *arrays)


def sds(shape, dtype):
    return jax.ShapeDtypeStruct(shape, dtype)


def turn(x, cosine, sine):
    tiles = []
    low = lax.broadcasted_iota(jnp.int32, (1, 128), 1) % HEAD_DIM < HEAD_DIM // 2
    for t in range(x.shape[1] // 128):
        part = x[:, 128 * t : 128 * t + 128]
        other = jnp.where(low, pltpu.roll(part, 96, 1), pltpu.roll(part, 32, 1))
        tiles.append(part * cosine + other * sine)
    return tiles


def turn_kv(x, cosine, sine):
    lane = lax.broadcasted_iota(jnp.int32, (1, 128), 1)
    first, second = turn(x[:, :256], cosine, sine)
    second = jnp.where(lane < KW - 128, second, x[:, 128:256])
    return jnp.concatenate([first, second, x[:, 256:]], axis=1)


def tables(seq, order, cos_ref, sin_ref):
    cosine = jnp.concatenate([cos_ref[seq ^ o] for o in order], axis=0)
    sine = jnp.concatenate([sin_ref[seq ^ o] for o in order], axis=0)
    return cosine, sine


def heads_to_rows(x, g):
    return jnp.concatenate(
        [x[:, HEAD_DIM * h : HEAD_DIM * (h + 1)] for h in range(GROUP * g, GROUP * (g + 1))], axis=0
    )


def rows_to_heads(parts, length):
    return jnp.concatenate(
        [p[length * r : length * (r + 1)] for p in parts for r in range(GROUP)], axis=1
    )


def attention_forward(order, length, seq_ref, blocks, wq, wkv, bq, bkv, gain, cos, sin, mask,
                      att_o, q_o, k_o, v_o, lse_o):
    seq = seq_ref[0]
    cosine, sine = tables(seq, order, cos, sin)
    width = gain.shape[1]
    for b in range(blocks.shape[1] // length):
        x = blocks[:, b * length : (b + 1) * length, :width].astype(F32)
        x = x.reshape(len(order) * length, width)
        first = (norm_parts(x)[1] * gain[...]).astype(BF)
        kv = dot(first, wkv[...], 1, 0) + bkv[...]
        q = dot(first[:length], wq[...], 1, 0) + bq[...]
        q = jnp.concatenate(turn(q, cosine[:length], sine[:length]), axis=1).astype(BF)
        q = q * jnp.asarray(HEAD_DIM ** (-0.5), BF)
        kv = turn_kv(kv, cosine, sine).astype(BF)
        allowed = jnp.concatenate([mask[b]] * GROUP, axis=0) > 0.0
        parts = []
        for g in range(KV_HEADS):
            qg = heads_to_rows(q, g)
            kg = kv[:, HEAD_DIM * g : HEAD_DIM * (g + 1)]
            vg = kv[:, KW + HEAD_DIM * g : KW + HEAD_DIM * (g + 1)]
            q_o[b, g] = qg
            k_o[b, g] = kg
            v_o[b, g] = vg
            scores = jnp.where(allowed, dot(qg, kg, 1, 1), MASKED)
            top = jnp.max(scores, axis=-1, keepdims=True)
            e = jnp.exp(scores - top)
            total = jnp.sum(e, axis=-1, keepdims=True)
            lse_o[b, g] = jnp.log(total) + top
            probs = (e * (1.0 / total)).astype(BF)
            parts.append(dot(probs, vg, 1, 0))
        att_o[b * length : (b + 1) * length, :] = rows_to_heads(parts, length).astype(BF)


def feed_forward(attended, source, wo, wgu, wd, gain, cot, weight,
                 out_o, down_o, gu_o, mid_o, wout_o, attg_o, gain_o):
    units = wd.shape[0]
    step = units // 3
    att = attended[...]
    middle = source[...].astype(F32) + dot(att, wo[...], 1, 0)
    scale_two, normed = norm_parts(middle)
    g2 = gain[...]
    second = (normed * g2).astype(BF)
    out_grad = cot[...].astype(F32) * weight[...]
    feed_grad = out_grad.astype(BF)
    feed = None
    back = None
    for j in range(0, units, step):
        wg = wgu[:, j : j + step]
        wu = wgu[:, units + j : units + j + step]
        wdj = wd[j : j + step, :]
        gate = dot(second, wg, 1, 0)
        up = dot(second, wu, 1, 0)
        sig = jax.nn.sigmoid(gate)
        act = gate * sig
        product = (act * up).astype(BF)
        part = dot(product, wdj, 1, 0)
        feed = part if feed is None else feed + part
        down_o[j : j + step, :] = dot(product, feed_grad, 0, 0).astype(BF)
        pgrad = dot(feed_grad, wdj, 1, 1)
        ggrad = (pgrad * up * (sig * (1.0 + gate * (1.0 - sig)))).astype(BF)
        ugrad = (pgrad * act).astype(BF)
        gu_o[:, j : j + step] = dot(second, ggrad, 0, 0).astype(BF)
        gu_o[:, units + j : units + j + step] = dot(second, ugrad, 0, 0).astype(BF)
        part = dot(ggrad, wg, 1, 1) + dot(ugrad, wu, 1, 1)
        back = part if back is None else back + part
    out_o[...] = (middle + feed).astype(BF)
    gain_o[...] = jnp.sum(back * normed, axis=0, keepdims=True)
    middle_grad = out_grad + norm_back(back, g2, scale_two, normed)
    mid_o[...] = middle_grad
    branch = middle_grad.astype(BF)
    wout_o[...] = dot(att, branch, 0, 0).astype(BF)
    attg_o[...] = dot(branch, wo[...], 1, 1).astype(BF)


def attention_backward(order, length, seq_ref, blocks, wq, wkv, gain, cos, sin, mask, q_i, k_i, v_i,
                       lse, attg, dq_o, dkv_o, wgrad_o, bias_o, gain_o):
    seq = seq_ref[0]
    cosine, sine = tables(seq, order, cos, sin)
    width = gain.shape[1]
    q_wgrad = kv_wgrad = bias_q = bias_kv = gain_sum = None
    for b in range(blocks.shape[1] // length):
        x = blocks[:, b * length : (b + 1) * length, :width].astype(F32)
        x = x.reshape(len(order) * length, width)
        normed = norm_parts(x)[1]
        first = (normed * gain[...]).astype(BF)
        allowed = jnp.concatenate([mask[b]] * GROUP, axis=0) > 0.0
        ag = attg[b * length : (b + 1) * length, :]
        dqs, dks, dvs = [], [], []
        for g in range(KV_HEADS):
            qg, kg, vg = q_i[b, g], k_i[b, g], v_i[b, g]
            agg = heads_to_rows(ag, g)
            p = jnp.exp(jnp.where(allowed, dot(qg, kg, 1, 1), MASKED) - lse[b, g])
            dvs.append(dot(p.astype(BF), agg, 0, 0))
            pg = dot(agg, vg, 1, 1)
            inner = jnp.sum(p * pg, axis=-1, keepdims=True)
            ds = (p * (pg - inner)).astype(BF)
            dqs.append(dot(ds, kg, 1, 0) * HEAD_DIM ** (-0.5))
            dks.append(dot(ds, qg, 0, 0))
        dq = rows_to_heads(dqs, length)
        dq = jnp.concatenate([dq, jnp.zeros((length, 64), F32)], axis=1)
        dq = jnp.concatenate(turn(dq, cosine[:length], -sine[:length]), axis=1).astype(BF)
        dkv = jnp.concatenate(dks + dvs, axis=1)
        dkv = turn_kv(dkv, cosine, -sine).astype(BF)
        dq_o[b * length : (b + 1) * length, :] = dq
        for r in range(len(order)):
            dkv_o[r, b * length : (b + 1) * length, :] = dkv[r * length : (r + 1) * length, :]
        wq_part = dot(first[:length], dq, 0, 0)
        wkv_part = dot(first, dkv, 0, 0)
        bq_part = jnp.sum(dq.astype(F32), axis=0, keepdims=True)
        bkv_part = jnp.sum(dkv.astype(F32), axis=0, keepdims=True)
        e_kv = dot(dkv, wkv[...], 1, 1) * normed
        e_q = dot(dq[:, :QW], wq[:, :QW], 1, 1) * normed[:length]
        g_part = jnp.sum(e_kv, axis=0, keepdims=True) + jnp.sum(e_q, axis=0, keepdims=True)
        if q_wgrad is None:
            q_wgrad, kv_wgrad, bias_q, bias_kv, gain_sum = wq_part, wkv_part, bq_part, bkv_part, g_part
        else:
            q_wgrad, kv_wgrad = q_wgrad + wq_part, kv_wgrad + wkv_part
            bias_q, bias_kv, gain_sum = bias_q + bq_part, bias_kv + bkv_part, gain_sum + g_part
    wgrad_o[...] = jnp.concatenate([q_wgrad[:, :QW], kv_wgrad], axis=1).astype(BF)
    bias_o[...] = jnp.concatenate([bias_q[:, :QW], bias_kv], axis=1)
    gain_o[...] = gain_sum


def input_gradient(dq, own, a, b, c, source, mid, wq, wkv, gain, out_o):
    kv = own[...].astype(F32) + a[...].astype(F32) + b[...].astype(F32) + c[...].astype(F32)
    first_grad = dot(dq[:, :QW], wq[:, :QW], 1, 1) + dot(kv.astype(BF), wkv[...], 1, 1)
    scale_one, normed = norm_parts(source[...].astype(F32))
    out_o[...] = mid[...] + norm_back(first_grad, gain[...], scale_one, normed)

def chosen(flag, a, b):
    return jnp.where(flag != 0, b, a)


class Blocks:
    def __init__(self, *refs):
        self.refs = refs
        self.shape = (len(refs),) + refs[0].shape

    def __getitem__(self, key):
        return jnp.stack([ref[key[1:]] for ref in self.refs])


def cut_qkv(core_bit, meta, w_hbm, bias_hbm, gains_hbm, out_o, w, bias, gains, all_s, sems):
    pairs = ((w_hbm, w), (bias_hbm, bias), (gains_hbm, gains))
    copies = [pltpu.make_async_copy(a, b, sems.at[i]) for i, (a, b) in enumerate(pairs)]
    for copy in copies:
        copy.start()
    for copy in copies:
        copy.wait()
    rows = w.shape[0]
    n = bias.shape[1]
    all_s[:rows, :] = w[...].astype(F32)
    all_s[rows:, :] = jnp.zeros((8, w.shape[1]), F32)
    all_s[rows : rows + 1, :n] = bias[...].astype(F32)
    for i in range(2):
        all_s[rows : rows + 1, n + rows * i : n + rows * (i + 1)] = gains[i : i + 1, :].astype(F32)
    half = out_o.shape[0]
    at = pl.multiple_of((meta[0] & core_bit) * half, 8)
    out_o[...] = all_s[pl.ds(at, half), :].astype(BF)


def first_forward(order, length, d_rows, n_bias, meta, b0, b1, b2, b3, a00, a10, a01, a11, cos, sin, mask,
                  att_o, q_o, k_o, v_o, lse_o, w_o, gain_o, w_s, b_s):
    blocks = Blocks(b0, b1, b2, b3)
    core, x = meta[0] & 1, meta[1] & 1
    cut = a00.shape[2]
    for x_rel, c_rel, piece in ((0, 0, a00), (1, 0, a10), (0, 1, a01), (1, 1, a11)):
        for z0 in range(2):
            for z1 in range(2):
                at = (z1 * 4 + z0 * 2 + (x ^ x_rel)) * 2 * cut + (core ^ c_rel) * cut
                w_s[pl.ds(pl.multiple_of(at, 8), cut), :] = piece[z0, z1].astype(F32)
    n_f = w_s.shape[0] // (2 * cut)
    starts = [2 * cut * f for f in range(n_f)]
    w_o[...] = jnp.concatenate([w_s[at : at + d_rows, :] for at in starts], axis=0).astype(BF)
    lines = [w_s[at + d_rows : at + d_rows + 1, :] for at in starts]
    b_s[...] = jnp.concatenate([line[:, :n_bias] for line in lines], axis=1)
    for i in range(2):
        at = n_bias + d_rows * i
        gain_o[i : i + 1, :] = jnp.concatenate([line[:, at : at + d_rows] for line in lines], axis=1)
    wide = QW + 64
    attention_forward(order, length, meta, blocks, w_o[:, :wide], w_o[:, QW:], b_s[:, :wide], b_s[:, QW:],
                      gain_o[0:1, :], cos, sin, mask, att_o, q_o, k_o, v_o, lse_o)


def turned(out, value):
    length = out.shape[2]
    for b in range(out.shape[0]):
        out[b] = value[length * b : length * (b + 1)].T.astype(out.dtype)


def rel(meta, f):
    r = f ^ meta[1]
    return r & 1, (r >> 1) & 1, (r >> 2) & 1


def feed_forward_pieces(d_rows, ff_rows, meta, attended, source, b00, b10, b01, b11,
                        g000, g100, g010, g110, g001, g101, g011, g111, gains, cot, weight,
                        out_o, gk_o, gg_o, dk_o, dg_o, mid_o, attg_o, gain_o, down_s, wout_s):
    core, y, x_own, z0_own = meta[0] & 1, (meta[0] >> 1) & 1, meta[1] & 1, (meta[1] >> 1) & 1
    n_f = 8
    hf = n_f // 2
    part_d = ff_rows // 4
    part_o = d_rows // 3
    cut = b00.shape[2] - ff_rows // 2

    def b_rows(z0, z1, x, c, rows):
        low = chosen(z0_own ^ z0, b00[z1, x, rows, :], b10[z1, x, rows, :])
        high = chosen(z0_own ^ z0, b01[z1, x, rows, :], b11[z1, x, rows, :])
        return chosen(core ^ c, low, high)

    def quarter(near, far):
        parts = []
        for f in range(n_f):
            z1, z0, x = f >> 2, (f >> 1) & 1, f & 1
            mine, other = near[z0, z1].astype(F32), far[z0, z1].astype(F32)
            parts.append(chosen(x_own ^ x, mine, other))
        return jnp.concatenate(parts, axis=0).astype(BF)

    wo = []
    for f in range(n_f):
        z1, z0, x = f >> 2, (f >> 1) & 1, f & 1
        wo.append(b_rows(z0, z1, x, 0, slice(ff_rows // 2, None)).astype(F32))
        wo.append(b_rows(z0, z1, x, 1, slice(ff_rows // 2, None)).astype(F32)[: d_rows - cut])
    wo = jnp.concatenate(wo, axis=0).astype(BF)
    att = attended[...]
    middle = source[...].astype(F32) + dot(att, wo, 1, 0)
    scale_two, normed = norm_parts(middle)
    g2 = gains[1:2, :]
    second = (normed * g2).astype(BF)
    out_grad = cot[...].astype(F32) * weight[...]
    feed_grad = out_grad.astype(BF)
    feed = back = None
    for c_rel in (1, 0):
        first_q = quarter(g001, g101) if c_rel else quarter(g000, g100)
        second_q = quarter(g011, g111) if c_rel else quarter(g010, g110)
        wg = chosen(y, first_q, second_q)
        wu = chosen(y, second_q, first_q)
        h = core ^ c_rel
        wd = []
        for i in range(hf):
            for c in range(2):
                wd.append(b_rows(i >> 1, h, i & 1, c, slice(0, ff_rows // 2)))
        wd = jnp.concatenate(wd, axis=0)
        gate = dot(second, wg, 1, 0)
        up = dot(second, wu, 1, 0)
        sig = jax.nn.sigmoid(gate)
        act = gate * sig
        product = (act * up).astype(BF)
        part = dot(product, wd, 1, 0)
        feed = part if feed is None else feed + part
        down_s[...] = dot(product, feed_grad, 0, 0)
        pgrad = dot(feed_grad, wd, 1, 1)
        ggrad = (pgrad * up * (sig * (1.0 + gate * (1.0 - sig)))).astype(BF)
        ugrad = (pgrad * act).astype(BF)
        part = dot(ggrad, wg, 1, 1) + dot(ugrad, wu, 1, 1)
        back = part if back is None else back + part
        for i in range(hf):
            x, z0, z1 = rel(meta, hf * h + i)
            for yy in range(2):
                for c_to, to in ((0, dk_o), (1, dg_o)):
                    at = pl.multiple_of(i * ff_rows + (yy * 2 + (core ^ c_to)) * part_d, 16)
                    to[y ^ yy, x, z0, z1, :part_d, :] = down_s[pl.ds(at, part_d), :].astype(BF)
        to = gg_o if c_rel else gk_o
        for yy, grad in ((0, ggrad), (1, ugrad)):
            wgrad = dot(second, grad, 0, 0)
            for f in range(n_f):
                x, z0, z1 = rel(meta, f)
                to[x, z0, z1, yy] = wgrad[d_rows * f : d_rows * (f + 1), :].astype(BF)
    turned(out_o, middle + feed)
    gain_o[...] = jnp.sum(back * normed, axis=0, keepdims=True)
    middle_grad = out_grad + norm_back(back, g2, scale_two, normed)
    mid_o[...] = middle_grad
    branch = middle_grad.astype(BF)
    attg_o[...] = dot(branch, wo, 1, 1).astype(BF)
    wout = dot(att, branch, 0, 0)
    for f in range(n_f):
        wout_s[f, :d_rows, :] = wout[d_rows * f : d_rows * (f + 1), :]
        wout_s[f, d_rows:, :] = jnp.zeros((part_o, wout.shape[1]), F32)
    for f in range(n_f):
        x, z0, z1 = rel(meta, f)
        for yy in range(2):
            for c_to, to in ((0, dk_o), (1, dg_o)):
                at = pl.multiple_of((yy * 2 + (core ^ c_to)) * part_o, 8)
                to[y ^ yy, x, z0, z1, part_d:, :] = wout_s[f, pl.ds(at, part_o), :].astype(BF)


def attention_backward_pieces(order, length, d_rows, meta, b0, b1, b2, b3, w, gains, cos, sin, mask, q_i, k_i, v_i,
                              lse, attg, gain_two, dq_o, dk_o, dg_o, rk_o, rg_o, w_s, bias_s, gain_s, small_s):
    blocks = Blocks(b0, b1, b2, b3)
    half = len(order) // 2

    class Pieces:
        def __setitem__(self, key, value):
            ref = dk_o if key[0] < half else dg_o
            ref[(key[0] % half,) + key[1:]] = value

    class Wgrad:
        def __setitem__(self, key, value):
            w_s[:, : 2 * KW] = value[:, QW:].astype(F32)
            w_s[:, 2 * KW : 2 * KW + QW] = value[:, :QW].astype(F32)
            w_s[:, 2 * KW + QW :] = jnp.zeros((value.shape[0], 64), F32)

    wide = QW + 64
    attention_backward(order, length, meta, blocks, w[:, :wide], w[:, QW:], gains[0:1, :], cos, sin, mask,
                       q_i, k_i, v_i, lse, attg, dq_o, Pieces(), Wgrad(), bias_s, gain_s)
    n_f = small_s.shape[0]
    qk, v = (QW + KW) // n_f, KW // n_f
    bias, g1, g2 = bias_s[...], gain_s[...], gain_two[...]
    for f in range(n_f):
        line = jnp.concatenate(
            [
                bias[:, qk * f : qk * (f + 1)],
                bias[:, QW + KW + v * f : QW + KW + v * (f + 1)],
                g1[:, d_rows * f : d_rows * (f + 1)],
                jnp.zeros((1, 256 - qk - v - d_rows), F32),
                g2[:, d_rows * f : d_rows * (f + 1)],
                jnp.zeros((1, 768 - d_rows), F32),
            ],
            axis=1,
        )
        small_s[f] = jnp.broadcast_to(line, (8, 1024))
    core, y = meta[0] & 1, (meta[0] >> 1) & 1
    for f in range(n_f):
        x, z0, z1 = rel(meta, f)
        for yy in range(2):
            for c_to, to in ((0, rk_o), (1, rg_o)):
                at = pl.multiple_of((yy * 2 + (core ^ c_to)) * 256, 256)
                block = [w_s[d_rows * f : d_rows * (f + 1), pl.ds(at, 256)], small_s[f, :, pl.ds(at, 256)]]
                to[y ^ yy, x, z0, z1] = jnp.concatenate(block, axis=0).astype(BF)


def input_gradient_two(dq, own, other, source, mid, w, gains, out_o):
    kv = (own[...].astype(F32) + other[...].astype(F32)).astype(BF)
    first_grad = dot(dq[:, :QW], w[:, :QW], 1, 1) + dot(kv, w[:, QW:], 1, 1)
    scale_one, normed = norm_parts(source[...].astype(F32))
    turned(out_o, mid[...] + norm_back(first_grad, gains[0:1, :], scale_one, normed))


def place_gate(meta, near, far, out_o):
    core = meta[0] & 1
    n = near.shape[2]
    for pieces, c_rel in ((near, 0), (far, 1)):
        for yy in range(2):
            at = pl.multiple_of((yy * 2 + (core ^ c_rel)) * n, 128)
            out_o[:, pl.ds(at, n)] = pieces[yy].astype(F32)


def place_down(part_d, meta, p00, p10, p01, p11, out_o, wout_o):
    seq = meta[0]
    part_o = p00.shape[0] - part_d
    for piece, o in ((p00[...], 0), (p10[...], 2), (p01[...], 1), (p11[...], 3)):
        piece = piece.astype(F32)
        to = seq ^ o
        out_o[pl.ds(pl.multiple_of(to * part_d, 16), part_d), :] = piece[:part_d]

        @pl.when(to < 3)
        def _():
            wout_o[pl.ds(pl.multiple_of(to * part_o, 8), part_o), :] = piece[part_d:]


def place_qkv(qk, v, meta, p00, p10, p01, p11, w_o, bqk_o, bv_o, gains_o, all_s):
    seq = meta[0]
    n = p00.shape[1]
    for piece, o in ((p00[...], 0), (p10[...], 2), (p01[...], 1), (p11[...], 3)):
        all_s[:, pl.ds(pl.multiple_of((seq ^ o) * n, 128), n)] = piece.astype(F32)
    d_rows = w_o.shape[0]
    w_o[:, :QW] = all_s[:d_rows, 2 * KW : 2 * KW + QW]
    w_o[:, QW:] = all_s[:d_rows, : 2 * KW]
    line = all_s[d_rows : d_rows + 1, :]
    bqk_o[...] = line[:, :qk]
    bv_o[...] = line[:, qk : qk + v]
    gains_o[0:1, :] = line[:, qk + v : qk + v + d_rows]
    gains_o[1:2, :] = line[:, 256 : 256 + d_rows]


def place_all(part_d, qk, v, meta, near, far, d0, d1, d2, d3, r0, r1, r2, r3,
              gate_o, down_o, wout_o, w_o, bqk_o, bv_o, gains_o, all_s):
    place_gate(meta, near, far, gate_o)
    place_down(part_d, meta, d0, d1, d2, d3, down_o, wout_o)
    place_qkv(qk, v, meta, r0, r1, r2, r3, w_o, bqk_o, bv_o, gains_o, all_s)


class Net:
    def __init__(self, n_fsdp, n_seq):
        self.n_fsdp, self.n_seq = n_fsdp, n_seq
        self.total = n_fsdp * n_seq
        f, s = lax.axis_index("fsdp"), lax.axis_index("seq")
        self.index = f * n_seq + s
        self.seq_bits = [1 << b for b in range(n_seq.bit_length() - 1)]
        self.fsdp_bits = [n_seq << b for b in range(n_fsdp.bit_length() - 1)]

    def swap(self, value, mask):
        pairs = [(i, i ^ mask) for i in range(self.total)]
        return lax.ppermute(value, ("fsdp", "seq"), pairs)

    def bit(self, mask):
        return (self.index & mask) != 0

    def both(self, mine, mask, axis, other=None):
        other = self.swap(mine, mask) if other is None else other
        high = self.bit(mask)
        return jnp.stack([jnp.where(high, other, mine), jnp.where(high, mine, other)], axis=axis)

    def half(self, value, mask, axis):
        return lax.dynamic_index_in_dim(
            value, self.bit(mask).astype(jnp.int32), axis, keepdims=False
        )

    def add_half(self, value, mask, axis):
        mine = self.bit(mask).astype(jnp.int32)
        keep = lax.dynamic_index_in_dim(value, mine, axis, keepdims=False)
        give = lax.dynamic_index_in_dim(value, 1 - mine, axis, keepdims=False)
        got = self.swap(give, mask)
        return (keep.astype(F32) + got.astype(F32)).astype(value.dtype)

    def gather_fsdp(self, value):
        for step, mask in enumerate(reversed(self.fsdp_bits)):
            value = self.both(value, mask, step)
        return value

    def scatter_fsdp(self, value, first_axis=0):
        count = len(self.fsdp_bits)
        for step, mask in enumerate(self.fsdp_bits):
            value = self.add_half(value, mask, first_axis + count - 1 - step)
        return value


def on_device(
    hidden, w_qkv, b_qkv, w_out, w_gate_up, w_down, norm_gains, segment_ids, token_counts, cotangent,
    n_fsdp, n_seq,
):
    net = Net(n_fsdp, n_seq)
    micro, batch, length, width = hidden.shape
    full_length = length * n_seq
    tokens_micro = batch * n_fsdp * full_length
    scale = HEAD_DIM ** (-0.5)
    rows = micro * batch * length
    d_rows = w_qkv.shape[0]
    ff_rows = w_down.shape[0]
    units = w_gate_up.shape[1] // 2
    qkv_w = w_qkv.shape[1]
    core = net.seq_bits[0]
    f_lead = (2,) * len(net.fsdp_bits)

    ids = segment_ids.reshape(rows, 1).astype(BF)
    block = jnp.concatenate(
        [hidden.reshape(rows, width), jnp.broadcast_to(ids, (rows, 64))], axis=1
    )
    blocks = block[None]
    for mask in reversed(net.seq_bits):
        blocks = jnp.concatenate([blocks, net.swap(blocks, mask)], axis=0)
    order = [0]
    for mask in reversed(net.seq_bits):
        order = order + [o ^ mask for o in order]
    seq_index = lax.axis_index("seq")
    block_ids = [seq_index ^ o for o in order]

    pad_rows = -(d_rows + 1) % 16 + 1
    extra = jnp.zeros((pad_rows, qkv_w), BF)
    small = jnp.concatenate([b_qkv, norm_gains.reshape(-1)])
    extra = extra.at[0, : small.shape[0]].set(small)
    shard_a = jnp.concatenate([w_qkv, extra], axis=0).reshape(2, -1, qkv_w)
    got_a = net.gather_fsdp(net.half(shard_a, core, 0))
    full_a = net.both(got_a, core, len(f_lead)).reshape(n_fsdp, d_rows + pad_rows, qkv_w)
    wf_qkv = full_a[:, :d_rows].reshape(n_fsdp * d_rows, qkv_w)
    smalls = full_a[:, d_rows]
    n_bias = b_qkv.shape[0]
    bias = smalls[:, :n_bias].reshape(-1).astype(F32)
    gains = smalls[:, n_bias : n_bias + 2 * d_rows].reshape(n_fsdp, 2, d_rows).astype(F32)
    gain_one = gains[:, 0].reshape(-1)
    gain_two = gains[:, 1].reshape(-1)

    pad_b = -(d_rows + ff_rows) % 16
    shard_b = jnp.concatenate([w_out, w_down, jnp.zeros((pad_b, width), BF)], axis=0)
    shard_b = shard_b.reshape(2, -1, width)
    got_b = net.gather_fsdp(net.half(shard_b, core, 0))

    parts = n_seq
    shard_c = w_gate_up.reshape(d_rows, parts, -1)
    got_c = net.gather_fsdp(lax.dynamic_index_in_dim(shard_c, seq_index, 1, keepdims=False))
    full_b = net.both(got_b, core, len(f_lead)).reshape(n_fsdp, -1, width)
    wf_out = full_b[:, :d_rows].reshape(n_fsdp * d_rows, width)
    wf_down = full_b[:, d_rows : d_rows + ff_rows].reshape(n_fsdp * ff_rows, width)
    got_c = got_c.reshape(n_fsdp * d_rows, -1)
    for mask in reversed(net.seq_bits):
        got_c = net.both(got_c, mask, got_c.ndim - 1)
    wf_gate_up = got_c.reshape(n_fsdp * d_rows, 2 * units)

    places = np.arange(full_length, dtype=np.float32)
    speeds = np.power(ROPE_BASE, -2.0 * np.arange(HEAD_DIM // 2, dtype=np.float32) / HEAD_DIM)
    angles = places[:, None] * speeds.astype(np.float32)[None, :]
    cos_t = np.tile(np.cos(angles), (1, 4)).reshape(n_seq, length, 128)
    sin_t = np.concatenate([-np.sin(angles), np.sin(angles)] * 2, axis=1).reshape(n_seq, length, 128)
    cos_t, sin_t = jnp.asarray(cos_t, F32), jnp.asarray(sin_t, F32)
    seqs = micro * batch
    seg_all = blocks[..., width].reshape(n_seq, seqs, length).transpose(1, 0, 2)
    own_places = seq_index * length + jnp.arange(length, dtype=jnp.int32)
    key_places = jnp.stack(block_ids)[:, None] * length + jnp.arange(length, dtype=jnp.int32)
    allowed = (seg_all[:, 0, :, None] == seg_all.reshape(seqs, 1, -1)) & (
        own_places[None, :, None] >= key_places.reshape(1, 1, -1)
    )
    allowed = allowed.astype(F32)
    seq_scalar = seq_index.astype(jnp.int32).reshape(1)
    wq, wkv = wf_qkv[:, : QW + 64], wf_qkv[:, QW:]
    gain_one, gain_two = gain_one[None], gain_two[None]
    source = hidden.reshape(rows, width)
    n_all = n_seq * rows
    attended, q_s, k_s, v_s, lse = call(
        functools.partial(attention_forward, order, length),
        [seq_scalar],
        [blocks, wq, wkv, bias[None, : QW + 64], bias[None, QW:], gain_one, cos_t, sin_t, allowed],
        [
            sds((rows, QW), BF),
            sds((seqs, KV_HEADS, GROUP * length, HEAD_DIM), BF),
            sds((seqs, KV_HEADS, full_length, HEAD_DIM), BF),
            sds((seqs, KV_HEADS, full_length, HEAD_DIM), BF),
            sds((seqs, KV_HEADS, GROUP * length, 1), F32),
        ],
        2 * n_all * width * 2 * KW + 2 * rows * width * QW + 4 * rows * full_length * QW,
    )

    weight = tokens_micro / token_counts.astype(F32)
    weight = jnp.repeat(weight, batch * length)[:, None]
    block_out, down_grad, gate_up_wgrad, middle_grad, out_wgrad, attended_grad, gain_two_grad = call(
        feed_forward,
        [],
        [attended, source, wf_out, wf_gate_up, wf_down, gain_two, cotangent.reshape(rows, width), weight],
        [
            sds((rows, width), BF),
            sds((units, width), BF),
            sds((width, 2 * units), BF),
            sds((rows, width), F32),
            sds((QW, width), BF),
            sds((rows, QW), BF),
            sds((1, width), F32),
        ],
        6 * rows * width * 3 * units + 6 * rows * width * QW,
    )
    block_out = block_out.reshape(hidden.shape)

    def seq_axes(value, axis, masks):
        for mask in masks:
            value = net.add_half(value, mask, axis)
        return value

    quarter = (2,) * len(net.seq_bits)
    n_f = len(f_lead)
    red_down = down_grad.reshape(f_lead + quarter + (ff_rows // n_seq, width))
    for step, mask in enumerate(net.seq_bits):
        red_down = net.add_half(red_down, mask, n_f + len(quarter) - 1 - step)
    red_down = net.scatter_fsdp(red_down)

    red_gate = gate_up_wgrad.reshape(f_lead + (d_rows,) + quarter + (2 * units // n_seq,))
    red_gate = net.add_half(red_gate, core, n_f + len(quarter))
    red_gate = net.add_half(red_gate, net.fsdp_bits[0], n_f - 1)
    for step, mask in enumerate(net.seq_bits[1:]):
        red_gate = net.add_half(red_gate, mask, n_f - 1 + len(quarter) - 1 - step)
    for step, mask in enumerate(net.fsdp_bits[1:]):
        red_gate = net.add_half(red_gate, mask, n_f - 2 - step)

    dq, dkv, qkv_wgrad, bias_grad, gain_one_grad = call(
        functools.partial(attention_backward, order, length),
        [seq_scalar],
        [blocks, wq, wkv, gain_one, cos_t, sin_t, allowed, q_s, k_s, v_s, lse, attended_grad],
        [
            sds((rows, QW + 64), BF),
            sds((n_seq, rows, 2 * KW), BF),
            sds((width, qkv_w), BF),
            sds((1, qkv_w), F32),
            sds((1, width), F32),
        ],
        4 * n_all * width * 2 * KW + 4 * rows * width * QW + 10 * rows * full_length * QW,
    )
    kv_parts = [dkv[0]]
    for place, mask_bits in enumerate(order):
        if mask_bits:
            kv_parts.append(net.swap(dkv[place], mask_bits))
    (hidden_grad,) = call(
        input_gradient,
        [],
        [dq, *kv_parts, source, middle_grad, wq, wkv, gain_one],
        [sds((rows, width), F32)],
        2 * rows * width * qkv_w,
    )
    hidden_grad = hidden_grad.reshape(hidden.shape)
    bias_grad, gain_one_grad, gain_two_grad = bias_grad[0], gain_one_grad[0], gain_two_grad[0]

    qk_rows, v_rows = (QW + KW) // n_fsdp, KW // n_fsdp
    small_grads = jnp.concatenate(
        [
            bias_grad[: QW + KW].reshape(n_fsdp, qk_rows),
            bias_grad[QW + KW :].reshape(n_fsdp, v_rows),
            gain_one_grad.reshape(n_fsdp, d_rows),
            gain_two_grad.reshape(n_fsdp, d_rows),
        ],
        axis=1,
    ).astype(BF)
    wide = qkv_w + width
    small_pad = jnp.zeros((n_fsdp, pad_rows, wide), BF)
    small_pad = small_pad.at[:, 0, : small_grads.shape[1]].set(small_grads)
    rest = jnp.concatenate([qkv_wgrad, out_wgrad], axis=1)
    rest = jnp.concatenate([rest.reshape(n_fsdp, d_rows, wide), small_pad], axis=1)
    rest = rest.reshape(f_lead + (d_rows + pad_rows,) + quarter + (wide // n_seq,))
    for step, mask in enumerate(net.seq_bits):
        rest = net.add_half(rest, mask, n_f + 1 + len(quarter) - 1 - step)
    rest = net.scatter_fsdp(rest)

    def seq_back(value, axis):
        for step, mask in enumerate(reversed(net.seq_bits)):
            value = net.both(value, mask, axis + step)
        return value

    out_down = seq_back(red_down, 0).reshape(ff_rows, width).astype(F32)
    out_gate = seq_back(red_gate, 1).reshape(d_rows, 2 * units).astype(F32)
    out_rest = seq_back(rest, 1).reshape(d_rows + pad_rows, wide).astype(F32)
    line = out_rest[d_rows]
    edge = qk_rows + v_rows
    return (
        block_out,
        hidden_grad,
        out_rest[:d_rows, :qkv_w],
        line[:qk_rows],
        line[qk_rows:edge],
        out_rest[:d_rows, qkv_w:],
        out_gate,
        out_down,
        line[edge : edge + 2 * d_rows].reshape(2, d_rows),
    )


def after(value, *others):
    return lax.optimization_barrier((value, *others))[0]


def rope_tables(full_length, n_seq):
    places = np.arange(full_length, dtype=np.float32)
    speeds = np.power(ROPE_BASE, -2.0 * np.arange(HEAD_DIM // 2, dtype=np.float32) / HEAD_DIM)
    angles = places[:, None] * speeds.astype(np.float32)[None, :]
    cos_t = np.tile(np.cos(angles), (1, 4)).reshape(n_seq, -1, 128)
    sin_t = np.concatenate([-np.sin(angles), np.sin(angles)] * 2, axis=1).reshape(n_seq, -1, 128)
    return jnp.asarray(cos_t, F32), jnp.asarray(sin_t, F32)


def on_device_tiled(
    hidden, w_qkv, b_qkv, w_out, w_gate_up, w_down, norm_gains, segment_ids, token_counts, cotangent,
    n_fsdp, n_seq,
):
    net = Net(n_fsdp, n_seq)
    micro, batch, length, width = hidden.shape
    full_length = length * n_seq
    tokens_micro = batch * n_fsdp * full_length
    rows = micro * batch * length
    seqs = micro * batch
    d_rows, qkv_w = w_qkv.shape
    ff_rows = w_down.shape[0]
    units = w_gate_up.shape[1] // 2
    n_bias = b_qkv.shape[0]
    core, ybit = net.seq_bits
    xbit, znear, zfar = net.fsdp_bits
    order = [0, 2, 1, 3]
    seq_index = lax.axis_index("seq")
    meta = jnp.stack([seq_index, lax.axis_index("fsdp")]).astype(jnp.int32)
    source = hidden.reshape(rows, width)

    small = [w_qkv, b_qkv[None], norm_gains]
    a0 = pl.pallas_call(
        functools.partial(cut_qkv, core),
        out_shape=sds(((d_rows + 8) // 2, qkv_w), BF),
        in_specs=[pl.BlockSpec(memory_space=pltpu.SMEM)] + [pl.BlockSpec(memory_space=pl.ANY)] * 3,
        out_specs=pl.BlockSpec(memory_space=pltpu.VMEM),
        scratch_shapes=[
            *[pltpu.VMEM(v.shape, BF) for v in small],
            pltpu.VMEM((d_rows + 8, qkv_w), F32),
            pltpu.SemaphoreType.DMA((3,)),
        ],
        compiler_params=pltpu.CompilerParams(vmem_limit_bytes=4 * 1024 * 1024),
    )(meta, *small)
    a1 = net.both(a0, zfar, 0)

    ids = segment_ids.reshape(rows, 1).astype(BF)
    block = jnp.concatenate([source, jnp.broadcast_to(ids, (rows, 64))], axis=1)
    block = after(block, a0)
    block_y = net.swap(block, ybit)
    block_c = net.swap(block, core)

    quarter = 2 * units // n_seq
    gu0 = lax.dynamic_slice_in_dim(after(w_gate_up, a0), seq_index * quarter, quarter, axis=1)
    half_b = jnp.concatenate(
        [
            w_down.reshape(2, ff_rows // 2, width),
            jnp.concatenate([w_out, jnp.zeros((8, width), BF)], axis=0).reshape(2, -1, width),
        ],
        axis=1,
    )
    a2 = net.both(a1, znear, 0)
    b0 = net.half(after(half_b, a0), core, 0)
    bx = net.both(b0, xbit, 0)
    a_x = net.swap(a2, xbit)
    a_c = net.swap(a2, core)
    gu1 = net.both(gu0, zfar, 0)
    b1 = net.both(after(bx, a2), zfar, 0)
    gu2 = net.both(after(gu1, a2), znear, 0)
    block_yc = net.swap(block_y, core)
    a_xc = net.swap(a_x, core)
    gu2 = after(gu2, a_x)
    gu_x = net.swap(gu2, xbit)
    gu_y = net.swap(gu2, ybit)
    gu_c = net.swap(gu2, core)
    b_z = net.swap(b1, znear)
    b_c = net.swap(b1, core)
    gu_xy = net.swap(gu_x, ybit)
    a_xc = after(a_xc, gu_x, b1)

    cos_t, sin_t = rope_tables(full_length, n_seq)
    block_ids = [seq_index ^ o for o in order]
    blocks = [block, block_y, block_c, block_yc]
    seg_all = jnp.stack([b[:, width].reshape(seqs, length) for b in blocks], axis=1)
    own_places = seq_index * length + jnp.arange(length, dtype=jnp.int32)
    key_places = jnp.stack(block_ids)[:, None] * length + jnp.arange(length, dtype=jnp.int32)
    allowed = (seg_all[:, 0, :, None] == seg_all.reshape(seqs, 1, -1)) & (
        own_places[None, :, None] >= key_places.reshape(1, 1, -1)
    )
    allowed = allowed.astype(F32)
    attended, q_s, k_s, v_s, lse, wf, gains = call(
        functools.partial(first_forward, order, length, d_rows, n_bias),
        [meta],
        [*blocks, a2, a_x, a_c, a_xc, cos_t, sin_t, allowed],
        [
            sds((rows, QW), BF),
            sds((seqs, KV_HEADS, GROUP * length, HEAD_DIM), BF),
            sds((seqs, KV_HEADS, full_length, HEAD_DIM), BF),
            sds((seqs, KV_HEADS, full_length, HEAD_DIM), BF),
            sds((seqs, KV_HEADS, GROUP * length, 1), F32),
            sds((width, qkv_w), BF),
            sds((2, width), F32),
        ],
        1.2e10,
        [(n_fsdp * (d_rows + 8), qkv_w), (1, qkv_w)],
        20,
    )
    gu_xy, b_z = after(gu_xy, attended), after(b_z, attended)
    gu_yc = net.swap(gu_y, core)
    gu_xc = net.swap(gu_x, core)
    b_zc = net.swap(b_z, core)
    gu_xyc = net.swap(gu_xy, core)
    gate_up = [gu2, gu_x, gu_y, gu_xy, gu_c, gu_xc, gu_yc, gu_xyc]

    weight = tokens_micro / token_counts.astype(F32)
    weight = jnp.repeat(weight, batch * length)[:, None]
    lead = (2, 2, 2, 2)
    block_out, gate_keep, gate_give, down_keep, down_give, middle_grad, attended_grad, gain_two = call(
        functools.partial(feed_forward_pieces, d_rows, ff_rows),
        [meta],
        [attended, source, b1, b_z, b_c, b_zc, *gate_up, gains, cotangent.reshape(rows, width), weight],
        [
            sds((seqs, width, length), BF),
            sds(lead + (d_rows, units // 2), BF),
            sds(lead + (d_rows, units // 2), BF),
            sds(lead + (ff_rows // 4 + d_rows // 3, width), BF),
            sds(lead + (ff_rows // 4 + d_rows // 3, width), BF),
            sds((rows, width), F32),
            sds((rows, QW), BF),
            sds((1, width), F32),
        ],
        1.4e10,
        [(units // 2, width), (n_fsdp, d_rows + d_rows // 3, width)],
        32,
    )
    block_out = block_out.reshape(micro, batch, width, length).swapaxes(2, 3)

    def add(keep, got):
        return (keep.astype(F32) + got.astype(F32)).astype(BF)

    def halves(keep, got):
        return add(keep[0], got[0]), add(keep[1], got[1])

    gate_got = net.swap(gate_give, core)
    down_got = net.swap(after(down_give, gate_got), core)
    gate, gate_give = halves(gate_keep, gate_got)
    gate_got = net.swap(gate_give, xbit)
    down, down_give = halves(down_keep, down_got)
    attended_grad = after(attended_grad, gate_give, down_give)
    down_got = net.swap(down_give, ybit)

    dq, dkv_keep, dkv_give, rest_keep, rest_give = call(
        functools.partial(attention_backward_pieces, order, length, d_rows),
        [meta],
        [*blocks, wf, gains, cos_t, sin_t, allowed, q_s, k_s, v_s, lse, attended_grad, gain_two],
        [
            sds((rows, QW + 64), BF),
            sds((2, rows, 2 * KW), BF),
            sds((2, rows, 2 * KW), BF),
            sds(lead + (d_rows + 8, 256), BF),
            sds(lead + (d_rows + 8, 256), BF),
        ],
        1.4e10,
        [(width, 1024), (1, qkv_w), (1, width), (n_fsdp, 8, 1024)],
        24,
    )
    gate, gate_give = halves(gate, after(gate_got, dq))
    gate_got = net.swap(gate_give, znear)
    down, down_give = halves(down, after(down_got, gate_give))
    dkv, dkv_give = halves(dkv_keep, after(net.swap(dkv_give, core), down_give))
    rest, rest_give = halves(rest_keep, after(net.swap(rest_give, core), down_give))
    dkv_got = net.swap(dkv_give, ybit)
    rest_got = net.swap(rest_give, ybit)
    down_got = net.swap(down_give, xbit)
    gate, gate_give = halves(gate, gate_got)
    gate_got = net.swap(gate_give, zfar)
    rest, rest_give = halves(rest, after(rest_got, gate_give))
    rest_got = net.swap(rest_give, xbit)
    (hidden_grad,) = call(
        input_gradient_two,
        [],
        [dq, dkv, after(dkv_got, rest_give), source, middle_grad, wf, gains],
        [sds((seqs, width, length), F32)],
        3e9,
        mib=16,
    )
    down, down_give = halves(down, after(down_got, hidden_grad))
    hidden_grad = hidden_grad.reshape(micro, batch, width, length).swapaxes(2, 3)
    down_got = net.swap(down_give, znear)
    gate = add(gate, gate_got)
    gate_got = net.swap(gate, ybit)
    rest, rest_give = halves(rest, after(rest_got, gate))
    rest_got = net.swap(rest_give, znear)
    down, down_give = halves(down, after(down_got, rest_give))
    down_got = net.swap(down_give, zfar)
    gate = add(gate, gate_got)
    rest, rest_give = halves(rest, rest_got)
    rest_got = net.swap(rest_give, zfar)
    down = add(down, after(down_got, rest_give))
    rest = add(rest, rest_got)

    def spread(part):
        other = net.swap(part, ybit)
        return [part, other, net.swap(part, core), net.swap(other, core)]

    gate = [gate, net.swap(gate, core)]
    qk, v = (QW + KW) // n_fsdp, KW // n_fsdp
    out_gate, out_down, out_wout, out_qkv, b_qk, b_v, out_gains = call(
        functools.partial(place_all, ff_rows // 4, qk, v),
        [meta],
        [*gate, *spread(down), *spread(rest)],
        [
            sds((d_rows, 2 * units), F32),
            sds((ff_rows, width), F32),
            sds((d_rows, width), F32),
            sds((d_rows, qkv_w), F32),
            sds((1, qk), F32),
            sds((1, v), F32),
            sds((2, d_rows), F32),
        ],
        3e9,
        [(d_rows + 8, 1024)],
        16,
    )
    return (
        block_out,
        hidden_grad,
        out_qkv,
        b_qk.reshape(qk),
        b_v.reshape(v),
        out_wout,
        out_gate,
        out_down,
        out_gains,
    )


def solution(mesh):
    n_fsdp, n_seq = mesh.shape["fsdp"], mesh.shape["seq"]
    in_specs = (
        P(None, "fsdp", "seq", None),
        P("fsdp", None),
        P("fsdp"),
        P("fsdp", None),
        P("fsdp", None),
        P("fsdp", None),
        P(None, "fsdp"),
        P(None, "fsdp", "seq"),
        P(),
        P(None, "fsdp", "seq", None),
    )
    out_specs = (
        P(None, "fsdp", "seq", None),
        P(None, "fsdp", "seq", None),
        P("fsdp", None),
        P("fsdp"),
        P("fsdp"),
        P("fsdp", None),
        P("fsdp", None),
        P("fsdp", None),
        P(None, "fsdp"),
    )

    def local(*args):
        body = on_device_tiled if (n_fsdp, n_seq) == (8, 4) else on_device
        return body(*args, n_fsdp=n_fsdp, n_seq=n_seq)

    return jax.shard_map(local, mesh=mesh, in_specs=in_specs, out_specs=out_specs, check_vma=False)
```

```python
import functools

import jax
import jax.numpy as jnp
import numpy as np
from jax import lax
from jax.experimental import pallas as pl
from jax.experimental.pallas import tpu as pltpu
from jax.sharding import PartitionSpec as P

HEADS = 9
KV_HEADS = 3
HEAD_DIM = 64
GROUP = HEADS // KV_HEADS
QW = HEADS * HEAD_DIM
KW = KV_HEADS * HEAD_DIM
EPS = 1e-05
ROPE_BASE = 100000.0
MASKED = -1000000000.0
BF = jnp.bfloat16
F32 = jnp.float32


def dot(a, b, ca, cb):
    return lax.dot_general(a, b, (((ca,), (cb,)), ((), ())), preferred_element_type=F32)


def rotary(values, cosine, sine):
    half = values.shape[-1] // 2
    a, b = values[..., :half], values[..., half:]
    return jnp.concatenate([a * cosine - b * sine, b * cosine + a * sine], axis=-1)


def norm_parts(values):
    factor = lax.rsqrt(jnp.mean(values * values, axis=-1, keepdims=True) + EPS)
    return factor, values * factor


def norm_back(grad_in, gain, factor, normed):
    scaled = grad_in * gain
    return factor * (scaled - normed * jnp.mean(scaled * normed, axis=-1, keepdims=True))


def whole(*shape_dtypes):
    return [pl.BlockSpec(memory_space=pltpu.VMEM) for _ in shape_dtypes]


def call(kernel, scalars, arrays, outs, flops, scratch=(), mib=52, fetched=()):
    specs = [pl.BlockSpec(memory_space=pltpu.SMEM)] * len(scalars) + whole(*arrays)
    specs += [pl.BlockSpec(memory_space=pl.ANY)] * len(fetched)
    arrays = [*arrays, *fetched]
    moved = sum(a.size * a.dtype.itemsize for a in arrays) + sum(
        int(np.prod(o.shape)) * o.dtype.itemsize for o in outs
    )
    return pl.pallas_call(
        kernel,
        out_shape=outs,
        in_specs=specs,
        out_specs=whole(*outs),
        scratch_shapes=[
            *[pltpu.VMEM(shape, F32) for shape in scratch],
            *[pltpu.VMEM(v.shape, v.dtype) for v in fetched],
            *([pltpu.SemaphoreType.DMA((len(fetched),))] if fetched else []),
        ],
        compiler_params=pltpu.CompilerParams(vmem_limit_bytes=mib * 1024 * 1024),
        cost_estimate=pl.CostEstimate(flops=int(flops), bytes_accessed=moved, transcendentals=0),
    )(*scalars, *arrays)


def sds(shape, dtype):
    return jax.ShapeDtypeStruct(shape, dtype)


def turn(x, cosine, sine):
    tiles = []
    low = lax.broadcasted_iota(jnp.int32, (1, 128), 1) % HEAD_DIM < HEAD_DIM // 2
    for t in range(x.shape[1] // 128):
        part = x[:, 128 * t : 128 * t + 128]
        other = jnp.where(low, pltpu.roll(part, 96, 1), pltpu.roll(part, 32, 1))
        tiles.append(part * cosine + other * sine)
    return tiles


def turn_kv(x, cosine, sine):
    lane = lax.broadcasted_iota(jnp.int32, (1, 128), 1)
    first, second = turn(x[:, :256], cosine, sine)
    second = jnp.where(lane < KW - 128, second, x[:, 128:256])
    return jnp.concatenate([first, second, x[:, 256:]], axis=1)


def tables(seq, order, cos_ref, sin_ref):
    cosine = jnp.concatenate([cos_ref[seq ^ o] for o in order], axis=0)
    sine = jnp.concatenate([sin_ref[seq ^ o] for o in order], axis=0)
    return cosine, sine


def heads_to_rows(x, g):
    return jnp.concatenate(
        [x[:, HEAD_DIM * h : HEAD_DIM * (h + 1)] for h in range(GROUP * g, GROUP * (g + 1))], axis=0
    )


def rows_to_heads(parts, length):
    return jnp.concatenate(
        [p[length * r : length * (r + 1)] for p in parts for r in range(GROUP)], axis=1
    )


def attention_forward(order, length, seq_ref, blocks, wq, wkv, bq, bkv, gain, cos, sin, mask,
                      att_o, q_o, k_o, v_o, lse_o):
    seq = seq_ref[0]
    cosine, sine = tables(seq, order, cos, sin)
    width = gain.shape[1]
    for b in range(blocks.shape[1] // length):
        x = blocks[:, b * length : (b + 1) * length, :width].astype(F32)
        x = x.reshape(len(order) * length, width)
        first = (norm_parts(x)[1] * gain[...]).astype(BF)
        kv = dot(first, wkv[...], 1, 0) + bkv[...]
        q = dot(first[:length], wq[...], 1, 0) + bq[...]
        q = jnp.concatenate(turn(q, cosine[:length], sine[:length]), axis=1).astype(BF)
        q = q * jnp.asarray(HEAD_DIM ** (-0.5), BF)
        kv = turn_kv(kv, cosine, sine).astype(BF)
        allowed = jnp.concatenate([mask[b]] * GROUP, axis=0) > 0.0
        parts = []
        for g in range(KV_HEADS):
            qg = heads_to_rows(q, g)
            kg = kv[:, HEAD_DIM * g : HEAD_DIM * (g + 1)]
            vg = kv[:, KW + HEAD_DIM * g : KW + HEAD_DIM * (g + 1)]
            q_o[b, g] = qg
            k_o[b, g] = kg
            v_o[b, g] = vg
            scores = jnp.where(allowed, dot(qg, kg, 1, 1), MASKED)
            top = jnp.max(scores, axis=-1, keepdims=True)
            e = jnp.exp(scores - top)
            total = jnp.sum(e, axis=-1, keepdims=True)
            lse_o[b, g] = jnp.log(total) + top
            probs = (e * (1.0 / total)).astype(BF)
            parts.append(dot(probs, vg, 1, 0))
        att_o[b * length : (b + 1) * length, :] = rows_to_heads(parts, length).astype(BF)


def feed_forward(attended, source, wo, wgu, wd, gain, cot, weight,
                 out_o, down_o, gu_o, mid_o, wout_o, attg_o, gain_o):
    units = wd.shape[0]
    step = units // 3
    att = attended[...]
    middle = source[...].astype(F32) + dot(att, wo[...], 1, 0)
    scale_two, normed = norm_parts(middle)
    g2 = gain[...]
    second = (normed * g2).astype(BF)
    out_grad = cot[...].astype(F32) * weight[...]
    feed_grad = out_grad.astype(BF)
    feed = None
    back = None
    for j in range(0, units, step):
        wg = wgu[:, j : j + step]
        wu = wgu[:, units + j : units + j + step]
        wdj = wd[j : j + step, :]
        gate = dot(second, wg, 1, 0)
        up = dot(second, wu, 1, 0)
        sig = jax.nn.sigmoid(gate)
        act = gate * sig
        product = (act * up).astype(BF)
        part = dot(product, wdj, 1, 0)
        feed = part if feed is None else feed + part
        down_o[j : j + step, :] = dot(product, feed_grad, 0, 0).astype(BF)
        pgrad = dot(feed_grad, wdj, 1, 1)
        ggrad = (pgrad * up * (sig * (1.0 + gate * (1.0 - sig)))).astype(BF)
        ugrad = (pgrad * act).astype(BF)
        gu_o[:, j : j + step] = dot(second, ggrad, 0, 0).astype(BF)
        gu_o[:, units + j : units + j + step] = dot(second, ugrad, 0, 0).astype(BF)
        part = dot(ggrad, wg, 1, 1) + dot(ugrad, wu, 1, 1)
        back = part if back is None else back + part
    out_o[...] = (middle + feed).astype(BF)
    gain_o[...] = jnp.sum(back * normed, axis=0, keepdims=True)
    middle_grad = out_grad + norm_back(back, g2, scale_two, normed)
    mid_o[...] = middle_grad
    branch = middle_grad.astype(BF)
    wout_o[...] = dot(att, branch, 0, 0).astype(BF)
    attg_o[...] = dot(branch, wo[...], 1, 1).astype(BF)


def attention_backward(order, length, seq_ref, blocks, wq, wkv, gain, cos, sin, mask, q_i, k_i, v_i,
                       lse, attg, dq_o, dkv_o, wgrad_o, bias_o, gain_o):
    seq = seq_ref[0]
    cosine, sine = tables(seq, order, cos, sin)
    width = gain.shape[1]
    q_wgrad = kv_wgrad = bias_q = bias_kv = gain_sum = None
    for b in range(blocks.shape[1] // length):
        x = blocks[:, b * length : (b + 1) * length, :width].astype(F32)
        x = x.reshape(len(order) * length, width)
        normed = norm_parts(x)[1]
        first = (normed * gain[...]).astype(BF)
        allowed = jnp.concatenate([mask[b]] * GROUP, axis=0) > 0.0
        ag = attg[b * length : (b + 1) * length, :]
        dqs, dks, dvs = [], [], []
        for g in range(KV_HEADS):
            qg, kg, vg = q_i[b, g], k_i[b, g], v_i[b, g]
            agg = heads_to_rows(ag, g)
            p = jnp.exp(jnp.where(allowed, dot(qg, kg, 1, 1), MASKED) - lse[b, g])
            dvs.append(dot(p.astype(BF), agg, 0, 0))
            pg = dot(agg, vg, 1, 1)
            inner = jnp.sum(p * pg, axis=-1, keepdims=True)
            ds = (p * (pg - inner)).astype(BF)
            dqs.append(dot(ds, kg, 1, 0) * HEAD_DIM ** (-0.5))
            dks.append(dot(ds, qg, 0, 0))
        dq = rows_to_heads(dqs, length)
        dq = jnp.concatenate([dq, jnp.zeros((length, 64), F32)], axis=1)
        dq = jnp.concatenate(turn(dq, cosine[:length], -sine[:length]), axis=1).astype(BF)
        dkv = jnp.concatenate(dks + dvs, axis=1)
        dkv = turn_kv(dkv, cosine, -sine).astype(BF)
        dq_o[b * length : (b + 1) * length, :] = dq
        for r in range(len(order)):
            dkv_o[r, b * length : (b + 1) * length, :] = dkv[r * length : (r + 1) * length, :]
        wq_part = dot(first[:length], dq, 0, 0)
        wkv_part = dot(first, dkv, 0, 0)
        bq_part = jnp.sum(dq.astype(F32), axis=0, keepdims=True)
        bkv_part = jnp.sum(dkv.astype(F32), axis=0, keepdims=True)
        e_kv = dot(dkv, wkv[...], 1, 1) * normed
        e_q = dot(dq[:, :QW], wq[:, :QW], 1, 1) * normed[:length]
        g_part = jnp.sum(e_kv, axis=0, keepdims=True) + jnp.sum(e_q, axis=0, keepdims=True)
        if q_wgrad is None:
            q_wgrad, kv_wgrad, bias_q, bias_kv, gain_sum = wq_part, wkv_part, bq_part, bkv_part, g_part
        else:
            q_wgrad, kv_wgrad = q_wgrad + wq_part, kv_wgrad + wkv_part
            bias_q, bias_kv, gain_sum = bias_q + bq_part, bias_kv + bkv_part, gain_sum + g_part
    wgrad_o[...] = jnp.concatenate([q_wgrad[:, :QW], kv_wgrad], axis=1).astype(BF)
    bias_o[...] = jnp.concatenate([bias_q[:, :QW], bias_kv], axis=1)
    gain_o[...] = gain_sum


def input_gradient(dq, own, a, b, c, source, mid, wq, wkv, gain, out_o):
    kv = own[...].astype(F32) + a[...].astype(F32) + b[...].astype(F32) + c[...].astype(F32)
    first_grad = dot(dq[:, :QW], wq[:, :QW], 1, 1) + dot(kv.astype(BF), wkv[...], 1, 1)
    scale_one, normed = norm_parts(source[...].astype(F32))
    out_o[...] = mid[...] + norm_back(first_grad, gain[...], scale_one, normed)

def chosen(flag, a, b):
    return jnp.where(flag != 0, b, a)


class Blocks:
    def __init__(self, *refs):
        self.refs = refs
        self.shape = (len(refs),) + refs[0].shape

    def __getitem__(self, key):
        return jnp.stack([ref[key[1:]] for ref in self.refs])


def cut_qkv(core_bit, meta, w_hbm, bias_hbm, gains_hbm, out_o, w, bias, gains, all_s, sems):
    pairs = ((w_hbm, w), (bias_hbm, bias), (gains_hbm, gains))
    copies = [pltpu.make_async_copy(a, b, sems.at[i]) for i, (a, b) in enumerate(pairs)]
    for copy in copies:
        copy.start()
    for copy in copies:
        copy.wait()
    rows = w.shape[0]
    n = bias.shape[1]
    all_s[:rows, :] = w[...].astype(F32)
    all_s[rows:, :] = jnp.zeros((8, w.shape[1]), F32)
    all_s[rows : rows + 1, :n] = bias[...].astype(F32)
    for i in range(2):
        all_s[rows : rows + 1, n + rows * i : n + rows * (i + 1)] = gains[i : i + 1, :].astype(F32)
    half = out_o.shape[0]
    at = pl.multiple_of((meta[0] & core_bit) * half, 8)
    out_o[...] = all_s[pl.ds(at, half), :].astype(BF)


def first_forward(order, length, d_rows, n_bias, meta, b0, b1, b2, b3, a00, a10, a01, a11, cos, sin, mask,
                  att_o, q_o, k_o, v_o, lse_o, w_o, gain_o, w_s, b_s):
    blocks = Blocks(b0, b1, b2, b3)
    core, x = meta[0] & 1, meta[1] & 1
    cut = a00.shape[2]
    for x_rel, c_rel, piece in ((0, 0, a00), (1, 0, a10), (0, 1, a01), (1, 1, a11)):
        for z0 in range(2):
            for z1 in range(2):
                at = (z1 * 4 + z0 * 2 + (x ^ x_rel)) * 2 * cut + (core ^ c_rel) * cut
                w_s[pl.ds(pl.multiple_of(at, 8), cut), :] = piece[z0, z1].astype(F32)
    n_f = w_s.shape[0] // (2 * cut)
    starts = [2 * cut * f for f in range(n_f)]
    w_o[...] = jnp.concatenate([w_s[at : at + d_rows, :] for at in starts], axis=0).astype(BF)
    lines = [w_s[at + d_rows : at + d_rows + 1, :] for at in starts]
    b_s[...] = jnp.concatenate([line[:, :n_bias] for line in lines], axis=1)
    for i in range(2):
        at = n_bias + d_rows * i
        gain_o[i : i + 1, :] = jnp.concatenate([line[:, at : at + d_rows] for line in lines], axis=1)
    wide = QW + 64
    attention_forward(order, length, meta, blocks, w_o[:, :wide], w_o[:, QW:], b_s[:, :wide], b_s[:, QW:],
                      gain_o[0:1, :], cos, sin, mask, att_o, q_o, k_o, v_o, lse_o)


def turned(out, value):
    length = out.shape[2]
    for b in range(out.shape[0]):
        out[b] = value[length * b : length * (b + 1)].T.astype(out.dtype)


def rel(meta, f):
    r = f ^ meta[1]
    return r & 1, (r >> 1) & 1, (r >> 2) & 1


def feed_forward_pieces(d_rows, ff_rows, meta, attended, source, gains, cot, weight, *refs):
    out_o, gk_o, gg_o, dk_o, dg_o, mid_o, attg_o, gain_o, down_s, wout_s = refs[12:22]
    copies = [pltpu.make_async_copy(refs[i], refs[22 + i], refs[34].at[i]) for i in range(12)]
    for copy in copies:
        copy.start()
    b00, b10, b01, b11, g001, g101, g011, g111, g000, g100, g010, g110 = refs[22:34]
    core, y, x_own = meta[0] & 1, (meta[0] >> 1) & 1, meta[1] & 1
    n_f = 8
    hf = n_f // 2
    part_d = ff_rows // 4
    part_o = d_rows // 3
    cut = b00.shape[2] - ff_rows // 2
    for copy in copies[:4]:
        copy.wait()

    def b_rows(z0, z1, x, c, rows):
        low = chosen(x_own ^ x, b00[z0, z1, rows, :], b10[z0, z1, rows, :])
        high = chosen(x_own ^ x, b01[z0, z1, rows, :], b11[z0, z1, rows, :])
        return chosen(core ^ c, low, high)

    def quarter(near, far):
        parts = []
        for f in range(n_f):
            z1, z0, x = f >> 2, (f >> 1) & 1, f & 1
            mine, other = near[z0, z1].astype(F32), far[z0, z1].astype(F32)
            parts.append(chosen(x_own ^ x, mine, other))
        return jnp.concatenate(parts, axis=0).astype(BF)

    wo = []
    for f in range(n_f):
        z1, z0, x = f >> 2, (f >> 1) & 1, f & 1
        wo.append(b_rows(z0, z1, x, 0, slice(ff_rows // 2, None)).astype(F32))
        wo.append(b_rows(z0, z1, x, 1, slice(ff_rows // 2, None)).astype(F32)[: d_rows - cut])
    wo = jnp.concatenate(wo, axis=0).astype(BF)
    att = attended[...]
    middle = source[...].astype(F32) + dot(att, wo, 1, 0)
    scale_two, normed = norm_parts(middle)
    g2 = gains[1:2, :]
    second = (normed * g2).astype(BF)
    out_grad = cot[...].astype(F32) * weight[...]
    feed_grad = out_grad.astype(BF)
    feed = back = None
    for c_rel in (1, 0):
        for copy in copies[8 - 4 * c_rel : 12 - 4 * c_rel]:
            copy.wait()
        first_q = quarter(g001, g101) if c_rel else quarter(g000, g100)
        second_q = quarter(g011, g111) if c_rel else quarter(g010, g110)
        wg = chosen(y, first_q, second_q)
        wu = chosen(y, second_q, first_q)
        h = core ^ c_rel
        wd = []
        for i in range(hf):
            for c in range(2):
                wd.append(b_rows(i >> 1, h, i & 1, c, slice(0, ff_rows // 2)))
        wd = jnp.concatenate(wd, axis=0)
        gate = dot(second, wg, 1, 0)
        up = dot(second, wu, 1, 0)
        sig = jax.nn.sigmoid(gate)
        act = gate * sig
        product = (act * up).astype(BF)
        part = dot(product, wd, 1, 0)
        feed = part if feed is None else feed + part
        down_s[...] = dot(product, feed_grad, 0, 0)
        pgrad = dot(feed_grad, wd, 1, 1)
        ggrad = (pgrad * up * (sig * (1.0 + gate * (1.0 - sig)))).astype(BF)
        ugrad = (pgrad * act).astype(BF)
        part = dot(ggrad, wg, 1, 1) + dot(ugrad, wu, 1, 1)
        back = part if back is None else back + part
        for i in range(hf):
            x, z0, z1 = rel(meta, hf * h + i)
            for yy in range(2):
                for c_to, to in ((0, dk_o), (1, dg_o)):
                    at = pl.multiple_of(i * ff_rows + (yy * 2 + (core ^ c_to)) * part_d, 16)
                    to[y ^ yy, x, z0, z1, :part_d, :] = down_s[pl.ds(at, part_d), :].astype(BF)
        to = gg_o if c_rel else gk_o
        for yy, grad in ((0, ggrad), (1, ugrad)):
            wgrad = dot(second, grad, 0, 0)
            for f in range(n_f):
                x, z0, z1 = rel(meta, f)
                to[x, z0, z1, yy] = wgrad[d_rows * f : d_rows * (f + 1), :].astype(BF)
    turned(out_o, middle + feed)
    gain_o[...] = jnp.sum(back * normed, axis=0, keepdims=True)
    middle_grad = out_grad + norm_back(back, g2, scale_two, normed)
    mid_o[...] = middle_grad
    branch = middle_grad.astype(BF)
    attg_o[...] = dot(branch, wo, 1, 1).astype(BF)
    wout = dot(att, branch, 0, 0)
    for f in range(n_f):
        wout_s[f, :d_rows, :] = wout[d_rows * f : d_rows * (f + 1), :]
        wout_s[f, d_rows:, :] = jnp.zeros((part_o, wout.shape[1]), F32)
    for f in range(n_f):
        x, z0, z1 = rel(meta, f)
        for yy in range(2):
            for c_to, to in ((0, dk_o), (1, dg_o)):
                at = pl.multiple_of((yy * 2 + (core ^ c_to)) * part_o, 8)
                to[y ^ yy, x, z0, z1, part_d:, :] = wout_s[f, pl.ds(at, part_o), :].astype(BF)


def attention_backward_pieces(order, length, d_rows, meta, b0, b1, b2, b3, w, gains, cos, sin, mask, q_i, k_i, v_i,
                              lse, attg, gain_two, dq_o, dk_o, dg_o, rk_o, rg_o, w_s, bias_s, gain_s, small_s):
    blocks = Blocks(b0, b1, b2, b3)
    half = len(order) // 2

    class Pieces:
        def __setitem__(self, key, value):
            ref = dk_o if key[0] < half else dg_o
            ref[(key[0] % half,) + key[1:]] = value

    class Wgrad:
        def __setitem__(self, key, value):
            w_s[:, : 2 * KW] = value[:, QW:].astype(F32)
            w_s[:, 2 * KW : 2 * KW + QW] = value[:, :QW].astype(F32)
            w_s[:, 2 * KW + QW :] = jnp.zeros((value.shape[0], 64), F32)

    wide = QW + 64
    attention_backward(order, length, meta, blocks, w[:, :wide], w[:, QW:], gains[0:1, :], cos, sin, mask,
                       q_i, k_i, v_i, lse, attg, dq_o, Pieces(), Wgrad(), bias_s, gain_s)
    n_f = small_s.shape[0]
    qk, v = (QW + KW) // n_f, KW // n_f
    bias, g1, g2 = bias_s[...], gain_s[...], gain_two[...]
    for f in range(n_f):
        line = jnp.concatenate(
            [
                bias[:, qk * f : qk * (f + 1)],
                bias[:, QW + KW + v * f : QW + KW + v * (f + 1)],
                g1[:, d_rows * f : d_rows * (f + 1)],
                jnp.zeros((1, 256 - qk - v - d_rows), F32),
                g2[:, d_rows * f : d_rows * (f + 1)],
                jnp.zeros((1, 768 - d_rows), F32),
            ],
            axis=1,
        )
        small_s[f] = jnp.broadcast_to(line, (8, 1024))
    core, y = meta[0] & 1, (meta[0] >> 1) & 1
    for f in range(n_f):
        x, z0, z1 = rel(meta, f)
        for yy in range(2):
            for c_to, to in ((0, rk_o), (1, rg_o)):
                at = pl.multiple_of((yy * 2 + (core ^ c_to)) * 256, 256)
                block = [w_s[d_rows * f : d_rows * (f + 1), pl.ds(at, 256)], small_s[f, :, pl.ds(at, 256)]]
                to[x, z0, z1, yy] = jnp.concatenate(block, axis=0).astype(BF)


def input_gradient_two(dq, own, other, source, mid, w, gains, out_o):
    kv = (own[...].astype(F32) + other[...].astype(F32)).astype(BF)
    first_grad = dot(dq[:, :QW], w[:, :QW], 1, 1) + dot(kv, w[:, QW:], 1, 1)
    scale_one, normed = norm_parts(source[...].astype(F32))
    turned(out_o, mid[...] + norm_back(first_grad, gains[0:1, :], scale_one, normed))


def place_gate(meta, near, far, out_o):
    core = meta[0] & 1
    n = near.shape[2]
    for pieces, c_rel in ((near, 0), (far, 1)):
        for yy in range(2):
            at = pl.multiple_of((yy * 2 + (core ^ c_rel)) * n, 128)
            out_o[:, pl.ds(at, n)] = pieces[yy].astype(F32)


def place_down(part_d, meta, p00, p10, p01, p11, out_o, wout_o):
    seq = meta[0]
    part_o = p00.shape[0] - part_d
    for piece, o in ((p00[...], 0), (p10[...], 2), (p01[...], 1), (p11[...], 3)):
        piece = piece.astype(F32)
        to = seq ^ o
        out_o[pl.ds(pl.multiple_of(to * part_d, 16), part_d), :] = piece[:part_d]

        @pl.when(to < 3)
        def _():
            wout_o[pl.ds(pl.multiple_of(to * part_o, 8), part_o), :] = piece[part_d:]


def place_qkv(qk, v, meta, near, far, w_o, bqk_o, bv_o, gains_o, all_s):
    place_gate(meta, near, far, all_s)
    d_rows = w_o.shape[0]
    w_o[:, :QW] = all_s[:d_rows, 2 * KW : 2 * KW + QW]
    w_o[:, QW:] = all_s[:d_rows, : 2 * KW]
    line = all_s[d_rows : d_rows + 1, :]
    bqk_o[...] = line[:, :qk]
    bv_o[...] = line[:, qk : qk + v]
    gains_o[0:1, :] = line[:, qk + v : qk + v + d_rows]
    gains_o[1:2, :] = line[:, 256 : 256 + d_rows]


def place_all(part_d, qk, v, meta, near, far, d0, d1, d2, d3, r_near, r_far,
              gate_o, down_o, wout_o, w_o, bqk_o, bv_o, gains_o, all_s):
    place_gate(meta, near, far, gate_o)
    place_down(part_d, meta, d0, d1, d2, d3, down_o, wout_o)
    place_qkv(qk, v, meta, r_near, r_far, w_o, bqk_o, bv_o, gains_o, all_s)


class Net:
    def __init__(self, n_fsdp, n_seq):
        self.n_fsdp, self.n_seq = n_fsdp, n_seq
        self.total = n_fsdp * n_seq
        f, s = lax.axis_index("fsdp"), lax.axis_index("seq")
        self.index = f * n_seq + s
        self.seq_bits = [1 << b for b in range(n_seq.bit_length() - 1)]
        self.fsdp_bits = [n_seq << b for b in range(n_fsdp.bit_length() - 1)]

    def swap(self, value, mask):
        pairs = [(i, i ^ mask) for i in range(self.total)]
        return lax.ppermute(value, ("fsdp", "seq"), pairs)

    def bit(self, mask):
        return (self.index & mask) != 0

    def both(self, mine, mask, axis, other=None):
        other = self.swap(mine, mask) if other is None else other
        high = self.bit(mask)
        return jnp.stack([jnp.where(high, other, mine), jnp.where(high, mine, other)], axis=axis)

    def half(self, value, mask, axis):
        return lax.dynamic_index_in_dim(
            value, self.bit(mask).astype(jnp.int32), axis, keepdims=False
        )

    def add_half(self, value, mask, axis):
        mine = self.bit(mask).astype(jnp.int32)
        keep = lax.dynamic_index_in_dim(value, mine, axis, keepdims=False)
        give = lax.dynamic_index_in_dim(value, 1 - mine, axis, keepdims=False)
        got = self.swap(give, mask)
        return (keep.astype(F32) + got.astype(F32)).astype(value.dtype)

    def gather_fsdp(self, value):
        for step, mask in enumerate(reversed(self.fsdp_bits)):
            value = self.both(value, mask, step)
        return value

    def scatter_fsdp(self, value, first_axis=0):
        count = len(self.fsdp_bits)
        for step, mask in enumerate(self.fsdp_bits):
            value = self.add_half(value, mask, first_axis + count - 1 - step)
        return value


def on_device(
    hidden, w_qkv, b_qkv, w_out, w_gate_up, w_down, norm_gains, segment_ids, token_counts, cotangent,
    n_fsdp, n_seq,
):
    net = Net(n_fsdp, n_seq)
    micro, batch, length, width = hidden.shape
    full_length = length * n_seq
    tokens_micro = batch * n_fsdp * full_length
    scale = HEAD_DIM ** (-0.5)
    rows = micro * batch * length
    d_rows = w_qkv.shape[0]
    ff_rows = w_down.shape[0]
    units = w_gate_up.shape[1] // 2
    qkv_w = w_qkv.shape[1]
    core = net.seq_bits[0]
    f_lead = (2,) * len(net.fsdp_bits)

    ids = segment_ids.reshape(rows, 1).astype(BF)
    block = jnp.concatenate(
        [hidden.reshape(rows, width), jnp.broadcast_to(ids, (rows, 64))], axis=1
    )
    blocks = block[None]
    for mask in reversed(net.seq_bits):
        blocks = jnp.concatenate([blocks, net.swap(blocks, mask)], axis=0)
    order = [0]
    for mask in reversed(net.seq_bits):
        order = order + [o ^ mask for o in order]
    seq_index = lax.axis_index("seq")
    block_ids = [seq_index ^ o for o in order]

    pad_rows = -(d_rows + 1) % 16 + 1
    extra = jnp.zeros((pad_rows, qkv_w), BF)
    small = jnp.concatenate([b_qkv, norm_gains.reshape(-1)])
    extra = extra.at[0, : small.shape[0]].set(small)
    shard_a = jnp.concatenate([w_qkv, extra], axis=0).reshape(2, -1, qkv_w)
    got_a = net.gather_fsdp(net.half(shard_a, core, 0))
    full_a = net.both(got_a, core, len(f_lead)).reshape(n_fsdp, d_rows + pad_rows, qkv_w)
    wf_qkv = full_a[:, :d_rows].reshape(n_fsdp * d_rows, qkv_w)
    smalls = full_a[:, d_rows]
    n_bias = b_qkv.shape[0]
    bias = smalls[:, :n_bias].reshape(-1).astype(F32)
    gains = smalls[:, n_bias : n_bias + 2 * d_rows].reshape(n_fsdp, 2, d_rows).astype(F32)
    gain_one = gains[:, 0].reshape(-1)
    gain_two = gains[:, 1].reshape(-1)

    pad_b = -(d_rows + ff_rows) % 16
    shard_b = jnp.concatenate([w_out, w_down, jnp.zeros((pad_b, width), BF)], axis=0)
    shard_b = shard_b.reshape(2, -1, width)
    got_b = net.gather_fsdp(net.half(shard_b, core, 0))

    parts = n_seq
    shard_c = w_gate_up.reshape(d_rows, parts, -1)
    got_c = net.gather_fsdp(lax.dynamic_index_in_dim(shard_c, seq_index, 1, keepdims=False))
    full_b = net.both(got_b, core, len(f_lead)).reshape(n_fsdp, -1, width)
    wf_out = full_b[:, :d_rows].reshape(n_fsdp * d_rows, width)
    wf_down = full_b[:, d_rows : d_rows + ff_rows].reshape(n_fsdp * ff_rows, width)
    got_c = got_c.reshape(n_fsdp * d_rows, -1)
    for mask in reversed(net.seq_bits):
        got_c = net.both(got_c, mask, got_c.ndim - 1)
    wf_gate_up = got_c.reshape(n_fsdp * d_rows, 2 * units)

    places = np.arange(full_length, dtype=np.float32)
    speeds = np.power(ROPE_BASE, -2.0 * np.arange(HEAD_DIM // 2, dtype=np.float32) / HEAD_DIM)
    angles = places[:, None] * speeds.astype(np.float32)[None, :]
    cos_t = np.tile(np.cos(angles), (1, 4)).reshape(n_seq, length, 128)
    sin_t = np.concatenate([-np.sin(angles), np.sin(angles)] * 2, axis=1).reshape(n_seq, length, 128)
    cos_t, sin_t = jnp.asarray(cos_t, F32), jnp.asarray(sin_t, F32)
    seqs = micro * batch
    seg_all = blocks[..., width].reshape(n_seq, seqs, length).transpose(1, 0, 2)
    own_places = seq_index * length + jnp.arange(length, dtype=jnp.int32)
    key_places = jnp.stack(block_ids)[:, None] * length + jnp.arange(length, dtype=jnp.int32)
    allowed = (seg_all[:, 0, :, None] == seg_all.reshape(seqs, 1, -1)) & (
        own_places[None, :, None] >= key_places.reshape(1, 1, -1)
    )
    allowed = allowed.astype(F32)
    seq_scalar = seq_index.astype(jnp.int32).reshape(1)
    wq, wkv = wf_qkv[:, : QW + 64], wf_qkv[:, QW:]
    gain_one, gain_two = gain_one[None], gain_two[None]
    source = hidden.reshape(rows, width)
    n_all = n_seq * rows
    attended, q_s, k_s, v_s, lse = call(
        functools.partial(attention_forward, order, length),
        [seq_scalar],
        [blocks, wq, wkv, bias[None, : QW + 64], bias[None, QW:], gain_one, cos_t, sin_t, allowed],
        [
            sds((rows, QW), BF),
            sds((seqs, KV_HEADS, GROUP * length, HEAD_DIM), BF),
            sds((seqs, KV_HEADS, full_length, HEAD_DIM), BF),
            sds((seqs, KV_HEADS, full_length, HEAD_DIM), BF),
            sds((seqs, KV_HEADS, GROUP * length, 1), F32),
        ],
        2 * n_all * width * 2 * KW + 2 * rows * width * QW + 4 * rows * full_length * QW,
    )

    weight = tokens_micro / token_counts.astype(F32)
    weight = jnp.repeat(weight, batch * length)[:, None]
    block_out, down_grad, gate_up_wgrad, middle_grad, out_wgrad, attended_grad, gain_two_grad = call(
        feed_forward,
        [],
        [attended, source, wf_out, wf_gate_up, wf_down, gain_two, cotangent.reshape(rows, width), weight],
        [
            sds((rows, width), BF),
            sds((units, width), BF),
            sds((width, 2 * units), BF),
            sds((rows, width), F32),
            sds((QW, width), BF),
            sds((rows, QW), BF),
            sds((1, width), F32),
        ],
        6 * rows * width * 3 * units + 6 * rows * width * QW,
    )
    block_out = block_out.reshape(hidden.shape)

    def seq_axes(value, axis, masks):
        for mask in masks:
            value = net.add_half(value, mask, axis)
        return value

    quarter = (2,) * len(net.seq_bits)
    n_f = len(f_lead)
    red_down = down_grad.reshape(f_lead + quarter + (ff_rows // n_seq, width))
    for step, mask in enumerate(net.seq_bits):
        red_down = net.add_half(red_down, mask, n_f + len(quarter) - 1 - step)
    red_down = net.scatter_fsdp(red_down)

    red_gate = gate_up_wgrad.reshape(f_lead + (d_rows,) + quarter + (2 * units // n_seq,))
    red_gate = net.add_half(red_gate, core, n_f + len(quarter))
    red_gate = net.add_half(red_gate, net.fsdp_bits[0], n_f - 1)
    for step, mask in enumerate(net.seq_bits[1:]):
        red_gate = net.add_half(red_gate, mask, n_f - 1 + len(quarter) - 1 - step)
    for step, mask in enumerate(net.fsdp_bits[1:]):
        red_gate = net.add_half(red_gate, mask, n_f - 2 - step)

    dq, dkv, qkv_wgrad, bias_grad, gain_one_grad = call(
        functools.partial(attention_backward, order, length),
        [seq_scalar],
        [blocks, wq, wkv, gain_one, cos_t, sin_t, allowed, q_s, k_s, v_s, lse, attended_grad],
        [
            sds((rows, QW + 64), BF),
            sds((n_seq, rows, 2 * KW), BF),
            sds((width, qkv_w), BF),
            sds((1, qkv_w), F32),
            sds((1, width), F32),
        ],
        4 * n_all * width * 2 * KW + 4 * rows * width * QW + 10 * rows * full_length * QW,
    )
    kv_parts = [dkv[0]]
    for place, mask_bits in enumerate(order):
        if mask_bits:
            kv_parts.append(net.swap(dkv[place], mask_bits))
    (hidden_grad,) = call(
        input_gradient,
        [],
        [dq, *kv_parts, source, middle_grad, wq, wkv, gain_one],
        [sds((rows, width), F32)],
        2 * rows * width * qkv_w,
    )
    hidden_grad = hidden_grad.reshape(hidden.shape)
    bias_grad, gain_one_grad, gain_two_grad = bias_grad[0], gain_one_grad[0], gain_two_grad[0]

    qk_rows, v_rows = (QW + KW) // n_fsdp, KW // n_fsdp
    small_grads = jnp.concatenate(
        [
            bias_grad[: QW + KW].reshape(n_fsdp, qk_rows),
            bias_grad[QW + KW :].reshape(n_fsdp, v_rows),
            gain_one_grad.reshape(n_fsdp, d_rows),
            gain_two_grad.reshape(n_fsdp, d_rows),
        ],
        axis=1,
    ).astype(BF)
    wide = qkv_w + width
    small_pad = jnp.zeros((n_fsdp, pad_rows, wide), BF)
    small_pad = small_pad.at[:, 0, : small_grads.shape[1]].set(small_grads)
    rest = jnp.concatenate([qkv_wgrad, out_wgrad], axis=1)
    rest = jnp.concatenate([rest.reshape(n_fsdp, d_rows, wide), small_pad], axis=1)
    rest = rest.reshape(f_lead + (d_rows + pad_rows,) + quarter + (wide // n_seq,))
    for step, mask in enumerate(net.seq_bits):
        rest = net.add_half(rest, mask, n_f + 1 + len(quarter) - 1 - step)
    rest = net.scatter_fsdp(rest)

    def seq_back(value, axis):
        for step, mask in enumerate(reversed(net.seq_bits)):
            value = net.both(value, mask, axis + step)
        return value

    out_down = seq_back(red_down, 0).reshape(ff_rows, width).astype(F32)
    out_gate = seq_back(red_gate, 1).reshape(d_rows, 2 * units).astype(F32)
    out_rest = seq_back(rest, 1).reshape(d_rows + pad_rows, wide).astype(F32)
    line = out_rest[d_rows]
    edge = qk_rows + v_rows
    return (
        block_out,
        hidden_grad,
        out_rest[:d_rows, :qkv_w],
        line[:qk_rows],
        line[qk_rows:edge],
        out_rest[:d_rows, qkv_w:],
        out_gate,
        out_down,
        line[edge : edge + 2 * d_rows].reshape(2, d_rows),
    )


def after(value, *others):
    return lax.optimization_barrier((value, *others))[0]


def rope_tables(full_length, n_seq):
    places = np.arange(full_length, dtype=np.float32)
    speeds = np.power(ROPE_BASE, -2.0 * np.arange(HEAD_DIM // 2, dtype=np.float32) / HEAD_DIM)
    angles = places[:, None] * speeds.astype(np.float32)[None, :]
    cos_t = np.tile(np.cos(angles), (1, 4)).reshape(n_seq, -1, 128)
    sin_t = np.concatenate([-np.sin(angles), np.sin(angles)] * 2, axis=1).reshape(n_seq, -1, 128)
    return jnp.asarray(cos_t, F32), jnp.asarray(sin_t, F32)


def on_device_tiled(
    hidden, w_qkv, b_qkv, w_out, w_gate_up, w_down, norm_gains, segment_ids, token_counts, cotangent,
    n_fsdp, n_seq,
):
    net = Net(n_fsdp, n_seq)
    micro, batch, length, width = hidden.shape
    full_length = length * n_seq
    tokens_micro = batch * n_fsdp * full_length
    rows = micro * batch * length
    seqs = micro * batch
    d_rows, qkv_w = w_qkv.shape
    ff_rows = w_down.shape[0]
    units = w_gate_up.shape[1] // 2
    n_bias = b_qkv.shape[0]
    core, ybit = net.seq_bits
    xbit, znear, zfar = net.fsdp_bits
    order = [0, 2, 1, 3]
    seq_index = lax.axis_index("seq")
    meta = jnp.stack([seq_index, lax.axis_index("fsdp")]).astype(jnp.int32)
    source = hidden.reshape(rows, width)

    small = [w_qkv, b_qkv[None], norm_gains]
    a0 = pl.pallas_call(
        functools.partial(cut_qkv, core),
        out_shape=sds(((d_rows + 8) // 2, qkv_w), BF),
        in_specs=[pl.BlockSpec(memory_space=pltpu.SMEM)] + [pl.BlockSpec(memory_space=pl.ANY)] * 3,
        out_specs=pl.BlockSpec(memory_space=pltpu.VMEM),
        scratch_shapes=[
            *[pltpu.VMEM(v.shape, BF) for v in small],
            pltpu.VMEM((d_rows + 8, qkv_w), F32),
            pltpu.SemaphoreType.DMA((3,)),
        ],
        compiler_params=pltpu.CompilerParams(vmem_limit_bytes=52 * 1024 * 1024),
    )(meta, *small)
    a1 = net.both(a0, zfar, 0)

    ids = segment_ids.reshape(rows, 1).astype(BF)
    block = jnp.concatenate([source, jnp.broadcast_to(ids, (rows, 64))], axis=1)
    block = after(block, a0)
    block_y = net.swap(block, ybit)
    block_c = net.swap(block, core)

    quarter = 2 * units // n_seq
    gu0 = lax.dynamic_slice_in_dim(after(w_gate_up, a0), seq_index * quarter, quarter, axis=1)
    half_b = jnp.concatenate(
        [
            w_down.reshape(2, ff_rows // 2, width),
            jnp.concatenate([w_out, jnp.zeros((8, width), BF)], axis=0).reshape(2, -1, width),
        ],
        axis=1,
    )
    a2 = net.both(a1, znear, 0)
    b0 = net.half(after(half_b, a2), core, 0)
    a_x = net.swap(a2, xbit)
    a_c = net.swap(a2, core)
    gu1 = net.both(gu0, zfar, 0)
    gu2 = net.both(after(gu1, a2), znear, 0)
    block_yc = net.swap(block_y, core)
    a_xc = net.swap(a_x, core)
    gu2 = after(gu2, a_x)
    gu_x = net.swap(gu2, xbit)
    gu_y = net.swap(gu2, ybit)
    gu_c = net.swap(gu2, core)
    b1 = net.both(b0, zfar, 0, after(net.swap(b0, zfar), gu2))
    b_z = net.swap(b1, znear)
    a_xc = after(a_xc, b1)

    cos_t, sin_t = rope_tables(full_length, n_seq)
    block_ids = [seq_index ^ o for o in order]
    blocks = [block, block_y, block_c, block_yc]
    seg_all = jnp.stack([b[:, width].reshape(seqs, length) for b in blocks], axis=1)
    own_places = seq_index * length + jnp.arange(length, dtype=jnp.int32)
    key_places = jnp.stack(block_ids)[:, None] * length + jnp.arange(length, dtype=jnp.int32)
    allowed = (seg_all[:, 0, :, None] == seg_all.reshape(seqs, 1, -1)) & (
        own_places[None, :, None] >= key_places.reshape(1, 1, -1)
    )
    allowed = allowed.astype(F32)
    attended, q_s, k_s, v_s, lse, wf, gains = call(
        functools.partial(first_forward, order, length, d_rows, n_bias),
        [meta],
        [*blocks, a2, a_x, a_c, a_xc, cos_t, sin_t, allowed],
        [
            sds((rows, QW), BF),
            sds((seqs, KV_HEADS, GROUP * length, HEAD_DIM), BF),
            sds((seqs, KV_HEADS, full_length, HEAD_DIM), BF),
            sds((seqs, KV_HEADS, full_length, HEAD_DIM), BF),
            sds((seqs, KV_HEADS, GROUP * length, 1), F32),
            sds((width, qkv_w), BF),
            sds((2, width), F32),
        ],
        1.2e10,
        [(n_fsdp * (d_rows + 8), qkv_w), (1, qkv_w)],
        20,
    )
    gu_y = after(gu_y, attended)
    gu_x, b_z = after(gu_x, gu_y), after(b_z, gu_y)
    gu_xy = net.swap(gu_x, ybit)
    b2 = net.both(b1, znear, 0, b_z)
    b_x = net.swap(b2, xbit)
    b_c = net.swap(b2, core)
    gu_yc = net.swap(gu_y, core)
    gu_xc = net.swap(gu_x, core)
    b_xc = net.swap(b_x, core)
    gu_xyc = net.swap(gu_xy, core)
    gate_up = [gu_c, gu_xc, gu_yc, gu_xyc, gu2, gu_x, gu_y, gu_xy]

    weight = tokens_micro / token_counts.astype(F32)
    weight = jnp.repeat(weight, batch * length)[:, None]
    lead = (2, 2, 2, 2)
    block_out, gate_keep, gate_give, down_keep, down_give, middle_grad, attended_grad, gain_two = call(
        functools.partial(feed_forward_pieces, d_rows, ff_rows),
        [meta],
        [attended, source, gains, cotangent.reshape(rows, width), weight],
        [
            sds((seqs, width, length), BF),
            sds(lead + (d_rows, units // 2), BF),
            sds(lead + (d_rows, units // 2), BF),
            sds(lead + (ff_rows // 4 + d_rows // 3, width), BF),
            sds(lead + (ff_rows // 4 + d_rows // 3, width), BF),
            sds((rows, width), F32),
            sds((rows, QW), BF),
            sds((1, width), F32),
        ],
        1.4e10,
        [(units // 2, width), (n_fsdp, d_rows + d_rows // 3, width)],
        fetched=[b2, b_x, b_c, b_xc, *gate_up],
    )
    block_out = block_out.reshape(micro, batch, width, length).swapaxes(2, 3)

    def add(keep, got):
        return (keep.astype(F32) + got.astype(F32)).astype(BF)

    def halves(keep, got):
        return add(keep[0], got[0]), add(keep[1], got[1])

    gate_got = net.swap(gate_give, core)
    down_got = net.swap(after(down_give, gate_got), core)
    gate, gate_give = halves(gate_keep, gate_got)
    gate_got = net.swap(gate_give, xbit)
    down, down_give = halves(down_keep, down_got)
    attended_grad = after(attended_grad, gate_give, down_give)
    down_got = net.swap(down_give, ybit)

    dq, dkv_keep, dkv_give, rest_keep, rest_give = call(
        functools.partial(attention_backward_pieces, order, length, d_rows),
        [meta],
        [*blocks, wf, gains, cos_t, sin_t, allowed, q_s, k_s, v_s, lse, attended_grad, gain_two],
        [
            sds((rows, QW + 64), BF),
            sds((2, rows, 2 * KW), BF),
            sds((2, rows, 2 * KW), BF),
            sds(lead + (d_rows + 8, 256), BF),
            sds(lead + (d_rows + 8, 256), BF),
        ],
        1.4e10,
        [(width, 1024), (1, qkv_w), (1, width), (n_fsdp, 8, 1024)],
    )
    gate, gate_give = halves(gate, after(gate_got, dq, down_got))
    gate_got = net.swap(gate_give, znear)
    down, down_give = halves(down, after(down_got, gate_give))
    down_got = net.swap(down_give, xbit)
    rest, rest_give = halves(rest_keep, after(net.swap(rest_give, core), down_give))
    rest_got = net.swap(rest_give, xbit)
    dkv, dkv_give = halves(dkv_keep, after(net.swap(dkv_give, core), rest_give))
    dkv_got = net.swap(dkv_give, ybit)
    (hidden_grad,) = call(
        input_gradient_two,
        [],
        [dq, dkv, dkv_got, source, middle_grad, wf, gains],
        [sds((seqs, width, length), F32)],
        3e9,
        mib=16,
    )
    gate, gate_give = halves(gate, after(gate_got, hidden_grad))
    gate_got = net.swap(gate_give, zfar)
    hidden_grad = hidden_grad.reshape(micro, batch, width, length).swapaxes(2, 3)
    down, down_give = halves(down, after(down_got, gate_give))
    down_got = net.swap(down_give, znear)
    rest, rest_give = halves(rest, after(rest_got, down_give))
    rest_got = net.swap(rest_give, znear)
    gate = add(gate, after(gate_got, rest_give))
    gate_got = net.swap(gate, ybit)
    down, down_give = halves(down, after(down_got, gate))
    down_got = net.swap(down_give, zfar)
    rest, rest_give = halves(rest, after(rest_got, down_give))
    rest_got = net.swap(rest_give, zfar)
    gate = add(gate, after(gate_got, rest_give))
    gate_far = net.swap(gate, core)
    down = add(down, after(down_got, gate))
    down_y = net.swap(down, ybit)
    down_c = net.swap(down, core)
    rest = add(rest, after(rest_got, down))
    rest_got = net.swap(rest, ybit)
    down_yc = net.swap(down_y, core)
    rest = add(rest, rest_got)
    rest_far = net.swap(rest, core)
    qk, v = (QW + KW) // n_fsdp, KW // n_fsdp
    out_gate, out_down, out_wout, out_qkv, b_qk, b_v, out_gains = call(
        functools.partial(place_all, ff_rows // 4, qk, v),
        [meta],
        [gate, gate_far, down, down_y, down_c, down_yc, rest, rest_far],
        [
            sds((d_rows, 2 * units), F32),
            sds((ff_rows, width), F32),
            sds((d_rows, width), F32),
            sds((d_rows, qkv_w), F32),
            sds((1, qk), F32),
            sds((1, v), F32),
            sds((2, d_rows), F32),
        ],
        3e9,
        [(d_rows + 8, 1024)],
        16,
    )
    return (
        block_out,
        hidden_grad,
        out_qkv,
        b_qk.reshape(qk),
        b_v.reshape(v),
        out_wout,
        out_gate,
        out_down,
        out_gains,
    )


def solution(mesh):
    n_fsdp, n_seq = mesh.shape["fsdp"], mesh.shape["seq"]
    in_specs = (
        P(None, "fsdp", "seq", None),
        P("fsdp", None),
        P("fsdp"),
        P("fsdp", None),
        P("fsdp", None),
        P("fsdp", None),
        P(None, "fsdp"),
        P(None, "fsdp", "seq"),
        P(),
        P(None, "fsdp", "seq", None),
    )
    out_specs = (
        P(None, "fsdp", "seq", None),
        P(None, "fsdp", "seq", None),
        P("fsdp", None),
        P("fsdp"),
        P("fsdp"),
        P("fsdp", None),
        P("fsdp", None),
        P("fsdp", None),
        P(None, "fsdp"),
    )

    def local(*args):
        body = on_device_tiled if (n_fsdp, n_seq) == (8, 4) else on_device
        return body(*args, n_fsdp=n_fsdp, n_seq=n_seq)

    return jax.shard_map(local, mesh=mesh, in_specs=in_specs, out_specs=out_specs, check_vma=False)
```

```python
import functools

import jax
import jax.numpy as jnp
import numpy as np
from jax import lax
from jax.experimental import pallas as pl
from jax.experimental.pallas import tpu as pltpu
from jax.sharding import PartitionSpec as P

HEADS = 9
KV_HEADS = 3
HEAD_DIM = 64
GROUP = HEADS // KV_HEADS
QW = HEADS * HEAD_DIM
KW = KV_HEADS * HEAD_DIM
EPS = 1e-05
ROPE_BASE = 100000.0
MASKED = -1000000000.0
BF = jnp.bfloat16
F32 = jnp.float32


def dot(a, b, ca, cb):
    return lax.dot_general(a, b, (((ca,), (cb,)), ((), ())), preferred_element_type=F32)


def rotary(values, cosine, sine):
    half = values.shape[-1] // 2
    a, b = values[..., :half], values[..., half:]
    return jnp.concatenate([a * cosine - b * sine, b * cosine + a * sine], axis=-1)


def norm_parts(values):
    factor = lax.rsqrt(jnp.mean(values * values, axis=-1, keepdims=True) + EPS)
    return factor, values * factor


def norm_back(grad_in, gain, factor, normed):
    scaled = grad_in * gain
    return factor * (scaled - normed * jnp.mean(scaled * normed, axis=-1, keepdims=True))


def whole(*shape_dtypes):
    return [pl.BlockSpec(memory_space=pltpu.VMEM) for _ in shape_dtypes]


def call(kernel, scalars, arrays, outs, flops, scratch=(), mib=52, fetched=(), landing=()):
    specs = [pl.BlockSpec(memory_space=pltpu.SMEM)] * len(scalars) + whole(*arrays)
    specs += [pl.BlockSpec(memory_space=pl.ANY)] * len(fetched)
    arrays = [*arrays, *fetched]
    moved = sum(a.size * a.dtype.itemsize for a in arrays) + sum(
        int(np.prod(o.shape)) * o.dtype.itemsize for o in outs
    )
    return pl.pallas_call(
        kernel,
        out_shape=outs,
        in_specs=specs,
        out_specs=whole(*outs),
        scratch_shapes=[
            *[pltpu.VMEM(shape, F32) for shape in scratch],
            *[pltpu.VMEM(shape, BF) for shape in landing],
            *([pltpu.SemaphoreType.DMA((len(fetched),))] if fetched else []),
        ],
        compiler_params=pltpu.CompilerParams(vmem_limit_bytes=mib * 1024 * 1024),
        cost_estimate=pl.CostEstimate(flops=int(flops), bytes_accessed=moved, transcendentals=0),
    )(*scalars, *arrays)


def sds(shape, dtype):
    return jax.ShapeDtypeStruct(shape, dtype)


def turn(x, cosine, sine):
    tiles = []
    low = lax.broadcasted_iota(jnp.int32, (1, 128), 1) % HEAD_DIM < HEAD_DIM // 2
    for t in range(x.shape[1] // 128):
        part = x[:, 128 * t : 128 * t + 128]
        other = jnp.where(low, pltpu.roll(part, 96, 1), pltpu.roll(part, 32, 1))
        tiles.append(part * cosine + other * sine)
    return tiles


def turn_kv(x, cosine, sine):
    lane = lax.broadcasted_iota(jnp.int32, (1, 128), 1)
    first, second = turn(x[:, :256], cosine, sine)
    second = jnp.where(lane < KW - 128, second, x[:, 128:256])
    return jnp.concatenate([first, second, x[:, 256:]], axis=1)


def tables(seq, order, cos_ref, sin_ref):
    cosine = jnp.concatenate([cos_ref[seq ^ o] for o in order], axis=0)
    sine = jnp.concatenate([sin_ref[seq ^ o] for o in order], axis=0)
    return cosine, sine


def heads_to_rows(x, g):
    return jnp.concatenate(
        [x[:, HEAD_DIM * h : HEAD_DIM * (h + 1)] for h in range(GROUP * g, GROUP * (g + 1))], axis=0
    )


def rows_to_heads(parts, length):
    return jnp.concatenate(
        [p[length * r : length * (r + 1)] for p in parts for r in range(GROUP)], axis=1
    )


def attention_forward(order, length, seq_ref, blocks, wq, wkv, bq, bkv, gain, cos, sin, mask,
                      att_o, q_o, k_o, v_o, lse_o):
    seq = seq_ref[0]
    cosine, sine = tables(seq, order, cos, sin)
    width = gain.shape[1]
    for b in range(blocks.shape[1] // length):
        x = blocks[:, b * length : (b + 1) * length, :width].astype(F32)
        x = x.reshape(len(order) * length, width)
        first = (norm_parts(x)[1] * gain[...]).astype(BF)
        kv = dot(first, wkv[...], 1, 0) + bkv[...]
        q = dot(first[:length], wq[...], 1, 0) + bq[...]
        q = jnp.concatenate(turn(q, cosine[:length], sine[:length]), axis=1).astype(BF)
        q = q * jnp.asarray(HEAD_DIM ** (-0.5), BF)
        kv = turn_kv(kv, cosine, sine).astype(BF)
        allowed = jnp.concatenate([mask[b]] * GROUP, axis=0) > 0.0
        parts = []
        for g in range(KV_HEADS):
            qg = heads_to_rows(q, g)
            kg = kv[:, HEAD_DIM * g : HEAD_DIM * (g + 1)]
            vg = kv[:, KW + HEAD_DIM * g : KW + HEAD_DIM * (g + 1)]
            q_o[b, g] = qg
            k_o[b, g] = kg
            v_o[b, g] = vg
            scores = jnp.where(allowed, dot(qg, kg, 1, 1), MASKED)
            top = jnp.max(scores, axis=-1, keepdims=True)
            e = jnp.exp(scores - top)
            total = jnp.sum(e, axis=-1, keepdims=True)
            lse_o[b, g] = jnp.log(total) + top
            probs = (e * (1.0 / total)).astype(BF)
            parts.append(dot(probs, vg, 1, 0))
        att_o[b * length : (b + 1) * length, :] = rows_to_heads(parts, length).astype(BF)


def feed_forward(attended, source, wo, wgu, wd, gain, cot, weight,
                 out_o, down_o, gu_o, mid_o, wout_o, attg_o, gain_o):
    units = wd.shape[0]
    step = units // 3
    att = attended[...]
    middle = source[...].astype(F32) + dot(att, wo[...], 1, 0)
    scale_two, normed = norm_parts(middle)
    g2 = gain[...]
    second = (normed * g2).astype(BF)
    out_grad = cot[...].astype(F32) * weight[...]
    feed_grad = out_grad.astype(BF)
    feed = None
    back = None
    for j in range(0, units, step):
        wg = wgu[:, j : j + step]
        wu = wgu[:, units + j : units + j + step]
        wdj = wd[j : j + step, :]
        gate = dot(second, wg, 1, 0)
        up = dot(second, wu, 1, 0)
        sig = jax.nn.sigmoid(gate)
        act = gate * sig
        product = (act * up).astype(BF)
        part = dot(product, wdj, 1, 0)
        feed = part if feed is None else feed + part
        down_o[j : j + step, :] = dot(product, feed_grad, 0, 0).astype(BF)
        pgrad = dot(feed_grad, wdj, 1, 1)
        ggrad = (pgrad * up * (sig * (1.0 + gate * (1.0 - sig)))).astype(BF)
        ugrad = (pgrad * act).astype(BF)
        gu_o[:, j : j + step] = dot(second, ggrad, 0, 0).astype(BF)
        gu_o[:, units + j : units + j + step] = dot(second, ugrad, 0, 0).astype(BF)
        part = dot(ggrad, wg, 1, 1) + dot(ugrad, wu, 1, 1)
        back = part if back is None else back + part
    out_o[...] = (middle + feed).astype(BF)
    gain_o[...] = jnp.sum(back * normed, axis=0, keepdims=True)
    middle_grad = out_grad + norm_back(back, g2, scale_two, normed)
    mid_o[...] = middle_grad
    branch = middle_grad.astype(BF)
    wout_o[...] = dot(att, branch, 0, 0).astype(BF)
    attg_o[...] = dot(branch, wo[...], 1, 1).astype(BF)


def attention_backward(order, length, seq_ref, blocks, wq, wkv, gain, cos, sin, mask, q_i, k_i, v_i,
                       lse, attg, dq_o, dkv_o, wgrad_o, bias_o, gain_o):
    seq = seq_ref[0]
    cosine, sine = tables(seq, order, cos, sin)
    width = gain.shape[1]
    q_wgrad = kv_wgrad = bias_q = bias_kv = gain_sum = None
    for b in range(blocks.shape[1] // length):
        x = blocks[:, b * length : (b + 1) * length, :width].astype(F32)
        x = x.reshape(len(order) * length, width)
        normed = norm_parts(x)[1]
        first = (normed * gain[...]).astype(BF)
        allowed = jnp.concatenate([mask[b]] * GROUP, axis=0) > 0.0
        ag = attg[b * length : (b + 1) * length, :]
        dqs, dks, dvs = [], [], []
        for g in range(KV_HEADS):
            qg, kg, vg = q_i[b, g], k_i[b, g], v_i[b, g]
            agg = heads_to_rows(ag, g)
            p = jnp.exp(jnp.where(allowed, dot(qg, kg, 1, 1), MASKED) - lse[b, g])
            dvs.append(dot(p.astype(BF), agg, 0, 0))
            pg = dot(agg, vg, 1, 1)
            inner = jnp.sum(p * pg, axis=-1, keepdims=True)
            ds = (p * (pg - inner)).astype(BF)
            dqs.append(dot(ds, kg, 1, 0) * HEAD_DIM ** (-0.5))
            dks.append(dot(ds, qg, 0, 0))
        dq = rows_to_heads(dqs, length)
        dq = jnp.concatenate([dq, jnp.zeros((length, 64), F32)], axis=1)
        dq = jnp.concatenate(turn(dq, cosine[:length], -sine[:length]), axis=1).astype(BF)
        dkv = jnp.concatenate(dks + dvs, axis=1)
        dkv = turn_kv(dkv, cosine, -sine).astype(BF)
        dq_o[b * length : (b + 1) * length, :] = dq
        for r in range(len(order)):
            dkv_o[r, b * length : (b + 1) * length, :] = dkv[r * length : (r + 1) * length, :]
        wq_part = dot(first[:length], dq, 0, 0)
        wkv_part = dot(first, dkv, 0, 0)
        bq_part = jnp.sum(dq.astype(F32), axis=0, keepdims=True)
        bkv_part = jnp.sum(dkv.astype(F32), axis=0, keepdims=True)
        e_kv = dot(dkv, wkv[...], 1, 1) * normed
        e_q = dot(dq[:, :QW], wq[:, :QW], 1, 1) * normed[:length]
        g_part = jnp.sum(e_kv, axis=0, keepdims=True) + jnp.sum(e_q, axis=0, keepdims=True)
        if q_wgrad is None:
            q_wgrad, kv_wgrad, bias_q, bias_kv, gain_sum = wq_part, wkv_part, bq_part, bkv_part, g_part
        else:
            q_wgrad, kv_wgrad = q_wgrad + wq_part, kv_wgrad + wkv_part
            bias_q, bias_kv, gain_sum = bias_q + bq_part, bias_kv + bkv_part, gain_sum + g_part
    wgrad_o[...] = jnp.concatenate([q_wgrad[:, :QW], kv_wgrad], axis=1).astype(BF)
    bias_o[...] = jnp.concatenate([bias_q[:, :QW], bias_kv], axis=1)
    gain_o[...] = gain_sum


def input_gradient(dq, own, a, b, c, source, mid, wq, wkv, gain, out_o):
    kv = own[...].astype(F32) + a[...].astype(F32) + b[...].astype(F32) + c[...].astype(F32)
    first_grad = dot(dq[:, :QW], wq[:, :QW], 1, 1) + dot(kv.astype(BF), wkv[...], 1, 1)
    scale_one, normed = norm_parts(source[...].astype(F32))
    out_o[...] = mid[...] + norm_back(first_grad, gain[...], scale_one, normed)

def chosen(flag, a, b):
    return jnp.where(flag != 0, b, a)


class Blocks:
    def __init__(self, *refs):
        self.refs = refs
        self.shape = (len(refs),) + refs[0].shape

    def __getitem__(self, key):
        return jnp.stack([ref[key[1:]] for ref in self.refs])


def cut_qkv(core_bit, meta, w_hbm, bias_hbm, gains_hbm, out_o, w, bias, gains, all_s, sems):
    pairs = ((w_hbm, w), (bias_hbm, bias), (gains_hbm, gains))
    copies = [pltpu.make_async_copy(a, b, sems.at[i]) for i, (a, b) in enumerate(pairs)]
    for copy in copies:
        copy.start()
    for copy in copies:
        copy.wait()
    rows = w.shape[0]
    n = bias.shape[1]
    all_s[:rows, :] = w[...].astype(F32)
    all_s[rows:, :] = jnp.zeros((8, w.shape[1]), F32)
    all_s[rows : rows + 1, :n] = bias[...].astype(F32)
    for i in range(2):
        all_s[rows : rows + 1, n + rows * i : n + rows * (i + 1)] = gains[i : i + 1, :].astype(F32)
    half = out_o.shape[0]
    at = pl.multiple_of((meta[0] & core_bit) * half, 8)
    out_o[...] = all_s[pl.ds(at, half), :].astype(BF)


def first_forward(order, length, d_rows, n_bias, meta, b0, b1, b2, b3, a00, a10, a01, a11, cos, sin, mask,
                  att_o, q_o, k_o, v_o, lse_o, w_o, gain_o, w_s, b_s):
    blocks = Blocks(b0, b1, b2, b3)
    core, x = meta[0] & 1, meta[1] & 1
    cut = a00.shape[2]
    for x_rel, c_rel, piece in ((0, 0, a00), (1, 0, a10), (0, 1, a01), (1, 1, a11)):
        for z0 in range(2):
            for z1 in range(2):
                at = (z1 * 4 + z0 * 2 + (x ^ x_rel)) * 2 * cut + (core ^ c_rel) * cut
                w_s[pl.ds(pl.multiple_of(at, 8), cut), :] = piece[z0, z1].astype(F32)
    n_f = w_s.shape[0] // (2 * cut)
    starts = [2 * cut * f for f in range(n_f)]
    w_o[...] = jnp.concatenate([w_s[at : at + d_rows, :] for at in starts], axis=0).astype(BF)
    lines = [w_s[at + d_rows : at + d_rows + 1, :] for at in starts]
    b_s[...] = jnp.concatenate([line[:, :n_bias] for line in lines], axis=1)
    for i in range(2):
        at = n_bias + d_rows * i
        gain_o[i : i + 1, :] = jnp.concatenate([line[:, at : at + d_rows] for line in lines], axis=1)
    wide = QW + 64
    attention_forward(order, length, meta, blocks, w_o[:, :wide], w_o[:, QW:], b_s[:, :wide], b_s[:, QW:],
                      gain_o[0:1, :], cos, sin, mask, att_o, q_o, k_o, v_o, lse_o)


def turned(out, value):
    length = out.shape[2]
    for b in range(out.shape[0]):
        out[b] = value[length * b : length * (b + 1)].T.astype(out.dtype)


def rel(meta, f):
    r = f ^ meta[1]
    return r & 1, (r >> 1) & 1, (r >> 2) & 1


def fetch_pieces(t, meta, refs, b_s, g_s, sems):
    core, y, x, z0 = meta[0] & 1, (meta[0] >> 1) & 1, meta[1] & 1, (meta[1] >> 1) & 1
    n = g_s.shape[-1]
    copies = []
    for i in range(8):
        at = (z0 ^ (i >> 2), x ^ ((i >> 1) & 1), core ^ (i & 1))
        copies.append(pltpu.make_async_copy(refs[i], b_s.at[at], sems.at[i]))
    for i in range(8):
        at = (y ^ ((i >> 1) & 1), core ^ (i & 1), x ^ (i >> 2))
        source = refs[8 + i].at[:, :, :, pl.ds(t * n, n)]
        copies.append(pltpu.make_async_copy(source, g_s.at[at], sems.at[8 + i]))
    for copy in copies:
        copy.start()
    return copies


def hidden_block(t, d_rows, ff_rows, meta, second, feed_grad, b_s, g_s, down_s, gk_o, gg_o, put_down):
    core, y, x_own, z1_own = meta[0] & 1, (meta[0] >> 1) & 1, meta[1] & 1, (meta[1] >> 2) & 1
    part_d = ff_rows // 4
    feed = back = None
    for c_rel in (1, 0):
        h = core ^ c_rel
        weights = []
        for yy in range(2):
            rows = [g_s[yy, h, f & 1, (f >> 1) & 1, f >> 2].astype(F32) for f in range(8)]
            weights.append(jnp.concatenate(rows, axis=0).astype(BF))
        wg, wu = weights
        wd = [b_s[t, x, c, h, : ff_rows // 2, :] for x in range(2) for c in range(2)]
        wd = jnp.concatenate(wd, axis=0)
        gate = dot(second, wg, 1, 0)
        up = dot(second, wu, 1, 0)
        sig = jax.nn.sigmoid(gate)
        act = gate * sig
        product = (act * up).astype(BF)
        pgrad = dot(feed_grad, wd, 1, 1)
        ggrad = (pgrad * up * (sig * (1.0 + gate * (1.0 - sig)))).astype(BF)
        ugrad = (pgrad * act).astype(BF)
        to = gg_o if c_rel else gk_o
        for yy, grad in ((0, ggrad), (1, ugrad)):
            wgrad = dot(second, grad, 0, 0)
            for f in range(8):
                x, z0, z1 = rel(meta, f)
                to[x, y ^ yy, z0, z1] = wgrad[d_rows * f : d_rows * (f + 1), :].astype(BF)
        down_s[...] = dot(product, feed_grad, 0, 0)
        for x in range(2):
            for yy in range(2):
                for c_to in range(2):
                    at = pl.multiple_of(x * ff_rows + (yy * 2 + (core ^ c_to)) * part_d, 16)
                    value = down_s[pl.ds(at, part_d), :].astype(BF)
                    put_down(c_to, y ^ yy, x ^ x_own, h ^ z1_own, value)
        part = dot(product, wd, 1, 0)
        feed = part if feed is None else feed + part
        part = dot(ggrad, wg, 1, 1) + dot(ugrad, wu, 1, 1)
        back = part if back is None else back + part
    return feed, back


def feed_forward_one(d_rows, ff_rows, meta, attended, source, gains, cot, weight, *refs):
    mid_o, feed_o, back_o, wo_o, gk_o, gg_o, dk_o, dg_o, down_s, b_s, g_s, sems = refs[16:]
    copies = fetch_pieces(0, meta, refs, b_s, g_s, sems)
    cut = b_s.shape[4] - ff_rows // 2
    for copy in copies[:8]:
        copy.wait()
    wo = []
    for f in range(8):
        for c in range(2):
            rows = b_s[(f >> 1) & 1, f & 1, c, f >> 2, ff_rows // 2 :, :].astype(F32)
            wo.append(rows if c == 0 else rows[: d_rows - cut])
    wo = jnp.concatenate(wo, axis=0).astype(BF)
    wo_o[...] = wo
    middle = source[...].astype(F32) + dot(attended[...], wo, 1, 0)
    mid_o[...] = middle
    second = (norm_parts(middle)[1] * gains[1:2, :]).astype(BF)
    feed_grad = (cot[...].astype(F32) * weight[...]).astype(BF)
    for copy in copies[8:]:
        copy.wait()

    def put_down(c_to, y, x, z1, value):
        (dg_o if c_to else dk_o)[y, x, z1] = value

    feed_o[...], back_o[...] = hidden_block(
        0, d_rows, ff_rows, meta, second, feed_grad, b_s, g_s, down_s, gk_o, gg_o, put_down
    )


def feed_forward_two(d_rows, ff_rows, meta, attended, gains, cot, weight, mid, feed, back, wo, dk_i, dg_i, *refs):
    out_o, gk_o, gg_o, dk_o, dg_o, midg_o, attg_o, gain_o, down_s, wout_s, b_s, g_s, sems = refs[16:]
    copies = fetch_pieces(1, meta, refs, b_s, g_s, sems)
    core, y, z0_own = meta[0] & 1, (meta[0] >> 1) & 1, (meta[1] >> 1) & 1
    part_d = ff_rows // 4
    part_o = d_rows // 3
    middle = mid[...]
    scale_two, normed = norm_parts(middle)
    g2 = gains[1:2, :]
    second = (normed * g2).astype(BF)
    out_grad = cot[...].astype(F32) * weight[...]
    feed_grad = out_grad.astype(BF)
    for first, to in ((dk_i, dk_o), (dg_i, dg_o)):
        for i in range(8):
            at = (i >> 2, (i >> 1) & 1, i & 1)
            to[at[0], at[1], z0_own, at[2], :part_d, :] = first[at]
    for copy in copies:
        copy.wait()

    def put_down(c_to, y, x, z1, value):
        (dg_o if c_to else dk_o)[y, x, 1 ^ z0_own, z1, :part_d, :] = value

    feed_part, back_part = hidden_block(
        1, d_rows, ff_rows, meta, second, feed_grad, b_s, g_s, down_s, gk_o, gg_o, put_down
    )
    turned(out_o, middle + (feed[...] + feed_part))
    back_all = back[...] + back_part
    gain_o[...] = jnp.sum(back_all * normed, axis=0, keepdims=True)
    middle_grad = out_grad + norm_back(back_all, g2, scale_two, normed)
    midg_o[...] = middle_grad
    branch = middle_grad.astype(BF)
    attg_o[...] = dot(branch, wo[...], 1, 1).astype(BF)
    wout = dot(attended[...], branch, 0, 0)
    for f in range(8):
        wout_s[f, :d_rows, :] = wout[d_rows * f : d_rows * (f + 1), :]
        wout_s[f, d_rows:, :] = jnp.zeros((part_o, wout.shape[1]), F32)
    for f in range(8):
        x, z0, z1 = rel(meta, f)
        for yy in range(2):
            for c_to, to in ((0, dk_o), (1, dg_o)):
                at = pl.multiple_of((yy * 2 + (core ^ c_to)) * part_o, 8)
                to[y ^ yy, x, z0, z1, part_d:, :] = wout_s[f, pl.ds(at, part_o), :].astype(BF)


def attention_backward_pieces(order, length, d_rows, meta, b0, b1, b2, b3, w, gains, cos, sin, mask, q_i, k_i, v_i,
                              lse, attg, gain_two, dq_o, dk_o, dg_o, rk_o, rg_o, w_s, bias_s, gain_s, small_s):
    blocks = Blocks(b0, b1, b2, b3)
    half = len(order) // 2

    class Pieces:
        def __setitem__(self, key, value):
            ref = dk_o if key[0] < half else dg_o
            ref[(key[0] % half,) + key[1:]] = value

    class Wgrad:
        def __setitem__(self, key, value):
            w_s[:, : 2 * KW] = value[:, QW:].astype(F32)
            w_s[:, 2 * KW : 2 * KW + QW] = value[:, :QW].astype(F32)
            w_s[:, 2 * KW + QW :] = jnp.zeros((value.shape[0], 64), F32)

    wide = QW + 64
    attention_backward(order, length, meta, blocks, w[:, :wide], w[:, QW:], gains[0:1, :], cos, sin, mask,
                       q_i, k_i, v_i, lse, attg, dq_o, Pieces(), Wgrad(), bias_s, gain_s)
    n_f = small_s.shape[0]
    qk, v = (QW + KW) // n_f, KW // n_f
    bias, g1, g2 = bias_s[...], gain_s[...], gain_two[...]
    for f in range(n_f):
        line = jnp.concatenate(
            [
                bias[:, qk * f : qk * (f + 1)],
                bias[:, QW + KW + v * f : QW + KW + v * (f + 1)],
                g1[:, d_rows * f : d_rows * (f + 1)],
                jnp.zeros((1, 256 - qk - v - d_rows), F32),
                g2[:, d_rows * f : d_rows * (f + 1)],
                jnp.zeros((1, 768 - d_rows), F32),
            ],
            axis=1,
        )
        small_s[f] = jnp.broadcast_to(line, (8, 1024))
    core, y = meta[0] & 1, (meta[0] >> 1) & 1
    for f in range(n_f):
        x, z0, z1 = rel(meta, f)
        for yy in range(2):
            for c_to, to in ((0, rk_o), (1, rg_o)):
                at = pl.multiple_of((yy * 2 + (core ^ c_to)) * 256, 256)
                block = [w_s[d_rows * f : d_rows * (f + 1), pl.ds(at, 256)], small_s[f, :, pl.ds(at, 256)]]
                to[x, z0, z1, yy] = jnp.concatenate(block, axis=0).astype(BF)


def input_gradient_two(dq, own, other, source, mid, w, gains, out_o):
    kv = (own[...].astype(F32) + other[...].astype(F32)).astype(BF)
    first_grad = dot(dq[:, :QW], w[:, :QW], 1, 1) + dot(kv, w[:, QW:], 1, 1)
    scale_one, normed = norm_parts(source[...].astype(F32))
    turned(out_o, mid[...] + norm_back(first_grad, gains[0:1, :], scale_one, normed))


def place_gate(meta, near, far, out_o):
    core = meta[0] & 1
    n = near.shape[2]
    for pieces, c_rel in ((near, 0), (far, 1)):
        for yy in range(2):
            at = pl.multiple_of((yy * 2 + (core ^ c_rel)) * n, 128)
            out_o[:, pl.ds(at, n)] = pieces[yy].astype(F32)


def place_quarters(meta, p00, p10, p01, p11, out_o):
    n = p00.shape[1]
    for piece, o in ((p00, 0), (p10, 2), (p01, 1), (p11, 3)):
        out_o[:, pl.ds(pl.multiple_of((meta[0] ^ o) * n, 128), n)] = piece[...].astype(F32)


def place_down(part_d, meta, p00, p10, p01, p11, out_o, wout_o):
    seq = meta[0]
    part_o = p00.shape[0] - part_d
    for piece, o in ((p00[...], 0), (p10[...], 2), (p01[...], 1), (p11[...], 3)):
        piece = piece.astype(F32)
        to = seq ^ o
        out_o[pl.ds(pl.multiple_of(to * part_d, 16), part_d), :] = piece[:part_d]

        @pl.when(to < 3)
        def _():
            wout_o[pl.ds(pl.multiple_of(to * part_o, 8), part_o), :] = piece[part_d:]


def place_qkv(qk, v, meta, near, far, w_o, bqk_o, bv_o, gains_o, all_s):
    place_gate(meta, near, far, all_s)
    d_rows = w_o.shape[0]
    w_o[:, :QW] = all_s[:d_rows, 2 * KW : 2 * KW + QW]
    w_o[:, QW:] = all_s[:d_rows, : 2 * KW]
    line = all_s[d_rows : d_rows + 1, :]
    bqk_o[...] = line[:, :qk]
    bv_o[...] = line[:, qk : qk + v]
    gains_o[0:1, :] = line[:, qk + v : qk + v + d_rows]
    gains_o[1:2, :] = line[:, 256 : 256 + d_rows]


def place_all(part_d, qk, v, meta, g0, g1, g2, g3, d0, d1, d2, d3, r_near, r_far,
              gate_o, down_o, wout_o, w_o, bqk_o, bv_o, gains_o, all_s):
    place_quarters(meta, g0, g1, g2, g3, gate_o)
    place_down(part_d, meta, d0, d1, d2, d3, down_o, wout_o)
    place_qkv(qk, v, meta, r_near, r_far, w_o, bqk_o, bv_o, gains_o, all_s)


class Net:
    def __init__(self, n_fsdp, n_seq):
        self.n_fsdp, self.n_seq = n_fsdp, n_seq
        self.total = n_fsdp * n_seq
        f, s = lax.axis_index("fsdp"), lax.axis_index("seq")
        self.index = f * n_seq + s
        self.seq_bits = [1 << b for b in range(n_seq.bit_length() - 1)]
        self.fsdp_bits = [n_seq << b for b in range(n_fsdp.bit_length() - 1)]

    def swap(self, value, mask):
        pairs = [(i, i ^ mask) for i in range(self.total)]
        return lax.ppermute(value, ("fsdp", "seq"), pairs)

    def bit(self, mask):
        return (self.index & mask) != 0

    def both(self, mine, mask, axis, other=None):
        other = self.swap(mine, mask) if other is None else other
        high = self.bit(mask)
        return jnp.stack([jnp.where(high, other, mine), jnp.where(high, mine, other)], axis=axis)

    def half(self, value, mask, axis):
        return lax.dynamic_index_in_dim(
            value, self.bit(mask).astype(jnp.int32), axis, keepdims=False
        )

    def add_half(self, value, mask, axis):
        mine = self.bit(mask).astype(jnp.int32)
        keep = lax.dynamic_index_in_dim(value, mine, axis, keepdims=False)
        give = lax.dynamic_index_in_dim(value, 1 - mine, axis, keepdims=False)
        got = self.swap(give, mask)
        return (keep.astype(F32) + got.astype(F32)).astype(value.dtype)

    def gather_fsdp(self, value):
        for step, mask in enumerate(reversed(self.fsdp_bits)):
            value = self.both(value, mask, step)
        return value

    def scatter_fsdp(self, value, first_axis=0):
        count = len(self.fsdp_bits)
        for step, mask in enumerate(self.fsdp_bits):
            value = self.add_half(value, mask, first_axis + count - 1 - step)
        return value


def on_device(
    hidden, w_qkv, b_qkv, w_out, w_gate_up, w_down, norm_gains, segment_ids, token_counts, cotangent,
    n_fsdp, n_seq,
):
    net = Net(n_fsdp, n_seq)
    micro, batch, length, width = hidden.shape
    full_length = length * n_seq
    tokens_micro = batch * n_fsdp * full_length
    scale = HEAD_DIM ** (-0.5)
    rows = micro * batch * length
    d_rows = w_qkv.shape[0]
    ff_rows = w_down.shape[0]
    units = w_gate_up.shape[1] // 2
    qkv_w = w_qkv.shape[1]
    core = net.seq_bits[0]
    f_lead = (2,) * len(net.fsdp_bits)

    ids = segment_ids.reshape(rows, 1).astype(BF)
    block = jnp.concatenate(
        [hidden.reshape(rows, width), jnp.broadcast_to(ids, (rows, 64))], axis=1
    )
    blocks = block[None]
    for mask in reversed(net.seq_bits):
        blocks = jnp.concatenate([blocks, net.swap(blocks, mask)], axis=0)
    order = [0]
    for mask in reversed(net.seq_bits):
        order = order + [o ^ mask for o in order]
    seq_index = lax.axis_index("seq")
    block_ids = [seq_index ^ o for o in order]

    pad_rows = -(d_rows + 1) % 16 + 1
    extra = jnp.zeros((pad_rows, qkv_w), BF)
    small = jnp.concatenate([b_qkv, norm_gains.reshape(-1)])
    extra = extra.at[0, : small.shape[0]].set(small)
    shard_a = jnp.concatenate([w_qkv, extra], axis=0).reshape(2, -1, qkv_w)
    got_a = net.gather_fsdp(net.half(shard_a, core, 0))
    full_a = net.both(got_a, core, len(f_lead)).reshape(n_fsdp, d_rows + pad_rows, qkv_w)
    wf_qkv = full_a[:, :d_rows].reshape(n_fsdp * d_rows, qkv_w)
    smalls = full_a[:, d_rows]
    n_bias = b_qkv.shape[0]
    bias = smalls[:, :n_bias].reshape(-1).astype(F32)
    gains = smalls[:, n_bias : n_bias + 2 * d_rows].reshape(n_fsdp, 2, d_rows).astype(F32)
    gain_one = gains[:, 0].reshape(-1)
    gain_two = gains[:, 1].reshape(-1)

    pad_b = -(d_rows + ff_rows) % 16
    shard_b = jnp.concatenate([w_out, w_down, jnp.zeros((pad_b, width), BF)], axis=0)
    shard_b = shard_b.reshape(2, -1, width)
    got_b = net.gather_fsdp(net.half(shard_b, core, 0))

    parts = n_seq
    shard_c = w_gate_up.reshape(d_rows, parts, -1)
    got_c = net.gather_fsdp(lax.dynamic_index_in_dim(shard_c, seq_index, 1, keepdims=False))
    full_b = net.both(got_b, core, len(f_lead)).reshape(n_fsdp, -1, width)
    wf_out = full_b[:, :d_rows].reshape(n_fsdp * d_rows, width)
    wf_down = full_b[:, d_rows : d_rows + ff_rows].reshape(n_fsdp * ff_rows, width)
    got_c = got_c.reshape(n_fsdp * d_rows, -1)
    for mask in reversed(net.seq_bits):
        got_c = net.both(got_c, mask, got_c.ndim - 1)
    wf_gate_up = got_c.reshape(n_fsdp * d_rows, 2 * units)

    places = np.arange(full_length, dtype=np.float32)
    speeds = np.power(ROPE_BASE, -2.0 * np.arange(HEAD_DIM // 2, dtype=np.float32) / HEAD_DIM)
    angles = places[:, None] * speeds.astype(np.float32)[None, :]
    cos_t = np.tile(np.cos(angles), (1, 4)).reshape(n_seq, length, 128)
    sin_t = np.concatenate([-np.sin(angles), np.sin(angles)] * 2, axis=1).reshape(n_seq, length, 128)
    cos_t, sin_t = jnp.asarray(cos_t, F32), jnp.asarray(sin_t, F32)
    seqs = micro * batch
    seg_all = blocks[..., width].reshape(n_seq, seqs, length).transpose(1, 0, 2)
    own_places = seq_index * length + jnp.arange(length, dtype=jnp.int32)
    key_places = jnp.stack(block_ids)[:, None] * length + jnp.arange(length, dtype=jnp.int32)
    allowed = (seg_all[:, 0, :, None] == seg_all.reshape(seqs, 1, -1)) & (
        own_places[None, :, None] >= key_places.reshape(1, 1, -1)
    )
    allowed = allowed.astype(F32)
    seq_scalar = seq_index.astype(jnp.int32).reshape(1)
    wq, wkv = wf_qkv[:, : QW + 64], wf_qkv[:, QW:]
    gain_one, gain_two = gain_one[None], gain_two[None]
    source = hidden.reshape(rows, width)
    n_all = n_seq * rows
    attended, q_s, k_s, v_s, lse = call(
        functools.partial(attention_forward, order, length),
        [seq_scalar],
        [blocks, wq, wkv, bias[None, : QW + 64], bias[None, QW:], gain_one, cos_t, sin_t, allowed],
        [
            sds((rows, QW), BF),
            sds((seqs, KV_HEADS, GROUP * length, HEAD_DIM), BF),
            sds((seqs, KV_HEADS, full_length, HEAD_DIM), BF),
            sds((seqs, KV_HEADS, full_length, HEAD_DIM), BF),
            sds((seqs, KV_HEADS, GROUP * length, 1), F32),
        ],
        2 * n_all * width * 2 * KW + 2 * rows * width * QW + 4 * rows * full_length * QW,
    )

    weight = tokens_micro / token_counts.astype(F32)
    weight = jnp.repeat(weight, batch * length)[:, None]
    block_out, down_grad, gate_up_wgrad, middle_grad, out_wgrad, attended_grad, gain_two_grad = call(
        feed_forward,
        [],
        [attended, source, wf_out, wf_gate_up, wf_down, gain_two, cotangent.reshape(rows, width), weight],
        [
            sds((rows, width), BF),
            sds((units, width), BF),
            sds((width, 2 * units), BF),
            sds((rows, width), F32),
            sds((QW, width), BF),
            sds((rows, QW), BF),
            sds((1, width), F32),
        ],
        6 * rows * width * 3 * units + 6 * rows * width * QW,
    )
    block_out = block_out.reshape(hidden.shape)

    def seq_axes(value, axis, masks):
        for mask in masks:
            value = net.add_half(value, mask, axis)
        return value

    quarter = (2,) * len(net.seq_bits)
    n_f = len(f_lead)
    red_down = down_grad.reshape(f_lead + quarter + (ff_rows // n_seq, width))
    for step, mask in enumerate(net.seq_bits):
        red_down = net.add_half(red_down, mask, n_f + len(quarter) - 1 - step)
    red_down = net.scatter_fsdp(red_down)

    red_gate = gate_up_wgrad.reshape(f_lead + (d_rows,) + quarter + (2 * units // n_seq,))
    red_gate = net.add_half(red_gate, core, n_f + len(quarter))
    red_gate = net.add_half(red_gate, net.fsdp_bits[0], n_f - 1)
    for step, mask in enumerate(net.seq_bits[1:]):
        red_gate = net.add_half(red_gate, mask, n_f - 1 + len(quarter) - 1 - step)
    for step, mask in enumerate(net.fsdp_bits[1:]):
        red_gate = net.add_half(red_gate, mask, n_f - 2 - step)

    dq, dkv, qkv_wgrad, bias_grad, gain_one_grad = call(
        functools.partial(attention_backward, order, length),
        [seq_scalar],
        [blocks, wq, wkv, gain_one, cos_t, sin_t, allowed, q_s, k_s, v_s, lse, attended_grad],
        [
            sds((rows, QW + 64), BF),
            sds((n_seq, rows, 2 * KW), BF),
            sds((width, qkv_w), BF),
            sds((1, qkv_w), F32),
            sds((1, width), F32),
        ],
        4 * n_all * width * 2 * KW + 4 * rows * width * QW + 10 * rows * full_length * QW,
    )
    kv_parts = [dkv[0]]
    for place, mask_bits in enumerate(order):
        if mask_bits:
            kv_parts.append(net.swap(dkv[place], mask_bits))
    (hidden_grad,) = call(
        input_gradient,
        [],
        [dq, *kv_parts, source, middle_grad, wq, wkv, gain_one],
        [sds((rows, width), F32)],
        2 * rows * width * qkv_w,
    )
    hidden_grad = hidden_grad.reshape(hidden.shape)
    bias_grad, gain_one_grad, gain_two_grad = bias_grad[0], gain_one_grad[0], gain_two_grad[0]

    qk_rows, v_rows = (QW + KW) // n_fsdp, KW // n_fsdp
    small_grads = jnp.concatenate(
        [
            bias_grad[: QW + KW].reshape(n_fsdp, qk_rows),
            bias_grad[QW + KW :].reshape(n_fsdp, v_rows),
            gain_one_grad.reshape(n_fsdp, d_rows),
            gain_two_grad.reshape(n_fsdp, d_rows),
        ],
        axis=1,
    ).astype(BF)
    wide = qkv_w + width
    small_pad = jnp.zeros((n_fsdp, pad_rows, wide), BF)
    small_pad = small_pad.at[:, 0, : small_grads.shape[1]].set(small_grads)
    rest = jnp.concatenate([qkv_wgrad, out_wgrad], axis=1)
    rest = jnp.concatenate([rest.reshape(n_fsdp, d_rows, wide), small_pad], axis=1)
    rest = rest.reshape(f_lead + (d_rows + pad_rows,) + quarter + (wide // n_seq,))
    for step, mask in enumerate(net.seq_bits):
        rest = net.add_half(rest, mask, n_f + 1 + len(quarter) - 1 - step)
    rest = net.scatter_fsdp(rest)

    def seq_back(value, axis):
        for step, mask in enumerate(reversed(net.seq_bits)):
            value = net.both(value, mask, axis + step)
        return value

    out_down = seq_back(red_down, 0).reshape(ff_rows, width).astype(F32)
    out_gate = seq_back(red_gate, 1).reshape(d_rows, 2 * units).astype(F32)
    out_rest = seq_back(rest, 1).reshape(d_rows + pad_rows, wide).astype(F32)
    line = out_rest[d_rows]
    edge = qk_rows + v_rows
    return (
        block_out,
        hidden_grad,
        out_rest[:d_rows, :qkv_w],
        line[:qk_rows],
        line[qk_rows:edge],
        out_rest[:d_rows, qkv_w:],
        out_gate,
        out_down,
        line[edge : edge + 2 * d_rows].reshape(2, d_rows),
    )


def after(value, *others):
    return lax.optimization_barrier((value, *others))[0]


def rope_tables(full_length, n_seq):
    places = np.arange(full_length, dtype=np.float32)
    speeds = np.power(ROPE_BASE, -2.0 * np.arange(HEAD_DIM // 2, dtype=np.float32) / HEAD_DIM)
    angles = places[:, None] * speeds.astype(np.float32)[None, :]
    cos_t = np.tile(np.cos(angles), (1, 4)).reshape(n_seq, -1, 128)
    sin_t = np.concatenate([-np.sin(angles), np.sin(angles)] * 2, axis=1).reshape(n_seq, -1, 128)
    return jnp.asarray(cos_t, F32), jnp.asarray(sin_t, F32)


def on_device_tiled(
    hidden, w_qkv, b_qkv, w_out, w_gate_up, w_down, norm_gains, segment_ids, token_counts, cotangent,
    n_fsdp, n_seq,
):
    net = Net(n_fsdp, n_seq)
    micro, batch, length, width = hidden.shape
    full_length = length * n_seq
    tokens_micro = batch * n_fsdp * full_length
    rows = micro * batch * length
    seqs = micro * batch
    d_rows, qkv_w = w_qkv.shape
    ff_rows = w_down.shape[0]
    units = w_gate_up.shape[1] // 2
    n_bias = b_qkv.shape[0]
    core, ybit = net.seq_bits
    xbit, znear, zfar = net.fsdp_bits
    order = [0, 2, 1, 3]
    seq_index = lax.axis_index("seq")
    meta = jnp.stack([seq_index, lax.axis_index("fsdp")]).astype(jnp.int32)
    source = hidden.reshape(rows, width)

    small = [w_qkv, b_qkv[None], norm_gains]
    a0 = pl.pallas_call(
        functools.partial(cut_qkv, core),
        out_shape=sds(((d_rows + 8) // 2, qkv_w), BF),
        in_specs=[pl.BlockSpec(memory_space=pltpu.SMEM)] + [pl.BlockSpec(memory_space=pl.ANY)] * 3,
        out_specs=pl.BlockSpec(memory_space=pltpu.VMEM),
        scratch_shapes=[
            *[pltpu.VMEM(v.shape, BF) for v in small],
            pltpu.VMEM((d_rows + 8, qkv_w), F32),
            pltpu.SemaphoreType.DMA((3,)),
        ],
        compiler_params=pltpu.CompilerParams(vmem_limit_bytes=52 * 1024 * 1024),
    )(meta, *small)
    a1 = net.both(a0, zfar, 0)

    ids = segment_ids.reshape(rows, 1).astype(BF)
    block = jnp.concatenate([source, jnp.broadcast_to(ids, (rows, 64))], axis=1)
    block = after(block, a0)
    block_y = net.swap(block, ybit)
    block_c = net.swap(block, core)

    quarter = 2 * units // n_seq
    gu0 = lax.dynamic_slice_in_dim(after(w_gate_up, a0), seq_index * quarter, quarter, axis=1)
    half_b = jnp.concatenate(
        [
            w_down.reshape(2, ff_rows // 2, width),
            jnp.concatenate([w_out, jnp.zeros((8, width), BF)], axis=0).reshape(2, -1, width),
        ],
        axis=1,
    )
    a2 = net.both(a1, znear, 0)
    b0 = net.half(after(half_b, a2), core, 0)
    a_x = net.swap(a2, xbit)
    a_c = net.swap(a2, core)
    gu1 = net.both(gu0, zfar, 0)
    gu2 = net.both(after(gu1, a2), znear, 0)
    block_yc = net.swap(block_y, core)
    a_xc = net.swap(a_x, core)
    gu2 = after(gu2, a_x)
    gu_x = net.swap(gu2, xbit)
    gu_y = net.swap(gu2, ybit)
    gu_c = net.swap(gu2, core)
    b1 = net.both(b0, zfar, 0, after(net.swap(b0, zfar), gu2))
    b_z = net.swap(b1, znear)
    b_x = net.swap(b1, xbit)
    b_c = net.swap(b1, core)
    a_xc = after(a_xc, b1)

    cos_t, sin_t = rope_tables(full_length, n_seq)
    block_ids = [seq_index ^ o for o in order]
    blocks = [block, block_y, block_c, block_yc]
    seg_all = jnp.stack([b[:, width].reshape(seqs, length) for b in blocks], axis=1)
    own_places = seq_index * length + jnp.arange(length, dtype=jnp.int32)
    key_places = jnp.stack(block_ids)[:, None] * length + jnp.arange(length, dtype=jnp.int32)
    allowed = (seg_all[:, 0, :, None] == seg_all.reshape(seqs, 1, -1)) & (
        own_places[None, :, None] >= key_places.reshape(1, 1, -1)
    )
    allowed = allowed.astype(F32)
    attended, q_s, k_s, v_s, lse, wf, gains = call(
        functools.partial(first_forward, order, length, d_rows, n_bias),
        [meta],
        [*blocks, a2, a_x, a_c, a_xc, cos_t, sin_t, allowed],
        [
            sds((rows, QW), BF),
            sds((seqs, KV_HEADS, GROUP * length, HEAD_DIM), BF),
            sds((seqs, KV_HEADS, full_length, HEAD_DIM), BF),
            sds((seqs, KV_HEADS, full_length, HEAD_DIM), BF),
            sds((seqs, KV_HEADS, GROUP * length, 1), F32),
            sds((width, qkv_w), BF),
            sds((2, width), F32),
        ],
        1.2e10,
        [(n_fsdp * (d_rows + 8), qkv_w), (1, qkv_w)],
        20,
    )
    gu_y = after(gu_y, attended)
    gu_x, b_z, b_x = after(gu_x, gu_y), after(b_z, gu_y), after(b_x, gu_y)
    gu_xy = net.swap(gu_x, ybit)
    b_zx = net.swap(b_z, xbit)
    gu_yc = net.swap(gu_y, core)
    gu_xc = net.swap(gu_x, core)
    b_zc = net.swap(b_z, core)
    b_xc = net.swap(b_x, core)
    b_zxc = net.swap(b_zx, core)
    gu_xyc = net.swap(gu_xy, core)
    pieces = [b1, b_c, b_x, b_xc, b_z, b_zc, b_zx, b_zxc]
    pieces += [gu2, gu_c, gu_y, gu_yc, gu_x, gu_xc, gu_xy, gu_xyc]

    weight = tokens_micro / token_counts.astype(F32)
    weight = jnp.repeat(weight, batch * length)[:, None]
    lead = (2, 2, 2, 2)
    cot = cotangent.reshape(rows, width)
    part = units // 4
    gate_lead = lead + (d_rows, part)
    landing = [(2, 2, 2, 2) + b1.shape[1:], (2, 2, 2, 2, 2, d_rows, part)]
    middle, feed_one, back_one, wf_out, keep_a, give_a, down_keep, down_give = call(
        functools.partial(feed_forward_one, d_rows, ff_rows),
        [meta],
        [attended, source, gains, cot, weight],
        [
            sds((rows, width), F32),
            sds((rows, width), F32),
            sds((rows, width), F32),
            sds((QW, width), BF),
            sds(gate_lead, BF),
            sds(gate_lead, BF),
            sds((2, 2, 2, ff_rows // 4, width), BF),
            sds((2, 2, 2, ff_rows // 4, width), BF),
        ],
        7e9,
        [(2 * ff_rows, width)],
        fetched=pieces,
        landing=landing,
    )
    got_a = net.swap(give_a, core)
    block_out, keep_b, give_b, down_keep, down_give, middle_grad, attended_grad, gain_two = call(
        functools.partial(feed_forward_two, d_rows, ff_rows),
        [meta],
        [attended, gains, cot, weight, middle, feed_one, back_one, wf_out, down_keep, down_give],
        [
            sds((seqs, width, length), BF),
            sds(gate_lead, BF),
            sds(gate_lead, BF),
            sds(lead + (ff_rows // 4 + d_rows // 3, width), BF),
            sds(lead + (ff_rows // 4 + d_rows // 3, width), BF),
            sds((rows, width), F32),
            sds((rows, QW), BF),
            sds((1, width), F32),
        ],
        8e9,
        [(2 * ff_rows, width), (n_fsdp, d_rows + d_rows // 3, width)],
        fetched=pieces,
        landing=landing,
    )
    block_out = block_out.reshape(micro, batch, width, length).swapaxes(2, 3)

    def add(keep, got):
        return (keep.astype(F32) + got.astype(F32)).astype(BF)

    def halves(keep, got):
        return add(keep[0], got[0]), add(keep[1], got[1])

    gate_a, give_a = halves(keep_a, after(got_a, attended_grad))
    got_a = net.swap(give_a, xbit)
    got_b = net.swap(after(give_b, give_a), core)
    down_got = net.swap(after(down_give, got_b), core)
    gate_b, give_b = halves(keep_b, got_b)
    got_b = net.swap(give_b, xbit)
    down, down_give = halves(down_keep, down_got)
    attended_grad = after(attended_grad, give_a, give_b, down_give)
    down_got = net.swap(down_give, ybit)

    dq, dkv_keep, dkv_give, rest_keep, rest_give = call(
        functools.partial(attention_backward_pieces, order, length, d_rows),
        [meta],
        [*blocks, wf, gains, cos_t, sin_t, allowed, q_s, k_s, v_s, lse, attended_grad, gain_two],
        [
            sds((rows, QW + 64), BF),
            sds((2, rows, 2 * KW), BF),
            sds((2, rows, 2 * KW), BF),
            sds(lead + (d_rows + 8, 256), BF),
            sds(lead + (d_rows + 8, 256), BF),
        ],
        1.4e10,
        [(width, 1024), (1, qkv_w), (1, width), (n_fsdp, 8, 1024)],
    )
    gate_a, give_a = halves(gate_a, after(got_a, dq))
    gate_b, give_b = halves(gate_b, after(got_b, down_got))
    gate_give = jnp.concatenate([give_a, give_b], axis=-1)
    gate = jnp.concatenate([gate_a, gate_b], axis=-1)
    gate_got = net.swap(gate_give, ybit)
    down, down_give = halves(down, after(down_got, gate_give))
    down_got = net.swap(down_give, xbit)
    rest, rest_give = halves(rest_keep, after(net.swap(rest_give, core), down_give))
    rest_got = net.swap(rest_give, xbit)
    dkv, dkv_give = halves(dkv_keep, after(net.swap(dkv_give, core), rest_give))
    dkv_got = net.swap(dkv_give, ybit)
    (hidden_grad,) = call(
        input_gradient_two,
        [],
        [dq, dkv, dkv_got, source, middle_grad, wf, gains],
        [sds((seqs, width, length), F32)],
        3e9,
        mib=16,
    )
    gate, gate_give = halves(gate, after(gate_got, hidden_grad))
    gate_got = net.swap(gate_give, znear)
    hidden_grad = hidden_grad.reshape(micro, batch, width, length).swapaxes(2, 3)
    down, down_give = halves(down, after(down_got, gate_give))
    down_got = net.swap(down_give, znear)
    rest, rest_give = halves(rest, after(rest_got, down_give))
    rest_got = net.swap(rest_give, znear)
    gate, gate_give = halves(gate, after(gate_got, rest_give))
    gate_got = net.swap(gate_give, zfar)
    down, down_give = halves(down, after(down_got, gate_give))
    down_got = net.swap(down_give, zfar)
    rest, rest_give = halves(rest, after(rest_got, down_give))
    rest_got = net.swap(rest_give, zfar)
    gate = add(gate, after(gate_got, rest_give))
    gate_y = net.swap(gate, ybit)
    gate_c = net.swap(gate, core)
    down = add(down, after(down_got, gate))
    down_y = net.swap(down, ybit)
    down_c = net.swap(down, core)
    rest = add(rest, after(rest_got, down))
    rest_got = net.swap(rest, ybit)
    down_yc = net.swap(down_y, core)
    gate_yc = net.swap(gate_y, core)
    rest = add(rest, rest_got)
    rest_far = net.swap(rest, core)
    qk, v = (QW + KW) // n_fsdp, KW // n_fsdp
    out_gate, out_down, out_wout, out_qkv, b_qk, b_v, out_gains = call(
        functools.partial(place_all, ff_rows // 4, qk, v),
        [meta],
        [gate, gate_y, gate_c, gate_yc, down, down_y, down_c, down_yc, rest, rest_far],
        [
            sds((d_rows, 2 * units), F32),
            sds((ff_rows, width), F32),
            sds((d_rows, width), F32),
            sds((d_rows, qkv_w), F32),
            sds((1, qk), F32),
            sds((1, v), F32),
            sds((2, d_rows), F32),
        ],
        3e9,
        [(d_rows + 8, 1024)],
        16,
    )
    return (
        block_out,
        hidden_grad,
        out_qkv,
        b_qk.reshape(qk),
        b_v.reshape(v),
        out_wout,
        out_gate,
        out_down,
        out_gains,
    )


def solution(mesh):
    n_fsdp, n_seq = mesh.shape["fsdp"], mesh.shape["seq"]
    in_specs = (
        P(None, "fsdp", "seq", None),
        P("fsdp", None),
        P("fsdp"),
        P("fsdp", None),
        P("fsdp", None),
        P("fsdp", None),
        P(None, "fsdp"),
        P(None, "fsdp", "seq"),
        P(),
        P(None, "fsdp", "seq", None),
    )
    out_specs = (
        P(None, "fsdp", "seq", None),
        P(None, "fsdp", "seq", None),
        P("fsdp", None),
        P("fsdp"),
        P("fsdp"),
        P("fsdp", None),
        P("fsdp", None),
        P("fsdp", None),
        P(None, "fsdp"),
    )

    def local(*args):
        body = on_device_tiled if (n_fsdp, n_seq) == (8, 4) else on_device
        return body(*args, n_fsdp=n_fsdp, n_seq=n_seq)

    return jax.shard_map(local, mesh=mesh, in_specs=in_specs, out_specs=out_specs, check_vma=False)
```

```python
import functools

import jax
import jax.numpy as jnp
import numpy as np
from jax import lax
from jax.experimental import pallas as pl
from jax.experimental.pallas import tpu as pltpu
from jax.sharding import PartitionSpec as P

HEADS = 9
KV_HEADS = 3
HEAD_DIM = 64
GROUP = HEADS // KV_HEADS
QW = HEADS * HEAD_DIM
KW = KV_HEADS * HEAD_DIM
EPS = 1e-05
ROPE_BASE = 100000.0
MASKED = -1000000000.0
BF = jnp.bfloat16
F32 = jnp.float32


def dot(a, b, ca, cb):
    return lax.dot_general(a, b, (((ca,), (cb,)), ((), ())), preferred_element_type=F32)


def rotary(values, cosine, sine):
    half = values.shape[-1] // 2
    a, b = values[..., :half], values[..., half:]
    return jnp.concatenate([a * cosine - b * sine, b * cosine + a * sine], axis=-1)


def norm_parts(values):
    factor = lax.rsqrt(jnp.mean(values * values, axis=-1, keepdims=True) + EPS)
    return factor, values * factor


def norm_back(grad_in, gain, factor, normed):
    scaled = grad_in * gain
    return factor * (scaled - normed * jnp.mean(scaled * normed, axis=-1, keepdims=True))


def whole(*shape_dtypes):
    return [pl.BlockSpec(memory_space=pltpu.VMEM) for _ in shape_dtypes]


def call(kernel, scalars, arrays, outs, flops, scratch=(), mib=52, fetched=(), landing=()):
    specs = [pl.BlockSpec(memory_space=pltpu.SMEM)] * len(scalars) + whole(*arrays)
    specs += [pl.BlockSpec(memory_space=pl.ANY)] * len(fetched)
    arrays = [*arrays, *fetched]
    moved = sum(a.size * a.dtype.itemsize for a in arrays) + sum(
        int(np.prod(o.shape)) * o.dtype.itemsize for o in outs
    )
    return pl.pallas_call(
        kernel,
        out_shape=outs,
        in_specs=specs,
        out_specs=whole(*outs),
        scratch_shapes=[
            *[pltpu.VMEM(shape, F32) for shape in scratch],
            *[pltpu.VMEM(shape, BF) for shape in landing],
            *([pltpu.SemaphoreType.DMA((len(fetched),))] if fetched else []),
        ],
        compiler_params=pltpu.CompilerParams(vmem_limit_bytes=mib * 1024 * 1024),
        cost_estimate=pl.CostEstimate(flops=int(flops), bytes_accessed=moved, transcendentals=0),
    )(*scalars, *arrays)


def sds(shape, dtype):
    return jax.ShapeDtypeStruct(shape, dtype)


def turn(x, cosine, sine):
    tiles = []
    low = lax.broadcasted_iota(jnp.int32, (1, 128), 1) % HEAD_DIM < HEAD_DIM // 2
    for t in range(x.shape[1] // 128):
        part = x[:, 128 * t : 128 * t + 128]
        other = jnp.where(low, pltpu.roll(part, 96, 1), pltpu.roll(part, 32, 1))
        tiles.append(part * cosine + other * sine)
    return tiles


def turn_kv(x, cosine, sine):
    lane = lax.broadcasted_iota(jnp.int32, (1, 128), 1)
    first, second = turn(x[:, :256], cosine, sine)
    second = jnp.where(lane < KW - 128, second, x[:, 128:256])
    return jnp.concatenate([first, second, x[:, 256:]], axis=1)


def tables(seq, order, cos_ref, sin_ref):
    cosine = jnp.concatenate([cos_ref[seq ^ o] for o in order], axis=0)
    sine = jnp.concatenate([sin_ref[seq ^ o] for o in order], axis=0)
    return cosine, sine


def heads_to_rows(x, g):
    return jnp.concatenate(
        [x[:, HEAD_DIM * h : HEAD_DIM * (h + 1)] for h in range(GROUP * g, GROUP * (g + 1))], axis=0
    )


def rows_to_heads(parts, length):
    return jnp.concatenate(
        [p[length * r : length * (r + 1)] for p in parts for r in range(GROUP)], axis=1
    )


def attention_forward(order, length, seq_ref, blocks, wq, wkv, bq, bkv, gain, cos, sin, mask,
                      att_o, q_o, k_o, v_o):
    seq = seq_ref[0]
    cosine, sine = tables(seq, order, cos, sin)
    width = gain.shape[1]
    for b in range(blocks.shape[1] // length):
        x = blocks[:, b * length : (b + 1) * length, :width].astype(F32)
        x = x.reshape(len(order) * length, width)
        first = (norm_parts(x)[1] * gain[...]).astype(BF)
        kv = dot(first, wkv[...], 1, 0) + bkv[...]
        q = dot(first[:length], wq[...], 1, 0) + bq[...]
        q = jnp.concatenate(turn(q, cosine[:length], sine[:length]), axis=1).astype(BF)
        q = q * jnp.asarray(HEAD_DIM ** (-0.5), BF)
        kv = turn_kv(kv, cosine, sine).astype(BF)
        allowed = jnp.concatenate([mask[b]] * GROUP, axis=0) > 0.0
        parts = []
        for g in range(KV_HEADS):
            qg = heads_to_rows(q, g)
            kg = kv[:, HEAD_DIM * g : HEAD_DIM * (g + 1)]
            vg = kv[:, KW + HEAD_DIM * g : KW + HEAD_DIM * (g + 1)]
            q_o[b, g] = qg
            k_o[b, g] = kg
            v_o[b, g] = vg
            scores = jnp.where(allowed, dot(qg, kg, 1, 1), MASKED)
            top = jnp.max(scores, axis=-1, keepdims=True)
            e = jnp.exp(scores - top)
            total = jnp.sum(e, axis=-1, keepdims=True)
            probs = (e * (1.0 / total)).astype(BF)
            parts.append(dot(probs, vg, 1, 0))
        att_o[b * length : (b + 1) * length, :] = rows_to_heads(parts, length).astype(BF)


def feed_forward(attended, source, wo, wgu, wd, gain, cot, weight,
                 out_o, down_o, gu_o, mid_o, wout_o, attg_o, gain_o):
    units = wd.shape[0]
    step = units // 3
    att = attended[...]
    middle = source[...].astype(F32) + dot(att, wo[...], 1, 0)
    scale_two, normed = norm_parts(middle)
    g2 = gain[...]
    second = (normed * g2).astype(BF)
    out_grad = cot[...].astype(F32) * weight[...]
    feed_grad = out_grad.astype(BF)
    feed = None
    back = None
    for j in range(0, units, step):
        wg = wgu[:, j : j + step]
        wu = wgu[:, units + j : units + j + step]
        wdj = wd[j : j + step, :]
        gate = dot(second, wg, 1, 0)
        up = dot(second, wu, 1, 0)
        sig = jax.nn.sigmoid(gate)
        act = gate * sig
        product = (act * up).astype(BF)
        part = dot(product, wdj, 1, 0)
        feed = part if feed is None else feed + part
        down_o[j : j + step, :] = dot(product, feed_grad, 0, 0).astype(BF)
        pgrad = dot(feed_grad, wdj, 1, 1)
        ggrad = (pgrad * up * (sig * (1.0 + gate * (1.0 - sig)))).astype(BF)
        ugrad = (pgrad * act).astype(BF)
        gu_o[:, j : j + step] = dot(second, ggrad, 0, 0).astype(BF)
        gu_o[:, units + j : units + j + step] = dot(second, ugrad, 0, 0).astype(BF)
        part = dot(ggrad, wg, 1, 1) + dot(ugrad, wu, 1, 1)
        back = part if back is None else back + part
    out_o[...] = (middle + feed).astype(BF)
    gain_o[...] = jnp.sum(back * normed, axis=0, keepdims=True)
    middle_grad = out_grad + norm_back(back, g2, scale_two, normed)
    mid_o[...] = middle_grad
    branch = middle_grad.astype(BF)
    wout_o[...] = dot(att, branch, 0, 0).astype(BF)
    attg_o[...] = dot(branch, wo[...], 1, 1).astype(BF)


def attention_backward(order, length, seq_ref, blocks, wq, wkv, gain, cos, sin, mask, q_i, k_i, v_i,
                       attg, dq_o, dkv_o, wgrad_o, bias_o, gain_o):
    seq = seq_ref[0]
    cosine, sine = tables(seq, order, cos, sin)
    width = gain.shape[1]
    q_wgrad = kv_wgrad = bias_q = bias_kv = gain_sum = None
    for b in range(blocks.shape[1] // length):
        x = blocks[:, b * length : (b + 1) * length, :width].astype(F32)
        x = x.reshape(len(order) * length, width)
        normed = norm_parts(x)[1]
        first = (normed * gain[...]).astype(BF)
        allowed = jnp.concatenate([mask[b]] * GROUP, axis=0) > 0.0
        ag = attg[b * length : (b + 1) * length, :]
        dqs, dks, dvs = [], [], []
        for g in range(KV_HEADS):
            qg, kg, vg = q_i[b, g], k_i[b, g], v_i[b, g]
            agg = heads_to_rows(ag, g)
            scores = jnp.where(allowed, dot(qg, kg, 1, 1), MASKED)
            e = jnp.exp(scores - jnp.max(scores, axis=-1, keepdims=True))
            p = e * (1.0 / jnp.sum(e, axis=-1, keepdims=True))
            dvs.append(dot(p.astype(BF), agg, 0, 0))
            pg = dot(agg, vg, 1, 1)
            inner = jnp.sum(p * pg, axis=-1, keepdims=True)
            ds = (p * (pg - inner)).astype(BF)
            dqs.append(dot(ds, kg, 1, 0) * HEAD_DIM ** (-0.5))
            dks.append(dot(ds, qg, 0, 0))
        dq = rows_to_heads(dqs, length)
        dq = jnp.concatenate([dq, jnp.zeros((length, 64), F32)], axis=1)
        dq = jnp.concatenate(turn(dq, cosine[:length], -sine[:length]), axis=1).astype(BF)
        dkv = jnp.concatenate(dks + dvs, axis=1)
        dkv = turn_kv(dkv, cosine, -sine).astype(BF)
        dq_o[b * length : (b + 1) * length, :] = dq
        for r in range(len(order)):
            dkv_o[r, b * length : (b + 1) * length, :] = dkv[r * length : (r + 1) * length, :]
        wq_part = dot(first[:length], dq, 0, 0)
        wkv_part = dot(first, dkv, 0, 0)
        bq_part = jnp.sum(dq.astype(F32), axis=0, keepdims=True)
        bkv_part = jnp.sum(dkv.astype(F32), axis=0, keepdims=True)
        e_kv = dot(dkv, wkv[...], 1, 1) * normed
        e_q = dot(dq[:, :QW], wq[:, :QW], 1, 1) * normed[:length]
        g_part = jnp.sum(e_kv, axis=0, keepdims=True) + jnp.sum(e_q, axis=0, keepdims=True)
        if q_wgrad is None:
            q_wgrad, kv_wgrad, bias_q, bias_kv, gain_sum = wq_part, wkv_part, bq_part, bkv_part, g_part
        else:
            q_wgrad, kv_wgrad = q_wgrad + wq_part, kv_wgrad + wkv_part
            bias_q, bias_kv, gain_sum = bias_q + bq_part, bias_kv + bkv_part, gain_sum + g_part
    wgrad_o[...] = jnp.concatenate([q_wgrad[:, :QW], kv_wgrad], axis=1).astype(BF)
    bias_o[...] = jnp.concatenate([bias_q[:, :QW], bias_kv], axis=1)
    gain_o[...] = gain_sum


def input_gradient(dq, own, a, b, c, source, mid, wq, wkv, gain, out_o):
    kv = own[...].astype(F32) + a[...].astype(F32) + b[...].astype(F32) + c[...].astype(F32)
    first_grad = dot(dq[:, :QW], wq[:, :QW], 1, 1) + dot(kv.astype(BF), wkv[...], 1, 1)
    scale_one, normed = norm_parts(source[...].astype(F32))
    out_o[...] = mid[...] + norm_back(first_grad, gain[...], scale_one, normed)

def chosen(flag, a, b):
    return jnp.where(flag != 0, b, a)


class Blocks:
    def __init__(self, *refs):
        self.refs = refs
        self.shape = (len(refs),) + refs[0].shape

    def __getitem__(self, key):
        return jnp.stack([ref[key[1:]] for ref in self.refs])


def cut_qkv(core_bit, meta, w_hbm, bias_hbm, gains_hbm, out_o, w, bias, gains, all_s, sems):
    pairs = ((w_hbm, w), (bias_hbm, bias), (gains_hbm, gains))
    copies = [pltpu.make_async_copy(a, b, sems.at[i]) for i, (a, b) in enumerate(pairs)]
    for copy in copies:
        copy.start()
    for copy in copies:
        copy.wait()
    rows = w.shape[0]
    n = bias.shape[1]
    all_s[:rows, :] = w[...].astype(F32)
    all_s[rows:, :] = jnp.zeros((8, w.shape[1]), F32)
    all_s[rows : rows + 1, :n] = bias[...].astype(F32)
    for i in range(2):
        all_s[rows : rows + 1, n + rows * i : n + rows * (i + 1)] = gains[i : i + 1, :].astype(F32)
    half = out_o.shape[0]
    at = pl.multiple_of((meta[0] & core_bit) * half, 8)
    out_o[...] = all_s[pl.ds(at, half), :].astype(BF)


def first_forward(order, length, d_rows, n_bias, meta, b0, b1, b2, b3, a00, a10, a01, a11, cos, sin, mask,
                  att_o, q_o, k_o, v_o, w_o, gain_o, w_s, b_s):
    blocks = Blocks(b0, b1, b2, b3)
    core, x = meta[0] & 1, meta[1] & 1
    cut = a00.shape[2]
    for x_rel, c_rel, piece in ((0, 0, a00), (1, 0, a10), (0, 1, a01), (1, 1, a11)):
        for z0 in range(2):
            for z1 in range(2):
                at = (z1 * 4 + z0 * 2 + (x ^ x_rel)) * 2 * cut + (core ^ c_rel) * cut
                w_s[pl.ds(pl.multiple_of(at, 8), cut), :] = piece[z0, z1].astype(F32)
    n_f = w_s.shape[0] // (2 * cut)
    starts = [2 * cut * f for f in range(n_f)]
    w_o[...] = jnp.concatenate([w_s[at : at + d_rows, :] for at in starts], axis=0).astype(BF)
    lines = [w_s[at + d_rows : at + d_rows + 1, :] for at in starts]
    b_s[...] = jnp.concatenate([line[:, :n_bias] for line in lines], axis=1)
    for i in range(2):
        at = n_bias + d_rows * i
        gain_o[i : i + 1, :] = jnp.concatenate([line[:, at : at + d_rows] for line in lines], axis=1)
    wide = QW + 64
    attention_forward(order, length, meta, blocks, w_o[:, :wide], w_o[:, QW:], b_s[:, :wide], b_s[:, QW:],
                      gain_o[0:1, :], cos, sin, mask, att_o, q_o, k_o, v_o)


def turned(out, value):
    length = out.shape[2]
    for b in range(out.shape[0]):
        out[b] = value[length * b : length * (b + 1)].T.astype(out.dtype)


def rel(meta, f):
    r = f ^ meta[1]
    return r & 1, (r >> 1) & 1, (r >> 2) & 1


def fetch_pieces(meta, refs, b_s, g_s, sems):
    core, y, x, z0 = meta[0] & 1, (meta[0] >> 1) & 1, meta[1] & 1, (meta[1] >> 1) & 1
    copies = []
    for i in range(8):
        at = (z0 ^ (i >> 2), x ^ ((i >> 1) & 1), core ^ (i & 1))
        copies.append(pltpu.make_async_copy(refs[i], b_s.at[at], sems.at[i]))
    for i in range(8):
        at = (y ^ ((i >> 1) & 1), core ^ (i & 1), x ^ (i >> 2))
        copies.append(pltpu.make_async_copy(refs[8 + i], g_s.at[at], sems.at[8 + i]))
    for copy in copies:
        copy.start()
    return copies


def feed_forward_pieces(d_rows, ff_rows, meta, attended, source, gains, cot, weight, *refs):
    out_o, ak_o, ag_o, bk_o, bg_o, dk_o, dg_o, mid_o, attg_o, gain_o, down_s, wout_s, b_s, g_s, sems = refs[16:]
    copies = fetch_pieces(meta, refs, b_s, g_s, sems)
    core, y = meta[0] & 1, (meta[0] >> 1) & 1
    part_d = ff_rows // 4
    part_o = d_rows // 3
    cut = b_s.shape[4] - ff_rows // 2
    half = g_s.shape[-1] // 2
    for copy in copies[:8]:
        copy.wait()
    wo = []
    for f in range(8):
        for c in range(2):
            rows = b_s[(f >> 1) & 1, f & 1, c, f >> 2, ff_rows // 2 :, :].astype(F32)
            wo.append(rows if c == 0 else rows[: d_rows - cut])
    wo = jnp.concatenate(wo, axis=0).astype(BF)
    att = attended[...]
    middle = source[...].astype(F32) + dot(att, wo, 1, 0)
    scale_two, normed = norm_parts(middle)
    g2 = gains[1:2, :]
    second = (normed * g2).astype(BF)
    out_grad = cot[...].astype(F32) * weight[...]
    feed_grad = out_grad.astype(BF)
    for copy in copies[8:]:
        copy.wait()
    feed = back = None
    for c_rel in (1, 0):
        h = core ^ c_rel
        weights = []
        for yy in range(2):
            rows = [g_s[yy, h, f & 1, (f >> 1) & 1, f >> 2].astype(F32) for f in range(8)]
            weights.append(jnp.concatenate(rows, axis=0).astype(BF))
        wg, wu = weights
        wd = [b_s[i >> 1, i & 1, c, h, : ff_rows // 2, :] for i in range(4) for c in range(2)]
        wd = jnp.concatenate(wd, axis=0)
        gate = dot(second, wg, 1, 0)
        up = dot(second, wu, 1, 0)
        sig = jax.nn.sigmoid(gate)
        act = gate * sig
        product = (act * up).astype(BF)
        part = dot(product, wd, 1, 0)
        feed = part if feed is None else feed + part
        down_s[...] = dot(product, feed_grad, 0, 0)
        pgrad = dot(feed_grad, wd, 1, 1)
        ggrad = (pgrad * up * (sig * (1.0 + gate * (1.0 - sig)))).astype(BF)
        ugrad = (pgrad * act).astype(BF)
        part = dot(ggrad, wg, 1, 1) + dot(ugrad, wu, 1, 1)
        back = part if back is None else back + part
        for i in range(4):
            x, z0, z1 = rel(meta, 4 * h + i)
            for yy in range(2):
                for c_to, to in ((0, dk_o), (1, dg_o)):
                    at = pl.multiple_of(i * ff_rows + (yy * 2 + (core ^ c_to)) * part_d, 16)
                    to[y ^ yy, x, z0, z1, :part_d, :] = down_s[pl.ds(at, part_d), :].astype(BF)
        to_a, to_b = (ag_o, bg_o) if c_rel else (ak_o, bk_o)
        for yy, grad in ((0, ggrad), (1, ugrad)):
            wgrad = dot(second, grad, 0, 0)
            for f in range(8):
                x, z0, z1 = rel(meta, f)
                block = wgrad[d_rows * f : d_rows * (f + 1), :].astype(BF)
                to_a[x, z0, z1, yy] = block[:, :half]
                to_b[z0, z1, x, yy] = block[:, half:]
    turned(out_o, middle + feed)
    gain_o[...] = jnp.sum(back * normed, axis=0, keepdims=True)
    middle_grad = out_grad + norm_back(back, g2, scale_two, normed)
    mid_o[...] = middle_grad
    branch = middle_grad.astype(BF)
    attg_o[...] = dot(branch, wo, 1, 1).astype(BF)
    wout = dot(att, branch, 0, 0)
    for f in range(8):
        wout_s[f, :d_rows, :] = wout[d_rows * f : d_rows * (f + 1), :]
        wout_s[f, d_rows:, :] = jnp.zeros((part_o, wout.shape[1]), F32)
    for f in range(8):
        x, z0, z1 = rel(meta, f)
        for yy in range(2):
            for c_to, to in ((0, dk_o), (1, dg_o)):
                at = pl.multiple_of((yy * 2 + (core ^ c_to)) * part_o, 8)
                to[y ^ yy, x, z0, z1, part_d:, :] = wout_s[f, pl.ds(at, part_o), :].astype(BF)


def attention_backward_pieces(order, length, d_rows, meta, b0, b1, b2, b3, w, gains, cos, sin, mask, q_i, k_i, v_i,
                              attg, gain_two, dq_o, dk_o, dg_o, rk_o, rg_o, w_s, bias_s, gain_s, small_s):
    blocks = Blocks(b0, b1, b2, b3)
    half = len(order) // 2

    class Pieces:
        def __setitem__(self, key, value):
            ref = dk_o if key[0] < half else dg_o
            ref[(key[0] % half,) + key[1:]] = value

    class Wgrad:
        def __setitem__(self, key, value):
            w_s[:, : 2 * KW] = value[:, QW:].astype(F32)
            w_s[:, 2 * KW : 2 * KW + QW] = value[:, :QW].astype(F32)
            w_s[:, 2 * KW + QW :] = jnp.zeros((value.shape[0], 64), F32)

    wide = QW + 64
    attention_backward(order, length, meta, blocks, w[:, :wide], w[:, QW:], gains[0:1, :], cos, sin, mask,
                       q_i, k_i, v_i, attg, dq_o, Pieces(), Wgrad(), bias_s, gain_s)
    n_f = small_s.shape[0]
    qk, v = (QW + KW) // n_f, KW // n_f
    bias, g1, g2 = bias_s[...], gain_s[...], gain_two[...]
    for f in range(n_f):
        line = jnp.concatenate(
            [
                bias[:, qk * f : qk * (f + 1)],
                bias[:, QW + KW + v * f : QW + KW + v * (f + 1)],
                g1[:, d_rows * f : d_rows * (f + 1)],
                jnp.zeros((1, 256 - qk - v - d_rows), F32),
                g2[:, d_rows * f : d_rows * (f + 1)],
                jnp.zeros((1, 768 - d_rows), F32),
            ],
            axis=1,
        )
        small_s[f] = jnp.broadcast_to(line, (8, 1024))
    core, y = meta[0] & 1, (meta[0] >> 1) & 1
    for f in range(n_f):
        x, z0, z1 = rel(meta, f)
        for yy in range(2):
            for c_to, to in ((0, rk_o), (1, rg_o)):
                at = pl.multiple_of((yy * 2 + (core ^ c_to)) * 256, 256)
                block = [w_s[d_rows * f : d_rows * (f + 1), pl.ds(at, 256)], small_s[f, :, pl.ds(at, 256)]]
                to[x, z0, z1, yy] = jnp.concatenate(block, axis=0).astype(BF)


def input_gradient_two(dq, own, other, source, mid, w, gains, out_o):
    kv = (own[...].astype(F32) + other[...].astype(F32)).astype(BF)
    first_grad = dot(dq[:, :QW], w[:, :QW], 1, 1) + dot(kv, w[:, QW:], 1, 1)
    scale_one, normed = norm_parts(source[...].astype(F32))
    turned(out_o, mid[...] + norm_back(first_grad, gains[0:1, :], scale_one, normed))


def place_gate(meta, near, far, out_o, parts=1, part=0):
    core = meta[0] & 1
    n = near.shape[2]
    for pieces, c_rel in ((near, 0), (far, 1)):
        for yy in range(2):
            at = pl.multiple_of(((yy * 2 + (core ^ c_rel)) * parts + part) * n, 128)
            out_o[:, pl.ds(at, n)] = pieces[yy].astype(F32)


def place_down(part_d, meta, p00, p10, p01, p11, out_o, wout_o):
    seq = meta[0]
    part_o = p00.shape[0] - part_d
    for piece, o in ((p00[...], 0), (p10[...], 2), (p01[...], 1), (p11[...], 3)):
        piece = piece.astype(F32)
        to = seq ^ o
        out_o[pl.ds(pl.multiple_of(to * part_d, 16), part_d), :] = piece[:part_d]

        @pl.when(to < 3)
        def _():
            wout_o[pl.ds(pl.multiple_of(to * part_o, 8), part_o), :] = piece[part_d:]


def place_qkv(qk, v, meta, near, far, w_o, bqk_o, bv_o, gains_o, all_s):
    place_gate(meta, near, far, all_s)
    d_rows = w_o.shape[0]
    w_o[:, :QW] = all_s[:d_rows, 2 * KW : 2 * KW + QW]
    w_o[:, QW:] = all_s[:d_rows, : 2 * KW]
    line = all_s[d_rows : d_rows + 1, :]
    bqk_o[...] = line[:, :qk]
    bv_o[...] = line[:, qk : qk + v]
    gains_o[0:1, :] = line[:, qk + v : qk + v + d_rows]
    gains_o[1:2, :] = line[:, 256 : 256 + d_rows]


def place_all(part_d, qk, v, meta, a_near, a_far, b_near, b_far, d0, d1, d2, d3, r_near, r_far,
              gate_o, down_o, wout_o, w_o, bqk_o, bv_o, gains_o, all_s):
    place_gate(meta, a_near, a_far, gate_o, 2, 0)
    place_gate(meta, b_near, b_far, gate_o, 2, 1)
    place_down(part_d, meta, d0, d1, d2, d3, down_o, wout_o)
    place_qkv(qk, v, meta, r_near, r_far, w_o, bqk_o, bv_o, gains_o, all_s)


class Net:
    def __init__(self, n_fsdp, n_seq):
        self.n_fsdp, self.n_seq = n_fsdp, n_seq
        self.total = n_fsdp * n_seq
        f, s = lax.axis_index("fsdp"), lax.axis_index("seq")
        self.index = f * n_seq + s
        self.seq_bits = [1 << b for b in range(n_seq.bit_length() - 1)]
        self.fsdp_bits = [n_seq << b for b in range(n_fsdp.bit_length() - 1)]

    def swap(self, value, mask):
        pairs = [(i, i ^ mask) for i in range(self.total)]
        return lax.ppermute(value, ("fsdp", "seq"), pairs)

    def bit(self, mask):
        return (self.index & mask) != 0

    def both(self, mine, mask, axis, other=None):
        other = self.swap(mine, mask) if other is None else other
        high = self.bit(mask)
        return jnp.stack([jnp.where(high, other, mine), jnp.where(high, mine, other)], axis=axis)

    def half(self, value, mask, axis):
        return lax.dynamic_index_in_dim(
            value, self.bit(mask).astype(jnp.int32), axis, keepdims=False
        )

    def add_half(self, value, mask, axis):
        mine = self.bit(mask).astype(jnp.int32)
        keep = lax.dynamic_index_in_dim(value, mine, axis, keepdims=False)
        give = lax.dynamic_index_in_dim(value, 1 - mine, axis, keepdims=False)
        got = self.swap(give, mask)
        return (keep.astype(F32) + got.astype(F32)).astype(value.dtype)

    def gather_fsdp(self, value):
        for step, mask in enumerate(reversed(self.fsdp_bits)):
            value = self.both(value, mask, step)
        return value

    def scatter_fsdp(self, value, first_axis=0):
        count = len(self.fsdp_bits)
        for step, mask in enumerate(self.fsdp_bits):
            value = self.add_half(value, mask, first_axis + count - 1 - step)
        return value


def on_device(
    hidden, w_qkv, b_qkv, w_out, w_gate_up, w_down, norm_gains, segment_ids, token_counts, cotangent,
    n_fsdp, n_seq,
):
    net = Net(n_fsdp, n_seq)
    micro, batch, length, width = hidden.shape
    full_length = length * n_seq
    tokens_micro = batch * n_fsdp * full_length
    scale = HEAD_DIM ** (-0.5)
    rows = micro * batch * length
    d_rows = w_qkv.shape[0]
    ff_rows = w_down.shape[0]
    units = w_gate_up.shape[1] // 2
    qkv_w = w_qkv.shape[1]
    core = net.seq_bits[0]
    f_lead = (2,) * len(net.fsdp_bits)

    ids = segment_ids.reshape(rows, 1).astype(BF)
    block = jnp.concatenate(
        [hidden.reshape(rows, width), jnp.broadcast_to(ids, (rows, 64))], axis=1
    )
    blocks = block[None]
    for mask in reversed(net.seq_bits):
        blocks = jnp.concatenate([blocks, net.swap(blocks, mask)], axis=0)
    order = [0]
    for mask in reversed(net.seq_bits):
        order = order + [o ^ mask for o in order]
    seq_index = lax.axis_index("seq")
    block_ids = [seq_index ^ o for o in order]

    pad_rows = -(d_rows + 1) % 16 + 1
    extra = jnp.zeros((pad_rows, qkv_w), BF)
    small = jnp.concatenate([b_qkv, norm_gains.reshape(-1)])
    extra = extra.at[0, : small.shape[0]].set(small)
    shard_a = jnp.concatenate([w_qkv, extra], axis=0).reshape(2, -1, qkv_w)
    got_a = net.gather_fsdp(net.half(shard_a, core, 0))
    full_a = net.both(got_a, core, len(f_lead)).reshape(n_fsdp, d_rows + pad_rows, qkv_w)
    wf_qkv = full_a[:, :d_rows].reshape(n_fsdp * d_rows, qkv_w)
    smalls = full_a[:, d_rows]
    n_bias = b_qkv.shape[0]
    bias = smalls[:, :n_bias].reshape(-1).astype(F32)
    gains = smalls[:, n_bias : n_bias + 2 * d_rows].reshape(n_fsdp, 2, d_rows).astype(F32)
    gain_one = gains[:, 0].reshape(-1)
    gain_two = gains[:, 1].reshape(-1)

    pad_b = -(d_rows + ff_rows) % 16
    shard_b = jnp.concatenate([w_out, w_down, jnp.zeros((pad_b, width), BF)], axis=0)
    shard_b = shard_b.reshape(2, -1, width)
    got_b = net.gather_fsdp(net.half(shard_b, core, 0))

    parts = n_seq
    shard_c = w_gate_up.reshape(d_rows, parts, -1)
    got_c = net.gather_fsdp(lax.dynamic_index_in_dim(shard_c, seq_index, 1, keepdims=False))
    full_b = net.both(got_b, core, len(f_lead)).reshape(n_fsdp, -1, width)
    wf_out = full_b[:, :d_rows].reshape(n_fsdp * d_rows, width)
    wf_down = full_b[:, d_rows : d_rows + ff_rows].reshape(n_fsdp * ff_rows, width)
    got_c = got_c.reshape(n_fsdp * d_rows, -1)
    for mask in reversed(net.seq_bits):
        got_c = net.both(got_c, mask, got_c.ndim - 1)
    wf_gate_up = got_c.reshape(n_fsdp * d_rows, 2 * units)

    places = np.arange(full_length, dtype=np.float32)
    speeds = np.power(ROPE_BASE, -2.0 * np.arange(HEAD_DIM // 2, dtype=np.float32) / HEAD_DIM)
    angles = places[:, None] * speeds.astype(np.float32)[None, :]
    cos_t = np.tile(np.cos(angles), (1, 4)).reshape(n_seq, length, 128)
    sin_t = np.concatenate([-np.sin(angles), np.sin(angles)] * 2, axis=1).reshape(n_seq, length, 128)
    cos_t, sin_t = jnp.asarray(cos_t, F32), jnp.asarray(sin_t, F32)
    seqs = micro * batch
    seg_all = blocks[..., width].reshape(n_seq, seqs, length).transpose(1, 0, 2)
    own_places = seq_index * length + jnp.arange(length, dtype=jnp.int32)
    key_places = jnp.stack(block_ids)[:, None] * length + jnp.arange(length, dtype=jnp.int32)
    allowed = (seg_all[:, 0, :, None] == seg_all.reshape(seqs, 1, -1)) & (
        own_places[None, :, None] >= key_places.reshape(1, 1, -1)
    )
    allowed = allowed.astype(F32)
    seq_scalar = seq_index.astype(jnp.int32).reshape(1)
    wq, wkv = wf_qkv[:, : QW + 64], wf_qkv[:, QW:]
    gain_one, gain_two = gain_one[None], gain_two[None]
    source = hidden.reshape(rows, width)
    n_all = n_seq * rows
    attended, q_s, k_s, v_s = call(
        functools.partial(attention_forward, order, length),
        [seq_scalar],
        [blocks, wq, wkv, bias[None, : QW + 64], bias[None, QW:], gain_one, cos_t, sin_t, allowed],
        [
            sds((rows, QW), BF),
            sds((seqs, KV_HEADS, GROUP * length, HEAD_DIM), BF),
            sds((seqs, KV_HEADS, full_length, HEAD_DIM), BF),
            sds((seqs, KV_HEADS, full_length, HEAD_DIM), BF),
        ],
        2 * n_all * width * 2 * KW + 2 * rows * width * QW + 4 * rows * full_length * QW,
    )

    weight = tokens_micro / token_counts.astype(F32)
    weight = jnp.repeat(weight, batch * length)[:, None]
    block_out, down_grad, gate_up_wgrad, middle_grad, out_wgrad, attended_grad, gain_two_grad = call(
        feed_forward,
        [],
        [attended, source, wf_out, wf_gate_up, wf_down, gain_two, cotangent.reshape(rows, width), weight],
        [
            sds((rows, width), BF),
            sds((units, width), BF),
            sds((width, 2 * units), BF),
            sds((rows, width), F32),
            sds((QW, width), BF),
            sds((rows, QW), BF),
            sds((1, width), F32),
        ],
        6 * rows * width * 3 * units + 6 * rows * width * QW,
    )
    block_out = block_out.reshape(hidden.shape)

    def seq_axes(value, axis, masks):
        for mask in masks:
            value = net.add_half(value, mask, axis)
        return value

    quarter = (2,) * len(net.seq_bits)
    n_f = len(f_lead)
    red_down = down_grad.reshape(f_lead + quarter + (ff_rows // n_seq, width))
    for step, mask in enumerate(net.seq_bits):
        red_down = net.add_half(red_down, mask, n_f + len(quarter) - 1 - step)
    red_down = net.scatter_fsdp(red_down)

    red_gate = gate_up_wgrad.reshape(f_lead + (d_rows,) + quarter + (2 * units // n_seq,))
    red_gate = net.add_half(red_gate, core, n_f + len(quarter))
    red_gate = net.add_half(red_gate, net.fsdp_bits[0], n_f - 1)
    for step, mask in enumerate(net.seq_bits[1:]):
        red_gate = net.add_half(red_gate, mask, n_f - 1 + len(quarter) - 1 - step)
    for step, mask in enumerate(net.fsdp_bits[1:]):
        red_gate = net.add_half(red_gate, mask, n_f - 2 - step)

    dq, dkv, qkv_wgrad, bias_grad, gain_one_grad = call(
        functools.partial(attention_backward, order, length),
        [seq_scalar],
        [blocks, wq, wkv, gain_one, cos_t, sin_t, allowed, q_s, k_s, v_s, attended_grad],
        [
            sds((rows, QW + 64), BF),
            sds((n_seq, rows, 2 * KW), BF),
            sds((width, qkv_w), BF),
            sds((1, qkv_w), F32),
            sds((1, width), F32),
        ],
        4 * n_all * width * 2 * KW + 4 * rows * width * QW + 10 * rows * full_length * QW,
    )
    kv_parts = [dkv[0]]
    for place, mask_bits in enumerate(order):
        if mask_bits:
            kv_parts.append(net.swap(dkv[place], mask_bits))
    (hidden_grad,) = call(
        input_gradient,
        [],
        [dq, *kv_parts, source, middle_grad, wq, wkv, gain_one],
        [sds((rows, width), F32)],
        2 * rows * width * qkv_w,
    )
    hidden_grad = hidden_grad.reshape(hidden.shape)
    bias_grad, gain_one_grad, gain_two_grad = bias_grad[0], gain_one_grad[0], gain_two_grad[0]

    qk_rows, v_rows = (QW + KW) // n_fsdp, KW // n_fsdp
    small_grads = jnp.concatenate(
        [
            bias_grad[: QW + KW].reshape(n_fsdp, qk_rows),
            bias_grad[QW + KW :].reshape(n_fsdp, v_rows),
            gain_one_grad.reshape(n_fsdp, d_rows),
            gain_two_grad.reshape(n_fsdp, d_rows),
        ],
        axis=1,
    ).astype(BF)
    wide = qkv_w + width
    small_pad = jnp.zeros((n_fsdp, pad_rows, wide), BF)
    small_pad = small_pad.at[:, 0, : small_grads.shape[1]].set(small_grads)
    rest = jnp.concatenate([qkv_wgrad, out_wgrad], axis=1)
    rest = jnp.concatenate([rest.reshape(n_fsdp, d_rows, wide), small_pad], axis=1)
    rest = rest.reshape(f_lead + (d_rows + pad_rows,) + quarter + (wide // n_seq,))
    for step, mask in enumerate(net.seq_bits):
        rest = net.add_half(rest, mask, n_f + 1 + len(quarter) - 1 - step)
    rest = net.scatter_fsdp(rest)

    def seq_back(value, axis):
        for step, mask in enumerate(reversed(net.seq_bits)):
            value = net.both(value, mask, axis + step)
        return value

    out_down = seq_back(red_down, 0).reshape(ff_rows, width).astype(F32)
    out_gate = seq_back(red_gate, 1).reshape(d_rows, 2 * units).astype(F32)
    out_rest = seq_back(rest, 1).reshape(d_rows + pad_rows, wide).astype(F32)
    line = out_rest[d_rows]
    edge = qk_rows + v_rows
    return (
        block_out,
        hidden_grad,
        out_rest[:d_rows, :qkv_w],
        line[:qk_rows],
        line[qk_rows:edge],
        out_rest[:d_rows, qkv_w:],
        out_gate,
        out_down,
        line[edge : edge + 2 * d_rows].reshape(2, d_rows),
    )


def after(value, *others):
    return lax.optimization_barrier((value, *others))[0]


def rope_tables(full_length, n_seq):
    places = np.arange(full_length, dtype=np.float32)
    speeds = np.power(ROPE_BASE, -2.0 * np.arange(HEAD_DIM // 2, dtype=np.float32) / HEAD_DIM)
    angles = places[:, None] * speeds.astype(np.float32)[None, :]
    cos_t = np.tile(np.cos(angles), (1, 4)).reshape(n_seq, -1, 128)
    sin_t = np.concatenate([-np.sin(angles), np.sin(angles)] * 2, axis=1).reshape(n_seq, -1, 128)
    return jnp.asarray(cos_t, F32), jnp.asarray(sin_t, F32)


def on_device_tiled(
    hidden, w_qkv, b_qkv, w_out, w_gate_up, w_down, norm_gains, segment_ids, token_counts, cotangent,
    n_fsdp, n_seq,
):
    net = Net(n_fsdp, n_seq)
    micro, batch, length, width = hidden.shape
    full_length = length * n_seq
    tokens_micro = batch * n_fsdp * full_length
    rows = micro * batch * length
    seqs = micro * batch
    d_rows, qkv_w = w_qkv.shape
    ff_rows = w_down.shape[0]
    units = w_gate_up.shape[1] // 2
    n_bias = b_qkv.shape[0]
    core, ybit = net.seq_bits
    xbit, znear, zfar = net.fsdp_bits
    order = [0, 2, 1, 3]
    seq_index = lax.axis_index("seq")
    meta = jnp.stack([seq_index, lax.axis_index("fsdp")]).astype(jnp.int32)
    source = hidden.reshape(rows, width)

    small = [w_qkv, b_qkv[None], norm_gains]
    a0 = pl.pallas_call(
        functools.partial(cut_qkv, core),
        out_shape=sds(((d_rows + 8) // 2, qkv_w), BF),
        in_specs=[pl.BlockSpec(memory_space=pltpu.SMEM)] + [pl.BlockSpec(memory_space=pl.ANY)] * 3,
        out_specs=pl.BlockSpec(memory_space=pltpu.VMEM),
        scratch_shapes=[
            *[pltpu.VMEM(v.shape, BF) for v in small],
            pltpu.VMEM((d_rows + 8, qkv_w), F32),
            pltpu.SemaphoreType.DMA((3,)),
        ],
        compiler_params=pltpu.CompilerParams(vmem_limit_bytes=52 * 1024 * 1024),
    )(meta, *small)
    a1 = net.both(a0, zfar, 0)

    ids = segment_ids.reshape(rows, 1).astype(BF)
    block = jnp.concatenate([source, jnp.broadcast_to(ids, (rows, 64))], axis=1)
    block = after(block, a0)
    block_y = net.swap(block, ybit)
    block_c = net.swap(block, core)

    quarter = 2 * units // n_seq
    gu0 = lax.dynamic_slice_in_dim(after(w_gate_up, a0), seq_index * quarter, quarter, axis=1)
    half_b = jnp.concatenate(
        [
            w_down.reshape(2, ff_rows // 2, width),
            jnp.concatenate([w_out, jnp.zeros((8, width), BF)], axis=0).reshape(2, -1, width),
        ],
        axis=1,
    )
    a2 = net.both(a1, znear, 0)
    b0 = net.half(after(half_b, a1), core, 0)
    a_x = net.swap(a2, xbit)
    a_c = net.swap(a2, core)
    gu1 = net.both(gu0, zfar, 0)
    gu2 = net.both(after(gu1, a2), znear, 0)
    block_yc = net.swap(block_y, core)
    a_xc = net.swap(a_x, core)
    gu_x = net.swap(gu2, xbit)
    gu_y = net.swap(gu2, ybit)
    gu_c = net.swap(gu2, core)
    b1 = net.swap(after(b0, gu2), zfar)
    a_xc = after(a_xc, gu2)

    cos_t, sin_t = rope_tables(full_length, n_seq)
    block_ids = [seq_index ^ o for o in order]
    blocks = [block, block_y, block_c, block_yc]
    seg_all = jnp.stack([b[:, width].reshape(seqs, length) for b in blocks], axis=1)
    own_places = seq_index * length + jnp.arange(length, dtype=jnp.int32)
    key_places = jnp.stack(block_ids)[:, None] * length + jnp.arange(length, dtype=jnp.int32)
    allowed = (seg_all[:, 0, :, None] == seg_all.reshape(seqs, 1, -1)) & (
        own_places[None, :, None] >= key_places.reshape(1, 1, -1)
    )
    allowed = allowed.astype(F32)
    attended, q_s, k_s, v_s, wf, gains = call(
        functools.partial(first_forward, order, length, d_rows, n_bias),
        [meta],
        [*blocks, a2, a_x, a_c, a_xc, cos_t, sin_t, allowed],
        [
            sds((rows, QW), BF),
            sds((seqs, KV_HEADS, GROUP * length, HEAD_DIM), BF),
            sds((seqs, KV_HEADS, full_length, HEAD_DIM), BF),
            sds((seqs, KV_HEADS, full_length, HEAD_DIM), BF),
            sds((width, qkv_w), BF),
            sds((2, width), F32),
        ],
        1.2e10,
        [(n_fsdp * (d_rows + 8), qkv_w), (1, qkv_w)],
    )
    b1 = net.both(b0, zfar, 0, after(b1, attended))
    b_z = net.swap(b1, znear)
    b_x = net.swap(b1, xbit)
    b_c = net.swap(b1, core)
    gu_y = after(gu_y, b1)
    gu_x = after(gu_x, b1)
    gu_xy = net.swap(gu_x, ybit)
    b_zx = net.swap(b_z, xbit)
    gu_yc = net.swap(gu_y, core)
    gu_xc = net.swap(gu_x, core)
    b_zc = net.swap(b_z, core)
    b_xc = net.swap(b_x, core)
    b_zxc = net.swap(b_zx, core)
    gu_xyc = net.swap(gu_xy, core)
    pieces = [b1, b_c, b_x, b_xc, b_z, b_zc, b_zx, b_zxc]
    pieces += [gu2, gu_c, gu_y, gu_yc, gu_x, gu_xc, gu_xy, gu_xyc]

    weight = tokens_micro / token_counts.astype(F32)
    weight = jnp.repeat(weight, batch * length)[:, None]
    lead = (2, 2, 2, 2)
    cot = cotangent.reshape(rows, width)
    gate_lead = lead + (d_rows, units // 4)
    block_out, a_keep, a_give, b_keep, b_give, down_keep, down_give, middle_grad, attended_grad, gain_two = call(
        functools.partial(feed_forward_pieces, d_rows, ff_rows),
        [meta],
        [attended, source, gains, cot, weight],
        [
            sds((seqs, width, length), BF),
            sds(gate_lead, BF),
            sds(gate_lead, BF),
            sds(gate_lead, BF),
            sds(gate_lead, BF),
            sds(lead + (ff_rows // 4 + d_rows // 3, width), BF),
            sds(lead + (ff_rows // 4 + d_rows // 3, width), BF),
            sds((rows, width), F32),
            sds((rows, QW), BF),
            sds((1, width), F32),
        ],
        1.4e10,
        [(units // 2, width), (n_fsdp, d_rows + d_rows // 3, width)],
        fetched=pieces,
        landing=[(2, 2, 2, 2) + b1.shape[1:], (2, 2, 2, 2, 2, d_rows, units // 2)],
    )
    block_out = block_out.reshape(micro, batch, width, length).swapaxes(2, 3)

    def add(keep, got):
        return (keep.astype(F32) + got.astype(F32)).astype(BF)

    def halves(keep, got):
        return add(keep[0], got[0]), add(keep[1], got[1])

    a_got = net.swap(a_give, core)
    b_got = net.swap(after(b_give, a_got), core)
    down_got = net.swap(after(down_give, a_got), core)
    a, a_give = halves(a_keep, a_got)
    a_got = net.swap(a_give, xbit)
    b, b_give = halves(b_keep, b_got)
    b_got = net.swap(b_give, znear)
    down, down_give = halves(down_keep, down_got)
    attended_grad = after(attended_grad, a_give, b_give, down_give)
    down_got = net.swap(down_give, ybit)

    dq, dkv_keep, dkv_give, rest_keep, rest_give = call(
        functools.partial(attention_backward_pieces, order, length, d_rows),
        [meta],
        [*blocks, wf, gains, cos_t, sin_t, allowed, q_s, k_s, v_s, attended_grad, gain_two],
        [
            sds((rows, QW + 64), BF),
            sds((2, rows, 2 * KW), BF),
            sds((2, rows, 2 * KW), BF),
            sds(lead + (d_rows + 8, 256), BF),
            sds(lead + (d_rows + 8, 256), BF),
        ],
        1.4e10,
        [(width, 1024), (1, qkv_w), (1, width), (n_fsdp, 8, 1024)],
    )
    b, b_give = halves(b, after(b_got, dq))
    a, a_give = halves(a, after(a_got, b_give))
    b_got = net.swap(b_give, zfar)
    a_got = net.swap(a_give, znear)
    down, down_give = halves(down, after(down_got, a_give))
    down_got = net.swap(down_give, xbit)
    rest, rest_give = halves(rest_keep, after(net.swap(rest_give, core), down_give))
    rest_got = net.swap(rest_give, xbit)
    dkv, dkv_give = halves(dkv_keep, after(net.swap(dkv_give, core), rest_give))
    dkv_got = net.swap(dkv_give, ybit)
    a, a_give = halves(a, after(a_got, dkv_give))
    a_got = net.swap(a_give, zfar)
    b, b_give = halves(b, after(b_got, a_give))
    b_got = net.swap(b_give, xbit)
    (hidden_grad,) = call(
        input_gradient_two,
        [],
        [dq, dkv, after(dkv_got, b_give), source, middle_grad, wf, gains],
        [sds((seqs, width, length), F32)],
        3e9,
        mib=16,
    )
    down, down_give = halves(down, after(down_got, hidden_grad))
    hidden_grad = hidden_grad.reshape(micro, batch, width, length).swapaxes(2, 3)
    down_got = net.swap(down_give, znear)
    rest, rest_give = halves(rest, after(rest_got, down_give))
    rest_got = net.swap(rest_give, znear)
    a = add(a, after(a_got, rest_give))
    a_got = net.swap(a, ybit)
    b = add(b, after(b_got, a))
    b_got = net.swap(b, ybit)
    down, down_give = halves(down, after(down_got, b))
    down_got = net.swap(down_give, zfar)
    rest, rest_give = halves(rest, after(rest_got, down_give))
    rest_got = net.swap(rest_give, zfar)
    a = add(a, after(a_got, rest_give))
    a_far = net.swap(a, core)
    b = add(b, b_got)
    b_far = net.swap(b, core)
    down = add(down, after(down_got, a))
    down_y = net.swap(down, ybit)
    down_c = net.swap(down, core)
    rest = add(rest, after(rest_got, down))
    rest_got = net.swap(rest, ybit)
    down_yc = net.swap(down_y, core)
    rest = add(rest, rest_got)
    rest_far = net.swap(rest, core)
    qk, v = (QW + KW) // n_fsdp, KW // n_fsdp
    out_gate, out_down, out_wout, out_qkv, b_qk, b_v, out_gains = call(
        functools.partial(place_all, ff_rows // 4, qk, v),
        [meta],
        [a, a_far, b, b_far, down, down_y, down_c, down_yc, rest, rest_far],
        [
            sds((d_rows, 2 * units), F32),
            sds((ff_rows, width), F32),
            sds((d_rows, width), F32),
            sds((d_rows, qkv_w), F32),
            sds((1, qk), F32),
            sds((1, v), F32),
            sds((2, d_rows), F32),
        ],
        3e9,
        [(d_rows + 8, 1024)],
        16,
    )
    return (
        block_out,
        hidden_grad,
        out_qkv,
        b_qk.reshape(qk),
        b_v.reshape(v),
        out_wout,
        out_gate,
        out_down,
        out_gains,
    )


def solution(mesh):
    n_fsdp, n_seq = mesh.shape["fsdp"], mesh.shape["seq"]
    in_specs = (
        P(None, "fsdp", "seq", None),
        P("fsdp", None),
        P("fsdp"),
        P("fsdp", None),
        P("fsdp", None),
        P("fsdp", None),
        P(None, "fsdp"),
        P(None, "fsdp", "seq"),
        P(),
        P(None, "fsdp", "seq", None),
    )
    out_specs = (
        P(None, "fsdp", "seq", None),
        P(None, "fsdp", "seq", None),
        P("fsdp", None),
        P("fsdp"),
        P("fsdp"),
        P("fsdp", None),
        P("fsdp", None),
        P("fsdp", None),
        P(None, "fsdp"),
    )

    def local(*args):
        body = on_device_tiled if (n_fsdp, n_seq) == (8, 4) else on_device
        return body(*args, n_fsdp=n_fsdp, n_seq=n_seq)

    return jax.shard_map(local, mesh=mesh, in_specs=in_specs, out_specs=out_specs, check_vma=False)
```

```python
import functools

import jax
import jax.numpy as jnp
import numpy as np
from jax import lax
from jax.experimental import pallas as pl
from jax.experimental.pallas import tpu as pltpu
from jax.sharding import PartitionSpec as P

HEADS = 9
KV_HEADS = 3
HEAD_DIM = 64
GROUP = HEADS // KV_HEADS
QW = HEADS * HEAD_DIM
KW = KV_HEADS * HEAD_DIM
EPS = 1e-05
ROPE_BASE = 100000.0
MASKED = -1000000000.0
BF = jnp.bfloat16
F32 = jnp.float32


def dot(a, b, ca, cb):
    return lax.dot_general(a, b, (((ca,), (cb,)), ((), ())), preferred_element_type=F32)


def rotary(values, cosine, sine):
    half = values.shape[-1] // 2
    a, b = values[..., :half], values[..., half:]
    return jnp.concatenate([a * cosine - b * sine, b * cosine + a * sine], axis=-1)


def norm_parts(values):
    factor = lax.rsqrt(jnp.mean(values * values, axis=-1, keepdims=True) + EPS)
    return factor, values * factor


def norm_back(grad_in, gain, factor, normed):
    scaled = grad_in * gain
    return factor * (scaled - normed * jnp.mean(scaled * normed, axis=-1, keepdims=True))


def whole(*shape_dtypes):
    return [pl.BlockSpec(memory_space=pltpu.VMEM) for _ in shape_dtypes]


def call(kernel, scalars, arrays, outs, flops, scratch=(), mib=52, fetched=(), landing=()):
    specs = [pl.BlockSpec(memory_space=pltpu.SMEM)] * len(scalars) + whole(*arrays)
    specs += [pl.BlockSpec(memory_space=pltpu.HBM)] * len(fetched)
    arrays = [*arrays, *fetched]
    moved = sum(a.size * a.dtype.itemsize for a in arrays) + sum(
        int(np.prod(o.shape)) * o.dtype.itemsize for o in outs
    )
    return pl.pallas_call(
        kernel,
        out_shape=outs,
        in_specs=specs,
        out_specs=whole(*outs),
        scratch_shapes=[
            *[pltpu.VMEM(shape, F32) for shape in scratch],
            *[pltpu.VMEM(shape, BF) for shape in landing],
            *([pltpu.SemaphoreType.DMA((len(fetched),))] if fetched else []),
        ],
        compiler_params=pltpu.CompilerParams(vmem_limit_bytes=mib * 1024 * 1024),
        cost_estimate=pl.CostEstimate(flops=int(flops), bytes_accessed=moved, transcendentals=0),
    )(*scalars, *arrays)


def sds(shape, dtype):
    return jax.ShapeDtypeStruct(shape, dtype)


def turn(x, cosine, sine):
    tiles = []
    low = lax.broadcasted_iota(jnp.int32, (1, 128), 1) % HEAD_DIM < HEAD_DIM // 2
    for t in range(x.shape[1] // 128):
        part = x[:, 128 * t : 128 * t + 128]
        other = jnp.where(low, pltpu.roll(part, 96, 1), pltpu.roll(part, 32, 1))
        tiles.append(part * cosine + other * sine)
    return tiles


def turn_kv(x, cosine, sine):
    lane = lax.broadcasted_iota(jnp.int32, (1, 128), 1)
    first, second = turn(x[:, :256], cosine, sine)
    second = jnp.where(lane < KW - 128, second, x[:, 128:256])
    return jnp.concatenate([first, second, x[:, 256:]], axis=1)


def tables(seq, order, cos_ref, sin_ref):
    cosine = jnp.concatenate([cos_ref[seq ^ o] for o in order], axis=0)
    sine = jnp.concatenate([sin_ref[seq ^ o] for o in order], axis=0)
    return cosine, sine


def heads_to_rows(x, g):
    return jnp.concatenate(
        [x[:, HEAD_DIM * h : HEAD_DIM * (h + 1)] for h in range(GROUP * g, GROUP * (g + 1))], axis=0
    )


def rows_to_heads(parts, length):
    return jnp.concatenate(
        [p[length * r : length * (r + 1)] for p in parts for r in range(GROUP)], axis=1
    )


def attention_forward(order, length, seq_ref, blocks, wq, wkv, bq, bkv, gain, cos, sin, mask,
                      att_o, q_o, k_o, v_o):
    seq = seq_ref[0]
    cosine, sine = tables(seq, order, cos, sin)
    width = gain.shape[1]
    for b in range(blocks.shape[1] // length):
        x = blocks[:, b * length : (b + 1) * length, :width].astype(F32)
        x = x.reshape(len(order) * length, width)
        first = (norm_parts(x)[1] * gain[...]).astype(BF)
        kv = dot(first, wkv[...], 1, 0) + bkv[...]
        q = dot(first[:length], wq[...], 1, 0) + bq[...]
        q = jnp.concatenate(turn(q, cosine[:length], sine[:length]), axis=1).astype(BF)
        q = q * jnp.asarray(HEAD_DIM ** (-0.5), BF)
        kv = turn_kv(kv, cosine, sine).astype(BF)
        allowed = jnp.concatenate([mask[b]] * GROUP, axis=0) > 0.0
        parts = []
        for g in range(KV_HEADS):
            qg = heads_to_rows(q, g)
            kg = kv[:, HEAD_DIM * g : HEAD_DIM * (g + 1)]
            vg = kv[:, KW + HEAD_DIM * g : KW + HEAD_DIM * (g + 1)]
            q_o[b, g] = qg
            k_o[b, g] = kg
            v_o[b, g] = vg
            scores = jnp.where(allowed, dot(qg, kg, 1, 1), MASKED)
            top = jnp.max(scores, axis=-1, keepdims=True)
            e = jnp.exp(scores - top)
            total = jnp.sum(e, axis=-1, keepdims=True)
            probs = (e * (1.0 / total)).astype(BF)
            parts.append(dot(probs, vg, 1, 0))
        att_o[b * length : (b + 1) * length, :] = rows_to_heads(parts, length).astype(BF)


def feed_forward(attended, source, wo, wgu, wd, gain, cot, weight,
                 out_o, down_o, gu_o, mid_o, wout_o, attg_o, gain_o):
    units = wd.shape[0]
    step = units // 3
    att = attended[...]
    middle = source[...].astype(F32) + dot(att, wo[...], 1, 0)
    scale_two, normed = norm_parts(middle)
    g2 = gain[...]
    second = (normed * g2).astype(BF)
    out_grad = cot[...].astype(F32) * weight[...]
    feed_grad = out_grad.astype(BF)
    feed = None
    back = None
    for j in range(0, units, step):
        wg = wgu[:, j : j + step]
        wu = wgu[:, units + j : units + j + step]
        wdj = wd[j : j + step, :]
        gate = dot(second, wg, 1, 0)
        up = dot(second, wu, 1, 0)
        sig = jax.nn.sigmoid(gate)
        act = gate * sig
        product = (act * up).astype(BF)
        part = dot(product, wdj, 1, 0)
        feed = part if feed is None else feed + part
        down_o[j : j + step, :] = dot(product, feed_grad, 0, 0).astype(BF)
        pgrad = dot(feed_grad, wdj, 1, 1)
        ggrad = (pgrad * up * (sig * (1.0 + gate * (1.0 - sig)))).astype(BF)
        ugrad = (pgrad * act).astype(BF)
        gu_o[:, j : j + step] = dot(second, ggrad, 0, 0).astype(BF)
        gu_o[:, units + j : units + j + step] = dot(second, ugrad, 0, 0).astype(BF)
        part = dot(ggrad, wg, 1, 1) + dot(ugrad, wu, 1, 1)
        back = part if back is None else back + part
    out_o[...] = (middle + feed).astype(BF)
    gain_o[...] = jnp.sum(back * normed, axis=0, keepdims=True)
    middle_grad = out_grad + norm_back(back, g2, scale_two, normed)
    mid_o[...] = middle_grad
    branch = middle_grad.astype(BF)
    wout_o[...] = dot(att, branch, 0, 0).astype(BF)
    attg_o[...] = dot(branch, wo[...], 1, 1).astype(BF)


def attention_backward(order, length, seq_ref, blocks, wq, wkv, gain, cos, sin, mask, q_i, k_i, v_i,
                       attg, dq_o, dkv_o, wgrad_o, bias_o, gain_o):
    seq = seq_ref[0]
    cosine, sine = tables(seq, order, cos, sin)
    width = gain.shape[1]
    q_wgrad = kv_wgrad = bias_q = bias_kv = gain_sum = None
    for b in range(blocks.shape[1] // length):
        x = blocks[:, b * length : (b + 1) * length, :width].astype(F32)
        x = x.reshape(len(order) * length, width)
        normed = norm_parts(x)[1]
        first = (normed * gain[...]).astype(BF)
        allowed = jnp.concatenate([mask[b]] * GROUP, axis=0) > 0.0
        ag = attg[b * length : (b + 1) * length, :]
        dqs, dks, dvs = [], [], []
        for g in range(KV_HEADS):
            qg, kg, vg = q_i[b, g], k_i[b, g], v_i[b, g]
            agg = heads_to_rows(ag, g)
            scores = jnp.where(allowed, dot(qg, kg, 1, 1), MASKED)
            e = jnp.exp(scores - jnp.max(scores, axis=-1, keepdims=True))
            p = e * (1.0 / jnp.sum(e, axis=-1, keepdims=True))
            dvs.append(dot(p.astype(BF), agg, 0, 0))
            pg = dot(agg, vg, 1, 1)
            inner = jnp.sum(p * pg, axis=-1, keepdims=True)
            ds = (p * (pg - inner)).astype(BF)
            dqs.append(dot(ds, kg, 1, 0) * HEAD_DIM ** (-0.5))
            dks.append(dot(ds, qg, 0, 0))
        dq = rows_to_heads(dqs, length)
        dq = jnp.concatenate([dq, jnp.zeros((length, 64), F32)], axis=1)
        dq = jnp.concatenate(turn(dq, cosine[:length], -sine[:length]), axis=1).astype(BF)
        dkv = jnp.concatenate(dks + dvs, axis=1)
        dkv = turn_kv(dkv, cosine, -sine).astype(BF)
        dq_o[b * length : (b + 1) * length, :] = dq
        for r in range(len(order)):
            dkv_o[r, b * length : (b + 1) * length, :] = dkv[r * length : (r + 1) * length, :]
        wq_part = dot(first[:length], dq, 0, 0)
        wkv_part = dot(first, dkv, 0, 0)
        bq_part = jnp.sum(dq.astype(F32), axis=0, keepdims=True)
        bkv_part = jnp.sum(dkv.astype(F32), axis=0, keepdims=True)
        e_kv = dot(dkv, wkv[...], 1, 1) * normed
        e_q = dot(dq[:, :QW], wq[:, :QW], 1, 1) * normed[:length]
        g_part = jnp.sum(e_kv, axis=0, keepdims=True) + jnp.sum(e_q, axis=0, keepdims=True)
        if q_wgrad is None:
            q_wgrad, kv_wgrad, bias_q, bias_kv, gain_sum = wq_part, wkv_part, bq_part, bkv_part, g_part
        else:
            q_wgrad, kv_wgrad = q_wgrad + wq_part, kv_wgrad + wkv_part
            bias_q, bias_kv, gain_sum = bias_q + bq_part, bias_kv + bkv_part, gain_sum + g_part
    wgrad_o[...] = jnp.concatenate([q_wgrad[:, :QW], kv_wgrad], axis=1).astype(BF)
    bias_o[...] = jnp.concatenate([bias_q[:, :QW], bias_kv], axis=1)
    gain_o[...] = gain_sum


def input_gradient(dq, own, a, b, c, source, mid, wq, wkv, gain, out_o):
    kv = own[...].astype(F32) + a[...].astype(F32) + b[...].astype(F32) + c[...].astype(F32)
    first_grad = dot(dq[:, :QW], wq[:, :QW], 1, 1) + dot(kv.astype(BF), wkv[...], 1, 1)
    scale_one, normed = norm_parts(source[...].astype(F32))
    out_o[...] = mid[...] + norm_back(first_grad, gain[...], scale_one, normed)

def chosen(flag, a, b):
    return jnp.where(flag != 0, b, a)


class Blocks:
    def __init__(self, *refs):
        self.refs = refs
        self.shape = (len(refs),) + refs[0].shape

    def __getitem__(self, key):
        return jnp.stack([ref[key[1:]] for ref in self.refs])


def cut_qkv(core_bit, meta, w_hbm, bias_hbm, gains_hbm, out_o, w, bias, gains, all_s, sems):
    pairs = ((w_hbm, w), (bias_hbm, bias), (gains_hbm, gains))
    copies = [pltpu.make_async_copy(a, b, sems.at[i]) for i, (a, b) in enumerate(pairs)]
    for copy in copies:
        copy.start()
    for copy in copies:
        copy.wait()
    rows = w.shape[0]
    n = bias.shape[1]
    all_s[:rows, :] = w[...].astype(F32)
    all_s[rows:, :] = jnp.zeros((8, w.shape[1]), F32)
    all_s[rows : rows + 1, :n] = bias[...].astype(F32)
    for i in range(2):
        all_s[rows : rows + 1, n + rows * i : n + rows * (i + 1)] = gains[i : i + 1, :].astype(F32)
    half = out_o.shape[0]
    at = pl.multiple_of((meta[0] & core_bit) * half, 8)
    out_o[...] = all_s[pl.ds(at, half), :].astype(BF)


def first_forward(order, length, d_rows, n_bias, meta, b0, b1, b2, b3, a00, a10, a01, a11, cos, sin, mask,
                  att_o, q_o, k_o, v_o, w_o, gain_o, w_s, b_s):
    blocks = Blocks(b0, b1, b2, b3)
    core, x = meta[0] & 1, meta[1] & 1
    cut = a00.shape[2]
    for x_rel, c_rel, piece in ((0, 0, a00), (1, 0, a10), (0, 1, a01), (1, 1, a11)):
        for z0 in range(2):
            for z1 in range(2):
                at = (z1 * 4 + z0 * 2 + (x ^ x_rel)) * 2 * cut + (core ^ c_rel) * cut
                w_s[pl.ds(pl.multiple_of(at, 8), cut), :] = piece[z0, z1].astype(F32)
    n_f = w_s.shape[0] // (2 * cut)
    starts = [2 * cut * f for f in range(n_f)]
    w_o[...] = jnp.concatenate([w_s[at : at + d_rows, :] for at in starts], axis=0).astype(BF)
    lines = [w_s[at + d_rows : at + d_rows + 1, :] for at in starts]
    b_s[...] = jnp.concatenate([line[:, :n_bias] for line in lines], axis=1)
    for i in range(2):
        at = n_bias + d_rows * i
        gain_o[i : i + 1, :] = jnp.concatenate([line[:, at : at + d_rows] for line in lines], axis=1)
    wide = QW + 64
    attention_forward(order, length, meta, blocks, w_o[:, :wide], w_o[:, QW:], b_s[:, :wide], b_s[:, QW:],
                      gain_o[0:1, :], cos, sin, mask, att_o, q_o, k_o, v_o)


def turned(out, value):
    length = out.shape[2]
    for b in range(out.shape[0]):
        out[b] = value[length * b : length * (b + 1)].T.astype(out.dtype)


def rel(meta, f):
    r = f ^ meta[1]
    return r & 1, (r >> 1) & 1, (r >> 2) & 1


def fetch_pieces(meta, refs, b_s, g_s, sems):
    core, y, x, z0 = meta[0] & 1, (meta[0] >> 1) & 1, meta[1] & 1, (meta[1] >> 1) & 1
    copies = []
    for i in range(8):
        at = (z0 ^ (i >> 2), x ^ ((i >> 1) & 1), core ^ (i & 1))
        copies.append(pltpu.make_async_copy(refs[i], b_s.at[at], sems.at[i]))
    for i in range(8):
        at = (y ^ ((i >> 1) & 1), core ^ (i & 1), x ^ (i >> 2))
        copies.append(pltpu.make_async_copy(refs[8 + i], g_s.at[at], sems.at[8 + i]))
    for copy in copies:
        copy.start()
    return copies


def feed_forward_pieces(d_rows, ff_rows, meta, attended, source, gains, cot, weight, *refs):
    out_o, ak_o, ag_o, bk_o, bg_o, dk_o, dg_o, mid_o, attg_o, gain_o, down_s, wout_s, b_s, g_s, sems = refs[16:]
    copies = fetch_pieces(meta, refs, b_s, g_s, sems)
    core, y = meta[0] & 1, (meta[0] >> 1) & 1
    part_d = ff_rows // 4
    part_o = d_rows // 3
    cut = b_s.shape[4] - ff_rows // 2
    half = g_s.shape[-1] // 2
    for copy in copies[:8]:
        copy.wait()
    wo = []
    for f in range(8):
        for c in range(2):
            rows = b_s[(f >> 1) & 1, f & 1, c, f >> 2, ff_rows // 2 :, :].astype(F32)
            wo.append(rows if c == 0 else rows[: d_rows - cut])
    wo = jnp.concatenate(wo, axis=0).astype(BF)
    att = attended[...]
    middle = source[...].astype(F32) + dot(att, wo, 1, 0)
    scale_two, normed = norm_parts(middle)
    g2 = gains[1:2, :]
    second = (normed * g2).astype(BF)
    out_grad = cot[...].astype(F32) * weight[...]
    feed_grad = out_grad.astype(BF)
    for copy in copies[8:]:
        copy.wait()
    feed = back = None
    for c_rel in (1, 0):
        h = core ^ c_rel
        weights = []
        for yy in range(2):
            rows = [g_s[yy, h, f & 1, (f >> 1) & 1, f >> 2].astype(F32) for f in range(8)]
            weights.append(jnp.concatenate(rows, axis=0).astype(BF))
        wg, wu = weights
        wd = [b_s[i >> 1, i & 1, c, h, : ff_rows // 2, :] for i in range(4) for c in range(2)]
        wd = jnp.concatenate(wd, axis=0)
        gate = dot(second, wg, 1, 0)
        up = dot(second, wu, 1, 0)
        sig = jax.nn.sigmoid(gate)
        act = gate * sig
        product = (act * up).astype(BF)
        part = dot(product, wd, 1, 0)
        feed = part if feed is None else feed + part
        down_s[...] = dot(product, feed_grad, 0, 0)
        pgrad = dot(feed_grad, wd, 1, 1)
        ggrad = (pgrad * up * (sig * (1.0 + gate * (1.0 - sig)))).astype(BF)
        ugrad = (pgrad * act).astype(BF)
        part = dot(ggrad, wg, 1, 1) + dot(ugrad, wu, 1, 1)
        back = part if back is None else back + part
        for i in range(4):
            x, z0, z1 = rel(meta, 4 * h + i)
            for yy in range(2):
                for c_to, to in ((0, dk_o), (1, dg_o)):
                    at = pl.multiple_of(i * ff_rows + (yy * 2 + (core ^ c_to)) * part_d, 16)
                    to[y ^ yy, x, z0, z1, :part_d, :] = down_s[pl.ds(at, part_d), :].astype(BF)
        to_a, to_b = (ag_o, bg_o) if c_rel else (ak_o, bk_o)
        for yy, grad in ((0, ggrad), (1, ugrad)):
            wgrad = dot(second, grad, 0, 0)
            for f in range(8):
                x, z0, z1 = rel(meta, f)
                block = wgrad[d_rows * f : d_rows * (f + 1), :].astype(BF)
                to_a[x, z0, z1, yy] = block[:, :half]
                to_b[z0, z1, x, yy] = block[:, half:]
    turned(out_o, middle + feed)
    gain_o[...] = jnp.sum(back * normed, axis=0, keepdims=True)
    middle_grad = out_grad + norm_back(back, g2, scale_two, normed)
    mid_o[...] = middle_grad
    branch = middle_grad.astype(BF)
    attg_o[...] = dot(branch, wo, 1, 1).astype(BF)
    wout = dot(att, branch, 0, 0)
    for f in range(8):
        wout_s[f, :d_rows, :] = wout[d_rows * f : d_rows * (f + 1), :]
        wout_s[f, d_rows:, :] = jnp.zeros((part_o, wout.shape[1]), F32)
    for f in range(8):
        x, z0, z1 = rel(meta, f)
        for yy in range(2):
            for c_to, to in ((0, dk_o), (1, dg_o)):
                at = pl.multiple_of((yy * 2 + (core ^ c_to)) * part_o, 8)
                to[y ^ yy, x, z0, z1, part_d:, :] = wout_s[f, pl.ds(at, part_o), :].astype(BF)


def attention_backward_pieces(order, length, d_rows, meta, b0, b1, b2, b3, w, gains, cos, sin, mask, q_i, k_i, v_i,
                              attg, gain_two, dq_o, dk_o, dg_o, rk_o, rg_o, w_s, bias_s, gain_s, small_s):
    blocks = Blocks(b0, b1, b2, b3)
    half = len(order) // 2

    class Pieces:
        def __setitem__(self, key, value):
            ref = dk_o if key[0] < half else dg_o
            ref[(key[0] % half,) + key[1:]] = value

    class Wgrad:
        def __setitem__(self, key, value):
            w_s[:, : 2 * KW] = value[:, QW:].astype(F32)
            w_s[:, 2 * KW : 2 * KW + QW] = value[:, :QW].astype(F32)
            w_s[:, 2 * KW + QW :] = jnp.zeros((value.shape[0], 64), F32)

    wide = QW + 64
    attention_backward(order, length, meta, blocks, w[:, :wide], w[:, QW:], gains[0:1, :], cos, sin, mask,
                       q_i, k_i, v_i, attg, dq_o, Pieces(), Wgrad(), bias_s, gain_s)
    n_f = small_s.shape[0]
    qk, v = (QW + KW) // n_f, KW // n_f
    bias, g1, g2 = bias_s[...], gain_s[...], gain_two[...]
    for f in range(n_f):
        line = jnp.concatenate(
            [
                bias[:, qk * f : qk * (f + 1)],
                bias[:, QW + KW + v * f : QW + KW + v * (f + 1)],
                g1[:, d_rows * f : d_rows * (f + 1)],
                jnp.zeros((1, 256 - qk - v - d_rows), F32),
                g2[:, d_rows * f : d_rows * (f + 1)],
                jnp.zeros((1, 768 - d_rows), F32),
            ],
            axis=1,
        )
        small_s[f] = jnp.broadcast_to(line, (8, 1024))
    core, y = meta[0] & 1, (meta[0] >> 1) & 1
    for f in range(n_f):
        x, z0, z1 = rel(meta, f)
        for yy in range(2):
            for c_to, to in ((0, rk_o), (1, rg_o)):
                at = pl.multiple_of((yy * 2 + (core ^ c_to)) * 256, 256)
                block = [w_s[d_rows * f : d_rows * (f + 1), pl.ds(at, 256)], small_s[f, :, pl.ds(at, 256)]]
                to[x, z0, z1, yy] = jnp.concatenate(block, axis=0).astype(BF)


def input_gradient_two(dq, own, other, source, mid, w, gains, out_o):
    kv = (own[...].astype(F32) + other[...].astype(F32)).astype(BF)
    first_grad = dot(dq[:, :QW], w[:, :QW], 1, 1) + dot(kv, w[:, QW:], 1, 1)
    scale_one, normed = norm_parts(source[...].astype(F32))
    turned(out_o, mid[...] + norm_back(first_grad, gains[0:1, :], scale_one, normed))


def place_gate(meta, near, far, out_o, parts=1, part=0):
    core = meta[0] & 1
    n = near.shape[2]
    for pieces, c_rel in ((near, 0), (far, 1)):
        for yy in range(2):
            at = pl.multiple_of(((yy * 2 + (core ^ c_rel)) * parts + part) * n, 128)
            out_o[:, pl.ds(at, n)] = pieces[yy].astype(F32)


def place_down(part_d, meta, p00, p10, p01, p11, out_o, wout_o):
    seq = meta[0]
    part_o = p00.shape[0] - part_d
    for piece, o in ((p00[...], 0), (p10[...], 2), (p01[...], 1), (p11[...], 3)):
        piece = piece.astype(F32)
        to = seq ^ o
        out_o[pl.ds(pl.multiple_of(to * part_d, 16), part_d), :] = piece[:part_d]

        @pl.when(to < 3)
        def _():
            wout_o[pl.ds(pl.multiple_of(to * part_o, 8), part_o), :] = piece[part_d:]


def place_qkv(qk, v, meta, near, far, w_o, bqk_o, bv_o, gains_o, all_s):
    place_gate(meta, near, far, all_s)
    d_rows = w_o.shape[0]
    w_o[:, :QW] = all_s[:d_rows, 2 * KW : 2 * KW + QW]
    w_o[:, QW:] = all_s[:d_rows, : 2 * KW]
    line = all_s[d_rows : d_rows + 1, :]
    bqk_o[...] = line[:, :qk]
    bv_o[...] = line[:, qk : qk + v]
    gains_o[0:1, :] = line[:, qk + v : qk + v + d_rows]
    gains_o[1:2, :] = line[:, 256 : 256 + d_rows]


def place_all(part_d, qk, v, meta, a_near, a_far, b_near, b_far, d0, d1, d2, d3, r_near, r_far,
              gate_o, down_o, wout_o, w_o, bqk_o, bv_o, gains_o, all_s):
    place_gate(meta, a_near, a_far, gate_o, 2, 0)
    place_gate(meta, b_near, b_far, gate_o, 2, 1)
    place_down(part_d, meta, d0, d1, d2, d3, down_o, wout_o)
    place_qkv(qk, v, meta, r_near, r_far, w_o, bqk_o, bv_o, gains_o, all_s)


class Net:
    def __init__(self, n_fsdp, n_seq):
        self.n_fsdp, self.n_seq = n_fsdp, n_seq
        self.total = n_fsdp * n_seq
        f, s = lax.axis_index("fsdp"), lax.axis_index("seq")
        self.index = f * n_seq + s
        self.seq_bits = [1 << b for b in range(n_seq.bit_length() - 1)]
        self.fsdp_bits = [n_seq << b for b in range(n_fsdp.bit_length() - 1)]

    def swap(self, value, mask):
        pairs = [(i, i ^ mask) for i in range(self.total)]
        return lax.ppermute(value, ("fsdp", "seq"), pairs)

    def bit(self, mask):
        return (self.index & mask) != 0

    def both(self, mine, mask, axis, other=None):
        other = self.swap(mine, mask) if other is None else other
        high = self.bit(mask)
        return jnp.stack([jnp.where(high, other, mine), jnp.where(high, mine, other)], axis=axis)

    def half(self, value, mask, axis):
        return lax.dynamic_index_in_dim(
            value, self.bit(mask).astype(jnp.int32), axis, keepdims=False
        )

    def add_half(self, value, mask, axis):
        mine = self.bit(mask).astype(jnp.int32)
        keep = lax.dynamic_index_in_dim(value, mine, axis, keepdims=False)
        give = lax.dynamic_index_in_dim(value, 1 - mine, axis, keepdims=False)
        got = self.swap(give, mask)
        return (keep.astype(F32) + got.astype(F32)).astype(value.dtype)

    def gather_fsdp(self, value):
        for step, mask in enumerate(reversed(self.fsdp_bits)):
            value = self.both(value, mask, step)
        return value

    def scatter_fsdp(self, value, first_axis=0):
        count = len(self.fsdp_bits)
        for step, mask in enumerate(self.fsdp_bits):
            value = self.add_half(value, mask, first_axis + count - 1 - step)
        return value


def on_device(
    hidden, w_qkv, b_qkv, w_out, w_gate_up, w_down, norm_gains, segment_ids, token_counts, cotangent,
    n_fsdp, n_seq,
):
    net = Net(n_fsdp, n_seq)
    micro, batch, length, width = hidden.shape
    full_length = length * n_seq
    tokens_micro = batch * n_fsdp * full_length
    scale = HEAD_DIM ** (-0.5)
    rows = micro * batch * length
    d_rows = w_qkv.shape[0]
    ff_rows = w_down.shape[0]
    units = w_gate_up.shape[1] // 2
    qkv_w = w_qkv.shape[1]
    core = net.seq_bits[0]
    f_lead = (2,) * len(net.fsdp_bits)

    ids = segment_ids.reshape(rows, 1).astype(BF)
    block = jnp.concatenate(
        [hidden.reshape(rows, width), jnp.broadcast_to(ids, (rows, 64))], axis=1
    )
    blocks = block[None]
    for mask in reversed(net.seq_bits):
        blocks = jnp.concatenate([blocks, net.swap(blocks, mask)], axis=0)
    order = [0]
    for mask in reversed(net.seq_bits):
        order = order + [o ^ mask for o in order]
    seq_index = lax.axis_index("seq")
    block_ids = [seq_index ^ o for o in order]

    pad_rows = -(d_rows + 1) % 16 + 1
    extra = jnp.zeros((pad_rows, qkv_w), BF)
    small = jnp.concatenate([b_qkv, norm_gains.reshape(-1)])
    extra = extra.at[0, : small.shape[0]].set(small)
    shard_a = jnp.concatenate([w_qkv, extra], axis=0).reshape(2, -1, qkv_w)
    got_a = net.gather_fsdp(net.half(shard_a, core, 0))
    full_a = net.both(got_a, core, len(f_lead)).reshape(n_fsdp, d_rows + pad_rows, qkv_w)
    wf_qkv = full_a[:, :d_rows].reshape(n_fsdp * d_rows, qkv_w)
    smalls = full_a[:, d_rows]
    n_bias = b_qkv.shape[0]
    bias = smalls[:, :n_bias].reshape(-1).astype(F32)
    gains = smalls[:, n_bias : n_bias + 2 * d_rows].reshape(n_fsdp, 2, d_rows).astype(F32)
    gain_one = gains[:, 0].reshape(-1)
    gain_two = gains[:, 1].reshape(-1)

    pad_b = -(d_rows + ff_rows) % 16
    shard_b = jnp.concatenate([w_out, w_down, jnp.zeros((pad_b, width), BF)], axis=0)
    shard_b = shard_b.reshape(2, -1, width)
    got_b = net.gather_fsdp(net.half(shard_b, core, 0))

    parts = n_seq
    shard_c = w_gate_up.reshape(d_rows, parts, -1)
    got_c = net.gather_fsdp(lax.dynamic_index_in_dim(shard_c, seq_index, 1, keepdims=False))
    full_b = net.both(got_b, core, len(f_lead)).reshape(n_fsdp, -1, width)
    wf_out = full_b[:, :d_rows].reshape(n_fsdp * d_rows, width)
    wf_down = full_b[:, d_rows : d_rows + ff_rows].reshape(n_fsdp * ff_rows, width)
    got_c = got_c.reshape(n_fsdp * d_rows, -1)
    for mask in reversed(net.seq_bits):
        got_c = net.both(got_c, mask, got_c.ndim - 1)
    wf_gate_up = got_c.reshape(n_fsdp * d_rows, 2 * units)

    places = np.arange(full_length, dtype=np.float32)
    speeds = np.power(ROPE_BASE, -2.0 * np.arange(HEAD_DIM // 2, dtype=np.float32) / HEAD_DIM)
    angles = places[:, None] * speeds.astype(np.float32)[None, :]
    cos_t = np.tile(np.cos(angles), (1, 4)).reshape(n_seq, length, 128)
    sin_t = np.concatenate([-np.sin(angles), np.sin(angles)] * 2, axis=1).reshape(n_seq, length, 128)
    cos_t, sin_t = jnp.asarray(cos_t, F32), jnp.asarray(sin_t, F32)
    seqs = micro * batch
    seg_all = blocks[..., width].reshape(n_seq, seqs, length).transpose(1, 0, 2)
    own_places = seq_index * length + jnp.arange(length, dtype=jnp.int32)
    key_places = jnp.stack(block_ids)[:, None] * length + jnp.arange(length, dtype=jnp.int32)
    allowed = (seg_all[:, 0, :, None] == seg_all.reshape(seqs, 1, -1)) & (
        own_places[None, :, None] >= key_places.reshape(1, 1, -1)
    )
    allowed = allowed.astype(F32)
    seq_scalar = seq_index.astype(jnp.int32).reshape(1)
    wq, wkv = wf_qkv[:, : QW + 64], wf_qkv[:, QW:]
    gain_one, gain_two = gain_one[None], gain_two[None]
    source = hidden.reshape(rows, width)
    n_all = n_seq * rows
    attended, q_s, k_s, v_s = call(
        functools.partial(attention_forward, order, length),
        [seq_scalar],
        [blocks, wq, wkv, bias[None, : QW + 64], bias[None, QW:], gain_one, cos_t, sin_t, allowed],
        [
            sds((rows, QW), BF),
            sds((seqs, KV_HEADS, GROUP * length, HEAD_DIM), BF),
            sds((seqs, KV_HEADS, full_length, HEAD_DIM), BF),
            sds((seqs, KV_HEADS, full_length, HEAD_DIM), BF),
        ],
        2 * n_all * width * 2 * KW + 2 * rows * width * QW + 4 * rows * full_length * QW,
    )

    weight = tokens_micro / token_counts.astype(F32)
    weight = jnp.repeat(weight, batch * length)[:, None]
    block_out, down_grad, gate_up_wgrad, middle_grad, out_wgrad, attended_grad, gain_two_grad = call(
        feed_forward,
        [],
        [attended, source, wf_out, wf_gate_up, wf_down, gain_two, cotangent.reshape(rows, width), weight],
        [
            sds((rows, width), BF),
            sds((units, width), BF),
            sds((width, 2 * units), BF),
            sds((rows, width), F32),
            sds((QW, width), BF),
            sds((rows, QW), BF),
            sds((1, width), F32),
        ],
        6 * rows * width * 3 * units + 6 * rows * width * QW,
    )
    block_out = block_out.reshape(hidden.shape)

    def seq_axes(value, axis, masks):
        for mask in masks:
            value = net.add_half(value, mask, axis)
        return value

    quarter = (2,) * len(net.seq_bits)
    n_f = len(f_lead)
    red_down = down_grad.reshape(f_lead + quarter + (ff_rows // n_seq, width))
    for step, mask in enumerate(net.seq_bits):
        red_down = net.add_half(red_down, mask, n_f + len(quarter) - 1 - step)
    red_down = net.scatter_fsdp(red_down)

    red_gate = gate_up_wgrad.reshape(f_lead + (d_rows,) + quarter + (2 * units // n_seq,))
    red_gate = net.add_half(red_gate, core, n_f + len(quarter))
    red_gate = net.add_half(red_gate, net.fsdp_bits[0], n_f - 1)
    for step, mask in enumerate(net.seq_bits[1:]):
        red_gate = net.add_half(red_gate, mask, n_f - 1 + len(quarter) - 1 - step)
    for step, mask in enumerate(net.fsdp_bits[1:]):
        red_gate = net.add_half(red_gate, mask, n_f - 2 - step)

    dq, dkv, qkv_wgrad, bias_grad, gain_one_grad = call(
        functools.partial(attention_backward, order, length),
        [seq_scalar],
        [blocks, wq, wkv, gain_one, cos_t, sin_t, allowed, q_s, k_s, v_s, attended_grad],
        [
            sds((rows, QW + 64), BF),
            sds((n_seq, rows, 2 * KW), BF),
            sds((width, qkv_w), BF),
            sds((1, qkv_w), F32),
            sds((1, width), F32),
        ],
        4 * n_all * width * 2 * KW + 4 * rows * width * QW + 10 * rows * full_length * QW,
    )
    kv_parts = [dkv[0]]
    for place, mask_bits in enumerate(order):
        if mask_bits:
            kv_parts.append(net.swap(dkv[place], mask_bits))
    (hidden_grad,) = call(
        input_gradient,
        [],
        [dq, *kv_parts, source, middle_grad, wq, wkv, gain_one],
        [sds((rows, width), F32)],
        2 * rows * width * qkv_w,
    )
    hidden_grad = hidden_grad.reshape(hidden.shape)
    bias_grad, gain_one_grad, gain_two_grad = bias_grad[0], gain_one_grad[0], gain_two_grad[0]

    qk_rows, v_rows = (QW + KW) // n_fsdp, KW // n_fsdp
    small_grads = jnp.concatenate(
        [
            bias_grad[: QW + KW].reshape(n_fsdp, qk_rows),
            bias_grad[QW + KW :].reshape(n_fsdp, v_rows),
            gain_one_grad.reshape(n_fsdp, d_rows),
            gain_two_grad.reshape(n_fsdp, d_rows),
        ],
        axis=1,
    ).astype(BF)
    wide = qkv_w + width
    small_pad = jnp.zeros((n_fsdp, pad_rows, wide), BF)
    small_pad = small_pad.at[:, 0, : small_grads.shape[1]].set(small_grads)
    rest = jnp.concatenate([qkv_wgrad, out_wgrad], axis=1)
    rest = jnp.concatenate([rest.reshape(n_fsdp, d_rows, wide), small_pad], axis=1)
    rest = rest.reshape(f_lead + (d_rows + pad_rows,) + quarter + (wide // n_seq,))
    for step, mask in enumerate(net.seq_bits):
        rest = net.add_half(rest, mask, n_f + 1 + len(quarter) - 1 - step)
    rest = net.scatter_fsdp(rest)

    def seq_back(value, axis):
        for step, mask in enumerate(reversed(net.seq_bits)):
            value = net.both(value, mask, axis + step)
        return value

    out_down = seq_back(red_down, 0).reshape(ff_rows, width).astype(F32)
    out_gate = seq_back(red_gate, 1).reshape(d_rows, 2 * units).astype(F32)
    out_rest = seq_back(rest, 1).reshape(d_rows + pad_rows, wide).astype(F32)
    line = out_rest[d_rows]
    edge = qk_rows + v_rows
    return (
        block_out,
        hidden_grad,
        out_rest[:d_rows, :qkv_w],
        line[:qk_rows],
        line[qk_rows:edge],
        out_rest[:d_rows, qkv_w:],
        out_gate,
        out_down,
        line[edge : edge + 2 * d_rows].reshape(2, d_rows),
    )


def after(value, *others):
    return lax.optimization_barrier((value, *others))[0]


def rope_tables(full_length, n_seq):
    places = np.arange(full_length, dtype=np.float32)
    speeds = np.power(ROPE_BASE, -2.0 * np.arange(HEAD_DIM // 2, dtype=np.float32) / HEAD_DIM)
    angles = places[:, None] * speeds.astype(np.float32)[None, :]
    cos_t = np.tile(np.cos(angles), (1, 4)).reshape(n_seq, -1, 128)
    sin_t = np.concatenate([-np.sin(angles), np.sin(angles)] * 2, axis=1).reshape(n_seq, -1, 128)
    return jnp.asarray(cos_t, F32), jnp.asarray(sin_t, F32)


def on_device_tiled(
    hidden, w_qkv, b_qkv, w_out, w_gate_up, w_down, norm_gains, segment_ids, token_counts, cotangent,
    n_fsdp, n_seq,
):
    net = Net(n_fsdp, n_seq)
    micro, batch, length, width = hidden.shape
    full_length = length * n_seq
    tokens_micro = batch * n_fsdp * full_length
    rows = micro * batch * length
    seqs = micro * batch
    d_rows, qkv_w = w_qkv.shape
    ff_rows = w_down.shape[0]
    units = w_gate_up.shape[1] // 2
    n_bias = b_qkv.shape[0]
    core, ybit = net.seq_bits
    xbit, znear, zfar = net.fsdp_bits
    order = [0, 2, 1, 3]
    seq_index = lax.axis_index("seq")
    meta = jnp.stack([seq_index, lax.axis_index("fsdp")]).astype(jnp.int32)
    source = hidden.reshape(rows, width)

    small = [w_qkv, b_qkv[None], norm_gains]
    a0 = pl.pallas_call(
        functools.partial(cut_qkv, core),
        out_shape=sds(((d_rows + 8) // 2, qkv_w), BF),
        in_specs=[pl.BlockSpec(memory_space=pltpu.SMEM)] + [pl.BlockSpec(memory_space=pltpu.HBM)] * 3,
        out_specs=pl.BlockSpec(memory_space=pltpu.VMEM),
        scratch_shapes=[
            *[pltpu.VMEM(v.shape, BF) for v in small],
            pltpu.VMEM((d_rows + 8, qkv_w), F32),
            pltpu.SemaphoreType.DMA((3,)),
        ],
        compiler_params=pltpu.CompilerParams(vmem_limit_bytes=52 * 1024 * 1024),
    )(meta, *small)
    a1 = net.both(a0, zfar, 0)

    ids = segment_ids.reshape(rows, 1).astype(BF)
    block = jnp.concatenate([source, jnp.broadcast_to(ids, (rows, 64))], axis=1)
    block = after(block, a0)
    block_y = net.swap(block, ybit)
    block_c = net.swap(block, core)

    quarter = 2 * units // n_seq
    gu0 = lax.dynamic_slice_in_dim(after(w_gate_up, a0), seq_index * quarter, quarter, axis=1)
    half_b = jnp.concatenate(
        [
            w_down.reshape(2, ff_rows // 2, width),
            jnp.concatenate([w_out, jnp.zeros((8, width), BF)], axis=0).reshape(2, -1, width),
        ],
        axis=1,
    )
    a2 = net.both(a1, znear, 0)
    b0 = net.half(after(half_b, a2), core, 0)
    a_x = net.swap(a2, xbit)
    a_c = net.swap(a2, core)
    gu1 = net.both(gu0, zfar, 0)
    gu2 = net.both(after(gu1, a2), znear, 0)
    block_yc = net.swap(block_y, core)
    a_xc = net.swap(a_x, core)
    gu_x = net.swap(gu2, xbit)
    gu_y = net.swap(gu2, ybit)
    gu_c = net.swap(gu2, core)
    b1 = net.both(b0, zfar, 0, after(net.swap(b0, zfar), gu2))
    b_z = net.swap(b1, znear)
    b_x = net.swap(b1, xbit)
    b_c = net.swap(b1, core)
    a_xc = after(a_xc, b1)

    cos_t, sin_t = rope_tables(full_length, n_seq)
    block_ids = [seq_index ^ o for o in order]
    blocks = [block, block_y, block_c, block_yc]
    seg_all = jnp.stack([b[:, width].reshape(seqs, length) for b in blocks], axis=1)
    own_places = seq_index * length + jnp.arange(length, dtype=jnp.int32)
    key_places = jnp.stack(block_ids)[:, None] * length + jnp.arange(length, dtype=jnp.int32)
    allowed = (seg_all[:, 0, :, None] == seg_all.reshape(seqs, 1, -1)) & (
        own_places[None, :, None] >= key_places.reshape(1, 1, -1)
    )
    allowed = allowed.astype(F32)
    attended, q_s, k_s, v_s, wf, gains = call(
        functools.partial(first_forward, order, length, d_rows, n_bias),
        [meta],
        [*blocks, a2, a_x, a_c, a_xc, cos_t, sin_t, allowed],
        [
            sds((rows, QW), BF),
            sds((seqs, KV_HEADS, GROUP * length, HEAD_DIM), BF),
            sds((seqs, KV_HEADS, full_length, HEAD_DIM), BF),
            sds((seqs, KV_HEADS, full_length, HEAD_DIM), BF),
            sds((width, qkv_w), BF),
            sds((2, width), F32),
        ],
        1.2e10,
        [(n_fsdp * (d_rows + 8), qkv_w), (1, qkv_w)],
    )
    gu_y = after(gu_y, attended)
    gu_x, b_z, b_x = after(gu_x, gu_y), after(b_z, gu_y), after(b_x, gu_y)
    gu_xy = net.swap(gu_x, ybit)
    b_zx = net.swap(b_z, xbit)
    gu_yc = net.swap(gu_y, core)
    gu_xc = net.swap(gu_x, core)
    b_zc = net.swap(b_z, core)
    b_xc = net.swap(b_x, core)
    b_zxc = net.swap(b_zx, core)
    gu_xyc = net.swap(gu_xy, core)
    pieces = [b1, b_c, b_x, b_xc, b_z, b_zc, b_zx, b_zxc]
    pieces += [gu2, gu_c, gu_y, gu_yc, gu_x, gu_xc, gu_xy, gu_xyc]

    weight = tokens_micro / token_counts.astype(F32)
    weight = jnp.repeat(weight, batch * length)[:, None]
    lead = (2, 2, 2, 2)
    cot = cotangent.reshape(rows, width)
    gate_lead = lead + (d_rows, units // 4)
    block_out, a_keep, a_give, b_keep, b_give, down_keep, down_give, middle_grad, attended_grad, gain_two = call(
        functools.partial(feed_forward_pieces, d_rows, ff_rows),
        [meta],
        [attended, source, gains, cot, weight],
        [
            sds((seqs, width, length), BF),
            sds(gate_lead, BF),
            sds(gate_lead, BF),
            sds(gate_lead, BF),
            sds(gate_lead, BF),
            sds(lead + (ff_rows // 4 + d_rows // 3, width), BF),
            sds(lead + (ff_rows // 4 + d_rows // 3, width), BF),
            sds((rows, width), F32),
            sds((rows, QW), BF),
            sds((1, width), F32),
        ],
        1.4e10,
        [(units // 2, width), (n_fsdp, d_rows + d_rows // 3, width)],
        fetched=pieces,
        landing=[(2, 2, 2, 2) + b1.shape[1:], (2, 2, 2, 2, 2, d_rows, units // 2)],
    )
    block_out = block_out.reshape(micro, batch, width, length).swapaxes(2, 3)

    def add(keep, got):
        return (keep.astype(F32) + got.astype(F32)).astype(BF)

    def halves(keep, got):
        return add(keep[0], got[0]), add(keep[1], got[1])

    a_got = net.swap(a_give, core)
    b_got = net.swap(after(b_give, a_got), core)
    down_got = net.swap(after(down_give, a_got), core)
    a, a_give = halves(a_keep, a_got)
    a_got = net.swap(a_give, xbit)
    b, b_give = halves(b_keep, b_got)
    b_got = net.swap(b_give, znear)
    down, down_give = halves(down_keep, down_got)
    attended_grad = after(attended_grad, a_give, b_give, down_give)
    down_got = net.swap(down_give, ybit)

    dq, dkv_keep, dkv_give, rest_keep, rest_give = call(
        functools.partial(attention_backward_pieces, order, length, d_rows),
        [meta],
        [*blocks, wf, gains, cos_t, sin_t, allowed, q_s, k_s, v_s, attended_grad, gain_two],
        [
            sds((rows, QW + 64), BF),
            sds((2, rows, 2 * KW), BF),
            sds((2, rows, 2 * KW), BF),
            sds(lead + (d_rows + 8, 256), BF),
            sds(lead + (d_rows + 8, 256), BF),
        ],
        1.4e10,
        [(width, 1024), (1, qkv_w), (1, width), (n_fsdp, 8, 1024)],
    )
    b, b_give = halves(b, after(b_got, dq))
    a, a_give = halves(a, after(a_got, b_give))
    b_got = net.swap(b_give, zfar)
    a_got = net.swap(a_give, znear)
    rest, rest_give = halves(rest_keep, after(net.swap(rest_give, core), b_give, down_got))
    rest_got = net.swap(rest_give, xbit)
    down, down_give = halves(down, after(down_got, rest_give))
    down_got = net.swap(down_give, xbit)
    dkv, dkv_give = halves(dkv_keep, after(net.swap(dkv_give, core), down_give))
    dkv_got = net.swap(dkv_give, ybit)
    a, a_give = halves(a, after(a_got, dkv_give))
    a_got = net.swap(a_give, zfar)
    b, b_give = halves(b, after(b_got, a_give))
    b_got = net.swap(b_give, xbit)
    rest, rest_give = halves(rest, after(rest_got, b_give))
    rest_got = net.swap(rest_give, znear)
    down, down_give = halves(down, after(down_got, rest_give))
    down_got = net.swap(down_give, znear)
    (hidden_grad,) = call(
        input_gradient_two,
        [],
        [dq, dkv, after(dkv_got, down_give), source, middle_grad, wf, gains],
        [sds((seqs, width, length), F32)],
        3e9,
        mib=16,
    )
    a_got = after(a_got, hidden_grad)
    hidden_grad = hidden_grad.reshape(micro, batch, width, length).swapaxes(2, 3)
    a = add(a, a_got)
    a_got = net.swap(a, ybit)
    b = add(b, after(b_got, a))
    b_got = net.swap(b, ybit)
    rest, rest_give = halves(rest, after(rest_got, b))
    rest_got = net.swap(rest_give, zfar)
    down, down_give = halves(down, after(down_got, rest_give))
    down_got = net.swap(down_give, zfar)
    a = add(a, after(a_got, down_give))
    a_far = net.swap(a, core)
    b = add(b, b_got)
    b_far = net.swap(b, core)
    rest = add(rest, after(rest_got, a))
    rest_got = net.swap(rest, ybit)
    down = add(down, after(down_got, rest))
    down_y = net.swap(down, ybit)
    down_c = net.swap(down, core)
    down_yc = net.swap(down_y, core)
    rest = add(rest, rest_got)
    rest_far = net.swap(rest, core)
    qk, v = (QW + KW) // n_fsdp, KW // n_fsdp
    out_gate, out_down, out_wout, out_qkv, b_qk, b_v, out_gains = call(
        functools.partial(place_all, ff_rows // 4, qk, v),
        [meta],
        [a, a_far, b, b_far, down, down_y, down_c, down_yc, rest, rest_far],
        [
            sds((d_rows, 2 * units), F32),
            sds((ff_rows, width), F32),
            sds((d_rows, width), F32),
            sds((d_rows, qkv_w), F32),
            sds((1, qk), F32),
            sds((1, v), F32),
            sds((2, d_rows), F32),
        ],
        3e9,
        [(d_rows + 8, 1024)],
        16,
    )
    return (
        block_out,
        hidden_grad,
        out_qkv,
        b_qk.reshape(qk),
        b_v.reshape(v),
        out_wout,
        out_gate,
        out_down,
        out_gains,
    )


def solution(mesh):
    n_fsdp, n_seq = mesh.shape["fsdp"], mesh.shape["seq"]
    in_specs = (
        P(None, "fsdp", "seq", None),
        P("fsdp", None),
        P("fsdp"),
        P("fsdp", None),
        P("fsdp", None),
        P("fsdp", None),
        P(None, "fsdp"),
        P(None, "fsdp", "seq"),
        P(),
        P(None, "fsdp", "seq", None),
    )
    out_specs = (
        P(None, "fsdp", "seq", None),
        P(None, "fsdp", "seq", None),
        P("fsdp", None),
        P("fsdp"),
        P("fsdp"),
        P("fsdp", None),
        P("fsdp", None),
        P("fsdp", None),
        P(None, "fsdp"),
    )

    def local(*args):
        body = on_device_tiled if (n_fsdp, n_seq) == (8, 4) else on_device
        return body(*args, n_fsdp=n_fsdp, n_seq=n_seq)

    return jax.shard_map(local, mesh=mesh, in_specs=in_specs, out_specs=out_specs, check_vma=False)
```

```python
import functools

import jax
import jax.numpy as jnp
import numpy as np
from jax import lax
from jax.experimental import pallas as pl
from jax.experimental.pallas import tpu as pltpu
from jax.sharding import PartitionSpec as P

HEADS = 9
KV_HEADS = 3
HEAD_DIM = 64
GROUP = HEADS // KV_HEADS
QW = HEADS * HEAD_DIM
KW = KV_HEADS * HEAD_DIM
EPS = 1e-05
ROPE_BASE = 100000.0
MASKED = -1000000000.0
BF = jnp.bfloat16
F32 = jnp.float32


def dot(a, b, ca, cb):
    return lax.dot_general(a, b, (((ca,), (cb,)), ((), ())), preferred_element_type=F32)


def rotary(values, cosine, sine):
    half = values.shape[-1] // 2
    a, b = values[..., :half], values[..., half:]
    return jnp.concatenate([a * cosine - b * sine, b * cosine + a * sine], axis=-1)


def norm_parts(values):
    factor = lax.rsqrt(jnp.mean(values * values, axis=-1, keepdims=True) + EPS)
    return factor, values * factor


def norm_back(grad_in, gain, factor, normed):
    scaled = grad_in * gain
    return factor * (scaled - normed * jnp.mean(scaled * normed, axis=-1, keepdims=True))


def whole(*shape_dtypes):
    return [pl.BlockSpec(memory_space=pltpu.VMEM) for _ in shape_dtypes]


def call(kernel, scalars, arrays, outs, flops, scratch=(), mib=52, fetched=(), landing=()):
    specs = [pl.BlockSpec(memory_space=pltpu.SMEM)] * len(scalars) + whole(*arrays)
    specs += [pl.BlockSpec(memory_space=pltpu.HBM)] * len(fetched)
    arrays = [*arrays, *fetched]
    moved = sum(a.size * a.dtype.itemsize for a in arrays) + sum(
        int(np.prod(o.shape)) * o.dtype.itemsize for o in outs
    )
    return pl.pallas_call(
        kernel,
        out_shape=outs,
        in_specs=specs,
        out_specs=whole(*outs),
        scratch_shapes=[
            *[pltpu.VMEM(shape, F32) for shape in scratch],
            *[pltpu.VMEM(shape, BF) for shape in landing],
            *([pltpu.SemaphoreType.DMA((len(fetched),))] if fetched else []),
        ],
        compiler_params=pltpu.CompilerParams(vmem_limit_bytes=mib * 1024 * 1024),
        cost_estimate=pl.CostEstimate(flops=int(flops), bytes_accessed=moved, transcendentals=0),
    )(*scalars, *arrays)


def sds(shape, dtype):
    return jax.ShapeDtypeStruct(shape, dtype)


def turn(x, cosine, sine):
    tiles = []
    low = lax.broadcasted_iota(jnp.int32, (1, 128), 1) % HEAD_DIM < HEAD_DIM // 2
    for t in range(x.shape[1] // 128):
        part = x[:, 128 * t : 128 * t + 128]
        other = jnp.where(low, pltpu.roll(part, 96, 1), pltpu.roll(part, 32, 1))
        tiles.append(part * cosine + other * sine)
    return tiles


def turn_kv(x, cosine, sine):
    lane = lax.broadcasted_iota(jnp.int32, (1, 128), 1)
    first, second = turn(x[:, :256], cosine, sine)
    second = jnp.where(lane < KW - 128, second, x[:, 128:256])
    return jnp.concatenate([first, second, x[:, 256:]], axis=1)


def tables(seq, order, cos_ref, sin_ref):
    cosine = jnp.concatenate([cos_ref[seq ^ o] for o in order], axis=0)
    sine = jnp.concatenate([sin_ref[seq ^ o] for o in order], axis=0)
    return cosine, sine


def heads_to_rows(x, g):
    return jnp.concatenate(
        [x[:, HEAD_DIM * h : HEAD_DIM * (h + 1)] for h in range(GROUP * g, GROUP * (g + 1))], axis=0
    )


def rows_to_heads(parts, length):
    return jnp.concatenate(
        [p[length * r : length * (r + 1)] for p in parts for r in range(GROUP)], axis=1
    )


def attention_forward(order, length, seq_ref, blocks, wq, wkv, bq, bkv, gain, cos, sin, mask,
                      att_o, q_o, k_o, v_o):
    seq = seq_ref[0]
    cosine, sine = tables(seq, order, cos, sin)
    width = gain.shape[1]
    for b in range(blocks.shape[1] // length):
        x = blocks[:, b * length : (b + 1) * length, :width].astype(F32)
        x = x.reshape(len(order) * length, width)
        first = (norm_parts(x)[1] * gain[...]).astype(BF)
        kv = dot(first, wkv[...], 1, 0) + bkv[...]
        q = dot(first[:length], wq[...], 1, 0) + bq[...]
        q = jnp.concatenate(turn(q, cosine[:length], sine[:length]), axis=1).astype(BF)
        q = q * jnp.asarray(HEAD_DIM ** (-0.5), BF)
        kv = turn_kv(kv, cosine, sine).astype(BF)
        allowed = jnp.concatenate([mask[b]] * GROUP, axis=0) > 0.0
        parts = []
        for g in range(KV_HEADS):
            qg = heads_to_rows(q, g)
            kg = kv[:, HEAD_DIM * g : HEAD_DIM * (g + 1)]
            vg = kv[:, KW + HEAD_DIM * g : KW + HEAD_DIM * (g + 1)]
            q_o[b, g] = qg
            k_o[b, g] = kg
            v_o[b, g] = vg
            scores = jnp.where(allowed, dot(qg, kg, 1, 1), MASKED)
            top = jnp.max(scores, axis=-1, keepdims=True)
            e = jnp.exp(scores - top)
            total = jnp.sum(e, axis=-1, keepdims=True)
            probs = (e * (1.0 / total)).astype(BF)
            parts.append(dot(probs, vg, 1, 0))
        att_o[b * length : (b + 1) * length, :] = rows_to_heads(parts, length).astype(BF)


def feed_forward(attended, source, wo, wgu, wd, gain, cot, weight,
                 out_o, down_o, gu_o, mid_o, wout_o, attg_o, gain_o):
    units = wd.shape[0]
    step = units // 3
    att = attended[...]
    middle = source[...].astype(F32) + dot(att, wo[...], 1, 0)
    scale_two, normed = norm_parts(middle)
    g2 = gain[...]
    second = (normed * g2).astype(BF)
    out_grad = cot[...].astype(F32) * weight[...]
    feed_grad = out_grad.astype(BF)
    feed = None
    back = None
    for j in range(0, units, step):
        wg = wgu[:, j : j + step]
        wu = wgu[:, units + j : units + j + step]
        wdj = wd[j : j + step, :]
        gate = dot(second, wg, 1, 0)
        up = dot(second, wu, 1, 0)
        sig = jax.nn.sigmoid(gate)
        act = gate * sig
        product = (act * up).astype(BF)
        part = dot(product, wdj, 1, 0)
        feed = part if feed is None else feed + part
        down_o[j : j + step, :] = dot(product, feed_grad, 0, 0).astype(BF)
        pgrad = dot(feed_grad, wdj, 1, 1)
        ggrad = (pgrad * up * (sig * (1.0 + gate * (1.0 - sig)))).astype(BF)
        ugrad = (pgrad * act).astype(BF)
        gu_o[:, j : j + step] = dot(second, ggrad, 0, 0).astype(BF)
        gu_o[:, units + j : units + j + step] = dot(second, ugrad, 0, 0).astype(BF)
        part = dot(ggrad, wg, 1, 1) + dot(ugrad, wu, 1, 1)
        back = part if back is None else back + part
    out_o[...] = (middle + feed).astype(BF)
    gain_o[...] = jnp.sum(back * normed, axis=0, keepdims=True)
    middle_grad = out_grad + norm_back(back, g2, scale_two, normed)
    mid_o[...] = middle_grad
    branch = middle_grad.astype(BF)
    wout_o[...] = dot(att, branch, 0, 0).astype(BF)
    attg_o[...] = dot(branch, wo[...], 1, 1).astype(BF)


def attention_backward(order, length, seq_ref, blocks, wq, wkv, gain, cos, sin, mask, q_i, k_i, v_i,
                       attg, dq_o, dkv_o, wgrad_o, bias_o, gain_o):
    seq = seq_ref[0]
    cosine, sine = tables(seq, order, cos, sin)
    width = gain.shape[1]
    q_wgrad = kv_wgrad = bias_q = bias_kv = gain_sum = None
    for b in range(blocks.shape[1] // length):
        x = blocks[:, b * length : (b + 1) * length, :width].astype(F32)
        x = x.reshape(len(order) * length, width)
        normed = norm_parts(x)[1]
        first = (normed * gain[...]).astype(BF)
        allowed = jnp.concatenate([mask[b]] * GROUP, axis=0) > 0.0
        ag = attg[b * length : (b + 1) * length, :]
        dqs, dks, dvs = [], [], []
        for g in range(KV_HEADS):
            qg, kg, vg = q_i[b, g], k_i[b, g], v_i[b, g]
            agg = heads_to_rows(ag, g)
            scores = jnp.where(allowed, dot(qg, kg, 1, 1), MASKED)
            e = jnp.exp(scores - jnp.max(scores, axis=-1, keepdims=True))
            p = e * (1.0 / jnp.sum(e, axis=-1, keepdims=True))
            dvs.append(dot(p.astype(BF), agg, 0, 0))
            pg = dot(agg, vg, 1, 1)
            inner = jnp.sum(p * pg, axis=-1, keepdims=True)
            ds = (p * (pg - inner)).astype(BF)
            dqs.append(dot(ds, kg, 1, 0) * HEAD_DIM ** (-0.5))
            dks.append(dot(ds, qg, 0, 0))
        dq = rows_to_heads(dqs, length)
        dq = jnp.concatenate([dq, jnp.zeros((length, 64), F32)], axis=1)
        dq = jnp.concatenate(turn(dq, cosine[:length], -sine[:length]), axis=1).astype(BF)
        dkv = jnp.concatenate(dks + dvs, axis=1)
        dkv = turn_kv(dkv, cosine, -sine).astype(BF)
        dq_o[b * length : (b + 1) * length, :] = dq
        for r in range(len(order)):
            dkv_o[r, b * length : (b + 1) * length, :] = dkv[r * length : (r + 1) * length, :]
        wq_part = dot(first[:length], dq, 0, 0)
        wkv_part = dot(first, dkv, 0, 0)
        bq_part = jnp.sum(dq.astype(F32), axis=0, keepdims=True)
        bkv_part = jnp.sum(dkv.astype(F32), axis=0, keepdims=True)
        e_kv = dot(dkv, wkv[...], 1, 1) * normed
        e_q = dot(dq[:, :QW], wq[:, :QW], 1, 1) * normed[:length]
        g_part = jnp.sum(e_kv, axis=0, keepdims=True) + jnp.sum(e_q, axis=0, keepdims=True)
        if q_wgrad is None:
            q_wgrad, kv_wgrad, bias_q, bias_kv, gain_sum = wq_part, wkv_part, bq_part, bkv_part, g_part
        else:
            q_wgrad, kv_wgrad = q_wgrad + wq_part, kv_wgrad + wkv_part
            bias_q, bias_kv, gain_sum = bias_q + bq_part, bias_kv + bkv_part, gain_sum + g_part
    wgrad_o[...] = jnp.concatenate([q_wgrad[:, :QW], kv_wgrad], axis=1).astype(BF)
    bias_o[...] = jnp.concatenate([bias_q[:, :QW], bias_kv], axis=1)
    gain_o[...] = gain_sum


def input_gradient(dq, own, a, b, c, source, mid, wq, wkv, gain, out_o):
    kv = own[...].astype(F32) + a[...].astype(F32) + b[...].astype(F32) + c[...].astype(F32)
    first_grad = dot(dq[:, :QW], wq[:, :QW], 1, 1) + dot(kv.astype(BF), wkv[...], 1, 1)
    scale_one, normed = norm_parts(source[...].astype(F32))
    out_o[...] = mid[...] + norm_back(first_grad, gain[...], scale_one, normed)

def chosen(flag, a, b):
    return jnp.where(flag != 0, b, a)


class Blocks:
    def __init__(self, *refs):
        self.refs = refs
        self.shape = (len(refs),) + refs[0].shape

    def __getitem__(self, key):
        return jnp.stack([ref[key[1:]] for ref in self.refs])


def cut_qkv(core_bit, meta, w_hbm, bias_hbm, gains_hbm, out_o, w, bias, gains, all_s, sems):
    pairs = ((w_hbm, w), (bias_hbm, bias), (gains_hbm, gains))
    copies = [pltpu.make_async_copy(a, b, sems.at[i]) for i, (a, b) in enumerate(pairs)]
    for copy in copies:
        copy.start()
    for copy in copies:
        copy.wait()
    rows = w.shape[0]
    n = bias.shape[1]
    all_s[:rows, :] = w[...].astype(F32)
    all_s[rows:, :] = jnp.zeros((8, w.shape[1]), F32)
    all_s[rows : rows + 1, :n] = bias[...].astype(F32)
    for i in range(2):
        all_s[rows : rows + 1, n + rows * i : n + rows * (i + 1)] = gains[i : i + 1, :].astype(F32)
    half = out_o.shape[0]
    at = pl.multiple_of((meta[0] & core_bit) * half, 8)
    out_o[...] = all_s[pl.ds(at, half), :].astype(BF)


def first_forward(order, length, d_rows, n_bias, meta, b0, b1, b2, b3, a00, a10, a01, a11, cos, sin, mask,
                  att_o, q_o, k_o, v_o, w_o, gain_o, w_s, b_s):
    blocks = Blocks(b0, b1, b2, b3)
    core, x = meta[0] & 1, meta[1] & 1
    cut = a00.shape[2]
    for x_rel, c_rel, piece in ((0, 0, a00), (1, 0, a10), (0, 1, a01), (1, 1, a11)):
        for z0 in range(2):
            for z1 in range(2):
                at = (z1 * 4 + z0 * 2 + (x ^ x_rel)) * 2 * cut + (core ^ c_rel) * cut
                w_s[pl.ds(pl.multiple_of(at, 8), cut), :] = piece[z0, z1].astype(F32)
    n_f = w_s.shape[0] // (2 * cut)
    starts = [2 * cut * f for f in range(n_f)]
    w_o[...] = jnp.concatenate([w_s[at : at + d_rows, :] for at in starts], axis=0).astype(BF)
    lines = [w_s[at + d_rows : at + d_rows + 1, :] for at in starts]
    b_s[...] = jnp.concatenate([line[:, :n_bias] for line in lines], axis=1)
    for i in range(2):
        at = n_bias + d_rows * i
        gain_o[i : i + 1, :] = jnp.concatenate([line[:, at : at + d_rows] for line in lines], axis=1)
    wide = QW + 64
    attention_forward(order, length, meta, blocks, w_o[:, :wide], w_o[:, QW:], b_s[:, :wide], b_s[:, QW:],
                      gain_o[0:1, :], cos, sin, mask, att_o, q_o, k_o, v_o)


def turned(out, value):
    length = out.shape[2]
    for b in range(out.shape[0]):
        out[b] = value[length * b : length * (b + 1)].T.astype(out.dtype)


def rel(meta, f):
    r = f ^ meta[1]
    return r & 1, (r >> 1) & 1, (r >> 2) & 1


def fetch_pieces(meta, refs, b_s, g_s, sems):
    core, y, x, z0 = meta[0] & 1, (meta[0] >> 1) & 1, meta[1] & 1, (meta[1] >> 1) & 1
    copies = []
    for i in range(8):
        at = (z0 ^ (i >> 2), x ^ ((i >> 1) & 1), core ^ (i & 1))
        copies.append(pltpu.make_async_copy(refs[i], b_s.at[at], sems.at[i]))
    for i in range(8):
        at = (y ^ ((i >> 1) & 1), core ^ (i & 1), x ^ (i >> 2))
        copies.append(pltpu.make_async_copy(refs[8 + i], g_s.at[at], sems.at[8 + i]))
    for copy in copies:
        copy.start()
    return copies


def feed_forward_pieces(d_rows, ff_rows, meta, attended, source, gains, cot, weight, *refs):
    out_o, ak_o, ag_o, bk_o, bg_o, dk_o, dg_o, mid_o, attg_o, gain_o, down_s, wout_s, b_s, g_s, sems = refs[16:]
    copies = fetch_pieces(meta, refs, b_s, g_s, sems)
    core, y = meta[0] & 1, (meta[0] >> 1) & 1
    part_d = ff_rows // 4
    part_o = d_rows // 3
    cut = b_s.shape[4] - ff_rows // 2
    half = g_s.shape[-1] // 2
    for copy in copies[:8]:
        copy.wait()
    wo = []
    for f in range(8):
        for c in range(2):
            rows = b_s[(f >> 1) & 1, f & 1, c, f >> 2, ff_rows // 2 :, :].astype(F32)
            wo.append(rows if c == 0 else rows[: d_rows - cut])
    wo = jnp.concatenate(wo, axis=0).astype(BF)
    att = attended[...]
    middle = source[...].astype(F32) + dot(att, wo, 1, 0)
    scale_two, normed = norm_parts(middle)
    g2 = gains[1:2, :]
    second = (normed * g2).astype(BF)
    out_grad = cot[...].astype(F32) * weight[...]
    feed_grad = out_grad.astype(BF)
    for copy in copies[8:]:
        copy.wait()
    feed = back = None
    for c_rel in (1, 0):
        h = core ^ c_rel
        weights = []
        for yy in range(2):
            rows = [g_s[yy, h, f & 1, (f >> 1) & 1, f >> 2].astype(F32) for f in range(8)]
            weights.append(jnp.concatenate(rows, axis=0).astype(BF))
        wg, wu = weights
        wd = [b_s[i >> 1, i & 1, c, h, : ff_rows // 2, :] for i in range(4) for c in range(2)]
        wd = jnp.concatenate(wd, axis=0)
        gate = dot(second, wg, 1, 0)
        up = dot(second, wu, 1, 0)
        sig = jax.nn.sigmoid(gate)
        act = gate * sig
        product = (act * up).astype(BF)
        part = dot(product, wd, 1, 0)
        feed = part if feed is None else feed + part
        down_s[...] = dot(product, feed_grad, 0, 0)
        pgrad = dot(feed_grad, wd, 1, 1)
        ggrad = (pgrad * up * (sig * (1.0 + gate * (1.0 - sig)))).astype(BF)
        ugrad = (pgrad * act).astype(BF)
        part = dot(ggrad, wg, 1, 1) + dot(ugrad, wu, 1, 1)
        back = part if back is None else back + part
        for i in range(4):
            x, z0, z1 = rel(meta, 4 * h + i)
            for yy in range(2):
                for c_to, to in ((0, dk_o), (1, dg_o)):
                    at = pl.multiple_of(i * ff_rows + (yy * 2 + (core ^ c_to)) * part_d, 16)
                    to[y ^ yy, x, z0, z1, :part_d, :] = down_s[pl.ds(at, part_d), :].astype(BF)
        to_a, to_b = (ag_o, bg_o) if c_rel else (ak_o, bk_o)
        for yy, grad in ((0, ggrad), (1, ugrad)):
            wgrad = dot(second, grad, 0, 0)
            for f in range(8):
                x, z0, z1 = rel(meta, f)
                block = wgrad[d_rows * f : d_rows * (f + 1), :].astype(BF)
                to_a[x, z0, z1, yy] = block[:, :half]
                to_b[z0, z1, x, yy] = block[:, half:]
    turned(out_o, middle + feed)
    gain_o[...] = jnp.sum(back * normed, axis=0, keepdims=True)
    middle_grad = out_grad + norm_back(back, g2, scale_two, normed)
    mid_o[...] = middle_grad
    branch = middle_grad.astype(BF)
    attg_o[...] = dot(branch, wo, 1, 1).astype(BF)
    wout = dot(att, branch, 0, 0)
    for f in range(8):
        wout_s[f, :d_rows, :] = wout[d_rows * f : d_rows * (f + 1), :]
        wout_s[f, d_rows:, :] = jnp.zeros((part_o, wout.shape[1]), F32)
    for f in range(8):
        x, z0, z1 = rel(meta, f)
        for yy in range(2):
            for c_to, to in ((0, dk_o), (1, dg_o)):
                at = pl.multiple_of((yy * 2 + (core ^ c_to)) * part_o, 8)
                to[y ^ yy, x, z0, z1, part_d:, :] = wout_s[f, pl.ds(at, part_o), :].astype(BF)


def attention_backward_pieces(order, length, d_rows, meta, b0, b1, b2, b3, w, gains, cos, sin, mask, q_i, k_i, v_i,
                              attg, gain_two, dq_o, dk_o, dg_o, rk_o, rg_o, w_s, bias_s, gain_s, small_s):
    blocks = Blocks(b0, b1, b2, b3)
    half = len(order) // 2

    class Pieces:
        def __setitem__(self, key, value):
            ref = dk_o if key[0] < half else dg_o
            ref[(key[0] % half,) + key[1:]] = value

    class Wgrad:
        def __setitem__(self, key, value):
            w_s[:, : 2 * KW] = value[:, QW:].astype(F32)
            w_s[:, 2 * KW : 2 * KW + QW] = value[:, :QW].astype(F32)
            w_s[:, 2 * KW + QW :] = jnp.zeros((value.shape[0], 64), F32)

    wide = QW + 64
    attention_backward(order, length, meta, blocks, w[:, :wide], w[:, QW:], gains[0:1, :], cos, sin, mask,
                       q_i, k_i, v_i, attg, dq_o, Pieces(), Wgrad(), bias_s, gain_s)
    n_f = small_s.shape[0]
    qk, v = (QW + KW) // n_f, KW // n_f
    bias, g1, g2 = bias_s[...], gain_s[...], gain_two[...]
    for f in range(n_f):
        line = jnp.concatenate(
            [
                bias[:, qk * f : qk * (f + 1)],
                bias[:, QW + KW + v * f : QW + KW + v * (f + 1)],
                g1[:, d_rows * f : d_rows * (f + 1)],
                jnp.zeros((1, 256 - qk - v - d_rows), F32),
                g2[:, d_rows * f : d_rows * (f + 1)],
                jnp.zeros((1, 768 - d_rows), F32),
            ],
            axis=1,
        )
        small_s[f] = jnp.broadcast_to(line, (8, 1024))
    core, y = meta[0] & 1, (meta[0] >> 1) & 1
    for f in range(n_f):
        x, z0, z1 = rel(meta, f)
        for yy in range(2):
            for c_to, to in ((0, rk_o), (1, rg_o)):
                at = pl.multiple_of((yy * 2 + (core ^ c_to)) * 256, 256)
                block = [w_s[d_rows * f : d_rows * (f + 1), pl.ds(at, 256)], small_s[f, :, pl.ds(at, 256)]]
                to[y ^ yy, x, z0, z1] = jnp.concatenate(block, axis=0).astype(BF)


def input_gradient_two(dq, own, other, source, mid, w, gains, out_o):
    kv = (own[...].astype(F32) + other[...].astype(F32)).astype(BF)
    first_grad = dot(dq[:, :QW], w[:, :QW], 1, 1) + dot(kv, w[:, QW:], 1, 1)
    scale_one, normed = norm_parts(source[...].astype(F32))
    turned(out_o, mid[...] + norm_back(first_grad, gains[0:1, :], scale_one, normed))


def place_gate(meta, near, far, out_o, parts=1, part=0):
    core = meta[0] & 1
    n = near.shape[2]
    for pieces, c_rel in ((near, 0), (far, 1)):
        for yy in range(2):
            at = pl.multiple_of(((yy * 2 + (core ^ c_rel)) * parts + part) * n, 128)
            out_o[:, pl.ds(at, n)] = pieces[yy].astype(F32)


def place_down(part_d, meta, p00, p10, p01, p11, out_o, wout_o):
    seq = meta[0]
    part_o = p00.shape[0] - part_d
    for piece, o in ((p00[...], 0), (p10[...], 2), (p01[...], 1), (p11[...], 3)):
        piece = piece.astype(F32)
        to = seq ^ o
        out_o[pl.ds(pl.multiple_of(to * part_d, 16), part_d), :] = piece[:part_d]

        @pl.when(to < 3)
        def _():
            wout_o[pl.ds(pl.multiple_of(to * part_o, 8), part_o), :] = piece[part_d:]


def place_qkv(qk, v, meta, p00, p10, p01, p11, w_o, bqk_o, bv_o, gains_o, all_s):
    n = p00.shape[1]
    for piece, o in ((p00, 0), (p10, 2), (p01, 1), (p11, 3)):
        all_s[:, pl.ds(pl.multiple_of((meta[0] ^ o) * n, 128), n)] = piece[...].astype(F32)
    d_rows = w_o.shape[0]
    w_o[:, :QW] = all_s[:d_rows, 2 * KW : 2 * KW + QW]
    w_o[:, QW:] = all_s[:d_rows, : 2 * KW]
    line = all_s[d_rows : d_rows + 1, :]
    bqk_o[...] = line[:, :qk]
    bv_o[...] = line[:, qk : qk + v]
    gains_o[0:1, :] = line[:, qk + v : qk + v + d_rows]
    gains_o[1:2, :] = line[:, 256 : 256 + d_rows]


def place_all(part_d, qk, v, meta, a_near, a_far, b_near, b_far, d0, d1, d2, d3, r0, r1, r2, r3,
              gate_o, down_o, wout_o, w_o, bqk_o, bv_o, gains_o, all_s):
    place_gate(meta, a_near, a_far, gate_o, 2, 0)
    place_gate(meta, b_near, b_far, gate_o, 2, 1)
    place_down(part_d, meta, d0, d1, d2, d3, down_o, wout_o)
    place_qkv(qk, v, meta, r0, r1, r2, r3, w_o, bqk_o, bv_o, gains_o, all_s)


class Net:
    def __init__(self, n_fsdp, n_seq):
        self.n_fsdp, self.n_seq = n_fsdp, n_seq
        self.total = n_fsdp * n_seq
        f, s = lax.axis_index("fsdp"), lax.axis_index("seq")
        self.index = f * n_seq + s
        self.seq_bits = [1 << b for b in range(n_seq.bit_length() - 1)]
        self.fsdp_bits = [n_seq << b for b in range(n_fsdp.bit_length() - 1)]

    def swap(self, value, mask):
        pairs = [(i, i ^ mask) for i in range(self.total)]
        return lax.ppermute(value, ("fsdp", "seq"), pairs)

    def bit(self, mask):
        return (self.index & mask) != 0

    def both(self, mine, mask, axis, other=None):
        other = self.swap(mine, mask) if other is None else other
        high = self.bit(mask)
        return jnp.stack([jnp.where(high, other, mine), jnp.where(high, mine, other)], axis=axis)

    def half(self, value, mask, axis):
        return lax.dynamic_index_in_dim(
            value, self.bit(mask).astype(jnp.int32), axis, keepdims=False
        )

    def add_half(self, value, mask, axis):
        mine = self.bit(mask).astype(jnp.int32)
        keep = lax.dynamic_index_in_dim(value, mine, axis, keepdims=False)
        give = lax.dynamic_index_in_dim(value, 1 - mine, axis, keepdims=False)
        got = self.swap(give, mask)
        return (keep.astype(F32) + got.astype(F32)).astype(value.dtype)

    def gather_fsdp(self, value):
        for step, mask in enumerate(reversed(self.fsdp_bits)):
            value = self.both(value, mask, step)
        return value

    def scatter_fsdp(self, value, first_axis=0):
        count = len(self.fsdp_bits)
        for step, mask in enumerate(self.fsdp_bits):
            value = self.add_half(value, mask, first_axis + count - 1 - step)
        return value


def on_device(
    hidden, w_qkv, b_qkv, w_out, w_gate_up, w_down, norm_gains, segment_ids, token_counts, cotangent,
    n_fsdp, n_seq,
):
    net = Net(n_fsdp, n_seq)
    micro, batch, length, width = hidden.shape
    full_length = length * n_seq
    tokens_micro = batch * n_fsdp * full_length
    scale = HEAD_DIM ** (-0.5)
    rows = micro * batch * length
    d_rows = w_qkv.shape[0]
    ff_rows = w_down.shape[0]
    units = w_gate_up.shape[1] // 2
    qkv_w = w_qkv.shape[1]
    core = net.seq_bits[0]
    f_lead = (2,) * len(net.fsdp_bits)

    ids = segment_ids.reshape(rows, 1).astype(BF)
    block = jnp.concatenate(
        [hidden.reshape(rows, width), jnp.broadcast_to(ids, (rows, 64))], axis=1
    )
    blocks = block[None]
    for mask in reversed(net.seq_bits):
        blocks = jnp.concatenate([blocks, net.swap(blocks, mask)], axis=0)
    order = [0]
    for mask in reversed(net.seq_bits):
        order = order + [o ^ mask for o in order]
    seq_index = lax.axis_index("seq")
    block_ids = [seq_index ^ o for o in order]

    pad_rows = -(d_rows + 1) % 16 + 1
    extra = jnp.zeros((pad_rows, qkv_w), BF)
    small = jnp.concatenate([b_qkv, norm_gains.reshape(-1)])
    extra = extra.at[0, : small.shape[0]].set(small)
    shard_a = jnp.concatenate([w_qkv, extra], axis=0).reshape(2, -1, qkv_w)
    got_a = net.gather_fsdp(net.half(shard_a, core, 0))
    full_a = net.both(got_a, core, len(f_lead)).reshape(n_fsdp, d_rows + pad_rows, qkv_w)
    wf_qkv = full_a[:, :d_rows].reshape(n_fsdp * d_rows, qkv_w)
    smalls = full_a[:, d_rows]
    n_bias = b_qkv.shape[0]
    bias = smalls[:, :n_bias].reshape(-1).astype(F32)
    gains = smalls[:, n_bias : n_bias + 2 * d_rows].reshape(n_fsdp, 2, d_rows).astype(F32)
    gain_one = gains[:, 0].reshape(-1)
    gain_two = gains[:, 1].reshape(-1)

    pad_b = -(d_rows + ff_rows) % 16
    shard_b = jnp.concatenate([w_out, w_down, jnp.zeros((pad_b, width), BF)], axis=0)
    shard_b = shard_b.reshape(2, -1, width)
    got_b = net.gather_fsdp(net.half(shard_b, core, 0))

    parts = n_seq
    shard_c = w_gate_up.reshape(d_rows, parts, -1)
    got_c = net.gather_fsdp(lax.dynamic_index_in_dim(shard_c, seq_index, 1, keepdims=False))
    full_b = net.both(got_b, core, len(f_lead)).reshape(n_fsdp, -1, width)
    wf_out = full_b[:, :d_rows].reshape(n_fsdp * d_rows, width)
    wf_down = full_b[:, d_rows : d_rows + ff_rows].reshape(n_fsdp * ff_rows, width)
    got_c = got_c.reshape(n_fsdp * d_rows, -1)
    for mask in reversed(net.seq_bits):
        got_c = net.both(got_c, mask, got_c.ndim - 1)
    wf_gate_up = got_c.reshape(n_fsdp * d_rows, 2 * units)

    places = np.arange(full_length, dtype=np.float32)
    speeds = np.power(ROPE_BASE, -2.0 * np.arange(HEAD_DIM // 2, dtype=np.float32) / HEAD_DIM)
    angles = places[:, None] * speeds.astype(np.float32)[None, :]
    cos_t = np.tile(np.cos(angles), (1, 4)).reshape(n_seq, length, 128)
    sin_t = np.concatenate([-np.sin(angles), np.sin(angles)] * 2, axis=1).reshape(n_seq, length, 128)
    cos_t, sin_t = jnp.asarray(cos_t, F32), jnp.asarray(sin_t, F32)
    seqs = micro * batch
    seg_all = blocks[..., width].reshape(n_seq, seqs, length).transpose(1, 0, 2)
    own_places = seq_index * length + jnp.arange(length, dtype=jnp.int32)
    key_places = jnp.stack(block_ids)[:, None] * length + jnp.arange(length, dtype=jnp.int32)
    allowed = (seg_all[:, 0, :, None] == seg_all.reshape(seqs, 1, -1)) & (
        own_places[None, :, None] >= key_places.reshape(1, 1, -1)
    )
    allowed = allowed.astype(F32)
    seq_scalar = seq_index.astype(jnp.int32).reshape(1)
    wq, wkv = wf_qkv[:, : QW + 64], wf_qkv[:, QW:]
    gain_one, gain_two = gain_one[None], gain_two[None]
    source = hidden.reshape(rows, width)
    n_all = n_seq * rows
    attended, q_s, k_s, v_s = call(
        functools.partial(attention_forward, order, length),
        [seq_scalar],
        [blocks, wq, wkv, bias[None, : QW + 64], bias[None, QW:], gain_one, cos_t, sin_t, allowed],
        [
            sds((rows, QW), BF),
            sds((seqs, KV_HEADS, GROUP * length, HEAD_DIM), BF),
            sds((seqs, KV_HEADS, full_length, HEAD_DIM), BF),
            sds((seqs, KV_HEADS, full_length, HEAD_DIM), BF),
        ],
        2 * n_all * width * 2 * KW + 2 * rows * width * QW + 4 * rows * full_length * QW,
    )

    weight = tokens_micro / token_counts.astype(F32)
    weight = jnp.repeat(weight, batch * length)[:, None]
    block_out, down_grad, gate_up_wgrad, middle_grad, out_wgrad, attended_grad, gain_two_grad = call(
        feed_forward,
        [],
        [attended, source, wf_out, wf_gate_up, wf_down, gain_two, cotangent.reshape(rows, width), weight],
        [
            sds((rows, width), BF),
            sds((units, width), BF),
            sds((width, 2 * units), BF),
            sds((rows, width), F32),
            sds((QW, width), BF),
            sds((rows, QW), BF),
            sds((1, width), F32),
        ],
        6 * rows * width * 3 * units + 6 * rows * width * QW,
    )
    block_out = block_out.reshape(hidden.shape)

    def seq_axes(value, axis, masks):
        for mask in masks:
            value = net.add_half(value, mask, axis)
        return value

    quarter = (2,) * len(net.seq_bits)
    n_f = len(f_lead)
    red_down = down_grad.reshape(f_lead + quarter + (ff_rows // n_seq, width))
    for step, mask in enumerate(net.seq_bits):
        red_down = net.add_half(red_down, mask, n_f + len(quarter) - 1 - step)
    red_down = net.scatter_fsdp(red_down)

    red_gate = gate_up_wgrad.reshape(f_lead + (d_rows,) + quarter + (2 * units // n_seq,))
    red_gate = net.add_half(red_gate, core, n_f + len(quarter))
    red_gate = net.add_half(red_gate, net.fsdp_bits[0], n_f - 1)
    for step, mask in enumerate(net.seq_bits[1:]):
        red_gate = net.add_half(red_gate, mask, n_f - 1 + len(quarter) - 1 - step)
    for step, mask in enumerate(net.fsdp_bits[1:]):
        red_gate = net.add_half(red_gate, mask, n_f - 2 - step)

    dq, dkv, qkv_wgrad, bias_grad, gain_one_grad = call(
        functools.partial(attention_backward, order, length),
        [seq_scalar],
        [blocks, wq, wkv, gain_one, cos_t, sin_t, allowed, q_s, k_s, v_s, attended_grad],
        [
            sds((rows, QW + 64), BF),
            sds((n_seq, rows, 2 * KW), BF),
            sds((width, qkv_w), BF),
            sds((1, qkv_w), F32),
            sds((1, width), F32),
        ],
        4 * n_all * width * 2 * KW + 4 * rows * width * QW + 10 * rows * full_length * QW,
    )
    kv_parts = [dkv[0]]
    for place, mask_bits in enumerate(order):
        if mask_bits:
            kv_parts.append(net.swap(dkv[place], mask_bits))
    (hidden_grad,) = call(
        input_gradient,
        [],
        [dq, *kv_parts, source, middle_grad, wq, wkv, gain_one],
        [sds((rows, width), F32)],
        2 * rows * width * qkv_w,
    )
    hidden_grad = hidden_grad.reshape(hidden.shape)
    bias_grad, gain_one_grad, gain_two_grad = bias_grad[0], gain_one_grad[0], gain_two_grad[0]

    qk_rows, v_rows = (QW + KW) // n_fsdp, KW // n_fsdp
    small_grads = jnp.concatenate(
        [
            bias_grad[: QW + KW].reshape(n_fsdp, qk_rows),
            bias_grad[QW + KW :].reshape(n_fsdp, v_rows),
            gain_one_grad.reshape(n_fsdp, d_rows),
            gain_two_grad.reshape(n_fsdp, d_rows),
        ],
        axis=1,
    ).astype(BF)
    wide = qkv_w + width
    small_pad = jnp.zeros((n_fsdp, pad_rows, wide), BF)
    small_pad = small_pad.at[:, 0, : small_grads.shape[1]].set(small_grads)
    rest = jnp.concatenate([qkv_wgrad, out_wgrad], axis=1)
    rest = jnp.concatenate([rest.reshape(n_fsdp, d_rows, wide), small_pad], axis=1)
    rest = rest.reshape(f_lead + (d_rows + pad_rows,) + quarter + (wide // n_seq,))
    for step, mask in enumerate(net.seq_bits):
        rest = net.add_half(rest, mask, n_f + 1 + len(quarter) - 1 - step)
    rest = net.scatter_fsdp(rest)

    def seq_back(value, axis):
        for step, mask in enumerate(reversed(net.seq_bits)):
            value = net.both(value, mask, axis + step)
        return value

    out_down = seq_back(red_down, 0).reshape(ff_rows, width).astype(F32)
    out_gate = seq_back(red_gate, 1).reshape(d_rows, 2 * units).astype(F32)
    out_rest = seq_back(rest, 1).reshape(d_rows + pad_rows, wide).astype(F32)
    line = out_rest[d_rows]
    edge = qk_rows + v_rows
    return (
        block_out,
        hidden_grad,
        out_rest[:d_rows, :qkv_w],
        line[:qk_rows],
        line[qk_rows:edge],
        out_rest[:d_rows, qkv_w:],
        out_gate,
        out_down,
        line[edge : edge + 2 * d_rows].reshape(2, d_rows),
    )


def after(value, *others):
    return lax.optimization_barrier((value, *others))[0]


def rope_tables(full_length, n_seq):
    places = np.arange(full_length, dtype=np.float32)
    speeds = np.power(ROPE_BASE, -2.0 * np.arange(HEAD_DIM // 2, dtype=np.float32) / HEAD_DIM)
    angles = places[:, None] * speeds.astype(np.float32)[None, :]
    cos_t = np.tile(np.cos(angles), (1, 4)).reshape(n_seq, -1, 128)
    sin_t = np.concatenate([-np.sin(angles), np.sin(angles)] * 2, axis=1).reshape(n_seq, -1, 128)
    return jnp.asarray(cos_t, F32), jnp.asarray(sin_t, F32)


def on_device_tiled(
    hidden, w_qkv, b_qkv, w_out, w_gate_up, w_down, norm_gains, segment_ids, token_counts, cotangent,
    n_fsdp, n_seq,
):
    net = Net(n_fsdp, n_seq)
    micro, batch, length, width = hidden.shape
    full_length = length * n_seq
    tokens_micro = batch * n_fsdp * full_length
    rows = micro * batch * length
    seqs = micro * batch
    d_rows, qkv_w = w_qkv.shape
    ff_rows = w_down.shape[0]
    units = w_gate_up.shape[1] // 2
    n_bias = b_qkv.shape[0]
    core, ybit = net.seq_bits
    xbit, znear, zfar = net.fsdp_bits
    order = [0, 2, 1, 3]
    seq_index = lax.axis_index("seq")
    meta = jnp.stack([seq_index, lax.axis_index("fsdp")]).astype(jnp.int32)
    source = hidden.reshape(rows, width)

    small = [w_qkv, b_qkv[None], norm_gains]
    a0 = pl.pallas_call(
        functools.partial(cut_qkv, core),
        out_shape=sds(((d_rows + 8) // 2, qkv_w), BF),
        in_specs=[pl.BlockSpec(memory_space=pltpu.SMEM)] + [pl.BlockSpec(memory_space=pltpu.HBM)] * 3,
        out_specs=pl.BlockSpec(memory_space=pltpu.VMEM),
        scratch_shapes=[
            *[pltpu.VMEM(v.shape, BF) for v in small],
            pltpu.VMEM((d_rows + 8, qkv_w), F32),
            pltpu.SemaphoreType.DMA((3,)),
        ],
        compiler_params=pltpu.CompilerParams(vmem_limit_bytes=52 * 1024 * 1024),
    )(meta, *small)
    a1 = net.both(a0, zfar, 0)

    ids = segment_ids.reshape(rows, 1).astype(BF)
    block = jnp.concatenate([source, jnp.broadcast_to(ids, (rows, 64))], axis=1)
    block = after(block, a0)
    block_y = net.swap(block, ybit)
    block_c = net.swap(block, core)

    quarter = 2 * units // n_seq
    gu0 = lax.dynamic_slice_in_dim(after(w_gate_up, a0), seq_index * quarter, quarter, axis=1)
    half_b = jnp.concatenate(
        [
            w_down.reshape(2, ff_rows // 2, width),
            jnp.concatenate([w_out, jnp.zeros((8, width), BF)], axis=0).reshape(2, -1, width),
        ],
        axis=1,
    )
    a2 = net.both(a1, znear, 0)
    a_x = net.swap(a2, xbit)
    a_c = net.swap(a2, core)
    gu1 = net.both(gu0, zfar, 0)
    gu2 = net.both(after(gu1, a2), znear, 0)
    block_yc = net.swap(block_y, core)
    a_xc = net.swap(a_x, core)
    gu_x = net.swap(gu2, xbit)
    gu_y = net.swap(gu2, ybit)
    gu_c = net.swap(gu2, core)
    b0 = net.half(after(half_b, gu2), core, 0)
    b1 = net.both(b0, zfar, 0)
    b_z = net.swap(b1, znear)
    b_x = net.swap(b1, xbit)
    b_c = net.swap(b1, core)
    a_xc = after(a_xc, b1)

    cos_t, sin_t = rope_tables(full_length, n_seq)
    block_ids = [seq_index ^ o for o in order]
    blocks = [block, block_y, block_c, block_yc]
    seg_all = jnp.stack([b[:, width].reshape(seqs, length) for b in blocks], axis=1)
    own_places = seq_index * length + jnp.arange(length, dtype=jnp.int32)
    key_places = jnp.stack(block_ids)[:, None] * length + jnp.arange(length, dtype=jnp.int32)
    allowed = (seg_all[:, 0, :, None] == seg_all.reshape(seqs, 1, -1)) & (
        own_places[None, :, None] >= key_places.reshape(1, 1, -1)
    )
    allowed = allowed.astype(F32)
    attended, q_s, k_s, v_s, wf, gains = call(
        functools.partial(first_forward, order, length, d_rows, n_bias),
        [meta],
        [*blocks, a2, a_x, a_c, a_xc, cos_t, sin_t, allowed],
        [
            sds((rows, QW), BF),
            sds((seqs, KV_HEADS, GROUP * length, HEAD_DIM), BF),
            sds((seqs, KV_HEADS, full_length, HEAD_DIM), BF),
            sds((seqs, KV_HEADS, full_length, HEAD_DIM), BF),
            sds((width, qkv_w), BF),
            sds((2, width), F32),
        ],
        1.2e10,
        [(n_fsdp * (d_rows + 8), qkv_w), (1, qkv_w)],
    )
    gu_y = after(gu_y, attended)
    gu_x, b_z, b_x = after(gu_x, gu_y), after(b_z, gu_y), after(b_x, gu_y)
    gu_xy = net.swap(gu_x, ybit)
    b_zx = net.swap(b_z, xbit)
    gu_yc = net.swap(gu_y, core)
    gu_xc = net.swap(gu_x, core)
    b_zc = net.swap(b_z, core)
    b_xc = net.swap(b_x, core)
    b_zxc = net.swap(b_zx, core)
    gu_xyc = net.swap(gu_xy, core)
    pieces = [b1, b_c, b_x, b_xc, b_z, b_zc, b_zx, b_zxc]
    pieces += [gu2, gu_c, gu_y, gu_yc, gu_x, gu_xc, gu_xy, gu_xyc]

    weight = tokens_micro / token_counts.astype(F32)
    weight = jnp.repeat(weight, batch * length)[:, None]
    lead = (2, 2, 2, 2)
    cot = cotangent.reshape(rows, width)
    gate_lead = lead + (d_rows, units // 4)
    block_out, a_keep, a_give, b_keep, b_give, down_keep, down_give, middle_grad, attended_grad, gain_two = call(
        functools.partial(feed_forward_pieces, d_rows, ff_rows),
        [meta],
        [attended, source, gains, cot, weight],
        [
            sds((seqs, width, length), BF),
            sds(gate_lead, BF),
            sds(gate_lead, BF),
            sds(gate_lead, BF),
            sds(gate_lead, BF),
            sds(lead + (ff_rows // 4 + d_rows // 3, width), BF),
            sds(lead + (ff_rows // 4 + d_rows // 3, width), BF),
            sds((rows, width), F32),
            sds((rows, QW), BF),
            sds((1, width), F32),
        ],
        1.4e10,
        [(units // 2, width), (n_fsdp, d_rows + d_rows // 3, width)],
        fetched=pieces,
        landing=[(2, 2, 2, 2) + b1.shape[1:], (2, 2, 2, 2, 2, d_rows, units // 2)],
    )
    block_out = block_out.reshape(micro, batch, width, length).swapaxes(2, 3)

    def add(keep, got):
        return (keep.astype(F32) + got.astype(F32)).astype(BF)

    def halves(keep, got):
        return add(keep[0], got[0]), add(keep[1], got[1])

    a_got = net.swap(a_give, core)
    b_got = net.swap(after(b_give, a_got), core)
    down_got = net.swap(after(down_give, a_got), core)
    a, a_give = halves(a_keep, a_got)
    a_got = net.swap(a_give, xbit)
    b, b_give = halves(b_keep, b_got)
    b_got = net.swap(b_give, znear)
    down, down_give = halves(down_keep, down_got)
    attended_grad = after(attended_grad, a_give, b_give, down_give)
    down_got = net.swap(down_give, ybit)

    dq, dkv_keep, dkv_give, rest_keep, rest_give = call(
        functools.partial(attention_backward_pieces, order, length, d_rows),
        [meta],
        [*blocks, wf, gains, cos_t, sin_t, allowed, q_s, k_s, v_s, attended_grad, gain_two],
        [
            sds((rows, QW + 64), BF),
            sds((2, rows, 2 * KW), BF),
            sds((2, rows, 2 * KW), BF),
            sds(lead + (d_rows + 8, 256), BF),
            sds(lead + (d_rows + 8, 256), BF),
        ],
        1.4e10,
        [(width, 1024), (1, qkv_w), (1, width), (n_fsdp, 8, 1024)],
    )
    b, b_give = halves(b, after(b_got, dq))
    a, a_give = halves(a, after(a_got, b_give))
    b_got = net.swap(b_give, zfar)
    a_got = net.swap(a_give, znear)
    rest, rest_give = halves(rest_keep, after(net.swap(rest_give, core), b_give, down_got))
    rest_got = net.swap(rest_give, ybit)
    down, down_give = halves(down, after(down_got, rest_give))
    down_got = net.swap(down_give, xbit)
    dkv, dkv_give = halves(dkv_keep, after(net.swap(dkv_give, core), down_give))
    dkv_got = net.swap(dkv_give, ybit)
    a, a_give = halves(a, after(a_got, dkv_give))
    a_got = net.swap(a_give, zfar)
    rest, rest_give = halves(rest, after(rest_got, a_give))
    rest_got = net.swap(rest_give, xbit)
    b, b_give = halves(b, after(b_got, rest_give))
    b_got = net.swap(b_give, xbit)
    down, down_give = halves(down, after(down_got, b_give))
    down_got = net.swap(down_give, znear)
    (hidden_grad,) = call(
        input_gradient_two,
        [],
        [dq, dkv, after(dkv_got, down_give), source, middle_grad, wf, gains],
        [sds((seqs, width, length), F32)],
        3e9,
        mib=16,
    )
    rest, rest_give = halves(rest, after(rest_got, hidden_grad))
    hidden_grad = hidden_grad.reshape(micro, batch, width, length).swapaxes(2, 3)
    rest_got = net.swap(rest_give, znear)
    a = add(a, after(a_got, rest_give))
    a_got = net.swap(a, ybit)
    b = add(b, after(b_got, a))
    b_got = net.swap(b, ybit)
    down, down_give = halves(down, after(down_got, b))
    down_got = net.swap(down_give, zfar)
    rest, rest_give = halves(rest, after(rest_got, down_give))
    rest_got = net.swap(rest_give, zfar)
    a = add(a, after(a_got, rest_give))
    a_far = net.swap(a, core)
    b = add(b, b_got)
    b_far = net.swap(b, core)
    down = add(down, after(down_got, a))
    down_y = net.swap(down, ybit)
    down_c = net.swap(down, core)
    rest = add(rest, after(rest_got, down))
    rest_y = net.swap(rest, ybit)
    rest_c = net.swap(after(rest, rest_y), core)
    down_yc = net.swap(down_y, core)
    rest_yc = net.swap(rest_y, core)
    qk, v = (QW + KW) // n_fsdp, KW // n_fsdp
    out_gate, out_down, out_wout, out_qkv, b_qk, b_v, out_gains = call(
        functools.partial(place_all, ff_rows // 4, qk, v),
        [meta],
        [a, a_far, b, b_far, down, down_y, down_c, down_yc, rest, rest_y, rest_c, rest_yc],
        [
            sds((d_rows, 2 * units), F32),
            sds((ff_rows, width), F32),
            sds((d_rows, width), F32),
            sds((d_rows, qkv_w), F32),
            sds((1, qk), F32),
            sds((1, v), F32),
            sds((2, d_rows), F32),
        ],
        3e9,
        [(d_rows + 8, 1024)],
        16,
    )
    return (
        block_out,
        hidden_grad,
        out_qkv,
        b_qk.reshape(qk),
        b_v.reshape(v),
        out_wout,
        out_gate,
        out_down,
        out_gains,
    )


def solution(mesh):
    n_fsdp, n_seq = mesh.shape["fsdp"], mesh.shape["seq"]
    in_specs = (
        P(None, "fsdp", "seq", None),
        P("fsdp", None),
        P("fsdp"),
        P("fsdp", None),
        P("fsdp", None),
        P("fsdp", None),
        P(None, "fsdp"),
        P(None, "fsdp", "seq"),
        P(),
        P(None, "fsdp", "seq", None),
    )
    out_specs = (
        P(None, "fsdp", "seq", None),
        P(None, "fsdp", "seq", None),
        P("fsdp", None),
        P("fsdp"),
        P("fsdp"),
        P("fsdp", None),
        P("fsdp", None),
        P("fsdp", None),
        P(None, "fsdp"),
    )

    def local(*args):
        body = on_device_tiled if (n_fsdp, n_seq) == (8, 4) else on_device
        return body(*args, n_fsdp=n_fsdp, n_seq=n_seq)

    return jax.shard_map(local, mesh=mesh, in_specs=in_specs, out_specs=out_specs, check_vma=False)
```

```python
import functools

import jax
import jax.numpy as jnp
import numpy as np
from jax import lax
from jax.experimental import pallas as pl
from jax.experimental.pallas import tpu as pltpu
from jax.sharding import PartitionSpec as P

HEADS = 9
KV_HEADS = 3
HEAD_DIM = 64
GROUP = HEADS // KV_HEADS
QW = HEADS * HEAD_DIM
KW = KV_HEADS * HEAD_DIM
EPS = 1e-05
ROPE_BASE = 100000.0
MASKED = -1000000000.0
BF = jnp.bfloat16
F32 = jnp.float32


def dot(a, b, ca, cb):
    return lax.dot_general(a, b, (((ca,), (cb,)), ((), ())), preferred_element_type=F32)


def rotary(values, cosine, sine):
    half = values.shape[-1] // 2
    a, b = values[..., :half], values[..., half:]
    return jnp.concatenate([a * cosine - b * sine, b * cosine + a * sine], axis=-1)


def norm_parts(values):
    factor = lax.rsqrt(jnp.mean(values * values, axis=-1, keepdims=True) + EPS)
    return factor, values * factor


def norm_back(grad_in, gain, factor, normed):
    scaled = grad_in * gain
    return factor * (scaled - normed * jnp.mean(scaled * normed, axis=-1, keepdims=True))


def whole(*shape_dtypes):
    return [pl.BlockSpec(memory_space=pltpu.VMEM) for _ in shape_dtypes]


def call(kernel, scalars, arrays, outs, flops, scratch=(), mib=52, fetched=(), landing=()):
    specs = [pl.BlockSpec(memory_space=pltpu.SMEM)] * len(scalars) + whole(*arrays)
    specs += [pl.BlockSpec(memory_space=pltpu.HBM)] * len(fetched)
    arrays = [*arrays, *fetched]
    moved = sum(a.size * a.dtype.itemsize for a in arrays) + sum(
        int(np.prod(o.shape)) * o.dtype.itemsize for o in outs
    )
    return pl.pallas_call(
        kernel,
        out_shape=outs,
        in_specs=specs,
        out_specs=whole(*outs),
        scratch_shapes=[
            *[pltpu.VMEM(shape, F32) for shape in scratch],
            *[pltpu.VMEM(shape, BF) for shape in landing],
            *([pltpu.SemaphoreType.DMA((len(fetched),))] if fetched else []),
        ],
        compiler_params=pltpu.CompilerParams(vmem_limit_bytes=mib * 1024 * 1024),
        cost_estimate=pl.CostEstimate(flops=int(flops), bytes_accessed=moved, transcendentals=0),
    )(*scalars, *arrays)


def sds(shape, dtype):
    return jax.ShapeDtypeStruct(shape, dtype)


def turn(x, cosine, sine):
    tiles = []
    low = lax.broadcasted_iota(jnp.int32, (1, 128), 1) % HEAD_DIM < HEAD_DIM // 2
    for t in range(x.shape[1] // 128):
        part = x[:, 128 * t : 128 * t + 128]
        other = jnp.where(low, pltpu.roll(part, 96, 1), pltpu.roll(part, 32, 1))
        tiles.append(part * cosine + other * sine)
    return tiles


def turn_kv(x, cosine, sine):
    lane = lax.broadcasted_iota(jnp.int32, (1, 128), 1)
    first, second = turn(x[:, :256], cosine, sine)
    second = jnp.where(lane < KW - 128, second, x[:, 128:256])
    return jnp.concatenate([first, second, x[:, 256:]], axis=1)


def tables(seq, order, cos_ref, sin_ref):
    cosine = jnp.concatenate([cos_ref[seq ^ o] for o in order], axis=0)
    sine = jnp.concatenate([sin_ref[seq ^ o] for o in order], axis=0)
    return cosine, sine


def heads_to_rows(x, g):
    return jnp.concatenate(
        [x[:, HEAD_DIM * h : HEAD_DIM * (h + 1)] for h in range(GROUP * g, GROUP * (g + 1))], axis=0
    )


def rows_to_heads(parts, length):
    return jnp.concatenate(
        [p[length * r : length * (r + 1)] for p in parts for r in range(GROUP)], axis=1
    )


def attention_forward(order, length, seq_ref, blocks, wq, wkv, bq, bkv, gain, cos, sin, mask,
                      att_o, q_o, k_o, v_o):
    seq = seq_ref[0]
    cosine, sine = tables(seq, order, cos, sin)
    width = gain.shape[1]
    for b in range(blocks.shape[1] // length):
        x = blocks[:, b * length : (b + 1) * length, :width].astype(F32)
        x = x.reshape(len(order) * length, width)
        first = (norm_parts(x)[1] * gain[...]).astype(BF)
        kv = dot(first, wkv[...], 1, 0) + bkv[...]
        q = dot(first[:length], wq[...], 1, 0) + bq[...]
        q = jnp.concatenate(turn(q, cosine[:length], sine[:length]), axis=1).astype(BF)
        q = q * jnp.asarray(HEAD_DIM ** (-0.5), BF)
        kv = turn_kv(kv, cosine, sine).astype(BF)
        allowed = jnp.concatenate([mask[b]] * GROUP, axis=0) > 0.0
        parts = []
        for g in range(KV_HEADS):
            qg = heads_to_rows(q, g)
            kg = kv[:, HEAD_DIM * g : HEAD_DIM * (g + 1)]
            vg = kv[:, KW + HEAD_DIM * g : KW + HEAD_DIM * (g + 1)]
            q_o[b, g] = qg
            k_o[b, g] = kg
            v_o[b, g] = vg
            scores = jnp.where(allowed, dot(qg, kg, 1, 1), MASKED)
            top = jnp.max(scores, axis=-1, keepdims=True)
            e = jnp.exp(scores - top)
            total = jnp.sum(e, axis=-1, keepdims=True)
            probs = (e * (1.0 / total)).astype(BF)
            parts.append(dot(probs, vg, 1, 0))
        att_o[b * length : (b + 1) * length, :] = rows_to_heads(parts, length).astype(BF)


def feed_forward(attended, source, wo, wgu, wd, gain, cot, weight,
                 out_o, down_o, gu_o, mid_o, wout_o, attg_o, gain_o):
    units = wd.shape[0]
    step = units // 3
    att = attended[...]
    middle = source[...].astype(F32) + dot(att, wo[...], 1, 0)
    scale_two, normed = norm_parts(middle)
    g2 = gain[...]
    second = (normed * g2).astype(BF)
    out_grad = cot[...].astype(F32) * weight[...]
    feed_grad = out_grad.astype(BF)
    feed = None
    back = None
    for j in range(0, units, step):
        wg = wgu[:, j : j + step]
        wu = wgu[:, units + j : units + j + step]
        wdj = wd[j : j + step, :]
        gate = dot(second, wg, 1, 0)
        up = dot(second, wu, 1, 0)
        sig = jax.nn.sigmoid(gate)
        act = gate * sig
        product = (act * up).astype(BF)
        part = dot(product, wdj, 1, 0)
        feed = part if feed is None else feed + part
        down_o[j : j + step, :] = dot(product, feed_grad, 0, 0).astype(BF)
        pgrad = dot(feed_grad, wdj, 1, 1)
        ggrad = (pgrad * up * (sig * (1.0 + gate * (1.0 - sig)))).astype(BF)
        ugrad = (pgrad * act).astype(BF)
        gu_o[:, j : j + step] = dot(second, ggrad, 0, 0).astype(BF)
        gu_o[:, units + j : units + j + step] = dot(second, ugrad, 0, 0).astype(BF)
        part = dot(ggrad, wg, 1, 1) + dot(ugrad, wu, 1, 1)
        back = part if back is None else back + part
    out_o[...] = (middle + feed).astype(BF)
    gain_o[...] = jnp.sum(back * normed, axis=0, keepdims=True)
    middle_grad = out_grad + norm_back(back, g2, scale_two, normed)
    mid_o[...] = middle_grad
    branch = middle_grad.astype(BF)
    wout_o[...] = dot(att, branch, 0, 0).astype(BF)
    attg_o[...] = dot(branch, wo[...], 1, 1).astype(BF)


def attention_backward(order, length, seq_ref, blocks, wq, wkv, gain, cos, sin, mask, q_i, k_i, v_i,
                       attg, dq_o, dkv_o, wgrad_o, bias_o, gain_o):
    seq = seq_ref[0]
    cosine, sine = tables(seq, order, cos, sin)
    width = gain.shape[1]
    q_wgrad = kv_wgrad = bias_q = bias_kv = gain_sum = None
    for b in range(blocks.shape[1] // length):
        x = blocks[:, b * length : (b + 1) * length, :width].astype(F32)
        x = x.reshape(len(order) * length, width)
        normed = norm_parts(x)[1]
        first = (normed * gain[...]).astype(BF)
        allowed = jnp.concatenate([mask[b]] * GROUP, axis=0) > 0.0
        ag = attg[b * length : (b + 1) * length, :]
        dqs, dks, dvs = [], [], []
        for g in range(KV_HEADS):
            qg, kg, vg = q_i[b, g], k_i[b, g], v_i[b, g]
            agg = heads_to_rows(ag, g)
            scores = jnp.where(allowed, dot(qg, kg, 1, 1), MASKED)
            e = jnp.exp(scores - jnp.max(scores, axis=-1, keepdims=True))
            p = e * (1.0 / jnp.sum(e, axis=-1, keepdims=True))
            dvs.append(dot(p.astype(BF), agg, 0, 0))
            pg = dot(agg, vg, 1, 1)
            inner = jnp.sum(p * pg, axis=-1, keepdims=True)
            ds = (p * (pg - inner)).astype(BF)
            dqs.append(dot(ds, kg, 1, 0) * HEAD_DIM ** (-0.5))
            dks.append(dot(ds, qg, 0, 0))
        dq = rows_to_heads(dqs, length)
        dq = jnp.concatenate([dq, jnp.zeros((length, 64), F32)], axis=1)
        dq = jnp.concatenate(turn(dq, cosine[:length], -sine[:length]), axis=1).astype(BF)
        dkv = jnp.concatenate(dks + dvs, axis=1)
        dkv = turn_kv(dkv, cosine, -sine).astype(BF)
        dq_o[b * length : (b + 1) * length, :] = dq
        for r in range(len(order)):
            dkv_o[r, b * length : (b + 1) * length, :] = dkv[r * length : (r + 1) * length, :]
        wq_part = dot(first[:length], dq, 0, 0)
        wkv_part = dot(first, dkv, 0, 0)
        bq_part = jnp.sum(dq.astype(F32), axis=0, keepdims=True)
        bkv_part = jnp.sum(dkv.astype(F32), axis=0, keepdims=True)
        e_kv = dot(dkv, wkv[...], 1, 1) * normed
        e_q = dot(dq[:, :QW], wq[:, :QW], 1, 1) * normed[:length]
        g_part = jnp.sum(e_kv, axis=0, keepdims=True) + jnp.sum(e_q, axis=0, keepdims=True)
        if q_wgrad is None:
            q_wgrad, kv_wgrad, bias_q, bias_kv, gain_sum = wq_part, wkv_part, bq_part, bkv_part, g_part
        else:
            q_wgrad, kv_wgrad = q_wgrad + wq_part, kv_wgrad + wkv_part
            bias_q, bias_kv, gain_sum = bias_q + bq_part, bias_kv + bkv_part, gain_sum + g_part
    wgrad_o[...] = jnp.concatenate([q_wgrad[:, :QW], kv_wgrad], axis=1).astype(BF)
    bias_o[...] = jnp.concatenate([bias_q[:, :QW], bias_kv], axis=1)
    gain_o[...] = gain_sum


def input_gradient(dq, own, a, b, c, source, mid, wq, wkv, gain, out_o):
    kv = own[...].astype(F32) + a[...].astype(F32) + b[...].astype(F32) + c[...].astype(F32)
    first_grad = dot(dq[:, :QW], wq[:, :QW], 1, 1) + dot(kv.astype(BF), wkv[...], 1, 1)
    scale_one, normed = norm_parts(source[...].astype(F32))
    out_o[...] = mid[...] + norm_back(first_grad, gain[...], scale_one, normed)

def chosen(flag, a, b):
    return jnp.where(flag != 0, b, a)


class Blocks:
    def __init__(self, *refs):
        self.refs = refs
        self.shape = (len(refs),) + refs[0].shape

    def __getitem__(self, key):
        return jnp.stack([ref[key[1:]] for ref in self.refs])


def cut_qkv(core_bit, meta, w_hbm, bias_hbm, gains_hbm, out_o, w, bias, gains, all_s, sems):
    pairs = ((w_hbm, w), (bias_hbm, bias), (gains_hbm, gains))
    copies = [pltpu.make_async_copy(a, b, sems.at[i]) for i, (a, b) in enumerate(pairs)]
    for copy in copies:
        copy.start()
    for copy in copies:
        copy.wait()
    rows = w.shape[0]
    n = bias.shape[1]
    all_s[:rows, :] = w[...].astype(F32)
    all_s[rows:, :] = jnp.zeros((8, w.shape[1]), F32)
    all_s[rows : rows + 1, :n] = bias[...].astype(F32)
    for i in range(2):
        all_s[rows : rows + 1, n + rows * i : n + rows * (i + 1)] = gains[i : i + 1, :].astype(F32)
    half = out_o.shape[0]
    at = pl.multiple_of((meta[0] & core_bit) * half, 8)
    out_o[...] = all_s[pl.ds(at, half), :].astype(BF)


def first_forward(order, length, d_rows, n_bias, meta, b0, b1, b2, b3, a00, a10, a01, a11, cos, sin, mask,
                  att_o, q_o, k_o, v_o, w_o, gain_o, w_s, b_s):
    blocks = Blocks(b0, b1, b2, b3)
    core, x = meta[0] & 1, meta[1] & 1
    cut = a00.shape[2]
    for x_rel, c_rel, piece in ((0, 0, a00), (1, 0, a10), (0, 1, a01), (1, 1, a11)):
        for z0 in range(2):
            for z1 in range(2):
                at = (z1 * 4 + z0 * 2 + (x ^ x_rel)) * 2 * cut + (core ^ c_rel) * cut
                w_s[pl.ds(pl.multiple_of(at, 8), cut), :] = piece[z0, z1].astype(F32)
    n_f = w_s.shape[0] // (2 * cut)
    starts = [2 * cut * f for f in range(n_f)]
    w_o[...] = jnp.concatenate([w_s[at : at + d_rows, :] for at in starts], axis=0).astype(BF)
    lines = [w_s[at + d_rows : at + d_rows + 1, :] for at in starts]
    b_s[...] = jnp.concatenate([line[:, :n_bias] for line in lines], axis=1)
    for i in range(2):
        at = n_bias + d_rows * i
        gain_o[i : i + 1, :] = jnp.concatenate([line[:, at : at + d_rows] for line in lines], axis=1)
    wide = QW + 64
    attention_forward(order, length, meta, blocks, w_o[:, :wide], w_o[:, QW:], b_s[:, :wide], b_s[:, QW:],
                      gain_o[0:1, :], cos, sin, mask, att_o, q_o, k_o, v_o)


def turned(out, value):
    length = out.shape[2]
    for b in range(out.shape[0]):
        out[b] = value[length * b : length * (b + 1)].T.astype(out.dtype)


def rel(meta, f):
    r = f ^ meta[1]
    return r & 1, (r >> 1) & 1, (r >> 2) & 1


def fetch_pieces(meta, refs, b_s, g_s, sems):
    core, y, x, z0 = meta[0] & 1, (meta[0] >> 1) & 1, meta[1] & 1, (meta[1] >> 1) & 1
    copies = []
    for i in range(8):
        at = (z0 ^ (i >> 2), x ^ ((i >> 1) & 1), core ^ (i & 1))
        copies.append(pltpu.make_async_copy(refs[i], b_s.at[at], sems.at[i]))
    for i in range(8):
        at = (y ^ ((i >> 1) & 1), core ^ (i & 1), x ^ (i >> 2))
        copies.append(pltpu.make_async_copy(refs[8 + i], g_s.at[at], sems.at[8 + i]))
    for copy in copies:
        copy.start()
    return copies


def feed_forward_pieces(d_rows, ff_rows, meta, attended, source, gains, cot, weight, *refs):
    out_o, ak_o, ag_o, bk_o, bg_o, dk_o, dg_o, mid_o, attg_o, gain_o, down_s, wout_s, b_s, g_s, sems = refs[16:]
    copies = fetch_pieces(meta, refs, b_s, g_s, sems)
    core, y = meta[0] & 1, (meta[0] >> 1) & 1
    part_d = ff_rows // 4
    part_o = d_rows // 3
    cut = b_s.shape[4] - ff_rows // 2
    half = g_s.shape[-1] // 2
    for copy in copies[:8]:
        copy.wait()
    wo = []
    for f in range(8):
        for c in range(2):
            rows = b_s[(f >> 1) & 1, f & 1, c, f >> 2, ff_rows // 2 :, :].astype(F32)
            wo.append(rows if c == 0 else rows[: d_rows - cut])
    wo = jnp.concatenate(wo, axis=0).astype(BF)
    att = attended[...]
    middle = source[...].astype(F32) + dot(att, wo, 1, 0)
    scale_two, normed = norm_parts(middle)
    g2 = gains[1:2, :]
    second = (normed * g2).astype(BF)
    out_grad = cot[...].astype(F32) * weight[...]
    feed_grad = out_grad.astype(BF)
    for copy in copies[8:]:
        copy.wait()
    feed = back = None
    for c_rel in (1, 0):
        h = core ^ c_rel
        weights = []
        for yy in range(2):
            rows = [g_s[yy, h, f & 1, (f >> 1) & 1, f >> 2].astype(F32) for f in range(8)]
            weights.append(jnp.concatenate(rows, axis=0).astype(BF))
        wg, wu = weights
        wd = [b_s[i >> 1, i & 1, c, h, : ff_rows // 2, :] for i in range(4) for c in range(2)]
        wd = jnp.concatenate(wd, axis=0)
        gate = dot(second, wg, 1, 0)
        up = dot(second, wu, 1, 0)
        sig = jax.nn.sigmoid(gate)
        act = gate * sig
        product = (act * up).astype(BF)
        part = dot(product, wd, 1, 0)
        feed = part if feed is None else feed + part
        down_s[...] = dot(product, feed_grad, 0, 0)
        pgrad = dot(feed_grad, wd, 1, 1)
        ggrad = (pgrad * up * (sig * (1.0 + gate * (1.0 - sig)))).astype(BF)
        ugrad = (pgrad * act).astype(BF)
        part = dot(ggrad, wg, 1, 1) + dot(ugrad, wu, 1, 1)
        back = part if back is None else back + part
        for i in range(4):
            x, z0, z1 = rel(meta, 4 * h + i)
            for yy in range(2):
                for c_to, to in ((0, dk_o), (1, dg_o)):
                    at = pl.multiple_of(i * ff_rows + (yy * 2 + (core ^ c_to)) * part_d, 16)
                    to[y ^ yy, x, z0, z1, :part_d, :] = down_s[pl.ds(at, part_d), :].astype(BF)
        to_a, to_b = (ag_o, bg_o) if c_rel else (ak_o, bk_o)
        for yy, grad in ((0, ggrad), (1, ugrad)):
            wgrad = dot(second, grad, 0, 0)
            for f in range(8):
                x, z0, z1 = rel(meta, f)
                block = wgrad[d_rows * f : d_rows * (f + 1), :].astype(BF)
                to_a[x, z0, z1, yy] = block[:, :half]
                to_b[z0, z1, x, yy] = block[:, half:]
    turned(out_o, middle + feed)
    gain_o[...] = jnp.sum(back * normed, axis=0, keepdims=True)
    middle_grad = out_grad + norm_back(back, g2, scale_two, normed)
    mid_o[...] = middle_grad
    branch = middle_grad.astype(BF)
    attg_o[...] = dot(branch, wo, 1, 1).astype(BF)
    wout = dot(att, branch, 0, 0)
    for f in range(8):
        wout_s[f, :d_rows, :] = wout[d_rows * f : d_rows * (f + 1), :]
        wout_s[f, d_rows:, :] = jnp.zeros((part_o, wout.shape[1]), F32)
    for f in range(8):
        x, z0, z1 = rel(meta, f)
        for yy in range(2):
            for c_to, to in ((0, dk_o), (1, dg_o)):
                at = pl.multiple_of((yy * 2 + (core ^ c_to)) * part_o, 8)
                to[y ^ yy, x, z0, z1, part_d:, :] = wout_s[f, pl.ds(at, part_o), :].astype(BF)


def attention_backward_pieces(order, length, d_rows, meta, b0, b1, b2, b3, w, gains, cos, sin, mask, q_i, k_i, v_i,
                              attg, gain_two, dq_o, dk_o, dg_o, rk_o, rg_o, w_s, bias_s, gain_s, small_s):
    blocks = Blocks(b0, b1, b2, b3)
    half = len(order) // 2

    class Pieces:
        def __setitem__(self, key, value):
            ref = dk_o if key[0] < half else dg_o
            ref[(key[0] % half,) + key[1:]] = value

    class Wgrad:
        def __setitem__(self, key, value):
            w_s[:, : 2 * KW] = value[:, QW:].astype(F32)
            w_s[:, 2 * KW : 2 * KW + QW] = value[:, :QW].astype(F32)
            w_s[:, 2 * KW + QW :] = jnp.zeros((value.shape[0], 64), F32)

    wide = QW + 64
    attention_backward(order, length, meta, blocks, w[:, :wide], w[:, QW:], gains[0:1, :], cos, sin, mask,
                       q_i, k_i, v_i, attg, dq_o, Pieces(), Wgrad(), bias_s, gain_s)
    n_f = small_s.shape[0]
    qk, v = (QW + KW) // n_f, KW // n_f
    bias, g1, g2 = bias_s[...], gain_s[...], gain_two[...]
    for f in range(n_f):
        line = jnp.concatenate(
            [
                bias[:, qk * f : qk * (f + 1)],
                bias[:, QW + KW + v * f : QW + KW + v * (f + 1)],
                g1[:, d_rows * f : d_rows * (f + 1)],
                jnp.zeros((1, 256 - qk - v - d_rows), F32),
                g2[:, d_rows * f : d_rows * (f + 1)],
                jnp.zeros((1, 768 - d_rows), F32),
            ],
            axis=1,
        )
        small_s[f] = jnp.broadcast_to(line, (8, 1024))
    core, y = meta[0] & 1, (meta[0] >> 1) & 1
    for f in range(n_f):
        x, z0, z1 = rel(meta, f)
        for yy in range(2):
            for c_to, to in ((0, rk_o), (1, rg_o)):
                at = pl.multiple_of((yy * 2 + (core ^ c_to)) * 256, 256)
                block = [w_s[d_rows * f : d_rows * (f + 1), pl.ds(at, 256)], small_s[f, :, pl.ds(at, 256)]]
                to[y ^ yy, x, z0, z1] = jnp.concatenate(block, axis=0).astype(BF)


def input_gradient_two(dq, own, other, source, mid, w, gains, out_o):
    kv = (own[...].astype(F32) + other[...].astype(F32)).astype(BF)
    first_grad = dot(dq[:, :QW], w[:, :QW], 1, 1) + dot(kv, w[:, QW:], 1, 1)
    scale_one, normed = norm_parts(source[...].astype(F32))
    turned(out_o, mid[...] + norm_back(first_grad, gains[0:1, :], scale_one, normed))


def place_gate(meta, near, far, out_o, parts=1, part=0):
    core = meta[0] & 1
    n = near.shape[2]
    for pieces, c_rel in ((near, 0), (far, 1)):
        for yy in range(2):
            at = pl.multiple_of(((yy * 2 + (core ^ c_rel)) * parts + part) * n, 128)
            out_o[:, pl.ds(at, n)] = pieces[yy].astype(F32)


def place_down(part_d, meta, p00, p10, p01, p11, out_o, wout_o):
    seq = meta[0]
    part_o = p00.shape[0] - part_d
    for piece, o in ((p00[...], 0), (p10[...], 2), (p01[...], 1), (p11[...], 3)):
        piece = piece.astype(F32)
        to = seq ^ o
        out_o[pl.ds(pl.multiple_of(to * part_d, 16), part_d), :] = piece[:part_d]

        @pl.when(to < 3)
        def _():
            wout_o[pl.ds(pl.multiple_of(to * part_o, 8), part_o), :] = piece[part_d:]


def place_qkv(qk, v, meta, p00, p10, p01, p11, w_o, bqk_o, bv_o, gains_o, all_s):
    n = p00.shape[1]
    for piece, o in ((p00, 0), (p10, 2), (p01, 1), (p11, 3)):
        all_s[:, pl.ds(pl.multiple_of((meta[0] ^ o) * n, 128), n)] = piece[...].astype(F32)
    d_rows = w_o.shape[0]
    w_o[:, :QW] = all_s[:d_rows, 2 * KW : 2 * KW + QW]
    w_o[:, QW:] = all_s[:d_rows, : 2 * KW]
    line = all_s[d_rows : d_rows + 1, :]
    bqk_o[...] = line[:, :qk]
    bv_o[...] = line[:, qk : qk + v]
    gains_o[0:1, :] = line[:, qk + v : qk + v + d_rows]
    gains_o[1:2, :] = line[:, 256 : 256 + d_rows]


def place_all(part_d, qk, v, meta, a_near, a_far, b_near, b_far, d0, d1, d2, d3, r0, r1, r2, r3,
              gate_o, down_o, wout_o, w_o, bqk_o, bv_o, gains_o, all_s):
    place_gate(meta, a_near, a_far, gate_o, 2, 0)
    place_gate(meta, b_near, b_far, gate_o, 2, 1)
    place_down(part_d, meta, d0, d1, d2, d3, down_o, wout_o)
    place_qkv(qk, v, meta, r0, r1, r2, r3, w_o, bqk_o, bv_o, gains_o, all_s)


class Net:
    def __init__(self, n_fsdp, n_seq):
        self.n_fsdp, self.n_seq = n_fsdp, n_seq
        self.total = n_fsdp * n_seq
        f, s = lax.axis_index("fsdp"), lax.axis_index("seq")
        self.index = f * n_seq + s
        self.seq_bits = [1 << b for b in range(n_seq.bit_length() - 1)]
        self.fsdp_bits = [n_seq << b for b in range(n_fsdp.bit_length() - 1)]

    def swap(self, value, mask):
        pairs = [(i, i ^ mask) for i in range(self.total)]
        return lax.ppermute(value, ("fsdp", "seq"), pairs)

    def bit(self, mask):
        return (self.index & mask) != 0

    def both(self, mine, mask, axis, other=None):
        other = self.swap(mine, mask) if other is None else other
        high = self.bit(mask)
        return jnp.stack([jnp.where(high, other, mine), jnp.where(high, mine, other)], axis=axis)

    def half(self, value, mask, axis):
        return lax.dynamic_index_in_dim(
            value, self.bit(mask).astype(jnp.int32), axis, keepdims=False
        )

    def add_half(self, value, mask, axis):
        mine = self.bit(mask).astype(jnp.int32)
        keep = lax.dynamic_index_in_dim(value, mine, axis, keepdims=False)
        give = lax.dynamic_index_in_dim(value, 1 - mine, axis, keepdims=False)
        got = self.swap(give, mask)
        return (keep.astype(F32) + got.astype(F32)).astype(value.dtype)

    def gather_fsdp(self, value):
        for step, mask in enumerate(reversed(self.fsdp_bits)):
            value = self.both(value, mask, step)
        return value

    def scatter_fsdp(self, value, first_axis=0):
        count = len(self.fsdp_bits)
        for step, mask in enumerate(self.fsdp_bits):
            value = self.add_half(value, mask, first_axis + count - 1 - step)
        return value


def on_device(
    hidden, w_qkv, b_qkv, w_out, w_gate_up, w_down, norm_gains, segment_ids, token_counts, cotangent,
    n_fsdp, n_seq,
):
    net = Net(n_fsdp, n_seq)
    micro, batch, length, width = hidden.shape
    full_length = length * n_seq
    tokens_micro = batch * n_fsdp * full_length
    scale = HEAD_DIM ** (-0.5)
    rows = micro * batch * length
    d_rows = w_qkv.shape[0]
    ff_rows = w_down.shape[0]
    units = w_gate_up.shape[1] // 2
    qkv_w = w_qkv.shape[1]
    core = net.seq_bits[0]
    f_lead = (2,) * len(net.fsdp_bits)

    ids = segment_ids.reshape(rows, 1).astype(BF)
    block = jnp.concatenate(
        [hidden.reshape(rows, width), jnp.broadcast_to(ids, (rows, 64))], axis=1
    )
    blocks = block[None]
    for mask in reversed(net.seq_bits):
        blocks = jnp.concatenate([blocks, net.swap(blocks, mask)], axis=0)
    order = [0]
    for mask in reversed(net.seq_bits):
        order = order + [o ^ mask for o in order]
    seq_index = lax.axis_index("seq")
    block_ids = [seq_index ^ o for o in order]

    pad_rows = -(d_rows + 1) % 16 + 1
    extra = jnp.zeros((pad_rows, qkv_w), BF)
    small = jnp.concatenate([b_qkv, norm_gains.reshape(-1)])
    extra = extra.at[0, : small.shape[0]].set(small)
    shard_a = jnp.concatenate([w_qkv, extra], axis=0).reshape(2, -1, qkv_w)
    got_a = net.gather_fsdp(net.half(shard_a, core, 0))
    full_a = net.both(got_a, core, len(f_lead)).reshape(n_fsdp, d_rows + pad_rows, qkv_w)
    wf_qkv = full_a[:, :d_rows].reshape(n_fsdp * d_rows, qkv_w)
    smalls = full_a[:, d_rows]
    n_bias = b_qkv.shape[0]
    bias = smalls[:, :n_bias].reshape(-1).astype(F32)
    gains = smalls[:, n_bias : n_bias + 2 * d_rows].reshape(n_fsdp, 2, d_rows).astype(F32)
    gain_one = gains[:, 0].reshape(-1)
    gain_two = gains[:, 1].reshape(-1)

    pad_b = -(d_rows + ff_rows) % 16
    shard_b = jnp.concatenate([w_out, w_down, jnp.zeros((pad_b, width), BF)], axis=0)
    shard_b = shard_b.reshape(2, -1, width)
    got_b = net.gather_fsdp(net.half(shard_b, core, 0))

    parts = n_seq
    shard_c = w_gate_up.reshape(d_rows, parts, -1)
    got_c = net.gather_fsdp(lax.dynamic_index_in_dim(shard_c, seq_index, 1, keepdims=False))
    full_b = net.both(got_b, core, len(f_lead)).reshape(n_fsdp, -1, width)
    wf_out = full_b[:, :d_rows].reshape(n_fsdp * d_rows, width)
    wf_down = full_b[:, d_rows : d_rows + ff_rows].reshape(n_fsdp * ff_rows, width)
    got_c = got_c.reshape(n_fsdp * d_rows, -1)
    for mask in reversed(net.seq_bits):
        got_c = net.both(got_c, mask, got_c.ndim - 1)
    wf_gate_up = got_c.reshape(n_fsdp * d_rows, 2 * units)

    places = np.arange(full_length, dtype=np.float32)
    speeds = np.power(ROPE_BASE, -2.0 * np.arange(HEAD_DIM // 2, dtype=np.float32) / HEAD_DIM)
    angles = places[:, None] * speeds.astype(np.float32)[None, :]
    cos_t = np.tile(np.cos(angles), (1, 4)).reshape(n_seq, length, 128)
    sin_t = np.concatenate([-np.sin(angles), np.sin(angles)] * 2, axis=1).reshape(n_seq, length, 128)
    cos_t, sin_t = jnp.asarray(cos_t, F32), jnp.asarray(sin_t, F32)
    seqs = micro * batch
    seg_all = blocks[..., width].reshape(n_seq, seqs, length).transpose(1, 0, 2)
    own_places = seq_index * length + jnp.arange(length, dtype=jnp.int32)
    key_places = jnp.stack(block_ids)[:, None] * length + jnp.arange(length, dtype=jnp.int32)
    allowed = (seg_all[:, 0, :, None] == seg_all.reshape(seqs, 1, -1)) & (
        own_places[None, :, None] >= key_places.reshape(1, 1, -1)
    )
    allowed = allowed.astype(F32)
    seq_scalar = seq_index.astype(jnp.int32).reshape(1)
    wq, wkv = wf_qkv[:, : QW + 64], wf_qkv[:, QW:]
    gain_one, gain_two = gain_one[None], gain_two[None]
    source = hidden.reshape(rows, width)
    n_all = n_seq * rows
    attended, q_s, k_s, v_s = call(
        functools.partial(attention_forward, order, length),
        [seq_scalar],
        [blocks, wq, wkv, bias[None, : QW + 64], bias[None, QW:], gain_one, cos_t, sin_t, allowed],
        [
            sds((rows, QW), BF),
            sds((seqs, KV_HEADS, GROUP * length, HEAD_DIM), BF),
            sds((seqs, KV_HEADS, full_length, HEAD_DIM), BF),
            sds((seqs, KV_HEADS, full_length, HEAD_DIM), BF),
        ],
        2 * n_all * width * 2 * KW + 2 * rows * width * QW + 4 * rows * full_length * QW,
    )

    weight = tokens_micro / token_counts.astype(F32)
    weight = jnp.repeat(weight, batch * length)[:, None]
    block_out, down_grad, gate_up_wgrad, middle_grad, out_wgrad, attended_grad, gain_two_grad = call(
        feed_forward,
        [],
        [attended, source, wf_out, wf_gate_up, wf_down, gain_two, cotangent.reshape(rows, width), weight],
        [
            sds((rows, width), BF),
            sds((units, width), BF),
            sds((width, 2 * units), BF),
            sds((rows, width), F32),
            sds((QW, width), BF),
            sds((rows, QW), BF),
            sds((1, width), F32),
        ],
        6 * rows * width * 3 * units + 6 * rows * width * QW,
    )
    block_out = block_out.reshape(hidden.shape)

    def seq_axes(value, axis, masks):
        for mask in masks:
            value = net.add_half(value, mask, axis)
        return value

    quarter = (2,) * len(net.seq_bits)
    n_f = len(f_lead)
    red_down = down_grad.reshape(f_lead + quarter + (ff_rows // n_seq, width))
    for step, mask in enumerate(net.seq_bits):
        red_down = net.add_half(red_down, mask, n_f + len(quarter) - 1 - step)
    red_down = net.scatter_fsdp(red_down)

    red_gate = gate_up_wgrad.reshape(f_lead + (d_rows,) + quarter + (2 * units // n_seq,))
    red_gate = net.add_half(red_gate, core, n_f + len(quarter))
    red_gate = net.add_half(red_gate, net.fsdp_bits[0], n_f - 1)
    for step, mask in enumerate(net.seq_bits[1:]):
        red_gate = net.add_half(red_gate, mask, n_f - 1 + len(quarter) - 1 - step)
    for step, mask in enumerate(net.fsdp_bits[1:]):
        red_gate = net.add_half(red_gate, mask, n_f - 2 - step)

    dq, dkv, qkv_wgrad, bias_grad, gain_one_grad = call(
        functools.partial(attention_backward, order, length),
        [seq_scalar],
        [blocks, wq, wkv, gain_one, cos_t, sin_t, allowed, q_s, k_s, v_s, attended_grad],
        [
            sds((rows, QW + 64), BF),
            sds((n_seq, rows, 2 * KW), BF),
            sds((width, qkv_w), BF),
            sds((1, qkv_w), F32),
            sds((1, width), F32),
        ],
        4 * n_all * width * 2 * KW + 4 * rows * width * QW + 10 * rows * full_length * QW,
    )
    kv_parts = [dkv[0]]
    for place, mask_bits in enumerate(order):
        if mask_bits:
            kv_parts.append(net.swap(dkv[place], mask_bits))
    (hidden_grad,) = call(
        input_gradient,
        [],
        [dq, *kv_parts, source, middle_grad, wq, wkv, gain_one],
        [sds((rows, width), F32)],
        2 * rows * width * qkv_w,
    )
    hidden_grad = hidden_grad.reshape(hidden.shape)
    bias_grad, gain_one_grad, gain_two_grad = bias_grad[0], gain_one_grad[0], gain_two_grad[0]

    qk_rows, v_rows = (QW + KW) // n_fsdp, KW // n_fsdp
    small_grads = jnp.concatenate(
        [
            bias_grad[: QW + KW].reshape(n_fsdp, qk_rows),
            bias_grad[QW + KW :].reshape(n_fsdp, v_rows),
            gain_one_grad.reshape(n_fsdp, d_rows),
            gain_two_grad.reshape(n_fsdp, d_rows),
        ],
        axis=1,
    ).astype(BF)
    wide = qkv_w + width
    small_pad = jnp.zeros((n_fsdp, pad_rows, wide), BF)
    small_pad = small_pad.at[:, 0, : small_grads.shape[1]].set(small_grads)
    rest = jnp.concatenate([qkv_wgrad, out_wgrad], axis=1)
    rest = jnp.concatenate([rest.reshape(n_fsdp, d_rows, wide), small_pad], axis=1)
    rest = rest.reshape(f_lead + (d_rows + pad_rows,) + quarter + (wide // n_seq,))
    for step, mask in enumerate(net.seq_bits):
        rest = net.add_half(rest, mask, n_f + 1 + len(quarter) - 1 - step)
    rest = net.scatter_fsdp(rest)

    def seq_back(value, axis):
        for step, mask in enumerate(reversed(net.seq_bits)):
            value = net.both(value, mask, axis + step)
        return value

    out_down = seq_back(red_down, 0).reshape(ff_rows, width).astype(F32)
    out_gate = seq_back(red_gate, 1).reshape(d_rows, 2 * units).astype(F32)
    out_rest = seq_back(rest, 1).reshape(d_rows + pad_rows, wide).astype(F32)
    line = out_rest[d_rows]
    edge = qk_rows + v_rows
    return (
        block_out,
        hidden_grad,
        out_rest[:d_rows, :qkv_w],
        line[:qk_rows],
        line[qk_rows:edge],
        out_rest[:d_rows, qkv_w:],
        out_gate,
        out_down,
        line[edge : edge + 2 * d_rows].reshape(2, d_rows),
    )


def after(value, *others):
    return lax.optimization_barrier((value, *others))[0]


def rope_tables(full_length, n_seq):
    places = np.arange(full_length, dtype=np.float32)
    speeds = np.power(ROPE_BASE, -2.0 * np.arange(HEAD_DIM // 2, dtype=np.float32) / HEAD_DIM)
    angles = places[:, None] * speeds.astype(np.float32)[None, :]
    cos_t = np.tile(np.cos(angles), (1, 4)).reshape(n_seq, -1, 128)
    sin_t = np.concatenate([-np.sin(angles), np.sin(angles)] * 2, axis=1).reshape(n_seq, -1, 128)
    return jnp.asarray(cos_t, F32), jnp.asarray(sin_t, F32)


def on_device_tiled(
    hidden, w_qkv, b_qkv, w_out, w_gate_up, w_down, norm_gains, segment_ids, token_counts, cotangent,
    n_fsdp, n_seq,
):
    net = Net(n_fsdp, n_seq)
    micro, batch, length, width = hidden.shape
    full_length = length * n_seq
    tokens_micro = batch * n_fsdp * full_length
    rows = micro * batch * length
    seqs = micro * batch
    d_rows, qkv_w = w_qkv.shape
    ff_rows = w_down.shape[0]
    units = w_gate_up.shape[1] // 2
    n_bias = b_qkv.shape[0]
    core, ybit = net.seq_bits
    xbit, znear, zfar = net.fsdp_bits
    order = [0, 2, 1, 3]
    seq_index = lax.axis_index("seq")
    meta = jnp.stack([seq_index, lax.axis_index("fsdp")]).astype(jnp.int32)
    source = hidden.reshape(rows, width)

    small = [w_qkv, b_qkv[None], norm_gains]
    a0 = pl.pallas_call(
        functools.partial(cut_qkv, core),
        out_shape=sds(((d_rows + 8) // 2, qkv_w), BF),
        in_specs=[pl.BlockSpec(memory_space=pltpu.SMEM)] + [pl.BlockSpec(memory_space=pltpu.HBM)] * 3,
        out_specs=pl.BlockSpec(memory_space=pltpu.VMEM),
        scratch_shapes=[
            *[pltpu.VMEM(v.shape, BF) for v in small],
            pltpu.VMEM((d_rows + 8, qkv_w), F32),
            pltpu.SemaphoreType.DMA((3,)),
        ],
        compiler_params=pltpu.CompilerParams(vmem_limit_bytes=52 * 1024 * 1024),
    )(meta, *small)
    a1 = net.both(a0, zfar, 0)

    ids = segment_ids.reshape(rows, 1).astype(BF)
    block = jnp.concatenate([source, jnp.broadcast_to(ids, (rows, 64))], axis=1)
    block = after(block, a0)
    block_y = net.swap(block, ybit)
    block_c = net.swap(block, core)

    quarter = 2 * units // n_seq
    gu0 = lax.dynamic_slice_in_dim(after(w_gate_up, a0), seq_index * quarter, quarter, axis=1)
    half_b = jnp.concatenate(
        [
            w_down.reshape(2, ff_rows // 2, width),
            jnp.concatenate([w_out, jnp.zeros((8, width), BF)], axis=0).reshape(2, -1, width),
        ],
        axis=1,
    )
    a2 = net.both(a1, znear, 0)
    a_x = net.swap(a2, xbit)
    a_c = net.swap(a2, core)
    gu1 = net.both(gu0, zfar, 0)
    gu2 = net.both(after(gu1, a2), znear, 0)
    block_yc = net.swap(block_y, core)
    a_xc = net.swap(a_x, core)
    gu_x = net.swap(gu2, xbit)
    gu_y = net.swap(gu2, ybit)
    gu_c = net.swap(gu2, core)
    b0 = net.half(after(half_b, a0), core, 0)
    b1 = net.both(b0, zfar, 0, after(net.swap(b0, zfar), a2))
    b_x = net.swap(b1, xbit)
    b_z = net.swap(after(b1, gu2), znear)
    b_c = net.swap(b1, core)
    a_xc = after(a_xc, b_x)

    cos_t, sin_t = rope_tables(full_length, n_seq)
    block_ids = [seq_index ^ o for o in order]
    blocks = [block, block_y, block_c, block_yc]
    seg_all = jnp.stack([b[:, width].reshape(seqs, length) for b in blocks], axis=1)
    own_places = seq_index * length + jnp.arange(length, dtype=jnp.int32)
    key_places = jnp.stack(block_ids)[:, None] * length + jnp.arange(length, dtype=jnp.int32)
    allowed = (seg_all[:, 0, :, None] == seg_all.reshape(seqs, 1, -1)) & (
        own_places[None, :, None] >= key_places.reshape(1, 1, -1)
    )
    allowed = allowed.astype(F32)
    attended, q_s, k_s, v_s, wf, gains = call(
        functools.partial(first_forward, order, length, d_rows, n_bias),
        [meta],
        [*blocks, a2, a_x, a_c, a_xc, cos_t, sin_t, allowed],
        [
            sds((rows, QW), BF),
            sds((seqs, KV_HEADS, GROUP * length, HEAD_DIM), BF),
            sds((seqs, KV_HEADS, full_length, HEAD_DIM), BF),
            sds((seqs, KV_HEADS, full_length, HEAD_DIM), BF),
            sds((width, qkv_w), BF),
            sds((2, width), F32),
        ],
        1.2e10,
        [(n_fsdp * (d_rows + 8), qkv_w), (1, qkv_w)],
    )
    gu_y = after(gu_y, attended)
    gu_x, b_z, b_x = after(gu_x, gu_y), after(b_z, gu_y), after(b_x, gu_y)
    gu_xy = net.swap(gu_x, ybit)
    b_zx = net.swap(b_z, xbit)
    gu_yc = net.swap(gu_y, core)
    gu_xc = net.swap(gu_x, core)
    b_zc = net.swap(b_z, core)
    b_xc = net.swap(b_x, core)
    b_zxc = net.swap(b_zx, core)
    gu_xyc = net.swap(gu_xy, core)
    pieces = [b1, b_c, b_x, b_xc, b_z, b_zc, b_zx, b_zxc]
    pieces += [gu2, gu_c, gu_y, gu_yc, gu_x, gu_xc, gu_xy, gu_xyc]

    weight = tokens_micro / token_counts.astype(F32)
    weight = jnp.repeat(weight, batch * length)[:, None]
    lead = (2, 2, 2, 2)
    cot = cotangent.reshape(rows, width)
    gate_lead = lead + (d_rows, units // 4)
    block_out, a_keep, a_give, b_keep, b_give, down_keep, down_give, middle_grad, attended_grad, gain_two = call(
        functools.partial(feed_forward_pieces, d_rows, ff_rows),
        [meta],
        [attended, source, gains, cot, weight],
        [
            sds((seqs, width, length), BF),
            sds(gate_lead, BF),
            sds(gate_lead, BF),
            sds(gate_lead, BF),
            sds(gate_lead, BF),
            sds(lead + (ff_rows // 4 + d_rows // 3, width), BF),
            sds(lead + (ff_rows // 4 + d_rows // 3, width), BF),
            sds((rows, width), F32),
            sds((rows, QW), BF),
            sds((1, width), F32),
        ],
        1.4e10,
        [(units // 2, width), (n_fsdp, d_rows + d_rows // 3, width)],
        fetched=pieces,
        landing=[(2, 2, 2, 2) + b1.shape[1:], (2, 2, 2, 2, 2, d_rows, units // 2)],
    )
    block_out = block_out.reshape(micro, batch, width, length).swapaxes(2, 3)

    def add(keep, got):
        return (keep.astype(F32) + got.astype(F32)).astype(BF)

    def halves(keep, got):
        return add(keep[0], got[0]), add(keep[1], got[1])

    a_got = net.swap(a_give, core)
    b_got = net.swap(after(b_give, a_got), core)
    down_got = net.swap(after(down_give, a_got), core)
    a, a_give = halves(a_keep, a_got)
    a_got = net.swap(a_give, xbit)
    b, b_give = halves(b_keep, b_got)
    b_got = net.swap(b_give, znear)
    down, down_give = halves(down_keep, down_got)
    attended_grad = after(attended_grad, a_give, b_give, down_give)
    down_got = net.swap(down_give, ybit)

    dq, dkv_keep, dkv_give, rest_keep, rest_give = call(
        functools.partial(attention_backward_pieces, order, length, d_rows),
        [meta],
        [*blocks, wf, gains, cos_t, sin_t, allowed, q_s, k_s, v_s, attended_grad, gain_two],
        [
            sds((rows, QW + 64), BF),
            sds((2, rows, 2 * KW), BF),
            sds((2, rows, 2 * KW), BF),
            sds(lead + (d_rows + 8, 256), BF),
            sds(lead + (d_rows + 8, 256), BF),
        ],
        1.4e10,
        [(width, 1024), (1, qkv_w), (1, width), (n_fsdp, 8, 1024)],
        24,
    )
    b, b_give = halves(b, after(b_got, dq))
    a, a_give = halves(a, after(a_got, b_give))
    b_got = net.swap(b_give, zfar)
    a_got = net.swap(a_give, znear)
    rest, rest_give = halves(rest_keep, after(net.swap(rest_give, core), b_give, down_got))
    rest_got = net.swap(rest_give, ybit)
    down, down_give = halves(down, after(down_got, rest_give))
    down_got = net.swap(down_give, xbit)
    dkv, dkv_give = halves(dkv_keep, after(net.swap(dkv_give, core), down_give))
    dkv_got = net.swap(dkv_give, ybit)
    a, a_give = halves(a, after(a_got, dkv_give))
    a_got = net.swap(a_give, zfar)
    rest, rest_give = halves(rest, after(rest_got, a_give))
    rest_got = net.swap(rest_give, xbit)
    b, b_give = halves(b, after(b_got, rest_give))
    b_got = net.swap(b_give, xbit)
    down, down_give = halves(down, after(down_got, b_give))
    down_got = net.swap(down_give, znear)
    (hidden_grad,) = call(
        input_gradient_two,
        [],
        [dq, dkv, after(dkv_got, down_give), source, middle_grad, wf, gains],
        [sds((seqs, width, length), F32)],
        3e9,
        mib=16,
    )
    rest, rest_give = halves(rest, after(rest_got, hidden_grad))
    hidden_grad = hidden_grad.reshape(micro, batch, width, length).swapaxes(2, 3)
    rest_got = net.swap(rest_give, znear)
    a = add(a, after(a_got, rest_give))
    a_got = net.swap(a, ybit)
    b = add(b, after(b_got, a))
    b_got = net.swap(b, ybit)
    down, down_give = halves(down, after(down_got, b))
    down_got = net.swap(down_give, zfar)
    rest, rest_give = halves(rest, after(rest_got, down_give))
    rest_got = net.swap(rest_give, zfar)
    a = add(a, after(a_got, rest_give))
    a_far = net.swap(a, core)
    b = add(b, b_got)
    b_far = net.swap(b, core)
    down = add(down, after(down_got, a))
    down_y = net.swap(down, ybit)
    down_c = net.swap(after(down, down_y), core)
    rest = add(rest, after(rest_got, down))
    rest_y = net.swap(rest, ybit)
    rest_c = net.swap(after(rest, rest_y), core)
    down_yc = net.swap(after(down_y, rest_y), core)
    rest_yc = net.swap(rest_y, core)
    qk, v = (QW + KW) // n_fsdp, KW // n_fsdp
    out_gate, out_down, out_wout, out_qkv, b_qk, b_v, out_gains = call(
        functools.partial(place_all, ff_rows // 4, qk, v),
        [meta],
        [a, a_far, b, b_far, down, down_y, down_c, down_yc, rest, rest_y, rest_c, rest_yc],
        [
            sds((d_rows, 2 * units), F32),
            sds((ff_rows, width), F32),
            sds((d_rows, width), F32),
            sds((d_rows, qkv_w), F32),
            sds((1, qk), F32),
            sds((1, v), F32),
            sds((2, d_rows), F32),
        ],
        3e9,
        [(d_rows + 8, 1024)],
        16,
    )
    return (
        block_out,
        hidden_grad,
        out_qkv,
        b_qk.reshape(qk),
        b_v.reshape(v),
        out_wout,
        out_gate,
        out_down,
        out_gains,
    )


def solution(mesh):
    n_fsdp, n_seq = mesh.shape["fsdp"], mesh.shape["seq"]
    in_specs = (
        P(None, "fsdp", "seq", None),
        P("fsdp", None),
        P("fsdp"),
        P("fsdp", None),
        P("fsdp", None),
        P("fsdp", None),
        P(None, "fsdp"),
        P(None, "fsdp", "seq"),
        P(),
        P(None, "fsdp", "seq", None),
    )
    out_specs = (
        P(None, "fsdp", "seq", None),
        P(None, "fsdp", "seq", None),
        P("fsdp", None),
        P("fsdp"),
        P("fsdp"),
        P("fsdp", None),
        P("fsdp", None),
        P("fsdp", None),
        P(None, "fsdp"),
    )

    def local(*args):
        body = on_device_tiled if (n_fsdp, n_seq) == (8, 4) else on_device
        return body(*args, n_fsdp=n_fsdp, n_seq=n_seq)

    return jax.shard_map(local, mesh=mesh, in_specs=in_specs, out_specs=out_specs, check_vma=False)
```

```python
import functools

import jax
import jax.numpy as jnp
import numpy as np
from jax import lax
from jax.experimental import pallas as pl
from jax.experimental.pallas import tpu as pltpu
from jax.sharding import PartitionSpec as P

HEADS = 9
KV_HEADS = 3
HEAD_DIM = 64
GROUP = HEADS // KV_HEADS
QW = HEADS * HEAD_DIM
KW = KV_HEADS * HEAD_DIM
EPS = 1e-05
ROPE_BASE = 100000.0
MASKED = -1000000000.0
BF = jnp.bfloat16
F32 = jnp.float32


def dot(a, b, ca, cb):
    return lax.dot_general(a, b, (((ca,), (cb,)), ((), ())), preferred_element_type=F32)


def rotary(values, cosine, sine):
    half = values.shape[-1] // 2
    a, b = values[..., :half], values[..., half:]
    return jnp.concatenate([a * cosine - b * sine, b * cosine + a * sine], axis=-1)


def norm_parts(values):
    factor = lax.rsqrt(jnp.mean(values * values, axis=-1, keepdims=True) + EPS)
    return factor, values * factor


def norm_back(grad_in, gain, factor, normed):
    scaled = grad_in * gain
    return factor * (scaled - normed * jnp.mean(scaled * normed, axis=-1, keepdims=True))


def whole(*shape_dtypes):
    return [pl.BlockSpec(memory_space=pltpu.VMEM) for _ in shape_dtypes]


def call(kernel, scalars, arrays, outs, flops, scratch=(), mib=52, fetched=(), landing=()):
    specs = [pl.BlockSpec(memory_space=pltpu.SMEM)] * len(scalars) + whole(*arrays)
    specs += [pl.BlockSpec(memory_space=pltpu.HBM)] * len(fetched)
    arrays = [*arrays, *fetched]
    moved = sum(a.size * a.dtype.itemsize for a in arrays) + sum(
        int(np.prod(o.shape)) * o.dtype.itemsize for o in outs
    )
    return pl.pallas_call(
        kernel,
        out_shape=outs,
        in_specs=specs,
        out_specs=whole(*outs),
        scratch_shapes=[
            *[pltpu.VMEM(shape, F32) for shape in scratch],
            *[pltpu.VMEM(shape, BF) for shape in landing],
            *([pltpu.SemaphoreType.DMA((len(fetched),))] if fetched else []),
        ],
        compiler_params=pltpu.CompilerParams(vmem_limit_bytes=mib * 1024 * 1024),
        cost_estimate=pl.CostEstimate(flops=int(flops), bytes_accessed=moved, transcendentals=0),
    )(*scalars, *arrays)


def sds(shape, dtype):
    return jax.ShapeDtypeStruct(shape, dtype)


def turn(x, cosine, sine):
    tiles = []
    low = lax.broadcasted_iota(jnp.int32, (1, 128), 1) % HEAD_DIM < HEAD_DIM // 2
    for t in range(x.shape[1] // 128):
        part = x[:, 128 * t : 128 * t + 128]
        other = jnp.where(low, pltpu.roll(part, 96, 1), pltpu.roll(part, 32, 1))
        tiles.append(part * cosine + other * sine)
    return tiles


def turn_kv(x, cosine, sine):
    lane = lax.broadcasted_iota(jnp.int32, (1, 128), 1)
    first, second = turn(x[:, :256], cosine, sine)
    second = jnp.where(lane < KW - 128, second, x[:, 128:256])
    return jnp.concatenate([first, second, x[:, 256:]], axis=1)


def tables(seq, order, cos_ref, sin_ref):
    cosine = jnp.concatenate([cos_ref[seq ^ o] for o in order], axis=0)
    sine = jnp.concatenate([sin_ref[seq ^ o] for o in order], axis=0)
    return cosine, sine


def heads_to_rows(x, g):
    return jnp.concatenate(
        [x[:, HEAD_DIM * h : HEAD_DIM * (h + 1)] for h in range(GROUP * g, GROUP * (g + 1))], axis=0
    )


def rows_to_heads(parts, length):
    return jnp.concatenate(
        [p[length * r : length * (r + 1)] for p in parts for r in range(GROUP)], axis=1
    )


def attention_forward(order, length, seq_ref, blocks, wq, wkv, bq, bkv, gain, cos, sin, mask,
                      att_o, q_o, k_o, v_o):
    seq = seq_ref[0]
    cosine, sine = tables(seq, order, cos, sin)
    width = gain.shape[1]
    for b in range(blocks.shape[1] // length):
        x = blocks[:, b * length : (b + 1) * length, :width].astype(F32)
        x = x.reshape(len(order) * length, width)
        first = (norm_parts(x)[1] * gain[...]).astype(BF)
        kv = dot(first, wkv[...], 1, 0) + bkv[...]
        q = dot(first[:length], wq[...], 1, 0) + bq[...]
        q = jnp.concatenate(turn(q, cosine[:length], sine[:length]), axis=1).astype(BF)
        q = q * jnp.asarray(HEAD_DIM ** (-0.5), BF)
        kv = turn_kv(kv, cosine, sine).astype(BF)
        allowed = jnp.concatenate([mask[b]] * GROUP, axis=0) > 0.0
        parts = []
        for g in range(KV_HEADS):
            qg = heads_to_rows(q, g)
            kg = kv[:, HEAD_DIM * g : HEAD_DIM * (g + 1)]
            vg = kv[:, KW + HEAD_DIM * g : KW + HEAD_DIM * (g + 1)]
            q_o[b, g] = qg
            k_o[b, g] = kg
            v_o[b, g] = vg
            scores = jnp.where(allowed, dot(qg, kg, 1, 1), MASKED)
            top = jnp.max(scores, axis=-1, keepdims=True)
            e = jnp.exp(scores - top)
            total = jnp.sum(e, axis=-1, keepdims=True)
            probs = (e * (1.0 / total)).astype(BF)
            parts.append(dot(probs, vg, 1, 0))
        att_o[b * length : (b + 1) * length, :] = rows_to_heads(parts, length).astype(BF)


def feed_forward(attended, source, wo, wgu, wd, gain, cot, weight,
                 out_o, down_o, gu_o, mid_o, wout_o, attg_o, gain_o):
    units = wd.shape[0]
    step = units // 3
    att = attended[...]
    middle = source[...].astype(F32) + dot(att, wo[...], 1, 0)
    scale_two, normed = norm_parts(middle)
    g2 = gain[...]
    second = (normed * g2).astype(BF)
    out_grad = cot[...].astype(F32) * weight[...]
    feed_grad = out_grad.astype(BF)
    feed = None
    back = None
    for j in range(0, units, step):
        wg = wgu[:, j : j + step]
        wu = wgu[:, units + j : units + j + step]
        wdj = wd[j : j + step, :]
        gate = dot(second, wg, 1, 0)
        up = dot(second, wu, 1, 0)
        sig = jax.nn.sigmoid(gate)
        act = gate * sig
        product = (act * up).astype(BF)
        part = dot(product, wdj, 1, 0)
        feed = part if feed is None else feed + part
        down_o[j : j + step, :] = dot(product, feed_grad, 0, 0).astype(BF)
        pgrad = dot(feed_grad, wdj, 1, 1)
        ggrad = (pgrad * up * (sig * (1.0 + gate * (1.0 - sig)))).astype(BF)
        ugrad = (pgrad * act).astype(BF)
        gu_o[:, j : j + step] = dot(second, ggrad, 0, 0).astype(BF)
        gu_o[:, units + j : units + j + step] = dot(second, ugrad, 0, 0).astype(BF)
        part = dot(ggrad, wg, 1, 1) + dot(ugrad, wu, 1, 1)
        back = part if back is None else back + part
    out_o[...] = (middle + feed).astype(BF)
    gain_o[...] = jnp.sum(back * normed, axis=0, keepdims=True)
    middle_grad = out_grad + norm_back(back, g2, scale_two, normed)
    mid_o[...] = middle_grad
    branch = middle_grad.astype(BF)
    wout_o[...] = dot(att, branch, 0, 0).astype(BF)
    attg_o[...] = dot(branch, wo[...], 1, 1).astype(BF)


def attention_backward(order, length, seq_ref, blocks, wq, wkv, gain, cos, sin, mask, q_i, k_i, v_i,
                       attg, dq_o, dkv_o, wgrad_o, bias_o, gain_o):
    seq = seq_ref[0]
    cosine, sine = tables(seq, order, cos, sin)
    width = gain.shape[1]
    q_wgrad = kv_wgrad = bias_q = bias_kv = gain_sum = None
    for b in range(blocks.shape[1] // length):
        x = blocks[:, b * length : (b + 1) * length, :width].astype(F32)
        x = x.reshape(len(order) * length, width)
        normed = norm_parts(x)[1]
        first = (normed * gain[...]).astype(BF)
        allowed = jnp.concatenate([mask[b]] * GROUP, axis=0) > 0.0
        ag = attg[b * length : (b + 1) * length, :]
        dqs, dks, dvs = [], [], []
        for g in range(KV_HEADS):
            qg, kg, vg = q_i[b, g], k_i[b, g], v_i[b, g]
            agg = heads_to_rows(ag, g)
            scores = jnp.where(allowed, dot(qg, kg, 1, 1), MASKED)
            e = jnp.exp(scores - jnp.max(scores, axis=-1, keepdims=True))
            p = e * (1.0 / jnp.sum(e, axis=-1, keepdims=True))
            dvs.append(dot(p.astype(BF), agg, 0, 0))
            pg = dot(agg, vg, 1, 1)
            inner = jnp.sum(p * pg, axis=-1, keepdims=True)
            ds = (p * (pg - inner)).astype(BF)
            dqs.append(dot(ds, kg, 1, 0) * HEAD_DIM ** (-0.5))
            dks.append(dot(ds, qg, 0, 0))
        dq = rows_to_heads(dqs, length)
        dq = jnp.concatenate([dq, jnp.zeros((length, 64), F32)], axis=1)
        dq = jnp.concatenate(turn(dq, cosine[:length], -sine[:length]), axis=1).astype(BF)
        dkv = jnp.concatenate(dks + dvs, axis=1)
        dkv = turn_kv(dkv, cosine, -sine).astype(BF)
        dq_o[b * length : (b + 1) * length, :] = dq
        for r in range(len(order)):
            dkv_o[r, b * length : (b + 1) * length, :] = dkv[r * length : (r + 1) * length, :]
        wq_part = dot(first[:length], dq, 0, 0)
        wkv_part = dot(first, dkv, 0, 0)
        bq_part = jnp.sum(dq.astype(F32), axis=0, keepdims=True)
        bkv_part = jnp.sum(dkv.astype(F32), axis=0, keepdims=True)
        e_kv = dot(dkv, wkv[...], 1, 1) * normed
        e_q = dot(dq[:, :QW], wq[:, :QW], 1, 1) * normed[:length]
        g_part = jnp.sum(e_kv, axis=0, keepdims=True) + jnp.sum(e_q, axis=0, keepdims=True)
        if q_wgrad is None:
            q_wgrad, kv_wgrad, bias_q, bias_kv, gain_sum = wq_part, wkv_part, bq_part, bkv_part, g_part
        else:
            q_wgrad, kv_wgrad = q_wgrad + wq_part, kv_wgrad + wkv_part
            bias_q, bias_kv, gain_sum = bias_q + bq_part, bias_kv + bkv_part, gain_sum + g_part
    wgrad_o[...] = jnp.concatenate([q_wgrad[:, :QW], kv_wgrad], axis=1).astype(BF)
    bias_o[...] = jnp.concatenate([bias_q[:, :QW], bias_kv], axis=1)
    gain_o[...] = gain_sum


def input_gradient(dq, own, a, b, c, source, mid, wq, wkv, gain, out_o):
    kv = own[...].astype(F32) + a[...].astype(F32) + b[...].astype(F32) + c[...].astype(F32)
    first_grad = dot(dq[:, :QW], wq[:, :QW], 1, 1) + dot(kv.astype(BF), wkv[...], 1, 1)
    scale_one, normed = norm_parts(source[...].astype(F32))
    out_o[...] = mid[...] + norm_back(first_grad, gain[...], scale_one, normed)

def chosen(flag, a, b):
    return jnp.where(flag != 0, b, a)


class Blocks:
    def __init__(self, *refs):
        self.refs = refs
        self.shape = (len(refs),) + refs[0].shape

    def __getitem__(self, key):
        return jnp.stack([ref[key[1:]] for ref in self.refs])


def cut_qkv(core_bit, meta, w_hbm, bias_hbm, gains_hbm, out_o, w, bias, gains, all_s, sems):
    pairs = ((w_hbm, w), (bias_hbm, bias), (gains_hbm, gains))
    copies = [pltpu.make_async_copy(a, b, sems.at[i]) for i, (a, b) in enumerate(pairs)]
    for copy in copies:
        copy.start()
    for copy in copies:
        copy.wait()
    rows = w.shape[0]
    n = bias.shape[1]
    all_s[:rows, :] = w[...].astype(F32)
    all_s[rows:, :] = jnp.zeros((8, w.shape[1]), F32)
    all_s[rows : rows + 1, :n] = bias[...].astype(F32)
    for i in range(2):
        all_s[rows : rows + 1, n + rows * i : n + rows * (i + 1)] = gains[i : i + 1, :].astype(F32)
    half = out_o.shape[0]
    at = pl.multiple_of((meta[0] & core_bit) * half, 8)
    out_o[...] = all_s[pl.ds(at, half), :].astype(BF)


def first_forward(order, length, d_rows, n_bias, meta, b0, b1, b2, b3, a00, a10, a01, a11, cos, sin, mask,
                  att_o, q_o, k_o, v_o, w_o, gain_o, w_s, b_s):
    blocks = Blocks(b0, b1, b2, b3)
    core, x = meta[0] & 1, meta[1] & 1
    cut = a00.shape[2]
    for x_rel, c_rel, piece in ((0, 0, a00), (1, 0, a10), (0, 1, a01), (1, 1, a11)):
        for z0 in range(2):
            for z1 in range(2):
                at = (z1 * 4 + z0 * 2 + (x ^ x_rel)) * 2 * cut + (core ^ c_rel) * cut
                w_s[pl.ds(pl.multiple_of(at, 8), cut), :] = piece[z0, z1].astype(F32)
    n_f = w_s.shape[0] // (2 * cut)
    starts = [2 * cut * f for f in range(n_f)]
    w_o[...] = jnp.concatenate([w_s[at : at + d_rows, :] for at in starts], axis=0).astype(BF)
    lines = [w_s[at + d_rows : at + d_rows + 1, :] for at in starts]
    b_s[...] = jnp.concatenate([line[:, :n_bias] for line in lines], axis=1)
    for i in range(2):
        at = n_bias + d_rows * i
        gain_o[i : i + 1, :] = jnp.concatenate([line[:, at : at + d_rows] for line in lines], axis=1)
    wide = QW + 64
    attention_forward(order, length, meta, blocks, w_o[:, :wide], w_o[:, QW:], b_s[:, :wide], b_s[:, QW:],
                      gain_o[0:1, :], cos, sin, mask, att_o, q_o, k_o, v_o)


def turned(out, value):
    length = out.shape[2]
    for b in range(out.shape[0]):
        out[b] = value[length * b : length * (b + 1)].T.astype(out.dtype)


def rel(meta, f):
    r = f ^ meta[1]
    return r & 1, (r >> 1) & 1, (r >> 2) & 1


def fetch_pieces(meta, refs, b_s, g_s, sems):
    core, y, x, z0 = meta[0] & 1, (meta[0] >> 1) & 1, meta[1] & 1, (meta[1] >> 1) & 1
    copies = []
    for i in range(8):
        at = (z0 ^ (i >> 2), x ^ ((i >> 1) & 1), core ^ (i & 1))
        copies.append(pltpu.make_async_copy(refs[i], b_s.at[at], sems.at[i]))
    for i in range(8):
        at = (y ^ ((i >> 1) & 1), core ^ (i & 1), x ^ (i >> 2))
        copies.append(pltpu.make_async_copy(refs[8 + i], g_s.at[at], sems.at[8 + i]))
    for copy in copies:
        copy.start()
    return copies


def feed_forward_pieces(d_rows, ff_rows, meta, attended, source, gains, cot, weight, *refs):
    out_o, ak_o, ag_o, bk_o, bg_o, dk_o, dg_o, mid_o, attg_o, gain_o, down_s, wout_s, b_s, g_s, sems = refs[16:]
    copies = fetch_pieces(meta, refs, b_s, g_s, sems)
    core, y = meta[0] & 1, (meta[0] >> 1) & 1
    part_d = ff_rows // 4
    part_o = d_rows // 3
    cut = b_s.shape[4] - ff_rows // 2
    half = g_s.shape[-1] // 2
    for copy in copies[:8]:
        copy.wait()
    wo = []
    for f in range(8):
        for c in range(2):
            rows = b_s[(f >> 1) & 1, f & 1, c, f >> 2, ff_rows // 2 :, :].astype(F32)
            wo.append(rows if c == 0 else rows[: d_rows - cut])
    wo = jnp.concatenate(wo, axis=0).astype(BF)
    att = attended[...]
    middle = source[...].astype(F32) + dot(att, wo, 1, 0)
    scale_two, normed = norm_parts(middle)
    g2 = gains[1:2, :]
    second = (normed * g2).astype(BF)
    out_grad = cot[...].astype(F32) * weight[...]
    feed_grad = out_grad.astype(BF)
    for copy in copies[8:]:
        copy.wait()
    feed = back = None
    for c_rel in (1, 0):
        h = core ^ c_rel
        weights = []
        for yy in range(2):
            rows = [g_s[yy, h, f & 1, (f >> 1) & 1, f >> 2].astype(F32) for f in range(8)]
            weights.append(jnp.concatenate(rows, axis=0).astype(BF))
        wg, wu = weights
        wd = [b_s[i >> 1, i & 1, c, h, : ff_rows // 2, :] for i in range(4) for c in range(2)]
        wd = jnp.concatenate(wd, axis=0)
        gate = dot(second, wg, 1, 0)
        up = dot(second, wu, 1, 0)
        sig = jax.nn.sigmoid(gate)
        act = gate * sig
        product = (act * up).astype(BF)
        part = dot(product, wd, 1, 0)
        feed = part if feed is None else feed + part
        down_s[...] = dot(product, feed_grad, 0, 0)
        pgrad = dot(feed_grad, wd, 1, 1)
        ggrad = (pgrad * up * (sig * (1.0 + gate * (1.0 - sig)))).astype(BF)
        ugrad = (pgrad * act).astype(BF)
        part = dot(ggrad, wg, 1, 1) + dot(ugrad, wu, 1, 1)
        back = part if back is None else back + part
        for i in range(4):
            x, z0, z1 = rel(meta, 4 * h + i)
            for yy in range(2):
                for c_to, to in ((0, dk_o), (1, dg_o)):
                    at = pl.multiple_of(i * ff_rows + (yy * 2 + (core ^ c_to)) * part_d, 16)
                    to[y ^ yy, x, z0, z1, :part_d, :] = down_s[pl.ds(at, part_d), :].astype(BF)
        to_a, to_b = (ag_o, bg_o) if c_rel else (ak_o, bk_o)
        for yy, grad in ((0, ggrad), (1, ugrad)):
            wgrad = dot(second, grad, 0, 0)
            for f in range(8):
                x, z0, z1 = rel(meta, f)
                block = wgrad[d_rows * f : d_rows * (f + 1), :].astype(BF)
                to_a[x, z0, z1, yy] = block[:, :half]
                to_b[z0, z1, x, yy] = block[:, half:]
    turned(out_o, middle + feed)
    gain_o[...] = jnp.sum(back * normed, axis=0, keepdims=True)
    middle_grad = out_grad + norm_back(back, g2, scale_two, normed)
    mid_o[...] = middle_grad
    branch = middle_grad.astype(BF)
    attg_o[...] = dot(branch, wo, 1, 1).astype(BF)
    wout = dot(att, branch, 0, 0)
    for f in range(8):
        wout_s[f, :d_rows, :] = wout[d_rows * f : d_rows * (f + 1), :]
        wout_s[f, d_rows:, :] = jnp.zeros((part_o, wout.shape[1]), F32)
    for f in range(8):
        x, z0, z1 = rel(meta, f)
        for yy in range(2):
            for c_to, to in ((0, dk_o), (1, dg_o)):
                at = pl.multiple_of((yy * 2 + (core ^ c_to)) * part_o, 8)
                to[y ^ yy, x, z0, z1, part_d:, :] = wout_s[f, pl.ds(at, part_o), :].astype(BF)


def attention_backward_pieces(order, length, d_rows, meta, b0, b1, b2, b3, w, gains, cos, sin, mask, q_i, k_i, v_i,
                              attg, gain_two, dq_o, dk_o, dg_o, rk_o, rg_o, w_s, bias_s, gain_s, small_s):
    blocks = Blocks(b0, b1, b2, b3)
    half = len(order) // 2

    class Pieces:
        def __setitem__(self, key, value):
            ref = dk_o if key[0] < half else dg_o
            ref[(key[0] % half,) + key[1:]] = value

    class Wgrad:
        def __setitem__(self, key, value):
            w_s[:, : 2 * KW] = value[:, QW:].astype(F32)
            w_s[:, 2 * KW : 2 * KW + QW] = value[:, :QW].astype(F32)
            w_s[:, 2 * KW + QW :] = jnp.zeros((value.shape[0], 64), F32)

    wide = QW + 64
    attention_backward(order, length, meta, blocks, w[:, :wide], w[:, QW:], gains[0:1, :], cos, sin, mask,
                       q_i, k_i, v_i, attg, dq_o, Pieces(), Wgrad(), bias_s, gain_s)
    n_f = small_s.shape[0]
    qk, v = (QW + KW) // n_f, KW // n_f
    bias, g1, g2 = bias_s[...], gain_s[...], gain_two[...]
    for f in range(n_f):
        line = jnp.concatenate(
            [
                bias[:, qk * f : qk * (f + 1)],
                bias[:, QW + KW + v * f : QW + KW + v * (f + 1)],
                g1[:, d_rows * f : d_rows * (f + 1)],
                jnp.zeros((1, 256 - qk - v - d_rows), F32),
                g2[:, d_rows * f : d_rows * (f + 1)],
                jnp.zeros((1, 768 - d_rows), F32),
            ],
            axis=1,
        )
        small_s[f] = jnp.broadcast_to(line, (8, 1024))
    core, y = meta[0] & 1, (meta[0] >> 1) & 1
    for f in range(n_f):
        x, z0, z1 = rel(meta, f)
        for yy in range(2):
            for c_to, to in ((0, rk_o), (1, rg_o)):
                at = pl.multiple_of((yy * 2 + (core ^ c_to)) * 256, 256)
                block = [w_s[d_rows * f : d_rows * (f + 1), pl.ds(at, 256)], small_s[f, :, pl.ds(at, 256)]]
                to[y ^ yy, x, z0, z1] = jnp.concatenate(block, axis=0).astype(BF)


def input_gradient_two(dq, own, other, source, mid, w, gains, out_o):
    kv = (own[...].astype(F32) + other[...].astype(F32)).astype(BF)
    first_grad = dot(dq[:, :QW], w[:, :QW], 1, 1) + dot(kv, w[:, QW:], 1, 1)
    scale_one, normed = norm_parts(source[...].astype(F32))
    turned(out_o, mid[...] + norm_back(first_grad, gains[0:1, :], scale_one, normed))


def place_gate(meta, near, far, out_o, parts=1, part=0):
    core = meta[0] & 1
    n = near.shape[2]
    for pieces, c_rel in ((near, 0), (far, 1)):
        for yy in range(2):
            at = pl.multiple_of(((yy * 2 + (core ^ c_rel)) * parts + part) * n, 128)
            out_o[:, pl.ds(at, n)] = pieces[yy].astype(F32)


def place_down(part_d, meta, p00, p10, p01, p11, out_o, wout_o):
    seq = meta[0]
    part_o = p00.shape[0] - part_d
    for piece, o in ((p00[...], 0), (p10[...], 2), (p01[...], 1), (p11[...], 3)):
        piece = piece.astype(F32)
        to = seq ^ o
        out_o[pl.ds(pl.multiple_of(to * part_d, 16), part_d), :] = piece[:part_d]

        @pl.when(to < 3)
        def _():
            wout_o[pl.ds(pl.multiple_of(to * part_o, 8), part_o), :] = piece[part_d:]


def place_qkv(qk, v, meta, p00, p10, p01, p11, w_o, bqk_o, bv_o, gains_o, all_s):
    n = p00.shape[1]
    for piece, o in ((p00, 0), (p10, 2), (p01, 1), (p11, 3)):
        all_s[:, pl.ds(pl.multiple_of((meta[0] ^ o) * n, 128), n)] = piece[...].astype(F32)
    d_rows = w_o.shape[0]
    w_o[:, :QW] = all_s[:d_rows, 2 * KW : 2 * KW + QW]
    w_o[:, QW:] = all_s[:d_rows, : 2 * KW]
    line = all_s[d_rows : d_rows + 1, :]
    bqk_o[...] = line[:, :qk]
    bv_o[...] = line[:, qk : qk + v]
    gains_o[0:1, :] = line[:, qk + v : qk + v + d_rows]
    gains_o[1:2, :] = line[:, 256 : 256 + d_rows]


def place_rest(part_d, qk, v, meta, d0, d1, d2, d3, r0, r1, far,
               down_o, wout_o, w_o, bqk_o, bv_o, gains_o, all_s):
    place_down(part_d, meta, d0, d1, d2, d3, down_o, wout_o)
    place_qkv(qk, v, meta, r0, r1, far.at[0], far.at[1], w_o, bqk_o, bv_o, gains_o, all_s)


def place_halves(meta, a_near, a_far, b_near, b_far, out_o):
    place_gate(meta, a_near, a_far, out_o, 2, 0)
    place_gate(meta, b_near, b_far, out_o, 2, 1)


class Net:
    def __init__(self, n_fsdp, n_seq):
        self.n_fsdp, self.n_seq = n_fsdp, n_seq
        self.total = n_fsdp * n_seq
        f, s = lax.axis_index("fsdp"), lax.axis_index("seq")
        self.index = f * n_seq + s
        self.seq_bits = [1 << b for b in range(n_seq.bit_length() - 1)]
        self.fsdp_bits = [n_seq << b for b in range(n_fsdp.bit_length() - 1)]

    def swap(self, value, mask):
        pairs = [(i, i ^ mask) for i in range(self.total)]
        return lax.ppermute(value, ("fsdp", "seq"), pairs)

    def bit(self, mask):
        return (self.index & mask) != 0

    def both(self, mine, mask, axis, other=None):
        other = self.swap(mine, mask) if other is None else other
        high = self.bit(mask)
        return jnp.stack([jnp.where(high, other, mine), jnp.where(high, mine, other)], axis=axis)

    def half(self, value, mask, axis):
        return lax.dynamic_index_in_dim(
            value, self.bit(mask).astype(jnp.int32), axis, keepdims=False
        )

    def add_half(self, value, mask, axis):
        mine = self.bit(mask).astype(jnp.int32)
        keep = lax.dynamic_index_in_dim(value, mine, axis, keepdims=False)
        give = lax.dynamic_index_in_dim(value, 1 - mine, axis, keepdims=False)
        got = self.swap(give, mask)
        return (keep.astype(F32) + got.astype(F32)).astype(value.dtype)

    def gather_fsdp(self, value):
        for step, mask in enumerate(reversed(self.fsdp_bits)):
            value = self.both(value, mask, step)
        return value

    def scatter_fsdp(self, value, first_axis=0):
        count = len(self.fsdp_bits)
        for step, mask in enumerate(self.fsdp_bits):
            value = self.add_half(value, mask, first_axis + count - 1 - step)
        return value


def on_device(
    hidden, w_qkv, b_qkv, w_out, w_gate_up, w_down, norm_gains, segment_ids, token_counts, cotangent,
    n_fsdp, n_seq,
):
    net = Net(n_fsdp, n_seq)
    micro, batch, length, width = hidden.shape
    full_length = length * n_seq
    tokens_micro = batch * n_fsdp * full_length
    scale = HEAD_DIM ** (-0.5)
    rows = micro * batch * length
    d_rows = w_qkv.shape[0]
    ff_rows = w_down.shape[0]
    units = w_gate_up.shape[1] // 2
    qkv_w = w_qkv.shape[1]
    core = net.seq_bits[0]
    f_lead = (2,) * len(net.fsdp_bits)

    ids = segment_ids.reshape(rows, 1).astype(BF)
    block = jnp.concatenate(
        [hidden.reshape(rows, width), jnp.broadcast_to(ids, (rows, 64))], axis=1
    )
    blocks = block[None]
    for mask in reversed(net.seq_bits):
        blocks = jnp.concatenate([blocks, net.swap(blocks, mask)], axis=0)
    order = [0]
    for mask in reversed(net.seq_bits):
        order = order + [o ^ mask for o in order]
    seq_index = lax.axis_index("seq")
    block_ids = [seq_index ^ o for o in order]

    pad_rows = -(d_rows + 1) % 16 + 1
    extra = jnp.zeros((pad_rows, qkv_w), BF)
    small = jnp.concatenate([b_qkv, norm_gains.reshape(-1)])
    extra = extra.at[0, : small.shape[0]].set(small)
    shard_a = jnp.concatenate([w_qkv, extra], axis=0).reshape(2, -1, qkv_w)
    got_a = net.gather_fsdp(net.half(shard_a, core, 0))
    full_a = net.both(got_a, core, len(f_lead)).reshape(n_fsdp, d_rows + pad_rows, qkv_w)
    wf_qkv = full_a[:, :d_rows].reshape(n_fsdp * d_rows, qkv_w)
    smalls = full_a[:, d_rows]
    n_bias = b_qkv.shape[0]
    bias = smalls[:, :n_bias].reshape(-1).astype(F32)
    gains = smalls[:, n_bias : n_bias + 2 * d_rows].reshape(n_fsdp, 2, d_rows).astype(F32)
    gain_one = gains[:, 0].reshape(-1)
    gain_two = gains[:, 1].reshape(-1)

    pad_b = -(d_rows + ff_rows) % 16
    shard_b = jnp.concatenate([w_out, w_down, jnp.zeros((pad_b, width), BF)], axis=0)
    shard_b = shard_b.reshape(2, -1, width)
    got_b = net.gather_fsdp(net.half(shard_b, core, 0))

    parts = n_seq
    shard_c = w_gate_up.reshape(d_rows, parts, -1)
    got_c = net.gather_fsdp(lax.dynamic_index_in_dim(shard_c, seq_index, 1, keepdims=False))
    full_b = net.both(got_b, core, len(f_lead)).reshape(n_fsdp, -1, width)
    wf_out = full_b[:, :d_rows].reshape(n_fsdp * d_rows, width)
    wf_down = full_b[:, d_rows : d_rows + ff_rows].reshape(n_fsdp * ff_rows, width)
    got_c = got_c.reshape(n_fsdp * d_rows, -1)
    for mask in reversed(net.seq_bits):
        got_c = net.both(got_c, mask, got_c.ndim - 1)
    wf_gate_up = got_c.reshape(n_fsdp * d_rows, 2 * units)

    places = np.arange(full_length, dtype=np.float32)
    speeds = np.power(ROPE_BASE, -2.0 * np.arange(HEAD_DIM // 2, dtype=np.float32) / HEAD_DIM)
    angles = places[:, None] * speeds.astype(np.float32)[None, :]
    cos_t = np.tile(np.cos(angles), (1, 4)).reshape(n_seq, length, 128)
    sin_t = np.concatenate([-np.sin(angles), np.sin(angles)] * 2, axis=1).reshape(n_seq, length, 128)
    cos_t, sin_t = jnp.asarray(cos_t, F32), jnp.asarray(sin_t, F32)
    seqs = micro * batch
    seg_all = blocks[..., width].reshape(n_seq, seqs, length).transpose(1, 0, 2)
    own_places = seq_index * length + jnp.arange(length, dtype=jnp.int32)
    key_places = jnp.stack(block_ids)[:, None] * length + jnp.arange(length, dtype=jnp.int32)
    allowed = (seg_all[:, 0, :, None] == seg_all.reshape(seqs, 1, -1)) & (
        own_places[None, :, None] >= key_places.reshape(1, 1, -1)
    )
    allowed = allowed.astype(F32)
    seq_scalar = seq_index.astype(jnp.int32).reshape(1)
    wq, wkv = wf_qkv[:, : QW + 64], wf_qkv[:, QW:]
    gain_one, gain_two = gain_one[None], gain_two[None]
    source = hidden.reshape(rows, width)
    n_all = n_seq * rows
    attended, q_s, k_s, v_s = call(
        functools.partial(attention_forward, order, length),
        [seq_scalar],
        [blocks, wq, wkv, bias[None, : QW + 64], bias[None, QW:], gain_one, cos_t, sin_t, allowed],
        [
            sds((rows, QW), BF),
            sds((seqs, KV_HEADS, GROUP * length, HEAD_DIM), BF),
            sds((seqs, KV_HEADS, full_length, HEAD_DIM), BF),
            sds((seqs, KV_HEADS, full_length, HEAD_DIM), BF),
        ],
        2 * n_all * width * 2 * KW + 2 * rows * width * QW + 4 * rows * full_length * QW,
    )

    weight = tokens_micro / token_counts.astype(F32)
    weight = jnp.repeat(weight, batch * length)[:, None]
    block_out, down_grad, gate_up_wgrad, middle_grad, out_wgrad, attended_grad, gain_two_grad = call(
        feed_forward,
        [],
        [attended, source, wf_out, wf_gate_up, wf_down, gain_two, cotangent.reshape(rows, width), weight],
        [
            sds((rows, width), BF),
            sds((units, width), BF),
            sds((width, 2 * units), BF),
            sds((rows, width), F32),
            sds((QW, width), BF),
            sds((rows, QW), BF),
            sds((1, width), F32),
        ],
        6 * rows * width * 3 * units + 6 * rows * width * QW,
    )
    block_out = block_out.reshape(hidden.shape)

    def seq_axes(value, axis, masks):
        for mask in masks:
            value = net.add_half(value, mask, axis)
        return value

    quarter = (2,) * len(net.seq_bits)
    n_f = len(f_lead)
    red_down = down_grad.reshape(f_lead + quarter + (ff_rows // n_seq, width))
    for step, mask in enumerate(net.seq_bits):
        red_down = net.add_half(red_down, mask, n_f + len(quarter) - 1 - step)
    red_down = net.scatter_fsdp(red_down)

    red_gate = gate_up_wgrad.reshape(f_lead + (d_rows,) + quarter + (2 * units // n_seq,))
    red_gate = net.add_half(red_gate, core, n_f + len(quarter))
    red_gate = net.add_half(red_gate, net.fsdp_bits[0], n_f - 1)
    for step, mask in enumerate(net.seq_bits[1:]):
        red_gate = net.add_half(red_gate, mask, n_f - 1 + len(quarter) - 1 - step)
    for step, mask in enumerate(net.fsdp_bits[1:]):
        red_gate = net.add_half(red_gate, mask, n_f - 2 - step)

    dq, dkv, qkv_wgrad, bias_grad, gain_one_grad = call(
        functools.partial(attention_backward, order, length),
        [seq_scalar],
        [blocks, wq, wkv, gain_one, cos_t, sin_t, allowed, q_s, k_s, v_s, attended_grad],
        [
            sds((rows, QW + 64), BF),
            sds((n_seq, rows, 2 * KW), BF),
            sds((width, qkv_w), BF),
            sds((1, qkv_w), F32),
            sds((1, width), F32),
        ],
        4 * n_all * width * 2 * KW + 4 * rows * width * QW + 10 * rows * full_length * QW,
    )
    kv_parts = [dkv[0]]
    for place, mask_bits in enumerate(order):
        if mask_bits:
            kv_parts.append(net.swap(dkv[place], mask_bits))
    (hidden_grad,) = call(
        input_gradient,
        [],
        [dq, *kv_parts, source, middle_grad, wq, wkv, gain_one],
        [sds((rows, width), F32)],
        2 * rows * width * qkv_w,
    )
    hidden_grad = hidden_grad.reshape(hidden.shape)
    bias_grad, gain_one_grad, gain_two_grad = bias_grad[0], gain_one_grad[0], gain_two_grad[0]

    qk_rows, v_rows = (QW + KW) // n_fsdp, KW // n_fsdp
    small_grads = jnp.concatenate(
        [
            bias_grad[: QW + KW].reshape(n_fsdp, qk_rows),
            bias_grad[QW + KW :].reshape(n_fsdp, v_rows),
            gain_one_grad.reshape(n_fsdp, d_rows),
            gain_two_grad.reshape(n_fsdp, d_rows),
        ],
        axis=1,
    ).astype(BF)
    wide = qkv_w + width
    small_pad = jnp.zeros((n_fsdp, pad_rows, wide), BF)
    small_pad = small_pad.at[:, 0, : small_grads.shape[1]].set(small_grads)
    rest = jnp.concatenate([qkv_wgrad, out_wgrad], axis=1)
    rest = jnp.concatenate([rest.reshape(n_fsdp, d_rows, wide), small_pad], axis=1)
    rest = rest.reshape(f_lead + (d_rows + pad_rows,) + quarter + (wide // n_seq,))
    for step, mask in enumerate(net.seq_bits):
        rest = net.add_half(rest, mask, n_f + 1 + len(quarter) - 1 - step)
    rest = net.scatter_fsdp(rest)

    def seq_back(value, axis):
        for step, mask in enumerate(reversed(net.seq_bits)):
            value = net.both(value, mask, axis + step)
        return value

    out_down = seq_back(red_down, 0).reshape(ff_rows, width).astype(F32)
    out_gate = seq_back(red_gate, 1).reshape(d_rows, 2 * units).astype(F32)
    out_rest = seq_back(rest, 1).reshape(d_rows + pad_rows, wide).astype(F32)
    line = out_rest[d_rows]
    edge = qk_rows + v_rows
    return (
        block_out,
        hidden_grad,
        out_rest[:d_rows, :qkv_w],
        line[:qk_rows],
        line[qk_rows:edge],
        out_rest[:d_rows, qkv_w:],
        out_gate,
        out_down,
        line[edge : edge + 2 * d_rows].reshape(2, d_rows),
    )


def after(value, *others):
    return lax.optimization_barrier((value, *others))[0]


def rope_tables(full_length, n_seq):
    places = np.arange(full_length, dtype=np.float32)
    speeds = np.power(ROPE_BASE, -2.0 * np.arange(HEAD_DIM // 2, dtype=np.float32) / HEAD_DIM)
    angles = places[:, None] * speeds.astype(np.float32)[None, :]
    cos_t = np.tile(np.cos(angles), (1, 4)).reshape(n_seq, -1, 128)
    sin_t = np.concatenate([-np.sin(angles), np.sin(angles)] * 2, axis=1).reshape(n_seq, -1, 128)
    return jnp.asarray(cos_t, F32), jnp.asarray(sin_t, F32)


def on_device_tiled(
    hidden, w_qkv, b_qkv, w_out, w_gate_up, w_down, norm_gains, segment_ids, token_counts, cotangent,
    n_fsdp, n_seq,
):
    net = Net(n_fsdp, n_seq)
    micro, batch, length, width = hidden.shape
    full_length = length * n_seq
    tokens_micro = batch * n_fsdp * full_length
    rows = micro * batch * length
    seqs = micro * batch
    d_rows, qkv_w = w_qkv.shape
    ff_rows = w_down.shape[0]
    units = w_gate_up.shape[1] // 2
    n_bias = b_qkv.shape[0]
    core, ybit = net.seq_bits
    xbit, znear, zfar = net.fsdp_bits
    order = [0, 2, 1, 3]
    seq_index = lax.axis_index("seq")
    meta = jnp.stack([seq_index, lax.axis_index("fsdp")]).astype(jnp.int32)
    source = hidden.reshape(rows, width)

    small = [w_qkv, b_qkv[None], norm_gains]
    a0 = pl.pallas_call(
        functools.partial(cut_qkv, core),
        out_shape=sds(((d_rows + 8) // 2, qkv_w), BF),
        in_specs=[pl.BlockSpec(memory_space=pltpu.SMEM)] + [pl.BlockSpec(memory_space=pltpu.HBM)] * 3,
        out_specs=pl.BlockSpec(memory_space=pltpu.VMEM),
        scratch_shapes=[
            *[pltpu.VMEM(v.shape, BF) for v in small],
            pltpu.VMEM((d_rows + 8, qkv_w), F32),
            pltpu.SemaphoreType.DMA((3,)),
        ],
        compiler_params=pltpu.CompilerParams(vmem_limit_bytes=52 * 1024 * 1024),
    )(meta, *small)
    a1 = net.both(a0, zfar, 0)

    ids = segment_ids.reshape(rows, 1).astype(BF)
    block = jnp.concatenate([source, jnp.broadcast_to(ids, (rows, 64))], axis=1)
    block = after(block, a0)
    block_y = net.swap(block, ybit)
    block_c = net.swap(block, core)

    quarter = 2 * units // n_seq
    gu0 = lax.dynamic_slice_in_dim(after(w_gate_up, a0), seq_index * quarter, quarter, axis=1)
    half_b = jnp.concatenate(
        [
            w_down.reshape(2, ff_rows // 2, width),
            jnp.concatenate([w_out, jnp.zeros((8, width), BF)], axis=0).reshape(2, -1, width),
        ],
        axis=1,
    )
    a2 = net.both(a1, znear, 0)
    a_x = net.swap(a2, xbit)
    a_c = net.swap(a2, core)
    gu1 = net.both(gu0, zfar, 0)
    gu2 = net.both(after(gu1, a2), znear, 0)
    block_yc = net.swap(block_y, core)
    a_xc = net.swap(a_x, core)
    gu_y = net.swap(gu2, ybit)
    gu_c = net.swap(gu2, core)
    b0 = net.half(after(half_b, a0), core, 0)
    b1 = net.both(b0, zfar, 0, after(net.swap(b0, zfar), a2))
    b_x = net.swap(b1, xbit)
    gu_x = net.swap(after(gu2, b_x), xbit)
    b_z = net.swap(after(b1, gu2), znear)
    b_c = net.swap(b1, core)
    a_xc = after(a_xc, b_x)

    cos_t, sin_t = rope_tables(full_length, n_seq)
    block_ids = [seq_index ^ o for o in order]
    blocks = [block, block_y, block_c, block_yc]
    seg_all = jnp.stack([b[:, width].reshape(seqs, length) for b in blocks], axis=1)
    own_places = seq_index * length + jnp.arange(length, dtype=jnp.int32)
    key_places = jnp.stack(block_ids)[:, None] * length + jnp.arange(length, dtype=jnp.int32)
    allowed = (seg_all[:, 0, :, None] == seg_all.reshape(seqs, 1, -1)) & (
        own_places[None, :, None] >= key_places.reshape(1, 1, -1)
    )
    allowed = allowed.astype(F32)
    attended, q_s, k_s, v_s, wf, gains = call(
        functools.partial(first_forward, order, length, d_rows, n_bias),
        [meta],
        [*blocks, a2, a_x, a_c, a_xc, cos_t, sin_t, allowed],
        [
            sds((rows, QW), BF),
            sds((seqs, KV_HEADS, GROUP * length, HEAD_DIM), BF),
            sds((seqs, KV_HEADS, full_length, HEAD_DIM), BF),
            sds((seqs, KV_HEADS, full_length, HEAD_DIM), BF),
            sds((width, qkv_w), BF),
            sds((2, width), F32),
        ],
        1.2e10,
        [(n_fsdp * (d_rows + 8), qkv_w), (1, qkv_w)],
    )
    gu_y = after(gu_y, attended)
    gu_x, b_z, b_x = after(gu_x, gu_y), after(b_z, gu_y), after(b_x, gu_y)
    gu_xy = net.swap(gu_x, ybit)
    b_zx = net.swap(b_z, xbit)
    gu_yc = net.swap(gu_y, core)
    gu_xc = net.swap(gu_x, core)
    b_zc = net.swap(b_z, core)
    b_xc = net.swap(b_x, core)
    b_zxc = net.swap(b_zx, core)
    gu_xyc = net.swap(gu_xy, core)
    pieces = [b1, b_c, b_x, b_xc, b_z, b_zc, b_zx, b_zxc]
    pieces += [gu2, gu_c, gu_y, gu_yc, gu_x, gu_xc, gu_xy, gu_xyc]

    weight = tokens_micro / token_counts.astype(F32)
    weight = jnp.repeat(weight, batch * length)[:, None]
    lead = (2, 2, 2, 2)
    cot = cotangent.reshape(rows, width)
    gate_lead = lead + (d_rows, units // 4)
    block_out, a_keep, a_give, b_keep, b_give, down_keep, down_give, middle_grad, attended_grad, gain_two = call(
        functools.partial(feed_forward_pieces, d_rows, ff_rows),
        [meta],
        [attended, source, gains, cot, weight],
        [
            sds((seqs, width, length), BF),
            sds(gate_lead, BF),
            sds(gate_lead, BF),
            sds(gate_lead, BF),
            sds(gate_lead, BF),
            sds(lead + (ff_rows // 4 + d_rows // 3, width), BF),
            sds(lead + (ff_rows // 4 + d_rows // 3, width), BF),
            sds((rows, width), F32),
            sds((rows, QW), BF),
            sds((1, width), F32),
        ],
        1.4e10,
        [(units // 2, width), (n_fsdp, d_rows + d_rows // 3, width)],
        fetched=pieces,
        landing=[(2, 2, 2, 2) + b1.shape[1:], (2, 2, 2, 2, 2, d_rows, units // 2)],
    )
    block_out = block_out.reshape(micro, batch, width, length).swapaxes(2, 3)

    def add(keep, got):
        return (keep.astype(F32) + got.astype(F32)).astype(BF)

    def halves(keep, got):
        return add(keep[0], got[0]), add(keep[1], got[1])

    a_got = net.swap(a_give, core)
    b_got = net.swap(after(b_give, a_got), core)
    down_got = net.swap(after(down_give, a_got), core)
    a, a_give = halves(a_keep, a_got)
    a_got = net.swap(a_give, xbit)
    b, b_give = halves(b_keep, b_got)
    b_got = net.swap(b_give, znear)
    down, down_give = halves(down_keep, down_got)
    attended_grad = after(attended_grad, a_give, b_give, down_give)
    down_got = net.swap(down_give, ybit)

    dq, dkv_keep, dkv_give, rest_keep, rest_give = call(
        functools.partial(attention_backward_pieces, order, length, d_rows),
        [meta],
        [*blocks, wf, gains, cos_t, sin_t, allowed, q_s, k_s, v_s, attended_grad, gain_two],
        [
            sds((rows, QW + 64), BF),
            sds((2, rows, 2 * KW), BF),
            sds((2, rows, 2 * KW), BF),
            sds(lead + (d_rows + 8, 256), BF),
            sds(lead + (d_rows + 8, 256), BF),
        ],
        1.4e10,
        [(width, 1024), (1, qkv_w), (1, width), (n_fsdp, 8, 1024)],
        24,
    )
    b, b_give = halves(b, after(b_got, dq))
    a, a_give = halves(a, after(a_got, b_give))
    b_got = net.swap(b_give, zfar)
    a_got = net.swap(a_give, znear)
    rest, rest_give = halves(rest_keep, after(net.swap(rest_give, core), b_give, down_got))
    rest_got = net.swap(rest_give, ybit)
    down, down_give = halves(down, after(down_got, rest_give))
    down_got = net.swap(down_give, xbit)
    dkv, dkv_give = halves(dkv_keep, after(net.swap(dkv_give, core), down_give))
    dkv_got = net.swap(dkv_give, ybit)
    a, a_give = halves(a, after(a_got, dkv_give))
    a_got = net.swap(a_give, zfar)
    rest, rest_give = halves(rest, after(rest_got, a_give))
    rest_got = net.swap(rest_give, xbit)
    b, b_give = halves(b, after(b_got, rest_give))
    b_got = net.swap(b_give, xbit)
    down, down_give = halves(down, after(down_got, b_give))
    down_got = net.swap(down_give, znear)
    (hidden_grad,) = call(
        input_gradient_two,
        [],
        [dq, dkv, after(dkv_got, down_give), source, middle_grad, wf, gains],
        [sds((seqs, width, length), F32)],
        3e9,
        mib=16,
    )
    rest, rest_give = halves(rest, after(rest_got, hidden_grad))
    hidden_grad = hidden_grad.reshape(micro, batch, width, length).swapaxes(2, 3)
    rest_got = net.swap(rest_give, znear)
    a = add(a, after(a_got, rest_give))
    a_got = net.swap(a, ybit)
    b = add(b, after(b_got, a))
    b_got = net.swap(b, ybit)
    down, down_give = halves(down, after(down_got, b))
    down_got = net.swap(down_give, zfar)
    rest, rest_give = halves(rest, after(rest_got, down_give))
    rest_got = net.swap(rest_give, zfar)
    a = add(a, after(a_got, rest_give))
    a_far = net.swap(a, core)
    b = add(b, b_got)
    b_far = net.swap(b, core)
    down = add(down, after(down_got, a))
    down_y = net.swap(down, ybit)
    down_c = net.swap(after(down, down_y), core)
    rest = add(rest, after(rest_got, down))
    rest_y = net.swap(rest, ybit)
    (out_gate,) = call(
        place_halves,
        [meta],
        [a, a_far, b, b_far],
        [sds((d_rows, 2 * units), F32)],
        1e9,
        mib=16,
    )
    rest_y = after(rest_y, out_gate)
    rest_far = net.swap(jnp.stack([rest, rest_y]), core)
    down_yc = net.swap(after(down_y, rest_y), core)
    qk, v = (QW + KW) // n_fsdp, KW // n_fsdp
    out_down, out_wout, out_qkv, b_qk, b_v, out_gains = call(
        functools.partial(place_rest, ff_rows // 4, qk, v),
        [meta],
        [down, down_y, down_c, down_yc, rest, rest_y, rest_far],
        [
            sds((ff_rows, width), F32),
            sds((d_rows, width), F32),
            sds((d_rows, qkv_w), F32),
            sds((1, qk), F32),
            sds((1, v), F32),
            sds((2, d_rows), F32),
        ],
        3e9,
        [(d_rows + 8, 1024)],
        16,
    )
    return (
        block_out,
        hidden_grad,
        out_qkv,
        b_qk.reshape(qk),
        b_v.reshape(v),
        out_wout,
        out_gate,
        out_down,
        out_gains,
    )


def solution(mesh):
    n_fsdp, n_seq = mesh.shape["fsdp"], mesh.shape["seq"]
    in_specs = (
        P(None, "fsdp", "seq", None),
        P("fsdp", None),
        P("fsdp"),
        P("fsdp", None),
        P("fsdp", None),
        P("fsdp", None),
        P(None, "fsdp"),
        P(None, "fsdp", "seq"),
        P(),
        P(None, "fsdp", "seq", None),
    )
    out_specs = (
        P(None, "fsdp", "seq", None),
        P(None, "fsdp", "seq", None),
        P("fsdp", None),
        P("fsdp"),
        P("fsdp"),
        P("fsdp", None),
        P("fsdp", None),
        P("fsdp", None),
        P(None, "fsdp"),
    )

    def local(*args):
        body = on_device_tiled if (n_fsdp, n_seq) == (8, 4) else on_device
        return body(*args, n_fsdp=n_fsdp, n_seq=n_seq)

    return jax.shard_map(local, mesh=mesh, in_specs=in_specs, out_specs=out_specs, check_vma=False)
```

```python
import functools

import jax
import jax.numpy as jnp
import numpy as np
from jax import lax
from jax.experimental import pallas as pl
from jax.experimental.pallas import tpu as pltpu
from jax.sharding import PartitionSpec as P

HEADS = 9
KV_HEADS = 3
HEAD_DIM = 64
GROUP = HEADS // KV_HEADS
QW = HEADS * HEAD_DIM
KW = KV_HEADS * HEAD_DIM
EPS = 1e-05
ROPE_BASE = 100000.0
MASKED = -1000000000.0
BF = jnp.bfloat16
F32 = jnp.float32


def dot(a, b, ca, cb):
    return lax.dot_general(a, b, (((ca,), (cb,)), ((), ())), preferred_element_type=F32)


def rotary(values, cosine, sine):
    half = values.shape[-1] // 2
    a, b = values[..., :half], values[..., half:]
    return jnp.concatenate([a * cosine - b * sine, b * cosine + a * sine], axis=-1)


def norm_parts(values):
    factor = lax.rsqrt(jnp.mean(values * values, axis=-1, keepdims=True) + EPS)
    return factor, values * factor


def norm_back(grad_in, gain, factor, normed):
    scaled = grad_in * gain
    return factor * (scaled - normed * jnp.mean(scaled * normed, axis=-1, keepdims=True))


def whole(*shape_dtypes):
    return [pl.BlockSpec(memory_space=pltpu.VMEM) for _ in shape_dtypes]


def call(kernel, scalars, arrays, outs, flops, scratch=(), mib=52, fetched=(), landing=()):
    specs = [pl.BlockSpec(memory_space=pltpu.SMEM)] * len(scalars) + whole(*arrays)
    specs += [pl.BlockSpec(memory_space=pltpu.HBM)] * len(fetched)
    arrays = [*arrays, *fetched]
    moved = sum(a.size * a.dtype.itemsize for a in arrays) + sum(
        int(np.prod(o.shape)) * o.dtype.itemsize for o in outs
    )
    return pl.pallas_call(
        kernel,
        out_shape=outs,
        in_specs=specs,
        out_specs=whole(*outs),
        scratch_shapes=[
            *[pltpu.VMEM(shape, F32) for shape in scratch],
            *[pltpu.VMEM(shape, BF) for shape in landing],
            *([pltpu.SemaphoreType.DMA((len(fetched),))] if fetched else []),
        ],
        compiler_params=pltpu.CompilerParams(vmem_limit_bytes=mib * 1024 * 1024),
        cost_estimate=pl.CostEstimate(flops=int(flops), bytes_accessed=moved, transcendentals=0),
    )(*scalars, *arrays)


def sds(shape, dtype):
    return jax.ShapeDtypeStruct(shape, dtype)


def turn(x, cosine, sine):
    tiles = []
    low = lax.broadcasted_iota(jnp.int32, (1, 128), 1) % HEAD_DIM < HEAD_DIM // 2
    for t in range(x.shape[1] // 128):
        part = x[:, 128 * t : 128 * t + 128]
        other = jnp.where(low, pltpu.roll(part, 96, 1), pltpu.roll(part, 32, 1))
        tiles.append(part * cosine + other * sine)
    return tiles


def turn_kv(x, cosine, sine):
    lane = lax.broadcasted_iota(jnp.int32, (1, 128), 1)
    first, second = turn(x[:, :256], cosine, sine)
    second = jnp.where(lane < KW - 128, second, x[:, 128:256])
    return jnp.concatenate([first, second, x[:, 256:]], axis=1)


def tables(seq, order, cos_ref, sin_ref):
    cosine = jnp.concatenate([cos_ref[seq ^ o] for o in order], axis=0)
    sine = jnp.concatenate([sin_ref[seq ^ o] for o in order], axis=0)
    return cosine, sine


def heads_to_rows(x, g):
    return jnp.concatenate(
        [x[:, HEAD_DIM * h : HEAD_DIM * (h + 1)] for h in range(GROUP * g, GROUP * (g + 1))], axis=0
    )


def rows_to_heads(parts, length):
    return jnp.concatenate(
        [p[length * r : length * (r + 1)] for p in parts for r in range(GROUP)], axis=1
    )


def attention_forward(order, length, seq_ref, blocks, wq, wkv, bq, bkv, gain, cos, sin, mask,
                      att_o, q_o, k_o, v_o):
    seq = seq_ref[0]
    cosine, sine = tables(seq, order, cos, sin)
    width = gain.shape[1]
    for b in range(blocks.shape[1] // length):
        x = blocks[:, b * length : (b + 1) * length, :width].astype(F32)
        x = x.reshape(len(order) * length, width)
        first = (norm_parts(x)[1] * gain[...]).astype(BF)
        kv = dot(first, wkv[...], 1, 0) + bkv[...]
        q = dot(first[:length], wq[...], 1, 0) + bq[...]
        q = jnp.concatenate(turn(q, cosine[:length], sine[:length]), axis=1).astype(BF)
        q = q * jnp.asarray(HEAD_DIM ** (-0.5), BF)
        kv = turn_kv(kv, cosine, sine).astype(BF)
        allowed = jnp.concatenate([mask[b]] * GROUP, axis=0) > 0.0
        parts = []
        for g in range(KV_HEADS):
            qg = heads_to_rows(q, g)
            kg = kv[:, HEAD_DIM * g : HEAD_DIM * (g + 1)]
            vg = kv[:, KW + HEAD_DIM * g : KW + HEAD_DIM * (g + 1)]
            q_o[b, g] = qg
            k_o[b, g] = kg
            v_o[b, g] = vg
            scores = jnp.where(allowed, dot(qg, kg, 1, 1), MASKED)
            top = jnp.max(scores, axis=-1, keepdims=True)
            e = jnp.exp(scores - top)
            total = jnp.sum(e, axis=-1, keepdims=True)
            probs = (e * (1.0 / total)).astype(BF)
            parts.append(dot(probs, vg, 1, 0))
        att_o[b * length : (b + 1) * length, :] = rows_to_heads(parts, length).astype(BF)


def feed_forward(attended, source, wo, wgu, wd, gain, cot, weight,
                 out_o, down_o, gu_o, mid_o, wout_o, attg_o, gain_o):
    units = wd.shape[0]
    step = units // 3
    att = attended[...]
    middle = source[...].astype(F32) + dot(att, wo[...], 1, 0)
    scale_two, normed = norm_parts(middle)
    g2 = gain[...]
    second = (normed * g2).astype(BF)
    out_grad = cot[...].astype(F32) * weight[...]
    feed_grad = out_grad.astype(BF)
    feed = None
    back = None
    for j in range(0, units, step):
        wg = wgu[:, j : j + step]
        wu = wgu[:, units + j : units + j + step]
        wdj = wd[j : j + step, :]
        gate = dot(second, wg, 1, 0)
        up = dot(second, wu, 1, 0)
        sig = jax.nn.sigmoid(gate)
        act = gate * sig
        product = (act * up).astype(BF)
        part = dot(product, wdj, 1, 0)
        feed = part if feed is None else feed + part
        down_o[j : j + step, :] = dot(product, feed_grad, 0, 0).astype(BF)
        pgrad = dot(feed_grad, wdj, 1, 1)
        ggrad = (pgrad * up * (sig * (1.0 + gate * (1.0 - sig)))).astype(BF)
        ugrad = (pgrad * act).astype(BF)
        gu_o[:, j : j + step] = dot(second, ggrad, 0, 0).astype(BF)
        gu_o[:, units + j : units + j + step] = dot(second, ugrad, 0, 0).astype(BF)
        part = dot(ggrad, wg, 1, 1) + dot(ugrad, wu, 1, 1)
        back = part if back is None else back + part
    out_o[...] = (middle + feed).astype(BF)
    gain_o[...] = jnp.sum(back * normed, axis=0, keepdims=True)
    middle_grad = out_grad + norm_back(back, g2, scale_two, normed)
    mid_o[...] = middle_grad
    branch = middle_grad.astype(BF)
    wout_o[...] = dot(att, branch, 0, 0).astype(BF)
    attg_o[...] = dot(branch, wo[...], 1, 1).astype(BF)


def attention_backward(order, length, seq_ref, blocks, wq, wkv, gain, cos, sin, mask, q_i, k_i, v_i,
                       attg, dq_o, dkv_o, wgrad_o, bias_o, gain_o):
    seq = seq_ref[0]
    cosine, sine = tables(seq, order, cos, sin)
    width = gain.shape[1]
    q_wgrad = kv_wgrad = bias_q = bias_kv = gain_sum = None
    for b in range(blocks.shape[1] // length):
        x = blocks[:, b * length : (b + 1) * length, :width].astype(F32)
        x = x.reshape(len(order) * length, width)
        normed = norm_parts(x)[1]
        first = (normed * gain[...]).astype(BF)
        allowed = jnp.concatenate([mask[b]] * GROUP, axis=0) > 0.0
        ag = attg[b * length : (b + 1) * length, :]
        dqs, dks, dvs = [], [], []
        for g in range(KV_HEADS):
            qg, kg, vg = q_i[b, g], k_i[b, g], v_i[b, g]
            agg = heads_to_rows(ag, g)
            scores = jnp.where(allowed, dot(qg, kg, 1, 1), MASKED)
            e = jnp.exp(scores - jnp.max(scores, axis=-1, keepdims=True))
            p = e * (1.0 / jnp.sum(e, axis=-1, keepdims=True))
            dvs.append(dot(p.astype(BF), agg, 0, 0))
            pg = dot(agg, vg, 1, 1)
            inner = jnp.sum(p * pg, axis=-1, keepdims=True)
            ds = (p * (pg - inner)).astype(BF)
            dqs.append(dot(ds, kg, 1, 0) * HEAD_DIM ** (-0.5))
            dks.append(dot(ds, qg, 0, 0))
        dq = rows_to_heads(dqs, length)
        dq = jnp.concatenate([dq, jnp.zeros((length, 64), F32)], axis=1)
        dq = jnp.concatenate(turn(dq, cosine[:length], -sine[:length]), axis=1).astype(BF)
        dkv = jnp.concatenate(dks + dvs, axis=1)
        dkv = turn_kv(dkv, cosine, -sine).astype(BF)
        dq_o[b * length : (b + 1) * length, :] = dq
        for r in range(len(order)):
            dkv_o[r, b * length : (b + 1) * length, :] = dkv[r * length : (r + 1) * length, :]
        wq_part = dot(first[:length], dq, 0, 0)
        wkv_part = dot(first, dkv, 0, 0)
        bq_part = jnp.sum(dq.astype(F32), axis=0, keepdims=True)
        bkv_part = jnp.sum(dkv.astype(F32), axis=0, keepdims=True)
        e_kv = dot(dkv, wkv[...], 1, 1) * normed
        e_q = dot(dq[:, :QW], wq[:, :QW], 1, 1) * normed[:length]
        g_part = jnp.sum(e_kv, axis=0, keepdims=True) + jnp.sum(e_q, axis=0, keepdims=True)
        if q_wgrad is None:
            q_wgrad, kv_wgrad, bias_q, bias_kv, gain_sum = wq_part, wkv_part, bq_part, bkv_part, g_part
        else:
            q_wgrad, kv_wgrad = q_wgrad + wq_part, kv_wgrad + wkv_part
            bias_q, bias_kv, gain_sum = bias_q + bq_part, bias_kv + bkv_part, gain_sum + g_part
    wgrad_o[...] = jnp.concatenate([q_wgrad[:, :QW], kv_wgrad], axis=1).astype(BF)
    bias_o[...] = jnp.concatenate([bias_q[:, :QW], bias_kv], axis=1)
    gain_o[...] = gain_sum


def input_gradient(dq, own, a, b, c, source, mid, wq, wkv, gain, out_o):
    kv = own[...].astype(F32) + a[...].astype(F32) + b[...].astype(F32) + c[...].astype(F32)
    first_grad = dot(dq[:, :QW], wq[:, :QW], 1, 1) + dot(kv.astype(BF), wkv[...], 1, 1)
    scale_one, normed = norm_parts(source[...].astype(F32))
    out_o[...] = mid[...] + norm_back(first_grad, gain[...], scale_one, normed)

def chosen(flag, a, b):
    return jnp.where(flag != 0, b, a)


class Blocks:
    def __init__(self, *refs):
        self.refs = refs
        self.shape = (len(refs),) + refs[0].shape

    def __getitem__(self, key):
        return jnp.stack([ref[key[1:]] for ref in self.refs])


def cut_qkv(core_bit, meta, w_hbm, bias_hbm, gains_hbm, out_o, w, bias, gains, all_s, sems):
    pairs = ((w_hbm, w), (bias_hbm, bias), (gains_hbm, gains))
    copies = [pltpu.make_async_copy(a, b, sems.at[i]) for i, (a, b) in enumerate(pairs)]
    for copy in copies:
        copy.start()
    for copy in copies:
        copy.wait()
    rows = w.shape[0]
    n = bias.shape[1]
    all_s[:rows, :] = w[...].astype(F32)
    all_s[rows:, :] = jnp.zeros((8, w.shape[1]), F32)
    all_s[rows : rows + 1, :n] = bias[...].astype(F32)
    for i in range(2):
        all_s[rows : rows + 1, n + rows * i : n + rows * (i + 1)] = gains[i : i + 1, :].astype(F32)
    half = out_o.shape[0]
    at = pl.multiple_of((meta[0] & core_bit) * half, 8)
    out_o[...] = all_s[pl.ds(at, half), :].astype(BF)


def first_forward(order, length, d_rows, n_bias, meta, b0, b1, b2, b3, a00, a10, a01, a11, cos, sin, mask,
                  att_o, q_o, k_o, v_o, w_o, gain_o, w_s, b_s):
    blocks = Blocks(b0, b1, b2, b3)
    core, x = meta[0] & 1, meta[1] & 1
    cut = a00.shape[2]
    for x_rel, c_rel, piece in ((0, 0, a00), (1, 0, a10), (0, 1, a01), (1, 1, a11)):
        for z0 in range(2):
            for z1 in range(2):
                at = (z1 * 4 + z0 * 2 + (x ^ x_rel)) * 2 * cut + (core ^ c_rel) * cut
                w_s[pl.ds(pl.multiple_of(at, 8), cut), :] = piece[z0, z1].astype(F32)
    n_f = w_s.shape[0] // (2 * cut)
    starts = [2 * cut * f for f in range(n_f)]
    w_o[...] = jnp.concatenate([w_s[at : at + d_rows, :] for at in starts], axis=0).astype(BF)
    lines = [w_s[at + d_rows : at + d_rows + 1, :] for at in starts]
    b_s[...] = jnp.concatenate([line[:, :n_bias] for line in lines], axis=1)
    for i in range(2):
        at = n_bias + d_rows * i
        gain_o[i : i + 1, :] = jnp.concatenate([line[:, at : at + d_rows] for line in lines], axis=1)
    wide = QW + 64
    attention_forward(order, length, meta, blocks, w_o[:, :wide], w_o[:, QW:], b_s[:, :wide], b_s[:, QW:],
                      gain_o[0:1, :], cos, sin, mask, att_o, q_o, k_o, v_o)


def turned(out, value):
    length = out.shape[2]
    for b in range(out.shape[0]):
        out[b] = value[length * b : length * (b + 1)].T.astype(out.dtype)


def rel(meta, f):
    r = f ^ meta[1]
    return r & 1, (r >> 1) & 1, (r >> 2) & 1


def fetch_pieces(meta, refs, b_s, g_s, sems):
    core, y, x, z0 = meta[0] & 1, (meta[0] >> 1) & 1, meta[1] & 1, (meta[1] >> 1) & 1
    copies = []
    for i in range(8):
        at = (z0 ^ (i >> 2), x ^ ((i >> 1) & 1), core ^ (i & 1))
        copies.append(pltpu.make_async_copy(refs[i], b_s.at[at], sems.at[i]))
    for i in range(8):
        at = (y ^ ((i >> 1) & 1), core ^ (i & 1), x ^ (i >> 2))
        copies.append(pltpu.make_async_copy(refs[8 + i], g_s.at[at], sems.at[8 + i]))
    for copy in copies:
        copy.start()
    return copies


def feed_forward_pieces(d_rows, ff_rows, meta, attended, source, gains, cot, weight, *refs):
    out_o, ak_o, ag_o, bk_o, bg_o, dk_o, dg_o, mid_o, attg_o, gain_o, down_s, wout_s, b_s, g_s, sems = refs[16:]
    copies = fetch_pieces(meta, refs, b_s, g_s, sems)
    core, y = meta[0] & 1, (meta[0] >> 1) & 1
    part_d = ff_rows // 4
    part_o = d_rows // 3
    cut = b_s.shape[4] - ff_rows // 2
    half = g_s.shape[-1] // 2
    for copy in copies[:8]:
        copy.wait()
    wo = []
    for f in range(8):
        for c in range(2):
            rows = b_s[(f >> 1) & 1, f & 1, c, f >> 2, ff_rows // 2 :, :].astype(F32)
            wo.append(rows if c == 0 else rows[: d_rows - cut])
    wo = jnp.concatenate(wo, axis=0).astype(BF)
    att = attended[...]
    middle = source[...].astype(F32) + dot(att, wo, 1, 0)
    scale_two, normed = norm_parts(middle)
    g2 = gains[1:2, :]
    second = (normed * g2).astype(BF)
    out_grad = cot[...].astype(F32) * weight[...]
    feed_grad = out_grad.astype(BF)
    for copy in copies[8:]:
        copy.wait()
    feed = back = None
    for c_rel in (1, 0):
        h = core ^ c_rel
        weights = []
        for yy in range(2):
            rows = [g_s[yy, h, f & 1, (f >> 1) & 1, f >> 2].astype(F32) for f in range(8)]
            weights.append(jnp.concatenate(rows, axis=0).astype(BF))
        wg, wu = weights
        wd = [b_s[i >> 1, i & 1, c, h, : ff_rows // 2, :] for i in range(4) for c in range(2)]
        wd = jnp.concatenate(wd, axis=0)
        gate = dot(second, wg, 1, 0)
        up = dot(second, wu, 1, 0)
        sig = jax.nn.sigmoid(gate)
        act = gate * sig
        product = (act * up).astype(BF)
        part = dot(product, wd, 1, 0)
        feed = part if feed is None else feed + part
        down_s[...] = dot(product, feed_grad, 0, 0)
        pgrad = dot(feed_grad, wd, 1, 1)
        ggrad = (pgrad * up * (sig * (1.0 + gate * (1.0 - sig)))).astype(BF)
        ugrad = (pgrad * act).astype(BF)
        part = dot(ggrad, wg, 1, 1) + dot(ugrad, wu, 1, 1)
        back = part if back is None else back + part
        for i in range(4):
            x, z0, z1 = rel(meta, 4 * h + i)
            for yy in range(2):
                for c_to, to in ((0, dk_o), (1, dg_o)):
                    at = pl.multiple_of(i * ff_rows + (yy * 2 + (core ^ c_to)) * part_d, 16)
                    to[y ^ yy, x, z0, z1, :part_d, :] = down_s[pl.ds(at, part_d), :].astype(BF)
        to_a, to_b = (ag_o, bg_o) if c_rel else (ak_o, bk_o)
        for yy, grad in ((0, ggrad), (1, ugrad)):
            wgrad = dot(second, grad, 0, 0)
            for f in range(8):
                x, z0, z1 = rel(meta, f)
                block = wgrad[d_rows * f : d_rows * (f + 1), :].astype(BF)
                to_a[x, z0, z1, yy] = block[:, :half]
                to_b[z0, z1, x, yy] = block[:, half:]
    turned(out_o, middle + feed)
    gain_o[...] = jnp.sum(back * normed, axis=0, keepdims=True)
    middle_grad = out_grad + norm_back(back, g2, scale_two, normed)
    mid_o[...] = middle_grad
    branch = middle_grad.astype(BF)
    attg_o[...] = dot(branch, wo, 1, 1).astype(BF)
    wout = dot(att, branch, 0, 0)
    for f in range(8):
        wout_s[f, :d_rows, :] = wout[d_rows * f : d_rows * (f + 1), :]
        wout_s[f, d_rows:, :] = jnp.zeros((part_o, wout.shape[1]), F32)
    for f in range(8):
        x, z0, z1 = rel(meta, f)
        for yy in range(2):
            for c_to, to in ((0, dk_o), (1, dg_o)):
                at = pl.multiple_of((yy * 2 + (core ^ c_to)) * part_o, 8)
                to[y ^ yy, x, z0, z1, part_d:, :] = wout_s[f, pl.ds(at, part_o), :].astype(BF)


def attention_backward_pieces(order, length, d_rows, meta, b0, b1, b2, b3, w, gains, cos, sin, mask, q_i, k_i, v_i,
                              attg, gain_two, dq_o, dk_o, dg_o, rk_o, rg_o, w_s, bias_s, gain_s, small_s):
    blocks = Blocks(b0, b1, b2, b3)
    half = len(order) // 2

    class Pieces:
        def __setitem__(self, key, value):
            ref = dk_o if key[0] < half else dg_o
            ref[(key[0] % half,) + key[1:]] = value

    class Wgrad:
        def __setitem__(self, key, value):
            w_s[:, : 2 * KW] = value[:, QW:].astype(F32)
            w_s[:, 2 * KW : 2 * KW + QW] = value[:, :QW].astype(F32)
            w_s[:, 2 * KW + QW :] = jnp.zeros((value.shape[0], 64), F32)

    wide = QW + 64
    attention_backward(order, length, meta, blocks, w[:, :wide], w[:, QW:], gains[0:1, :], cos, sin, mask,
                       q_i, k_i, v_i, attg, dq_o, Pieces(), Wgrad(), bias_s, gain_s)
    n_f = small_s.shape[0]
    qk, v = (QW + KW) // n_f, KW // n_f
    bias, g1, g2 = bias_s[...], gain_s[...], gain_two[...]
    for f in range(n_f):
        line = jnp.concatenate(
            [
                bias[:, qk * f : qk * (f + 1)],
                bias[:, QW + KW + v * f : QW + KW + v * (f + 1)],
                g1[:, d_rows * f : d_rows * (f + 1)],
                jnp.zeros((1, 256 - qk - v - d_rows), F32),
                g2[:, d_rows * f : d_rows * (f + 1)],
                jnp.zeros((1, 768 - d_rows), F32),
            ],
            axis=1,
        )
        small_s[f] = jnp.broadcast_to(line, (8, 1024))
    core, y = meta[0] & 1, (meta[0] >> 1) & 1
    for f in range(n_f):
        x, z0, z1 = rel(meta, f)
        for yy in range(2):
            for c_to, to in ((0, rk_o), (1, rg_o)):
                at = pl.multiple_of((yy * 2 + (core ^ c_to)) * 256, 256)
                block = [w_s[d_rows * f : d_rows * (f + 1), pl.ds(at, 256)], small_s[f, :, pl.ds(at, 256)]]
                to[y ^ yy, x, z0, z1] = jnp.concatenate(block, axis=0).astype(BF)


def input_gradient_two(dq, own, other, source, mid, w, gains, out_o):
    kv = (own[...].astype(F32) + other[...].astype(F32)).astype(BF)
    first_grad = dot(dq[:, :QW], w[:, :QW], 1, 1) + dot(kv, w[:, QW:], 1, 1)
    scale_one, normed = norm_parts(source[...].astype(F32))
    turned(out_o, mid[...] + norm_back(first_grad, gains[0:1, :], scale_one, normed))


def place_gate(meta, near, far, out_o, parts=1, part=0):
    core = meta[0] & 1
    n = near.shape[2]
    for pieces, c_rel in ((near, 0), (far, 1)):
        for yy in range(2):
            at = pl.multiple_of(((yy * 2 + (core ^ c_rel)) * parts + part) * n, 128)
            out_o[:, pl.ds(at, n)] = pieces[yy].astype(F32)


def place_down(part_d, meta, p00, p10, p01, p11, out_o, wout_o):
    seq = meta[0]
    part_o = p00.shape[0] - part_d
    for piece, o in ((p00[...], 0), (p10[...], 2), (p01[...], 1), (p11[...], 3)):
        piece = piece.astype(F32)
        to = seq ^ o
        out_o[pl.ds(pl.multiple_of(to * part_d, 16), part_d), :] = piece[:part_d]

        @pl.when(to < 3)
        def _():
            wout_o[pl.ds(pl.multiple_of(to * part_o, 8), part_o), :] = piece[part_d:]


def place_qkv(qk, v, meta, p00, p10, p01, p11, w_o, bqk_o, bv_o, gains_o, all_s):
    n = p00.shape[1]
    for piece, o in ((p00, 0), (p10, 2), (p01, 1), (p11, 3)):
        all_s[:, pl.ds(pl.multiple_of((meta[0] ^ o) * n, 128), n)] = piece[...].astype(F32)
    d_rows = w_o.shape[0]
    w_o[:, :QW] = all_s[:d_rows, 2 * KW : 2 * KW + QW]
    w_o[:, QW:] = all_s[:d_rows, : 2 * KW]
    line = all_s[d_rows : d_rows + 1, :]
    bqk_o[...] = line[:, :qk]
    bv_o[...] = line[:, qk : qk + v]
    gains_o[0:1, :] = line[:, qk + v : qk + v + d_rows]
    gains_o[1:2, :] = line[:, 256 : 256 + d_rows]


def place_all(part_d, qk, v, meta, a_near, a_far, b_near, b_far, d0, d1, d2, d3, r0, r1, r2, r3,
              gate_o, down_o, wout_o, w_o, bqk_o, bv_o, gains_o, all_s):
    place_gate(meta, a_near, a_far, gate_o, 2, 0)
    place_gate(meta, b_near, b_far, gate_o, 2, 1)
    place_down(part_d, meta, d0, d1, d2, d3, down_o, wout_o)
    place_qkv(qk, v, meta, r0, r1, r2, r3, w_o, bqk_o, bv_o, gains_o, all_s)


class Net:
    def __init__(self, n_fsdp, n_seq):
        self.n_fsdp, self.n_seq = n_fsdp, n_seq
        self.total = n_fsdp * n_seq
        f, s = lax.axis_index("fsdp"), lax.axis_index("seq")
        self.index = f * n_seq + s
        self.seq_bits = [1 << b for b in range(n_seq.bit_length() - 1)]
        self.fsdp_bits = [n_seq << b for b in range(n_fsdp.bit_length() - 1)]

    def swap(self, value, mask):
        pairs = [(i, i ^ mask) for i in range(self.total)]
        return lax.ppermute(value, ("fsdp", "seq"), pairs)

    def bit(self, mask):
        return (self.index & mask) != 0

    def both(self, mine, mask, axis, other=None):
        other = self.swap(mine, mask) if other is None else other
        high = self.bit(mask)
        return jnp.stack([jnp.where(high, other, mine), jnp.where(high, mine, other)], axis=axis)

    def half(self, value, mask, axis):
        return lax.dynamic_index_in_dim(
            value, self.bit(mask).astype(jnp.int32), axis, keepdims=False
        )

    def add_half(self, value, mask, axis):
        mine = self.bit(mask).astype(jnp.int32)
        keep = lax.dynamic_index_in_dim(value, mine, axis, keepdims=False)
        give = lax.dynamic_index_in_dim(value, 1 - mine, axis, keepdims=False)
        got = self.swap(give, mask)
        return (keep.astype(F32) + got.astype(F32)).astype(value.dtype)

    def gather_fsdp(self, value):
        for step, mask in enumerate(reversed(self.fsdp_bits)):
            value = self.both(value, mask, step)
        return value

    def scatter_fsdp(self, value, first_axis=0):
        count = len(self.fsdp_bits)
        for step, mask in enumerate(self.fsdp_bits):
            value = self.add_half(value, mask, first_axis + count - 1 - step)
        return value


def on_device(
    hidden, w_qkv, b_qkv, w_out, w_gate_up, w_down, norm_gains, segment_ids, token_counts, cotangent,
    n_fsdp, n_seq,
):
    net = Net(n_fsdp, n_seq)
    micro, batch, length, width = hidden.shape
    full_length = length * n_seq
    tokens_micro = batch * n_fsdp * full_length
    scale = HEAD_DIM ** (-0.5)
    rows = micro * batch * length
    d_rows = w_qkv.shape[0]
    ff_rows = w_down.shape[0]
    units = w_gate_up.shape[1] // 2
    qkv_w = w_qkv.shape[1]
    core = net.seq_bits[0]
    f_lead = (2,) * len(net.fsdp_bits)

    ids = segment_ids.reshape(rows, 1).astype(BF)
    block = jnp.concatenate(
        [hidden.reshape(rows, width), jnp.broadcast_to(ids, (rows, 64))], axis=1
    )
    blocks = block[None]
    for mask in reversed(net.seq_bits):
        blocks = jnp.concatenate([blocks, net.swap(blocks, mask)], axis=0)
    order = [0]
    for mask in reversed(net.seq_bits):
        order = order + [o ^ mask for o in order]
    seq_index = lax.axis_index("seq")
    block_ids = [seq_index ^ o for o in order]

    pad_rows = -(d_rows + 1) % 16 + 1
    extra = jnp.zeros((pad_rows, qkv_w), BF)
    small = jnp.concatenate([b_qkv, norm_gains.reshape(-1)])
    extra = extra.at[0, : small.shape[0]].set(small)
    shard_a = jnp.concatenate([w_qkv, extra], axis=0).reshape(2, -1, qkv_w)
    got_a = net.gather_fsdp(net.half(shard_a, core, 0))
    full_a = net.both(got_a, core, len(f_lead)).reshape(n_fsdp, d_rows + pad_rows, qkv_w)
    wf_qkv = full_a[:, :d_rows].reshape(n_fsdp * d_rows, qkv_w)
    smalls = full_a[:, d_rows]
    n_bias = b_qkv.shape[0]
    bias = smalls[:, :n_bias].reshape(-1).astype(F32)
    gains = smalls[:, n_bias : n_bias + 2 * d_rows].reshape(n_fsdp, 2, d_rows).astype(F32)
    gain_one = gains[:, 0].reshape(-1)
    gain_two = gains[:, 1].reshape(-1)

    pad_b = -(d_rows + ff_rows) % 16
    shard_b = jnp.concatenate([w_out, w_down, jnp.zeros((pad_b, width), BF)], axis=0)
    shard_b = shard_b.reshape(2, -1, width)
    got_b = net.gather_fsdp(net.half(shard_b, core, 0))

    parts = n_seq
    shard_c = w_gate_up.reshape(d_rows, parts, -1)
    got_c = net.gather_fsdp(lax.dynamic_index_in_dim(shard_c, seq_index, 1, keepdims=False))
    full_b = net.both(got_b, core, len(f_lead)).reshape(n_fsdp, -1, width)
    wf_out = full_b[:, :d_rows].reshape(n_fsdp * d_rows, width)
    wf_down = full_b[:, d_rows : d_rows + ff_rows].reshape(n_fsdp * ff_rows, width)
    got_c = got_c.reshape(n_fsdp * d_rows, -1)
    for mask in reversed(net.seq_bits):
        got_c = net.both(got_c, mask, got_c.ndim - 1)
    wf_gate_up = got_c.reshape(n_fsdp * d_rows, 2 * units)

    places = np.arange(full_length, dtype=np.float32)
    speeds = np.power(ROPE_BASE, -2.0 * np.arange(HEAD_DIM // 2, dtype=np.float32) / HEAD_DIM)
    angles = places[:, None] * speeds.astype(np.float32)[None, :]
    cos_t = np.tile(np.cos(angles), (1, 4)).reshape(n_seq, length, 128)
    sin_t = np.concatenate([-np.sin(angles), np.sin(angles)] * 2, axis=1).reshape(n_seq, length, 128)
    cos_t, sin_t = jnp.asarray(cos_t, F32), jnp.asarray(sin_t, F32)
    seqs = micro * batch
    seg_all = blocks[..., width].reshape(n_seq, seqs, length).transpose(1, 0, 2)
    own_places = seq_index * length + jnp.arange(length, dtype=jnp.int32)
    key_places = jnp.stack(block_ids)[:, None] * length + jnp.arange(length, dtype=jnp.int32)
    allowed = (seg_all[:, 0, :, None] == seg_all.reshape(seqs, 1, -1)) & (
        own_places[None, :, None] >= key_places.reshape(1, 1, -1)
    )
    allowed = allowed.astype(F32)
    seq_scalar = seq_index.astype(jnp.int32).reshape(1)
    wq, wkv = wf_qkv[:, : QW + 64], wf_qkv[:, QW:]
    gain_one, gain_two = gain_one[None], gain_two[None]
    source = hidden.reshape(rows, width)
    n_all = n_seq * rows
    attended, q_s, k_s, v_s = call(
        functools.partial(attention_forward, order, length),
        [seq_scalar],
        [blocks, wq, wkv, bias[None, : QW + 64], bias[None, QW:], gain_one, cos_t, sin_t, allowed],
        [
            sds((rows, QW), BF),
            sds((seqs, KV_HEADS, GROUP * length, HEAD_DIM), BF),
            sds((seqs, KV_HEADS, full_length, HEAD_DIM), BF),
            sds((seqs, KV_HEADS, full_length, HEAD_DIM), BF),
        ],
        2 * n_all * width * 2 * KW + 2 * rows * width * QW + 4 * rows * full_length * QW,
    )

    weight = tokens_micro / token_counts.astype(F32)
    weight = jnp.repeat(weight, batch * length)[:, None]
    block_out, down_grad, gate_up_wgrad, middle_grad, out_wgrad, attended_grad, gain_two_grad = call(
        feed_forward,
        [],
        [attended, source, wf_out, wf_gate_up, wf_down, gain_two, cotangent.reshape(rows, width), weight],
        [
            sds((rows, width), BF),
            sds((units, width), BF),
            sds((width, 2 * units), BF),
            sds((rows, width), F32),
            sds((QW, width), BF),
            sds((rows, QW), BF),
            sds((1, width), F32),
        ],
        6 * rows * width * 3 * units + 6 * rows * width * QW,
    )
    block_out = block_out.reshape(hidden.shape)

    def seq_axes(value, axis, masks):
        for mask in masks:
            value = net.add_half(value, mask, axis)
        return value

    quarter = (2,) * len(net.seq_bits)
    n_f = len(f_lead)
    red_down = down_grad.reshape(f_lead + quarter + (ff_rows // n_seq, width))
    for step, mask in enumerate(net.seq_bits):
        red_down = net.add_half(red_down, mask, n_f + len(quarter) - 1 - step)
    red_down = net.scatter_fsdp(red_down)

    red_gate = gate_up_wgrad.reshape(f_lead + (d_rows,) + quarter + (2 * units // n_seq,))
    red_gate = net.add_half(red_gate, core, n_f + len(quarter))
    red_gate = net.add_half(red_gate, net.fsdp_bits[0], n_f - 1)
    for step, mask in enumerate(net.seq_bits[1:]):
        red_gate = net.add_half(red_gate, mask, n_f - 1 + len(quarter) - 1 - step)
    for step, mask in enumerate(net.fsdp_bits[1:]):
        red_gate = net.add_half(red_gate, mask, n_f - 2 - step)

    dq, dkv, qkv_wgrad, bias_grad, gain_one_grad = call(
        functools.partial(attention_backward, order, length),
        [seq_scalar],
        [blocks, wq, wkv, gain_one, cos_t, sin_t, allowed, q_s, k_s, v_s, attended_grad],
        [
            sds((rows, QW + 64), BF),
            sds((n_seq, rows, 2 * KW), BF),
            sds((width, qkv_w), BF),
            sds((1, qkv_w), F32),
            sds((1, width), F32),
        ],
        4 * n_all * width * 2 * KW + 4 * rows * width * QW + 10 * rows * full_length * QW,
    )
    kv_parts = [dkv[0]]
    for place, mask_bits in enumerate(order):
        if mask_bits:
            kv_parts.append(net.swap(dkv[place], mask_bits))
    (hidden_grad,) = call(
        input_gradient,
        [],
        [dq, *kv_parts, source, middle_grad, wq, wkv, gain_one],
        [sds((rows, width), F32)],
        2 * rows * width * qkv_w,
    )
    hidden_grad = hidden_grad.reshape(hidden.shape)
    bias_grad, gain_one_grad, gain_two_grad = bias_grad[0], gain_one_grad[0], gain_two_grad[0]

    qk_rows, v_rows = (QW + KW) // n_fsdp, KW // n_fsdp
    small_grads = jnp.concatenate(
        [
            bias_grad[: QW + KW].reshape(n_fsdp, qk_rows),
            bias_grad[QW + KW :].reshape(n_fsdp, v_rows),
            gain_one_grad.reshape(n_fsdp, d_rows),
            gain_two_grad.reshape(n_fsdp, d_rows),
        ],
        axis=1,
    ).astype(BF)
    wide = qkv_w + width
    small_pad = jnp.zeros((n_fsdp, pad_rows, wide), BF)
    small_pad = small_pad.at[:, 0, : small_grads.shape[1]].set(small_grads)
    rest = jnp.concatenate([qkv_wgrad, out_wgrad], axis=1)
    rest = jnp.concatenate([rest.reshape(n_fsdp, d_rows, wide), small_pad], axis=1)
    rest = rest.reshape(f_lead + (d_rows + pad_rows,) + quarter + (wide // n_seq,))
    for step, mask in enumerate(net.seq_bits):
        rest = net.add_half(rest, mask, n_f + 1 + len(quarter) - 1 - step)
    rest = net.scatter_fsdp(rest)

    def seq_back(value, axis):
        for step, mask in enumerate(reversed(net.seq_bits)):
            value = net.both(value, mask, axis + step)
        return value

    out_down = seq_back(red_down, 0).reshape(ff_rows, width).astype(F32)
    out_gate = seq_back(red_gate, 1).reshape(d_rows, 2 * units).astype(F32)
    out_rest = seq_back(rest, 1).reshape(d_rows + pad_rows, wide).astype(F32)
    line = out_rest[d_rows]
    edge = qk_rows + v_rows
    return (
        block_out,
        hidden_grad,
        out_rest[:d_rows, :qkv_w],
        line[:qk_rows],
        line[qk_rows:edge],
        out_rest[:d_rows, qkv_w:],
        out_gate,
        out_down,
        line[edge : edge + 2 * d_rows].reshape(2, d_rows),
    )


def after(value, *others):
    return lax.optimization_barrier((value, *others))[0]


def rope_tables(full_length, n_seq):
    places = np.arange(full_length, dtype=np.float32)
    speeds = np.power(ROPE_BASE, -2.0 * np.arange(HEAD_DIM // 2, dtype=np.float32) / HEAD_DIM)
    angles = places[:, None] * speeds.astype(np.float32)[None, :]
    cos_t = np.tile(np.cos(angles), (1, 4)).reshape(n_seq, -1, 128)
    sin_t = np.concatenate([-np.sin(angles), np.sin(angles)] * 2, axis=1).reshape(n_seq, -1, 128)
    return jnp.asarray(cos_t, F32), jnp.asarray(sin_t, F32)


def on_device_tiled(
    hidden, w_qkv, b_qkv, w_out, w_gate_up, w_down, norm_gains, segment_ids, token_counts, cotangent,
    n_fsdp, n_seq,
):
    net = Net(n_fsdp, n_seq)
    micro, batch, length, width = hidden.shape
    full_length = length * n_seq
    tokens_micro = batch * n_fsdp * full_length
    rows = micro * batch * length
    seqs = micro * batch
    d_rows, qkv_w = w_qkv.shape
    ff_rows = w_down.shape[0]
    units = w_gate_up.shape[1] // 2
    n_bias = b_qkv.shape[0]
    core, ybit = net.seq_bits
    xbit, znear, zfar = net.fsdp_bits
    order = [0, 2, 1, 3]
    seq_index = lax.axis_index("seq")
    meta = jnp.stack([seq_index, lax.axis_index("fsdp")]).astype(jnp.int32)
    source = hidden.reshape(rows, width)

    small = [w_qkv, b_qkv[None], norm_gains]
    a0 = pl.pallas_call(
        functools.partial(cut_qkv, core),
        out_shape=sds(((d_rows + 8) // 2, qkv_w), BF),
        in_specs=[pl.BlockSpec(memory_space=pltpu.SMEM)] + [pl.BlockSpec(memory_space=pltpu.HBM)] * 3,
        out_specs=pl.BlockSpec(memory_space=pltpu.VMEM),
        scratch_shapes=[
            *[pltpu.VMEM(v.shape, BF) for v in small],
            pltpu.VMEM((d_rows + 8, qkv_w), F32),
            pltpu.SemaphoreType.DMA((3,)),
        ],
        compiler_params=pltpu.CompilerParams(vmem_limit_bytes=52 * 1024 * 1024),
    )(meta, *small)
    a1 = net.both(a0, zfar, 0)

    ids = segment_ids.reshape(rows, 1).astype(BF)
    block = jnp.concatenate([source, jnp.broadcast_to(ids, (rows, 64))], axis=1)
    block = after(block, a0)
    block_y = net.swap(block, ybit)
    block_c = net.swap(block, core)

    quarter = 2 * units // n_seq
    gu0 = lax.dynamic_slice_in_dim(after(w_gate_up, a0), seq_index * quarter, quarter, axis=1)
    half_b = jnp.concatenate(
        [
            w_down.reshape(2, ff_rows // 2, width),
            jnp.concatenate([w_out, jnp.zeros((8, width), BF)], axis=0).reshape(2, -1, width),
        ],
        axis=1,
    )
    a2 = net.both(a1, znear, 0)
    a_x = net.swap(a2, xbit)
    a_c = net.swap(a2, core)
    gu1 = net.both(gu0, zfar, 0)
    gu2 = net.both(after(gu1, a2), znear, 0)
    block_yc = net.swap(block_y, core)
    a_xc = net.swap(a_x, core)
    gu_x = net.swap(gu2, xbit)
    gu_y = net.swap(gu2, ybit)
    gu_c = net.swap(gu2, core)
    b0 = net.half(after(half_b, a0), core, 0)
    b1 = net.both(b0, zfar, 0, after(net.swap(b0, zfar), a2))
    b_x = net.swap(b1, xbit)
    b_z = net.swap(after(b1, gu2), znear)
    b_c = net.swap(b1, core)
    a_xc = after(a_xc, gu2, b1)

    cos_t, sin_t = rope_tables(full_length, n_seq)
    block_ids = [seq_index ^ o for o in order]
    blocks = [block, block_y, block_c, block_yc]
    seg_all = jnp.stack([b[:, width].reshape(seqs, length) for b in blocks], axis=1)
    own_places = seq_index * length + jnp.arange(length, dtype=jnp.int32)
    key_places = jnp.stack(block_ids)[:, None] * length + jnp.arange(length, dtype=jnp.int32)
    allowed = (seg_all[:, 0, :, None] == seg_all.reshape(seqs, 1, -1)) & (
        own_places[None, :, None] >= key_places.reshape(1, 1, -1)
    )
    allowed = allowed.astype(F32)
    attended, q_s, k_s, v_s, wf, gains = call(
        functools.partial(first_forward, order, length, d_rows, n_bias),
        [meta],
        [*blocks, a2, a_x, a_c, a_xc, cos_t, sin_t, allowed],
        [
            sds((rows, QW), BF),
            sds((seqs, KV_HEADS, GROUP * length, HEAD_DIM), BF),
            sds((seqs, KV_HEADS, full_length, HEAD_DIM), BF),
            sds((seqs, KV_HEADS, full_length, HEAD_DIM), BF),
            sds((width, qkv_w), BF),
            sds((2, width), F32),
        ],
        1.2e10,
        [(n_fsdp * (d_rows + 8), qkv_w), (1, qkv_w)],
    )
    gu_y = after(gu_y, attended)
    gu_x, b_z, b_x = after(gu_x, gu_y), after(b_z, gu_y), after(b_x, gu_y)
    gu_xy = net.swap(gu_x, ybit)
    b_zx = net.swap(b_z, xbit)
    gu_yc = net.swap(gu_y, core)
    gu_xc = net.swap(gu_x, core)
    b_zc = net.swap(b_z, core)
    b_xc = net.swap(b_x, core)
    b_zxc = net.swap(b_zx, core)
    gu_xyc = net.swap(gu_xy, core)
    pieces = [b1, b_c, b_x, b_xc, b_z, b_zc, b_zx, b_zxc]
    pieces += [gu2, gu_c, gu_y, gu_yc, gu_x, gu_xc, gu_xy, gu_xyc]

    weight = tokens_micro / token_counts.astype(F32)
    weight = jnp.repeat(weight, batch * length)[:, None]
    lead = (2, 2, 2, 2)
    cot = cotangent.reshape(rows, width)
    gate_lead = lead + (d_rows, units // 4)
    block_out, a_keep, a_give, b_keep, b_give, down_keep, down_give, middle_grad, attended_grad, gain_two = call(
        functools.partial(feed_forward_pieces, d_rows, ff_rows),
        [meta],
        [attended, source, gains, cot, weight],
        [
            sds((seqs, width, length), BF),
            sds(gate_lead, BF),
            sds(gate_lead, BF),
            sds(gate_lead, BF),
            sds(gate_lead, BF),
            sds(lead + (ff_rows // 4 + d_rows // 3, width), BF),
            sds(lead + (ff_rows // 4 + d_rows // 3, width), BF),
            sds((rows, width), F32),
            sds((rows, QW), BF),
            sds((1, width), F32),
        ],
        1.4e10,
        [(units // 2, width), (n_fsdp, d_rows + d_rows // 3, width)],
        fetched=pieces,
        landing=[(2, 2, 2, 2) + b1.shape[1:], (2, 2, 2, 2, 2, d_rows, units // 2)],
    )
    block_out = block_out.reshape(micro, batch, width, length).swapaxes(2, 3)

    def add(keep, got):
        return (keep.astype(F32) + got.astype(F32)).astype(BF)

    def halves(keep, got):
        return add(keep[0], got[0]), add(keep[1], got[1])

    down_got = net.swap(down_give, core)
    a_got = net.swap(after(a_give, down_got), core)
    b_got = net.swap(after(b_give, down_got), core)
    a, a_give = halves(a_keep, a_got)
    a_got = net.swap(a_give, xbit)
    b, b_give = halves(b_keep, b_got)
    b_got = net.swap(b_give, znear)
    down, down_give = halves(down_keep, down_got)
    attended_grad = after(attended_grad, a_give, b_give, down_give)
    down_got = net.swap(down_give, ybit)

    dq, dkv_keep, dkv_give, rest_keep, rest_give = call(
        functools.partial(attention_backward_pieces, order, length, d_rows),
        [meta],
        [*blocks, wf, gains, cos_t, sin_t, allowed, q_s, k_s, v_s, attended_grad, gain_two],
        [
            sds((rows, QW + 64), BF),
            sds((2, rows, 2 * KW), BF),
            sds((2, rows, 2 * KW), BF),
            sds(lead + (d_rows + 8, 256), BF),
            sds(lead + (d_rows + 8, 256), BF),
        ],
        1.4e10,
        [(width, 1024), (1, qkv_w), (1, width), (n_fsdp, 8, 1024)],
        24,
    )
    b, b_give = halves(b, after(b_got, dq))
    a, a_give = halves(a, after(a_got, b_give))
    b_got = net.swap(b_give, zfar)
    a_got = net.swap(a_give, znear)
    rest, rest_give = halves(rest_keep, after(net.swap(rest_give, core), b_give, down_got))
    rest_got = net.swap(rest_give, ybit)
    down, down_give = halves(down, after(down_got, rest_give))
    down_got = net.swap(down_give, xbit)
    dkv, dkv_give = halves(dkv_keep, after(net.swap(dkv_give, core), down_give))
    dkv_got = net.swap(dkv_give, ybit)
    a, a_give = halves(a, after(a_got, dkv_give))
    a_got = net.swap(a_give, zfar)
    rest, rest_give = halves(rest, after(rest_got, a_give))
    rest_got = net.swap(rest_give, xbit)
    b, b_give = halves(b, after(b_got, rest_give))
    b_got = net.swap(b_give, xbit)
    down, down_give = halves(down, after(down_got, b_give))
    down_got = net.swap(down_give, znear)
    (hidden_grad,) = call(
        input_gradient_two,
        [],
        [dq, dkv, after(dkv_got, down_give), source, middle_grad, wf, gains],
        [sds((seqs, width, length), F32)],
        3e9,
        mib=16,
    )
    rest, rest_give = halves(rest, after(rest_got, hidden_grad))
    hidden_grad = hidden_grad.reshape(micro, batch, width, length).swapaxes(2, 3)
    rest_got = net.swap(rest_give, znear)
    a = add(a, after(a_got, rest_give))
    a_got = net.swap(a, ybit)
    b = add(b, after(b_got, a))
    b_got = net.swap(b, ybit)
    down, down_give = halves(down, after(down_got, b))
    down_got = net.swap(down_give, zfar)
    rest, rest_give = halves(rest, after(rest_got, down_give))
    rest_got = net.swap(rest_give, zfar)
    a = add(a, after(a_got, rest_give))
    a_far = net.swap(a, core)
    b = add(b, b_got)
    b_far = net.swap(b, core)
    down = add(down, after(down_got, a))
    down_y = net.swap(down, ybit)
    down_c = net.swap(after(down, down_y), core)
    rest = add(rest, after(rest_got, down))
    rest_y = net.swap(rest, ybit)
    rest_c = net.swap(after(rest, rest_y), core)
    down_yc = net.swap(after(down_y, rest_y), core)
    rest_yc = net.swap(rest_y, core)
    qk, v = (QW + KW) // n_fsdp, KW // n_fsdp
    out_gate, out_down, out_wout, out_qkv, b_qk, b_v, out_gains = call(
        functools.partial(place_all, ff_rows // 4, qk, v),
        [meta],
        [a, a_far, b, b_far, down, down_y, down_c, down_yc, rest, rest_y, rest_c, rest_yc],
        [
            sds((d_rows, 2 * units), F32),
            sds((ff_rows, width), F32),
            sds((d_rows, width), F32),
            sds((d_rows, qkv_w), F32),
            sds((1, qk), F32),
            sds((1, v), F32),
            sds((2, d_rows), F32),
        ],
        3e9,
        [(d_rows + 8, 1024)],
        16,
    )
    return (
        block_out,
        hidden_grad,
        out_qkv,
        b_qk.reshape(qk),
        b_v.reshape(v),
        out_wout,
        out_gate,
        out_down,
        out_gains,
    )


def solution(mesh):
    n_fsdp, n_seq = mesh.shape["fsdp"], mesh.shape["seq"]
    in_specs = (
        P(None, "fsdp", "seq", None),
        P("fsdp", None),
        P("fsdp"),
        P("fsdp", None),
        P("fsdp", None),
        P("fsdp", None),
        P(None, "fsdp"),
        P(None, "fsdp", "seq"),
        P(),
        P(None, "fsdp", "seq", None),
    )
    out_specs = (
        P(None, "fsdp", "seq", None),
        P(None, "fsdp", "seq", None),
        P("fsdp", None),
        P("fsdp"),
        P("fsdp"),
        P("fsdp", None),
        P("fsdp", None),
        P("fsdp", None),
        P(None, "fsdp"),
    )

    def local(*args):
        body = on_device_tiled if (n_fsdp, n_seq) == (8, 4) else on_device
        return body(*args, n_fsdp=n_fsdp, n_seq=n_seq)

    return jax.shard_map(local, mesh=mesh, in_specs=in_specs, out_specs=out_specs, check_vma=False)
```

```python
import functools

import jax
import jax.numpy as jnp
import numpy as np
from jax import lax
from jax.experimental import pallas as pl
from jax.experimental.pallas import tpu as pltpu
from jax.sharding import PartitionSpec as P

HEADS = 9
KV_HEADS = 3
HEAD_DIM = 64
GROUP = HEADS // KV_HEADS
QW = HEADS * HEAD_DIM
KW = KV_HEADS * HEAD_DIM
EPS = 1e-05
ROPE_BASE = 100000.0
MASKED = -1000000000.0
BF = jnp.bfloat16
F32 = jnp.float32


def dot(a, b, ca, cb):
    return lax.dot_general(a, b, (((ca,), (cb,)), ((), ())), preferred_element_type=F32)


def rotary(values, cosine, sine):
    half = values.shape[-1] // 2
    a, b = values[..., :half], values[..., half:]
    return jnp.concatenate([a * cosine - b * sine, b * cosine + a * sine], axis=-1)


def norm_parts(values):
    factor = lax.rsqrt(jnp.mean(values * values, axis=-1, keepdims=True) + EPS)
    return factor, values * factor


def norm_back(grad_in, gain, factor, normed):
    scaled = grad_in * gain
    return factor * (scaled - normed * jnp.mean(scaled * normed, axis=-1, keepdims=True))


def whole(*shape_dtypes):
    return [pl.BlockSpec(memory_space=pltpu.VMEM) for _ in shape_dtypes]


def call(kernel, scalars, arrays, outs, flops, scratch=(), mib=52, fetched=(), landing=()):
    specs = [pl.BlockSpec(memory_space=pltpu.SMEM)] * len(scalars) + whole(*arrays)
    specs += [pl.BlockSpec(memory_space=pltpu.HBM)] * len(fetched)
    arrays = [*arrays, *fetched]
    moved = sum(a.size * a.dtype.itemsize for a in arrays) + sum(
        int(np.prod(o.shape)) * o.dtype.itemsize for o in outs
    )
    return pl.pallas_call(
        kernel,
        out_shape=outs,
        in_specs=specs,
        out_specs=whole(*outs),
        scratch_shapes=[
            *[pltpu.VMEM(shape, F32) for shape in scratch],
            *[pltpu.VMEM(shape, BF) for shape in landing],
            *([pltpu.SemaphoreType.DMA((len(fetched),))] if fetched else []),
        ],
        compiler_params=pltpu.CompilerParams(vmem_limit_bytes=mib * 1024 * 1024),
        cost_estimate=pl.CostEstimate(flops=int(flops), bytes_accessed=moved, transcendentals=0),
    )(*scalars, *arrays)


def sds(shape, dtype):
    return jax.ShapeDtypeStruct(shape, dtype)


def turn(x, cosine, sine):
    tiles = []
    low = lax.broadcasted_iota(jnp.int32, (1, 128), 1) % HEAD_DIM < HEAD_DIM // 2
    for t in range(x.shape[1] // 128):
        part = x[:, 128 * t : 128 * t + 128]
        other = jnp.where(low, pltpu.roll(part, 96, 1), pltpu.roll(part, 32, 1))
        tiles.append(part * cosine + other * sine)
    return tiles


def turn_kv(x, cosine, sine):
    lane = lax.broadcasted_iota(jnp.int32, (1, 128), 1)
    first, second = turn(x[:, :256], cosine, sine)
    second = jnp.where(lane < KW - 128, second, x[:, 128:256])
    return jnp.concatenate([first, second, x[:, 256:]], axis=1)


def tables(seq, order, cos_ref, sin_ref):
    cosine = jnp.concatenate([cos_ref[seq ^ o] for o in order], axis=0)
    sine = jnp.concatenate([sin_ref[seq ^ o] for o in order], axis=0)
    return cosine, sine


def heads_to_rows(x, g):
    return jnp.concatenate(
        [x[:, HEAD_DIM * h : HEAD_DIM * (h + 1)] for h in range(GROUP * g, GROUP * (g + 1))], axis=0
    )


def rows_to_heads(parts, length):
    return jnp.concatenate(
        [p[length * r : length * (r + 1)] for p in parts for r in range(GROUP)], axis=1
    )


def attention_forward(order, length, seq_ref, blocks, wq, wkv, bq, bkv, gain, cos, sin, mask,
                      att_o, q_o, k_o, v_o):
    seq = seq_ref[0]
    cosine, sine = tables(seq, order, cos, sin)
    width = gain.shape[1]
    for b in range(blocks.shape[1] // length):
        x = blocks[:, b * length : (b + 1) * length, :width].astype(F32)
        x = x.reshape(len(order) * length, width)
        first = (norm_parts(x)[1] * gain[...]).astype(BF)
        kv = dot(first, wkv[...], 1, 0) + bkv[...]
        q = dot(first[:length], wq[...], 1, 0) + bq[...]
        q = jnp.concatenate(turn(q, cosine[:length], sine[:length]), axis=1).astype(BF)
        q = q * jnp.asarray(HEAD_DIM ** (-0.5), BF)
        kv = turn_kv(kv, cosine, sine).astype(BF)
        allowed = jnp.concatenate([mask[b]] * GROUP, axis=0) > 0.0
        parts = []
        for g in range(KV_HEADS):
            qg = heads_to_rows(q, g)
            kg = kv[:, HEAD_DIM * g : HEAD_DIM * (g + 1)]
            vg = kv[:, KW + HEAD_DIM * g : KW + HEAD_DIM * (g + 1)]
            q_o[b, g] = qg
            k_o[b, g] = kg
            v_o[b, g] = vg
            scores = jnp.where(allowed, dot(qg, kg, 1, 1), MASKED)
            top = jnp.max(scores, axis=-1, keepdims=True)
            e = jnp.exp(scores - top)
            total = jnp.sum(e, axis=-1, keepdims=True)
            probs = (e * (1.0 / total)).astype(BF)
            parts.append(dot(probs, vg, 1, 0))
        att_o[b * length : (b + 1) * length, :] = rows_to_heads(parts, length).astype(BF)


def feed_forward(attended, source, wo, wgu, wd, gain, cot, weight,
                 out_o, down_o, gu_o, mid_o, wout_o, attg_o, gain_o):
    units = wd.shape[0]
    step = units // 3
    att = attended[...]
    middle = source[...].astype(F32) + dot(att, wo[...], 1, 0)
    scale_two, normed = norm_parts(middle)
    g2 = gain[...]
    second = (normed * g2).astype(BF)
    out_grad = cot[...].astype(F32) * weight[...]
    feed_grad = out_grad.astype(BF)
    feed = None
    back = None
    for j in range(0, units, step):
        wg = wgu[:, j : j + step]
        wu = wgu[:, units + j : units + j + step]
        wdj = wd[j : j + step, :]
        gate = dot(second, wg, 1, 0)
        up = dot(second, wu, 1, 0)
        sig = jax.nn.sigmoid(gate)
        act = gate * sig
        product = (act * up).astype(BF)
        part = dot(product, wdj, 1, 0)
        feed = part if feed is None else feed + part
        down_o[j : j + step, :] = dot(product, feed_grad, 0, 0).astype(BF)
        pgrad = dot(feed_grad, wdj, 1, 1)
        ggrad = (pgrad * up * (sig * (1.0 + gate * (1.0 - sig)))).astype(BF)
        ugrad = (pgrad * act).astype(BF)
        gu_o[:, j : j + step] = dot(second, ggrad, 0, 0).astype(BF)
        gu_o[:, units + j : units + j + step] = dot(second, ugrad, 0, 0).astype(BF)
        part = dot(ggrad, wg, 1, 1) + dot(ugrad, wu, 1, 1)
        back = part if back is None else back + part
    out_o[...] = (middle + feed).astype(BF)
    gain_o[...] = jnp.sum(back * normed, axis=0, keepdims=True)
    middle_grad = out_grad + norm_back(back, g2, scale_two, normed)
    mid_o[...] = middle_grad
    branch = middle_grad.astype(BF)
    wout_o[...] = dot(att, branch, 0, 0).astype(BF)
    attg_o[...] = dot(branch, wo[...], 1, 1).astype(BF)


def attention_backward(order, length, seq_ref, blocks, wq, wkv, gain, cos, sin, mask, q_i, k_i, v_i,
                       attg, dq_o, dkv_o, wgrad_o, bias_o, gain_o):
    seq = seq_ref[0]
    cosine, sine = tables(seq, order, cos, sin)
    width = gain.shape[1]
    q_wgrad = kv_wgrad = bias_q = bias_kv = gain_sum = None
    for b in range(blocks.shape[1] // length):
        x = blocks[:, b * length : (b + 1) * length, :width].astype(F32)
        x = x.reshape(len(order) * length, width)
        normed = norm_parts(x)[1]
        first = (normed * gain[...]).astype(BF)
        allowed = jnp.concatenate([mask[b]] * GROUP, axis=0) > 0.0
        ag = attg[b * length : (b + 1) * length, :]
        dqs, dks, dvs = [], [], []
        for g in range(KV_HEADS):
            qg, kg, vg = q_i[b, g], k_i[b, g], v_i[b, g]
            agg = heads_to_rows(ag, g)
            scores = jnp.where(allowed, dot(qg, kg, 1, 1), MASKED)
            e = jnp.exp(scores - jnp.max(scores, axis=-1, keepdims=True))
            p = e * (1.0 / jnp.sum(e, axis=-1, keepdims=True))
            dvs.append(dot(p.astype(BF), agg, 0, 0))
            pg = dot(agg, vg, 1, 1)
            inner = jnp.sum(p * pg, axis=-1, keepdims=True)
            ds = (p * (pg - inner)).astype(BF)
            dqs.append(dot(ds, kg, 1, 0) * HEAD_DIM ** (-0.5))
            dks.append(dot(ds, qg, 0, 0))
        dq = rows_to_heads(dqs, length)
        dq = jnp.concatenate([dq, jnp.zeros((length, 64), F32)], axis=1)
        dq = jnp.concatenate(turn(dq, cosine[:length], -sine[:length]), axis=1).astype(BF)
        dkv = jnp.concatenate(dks + dvs, axis=1)
        dkv = turn_kv(dkv, cosine, -sine).astype(BF)
        dq_o[b * length : (b + 1) * length, :] = dq
        for r in range(len(order)):
            dkv_o[r, b * length : (b + 1) * length, :] = dkv[r * length : (r + 1) * length, :]
        wq_part = dot(first[:length], dq, 0, 0)
        wkv_part = dot(first, dkv, 0, 0)
        bq_part = jnp.sum(dq.astype(F32), axis=0, keepdims=True)
        bkv_part = jnp.sum(dkv.astype(F32), axis=0, keepdims=True)
        e_kv = dot(dkv, wkv[...], 1, 1) * normed
        e_q = dot(dq[:, :QW], wq[:, :QW], 1, 1) * normed[:length]
        g_part = jnp.sum(e_kv, axis=0, keepdims=True) + jnp.sum(e_q, axis=0, keepdims=True)
        if q_wgrad is None:
            q_wgrad, kv_wgrad, bias_q, bias_kv, gain_sum = wq_part, wkv_part, bq_part, bkv_part, g_part
        else:
            q_wgrad, kv_wgrad = q_wgrad + wq_part, kv_wgrad + wkv_part
            bias_q, bias_kv, gain_sum = bias_q + bq_part, bias_kv + bkv_part, gain_sum + g_part
    wgrad_o[...] = jnp.concatenate([q_wgrad[:, :QW], kv_wgrad], axis=1).astype(BF)
    bias_o[...] = jnp.concatenate([bias_q[:, :QW], bias_kv], axis=1)
    gain_o[...] = gain_sum


def input_gradient(dq, own, a, b, c, source, mid, wq, wkv, gain, out_o):
    kv = own[...].astype(F32) + a[...].astype(F32) + b[...].astype(F32) + c[...].astype(F32)
    first_grad = dot(dq[:, :QW], wq[:, :QW], 1, 1) + dot(kv.astype(BF), wkv[...], 1, 1)
    scale_one, normed = norm_parts(source[...].astype(F32))
    out_o[...] = mid[...] + norm_back(first_grad, gain[...], scale_one, normed)

def chosen(flag, a, b):
    return jnp.where(flag != 0, b, a)


class Blocks:
    def __init__(self, *refs):
        self.refs = refs
        self.shape = (len(refs),) + refs[0].shape

    def __getitem__(self, key):
        return jnp.stack([ref[key[1:]] for ref in self.refs])


def cut_qkv(core_bit, meta, w_hbm, bias_hbm, gains_hbm, out_o, w, bias, gains, all_s, sems):
    pairs = ((w_hbm, w), (bias_hbm, bias), (gains_hbm, gains))
    copies = [pltpu.make_async_copy(a, b, sems.at[i]) for i, (a, b) in enumerate(pairs)]
    for copy in copies:
        copy.start()
    for copy in copies:
        copy.wait()
    rows = w.shape[0]
    n = bias.shape[1]
    all_s[:rows, :] = w[...].astype(F32)
    all_s[rows:, :] = jnp.zeros((8, w.shape[1]), F32)
    all_s[rows : rows + 1, :n] = bias[...].astype(F32)
    for i in range(2):
        all_s[rows : rows + 1, n + rows * i : n + rows * (i + 1)] = gains[i : i + 1, :].astype(F32)
    half = out_o.shape[0]
    at = pl.multiple_of((meta[0] & core_bit) * half, 8)
    out_o[...] = all_s[pl.ds(at, half), :].astype(BF)


def first_forward(order, length, d_rows, n_bias, meta, b0, b1, b2, b3, a00, a10, a01, a11, cos, sin, mask,
                  att_o, q_o, k_o, v_o, w_o, gain_o, w_s, b_s):
    blocks = Blocks(b0, b1, b2, b3)
    core, x = meta[0] & 1, meta[1] & 1
    cut = a00.shape[2]
    for x_rel, c_rel, piece in ((0, 0, a00), (1, 0, a10), (0, 1, a01), (1, 1, a11)):
        for z0 in range(2):
            for z1 in range(2):
                at = (z1 * 4 + z0 * 2 + (x ^ x_rel)) * 2 * cut + (core ^ c_rel) * cut
                w_s[pl.ds(pl.multiple_of(at, 8), cut), :] = piece[z0, z1].astype(F32)
    n_f = w_s.shape[0] // (2 * cut)
    starts = [2 * cut * f for f in range(n_f)]
    w_o[...] = jnp.concatenate([w_s[at : at + d_rows, :] for at in starts], axis=0).astype(BF)
    lines = [w_s[at + d_rows : at + d_rows + 1, :] for at in starts]
    b_s[...] = jnp.concatenate([line[:, :n_bias] for line in lines], axis=1)
    for i in range(2):
        at = n_bias + d_rows * i
        gain_o[i : i + 1, :] = jnp.concatenate([line[:, at : at + d_rows] for line in lines], axis=1)
    wide = QW + 64
    attention_forward(order, length, meta, blocks, w_o[:, :wide], w_o[:, QW:], b_s[:, :wide], b_s[:, QW:],
                      gain_o[0:1, :], cos, sin, mask, att_o, q_o, k_o, v_o)


def turned(out, value):
    length = out.shape[2]
    for b in range(out.shape[0]):
        out[b] = value[length * b : length * (b + 1)].T.astype(out.dtype)


def rel(meta, f):
    r = f ^ meta[1]
    return r & 1, (r >> 1) & 1, (r >> 2) & 1


def fetch_pieces(meta, refs, b_s, g_s, sems):
    core, y, x, z0 = meta[0] & 1, (meta[0] >> 1) & 1, meta[1] & 1, (meta[1] >> 1) & 1
    copies = []
    for i in range(8):
        at = (z0 ^ (i >> 2), x ^ ((i >> 1) & 1), core ^ (i & 1))
        copies.append(pltpu.make_async_copy(refs[i], b_s.at[at], sems.at[i]))
    for i in range(8):
        at = (y ^ ((i >> 1) & 1), core ^ (i & 1), x ^ (i >> 2))
        copies.append(pltpu.make_async_copy(refs[8 + i], g_s.at[at], sems.at[8 + i]))
    for copy in copies:
        copy.start()
    return copies


def feed_forward_pieces(d_rows, ff_rows, meta, attended, source, gains, cot, weight, *refs):
    out_o, ak_o, ag_o, bk_o, bg_o, dk_o, dg_o, mid_o, attg_o, gain_o, down_s, wout_s, b_s, g_s, sems = refs[16:]
    copies = fetch_pieces(meta, refs, b_s, g_s, sems)
    core, y = meta[0] & 1, (meta[0] >> 1) & 1
    part_d = ff_rows // 4
    part_o = d_rows // 3
    cut = b_s.shape[4] - ff_rows // 2
    half = g_s.shape[-1] // 2
    for copy in copies[:8]:
        copy.wait()
    wo = []
    for f in range(8):
        for c in range(2):
            rows = b_s[(f >> 1) & 1, f & 1, c, f >> 2, ff_rows // 2 :, :].astype(F32)
            wo.append(rows if c == 0 else rows[: d_rows - cut])
    wo = jnp.concatenate(wo, axis=0).astype(BF)
    att = attended[...]
    middle = source[...].astype(F32) + dot(att, wo, 1, 0)
    scale_two, normed = norm_parts(middle)
    g2 = gains[1:2, :]
    second = (normed * g2).astype(BF)
    out_grad = cot[...].astype(F32) * weight[...]
    feed_grad = out_grad.astype(BF)
    for copy in copies[8:]:
        copy.wait()
    feed = back = None
    for c_rel in (1, 0):
        h = core ^ c_rel
        weights = []
        for yy in range(2):
            rows = [g_s[yy, h, f & 1, (f >> 1) & 1, f >> 2].astype(F32) for f in range(8)]
            weights.append(jnp.concatenate(rows, axis=0).astype(BF))
        wg, wu = weights
        wd = [b_s[i >> 1, i & 1, c, h, : ff_rows // 2, :] for i in range(4) for c in range(2)]
        wd = jnp.concatenate(wd, axis=0)
        gate = dot(second, wg, 1, 0)
        up = dot(second, wu, 1, 0)
        sig = jax.nn.sigmoid(gate)
        act = gate * sig
        product = (act * up).astype(BF)
        part = dot(product, wd, 1, 0)
        feed = part if feed is None else feed + part
        down_s[...] = dot(product, feed_grad, 0, 0)
        pgrad = dot(feed_grad, wd, 1, 1)
        ggrad = (pgrad * up * (sig * (1.0 + gate * (1.0 - sig)))).astype(BF)
        ugrad = (pgrad * act).astype(BF)
        part = dot(ggrad, wg, 1, 1) + dot(ugrad, wu, 1, 1)
        back = part if back is None else back + part
        for i in range(4):
            x, z0, z1 = rel(meta, 4 * h + i)
            for yy in range(2):
                for c_to, to in ((0, dk_o), (1, dg_o)):
                    at = pl.multiple_of(i * ff_rows + (yy * 2 + (core ^ c_to)) * part_d, 16)
                    to[y ^ yy, x, z0, z1, :part_d, :] = down_s[pl.ds(at, part_d), :].astype(BF)
        to_a, to_b = (ag_o, bg_o) if c_rel else (ak_o, bk_o)
        for yy, grad in ((0, ggrad), (1, ugrad)):
            wgrad = dot(second, grad, 0, 0)
            for f in range(8):
                x, z0, z1 = rel(meta, f)
                block = wgrad[d_rows * f : d_rows * (f + 1), :].astype(BF)
                to_a[x, z0, z1, yy] = block[:, :half]
                to_b[z0, z1, x, yy] = block[:, half:]
    turned(out_o, middle + feed)
    gain_o[...] = jnp.sum(back * normed, axis=0, keepdims=True)
    middle_grad = out_grad + norm_back(back, g2, scale_two, normed)
    mid_o[...] = middle_grad
    branch = middle_grad.astype(BF)
    attg_o[...] = dot(branch, wo, 1, 1).astype(BF)
    wout = dot(att, branch, 0, 0)
    for f in range(8):
        wout_s[f, :d_rows, :] = wout[d_rows * f : d_rows * (f + 1), :]
        wout_s[f, d_rows:, :] = jnp.zeros((part_o, wout.shape[1]), F32)
    for f in range(8):
        x, z0, z1 = rel(meta, f)
        for yy in range(2):
            for c_to, to in ((0, dk_o), (1, dg_o)):
                at = pl.multiple_of((yy * 2 + (core ^ c_to)) * part_o, 8)
                to[y ^ yy, x, z0, z1, part_d:, :] = wout_s[f, pl.ds(at, part_o), :].astype(BF)


def attention_backward_pieces(order, length, d_rows, meta, b0, b1, b2, b3, w, gains, cos, sin, mask, q_i, k_i, v_i,
                              attg, gain_two, dq_o, dk_o, dg_o, rk_o, rg_o, w_s, bias_s, gain_s, small_s):
    blocks = Blocks(b0, b1, b2, b3)
    half = len(order) // 2

    class Pieces:
        def __setitem__(self, key, value):
            ref = dk_o if key[0] < half else dg_o
            ref[(key[0] % half,) + key[1:]] = value

    class Wgrad:
        def __setitem__(self, key, value):
            w_s[:, : 2 * KW] = value[:, QW:].astype(F32)
            w_s[:, 2 * KW : 2 * KW + QW] = value[:, :QW].astype(F32)
            w_s[:, 2 * KW + QW :] = jnp.zeros((value.shape[0], 64), F32)

    wide = QW + 64
    attention_backward(order, length, meta, blocks, w[:, :wide], w[:, QW:], gains[0:1, :], cos, sin, mask,
                       q_i, k_i, v_i, attg, dq_o, Pieces(), Wgrad(), bias_s, gain_s)
    n_f = small_s.shape[0]
    qk, v = (QW + KW) // n_f, KW // n_f
    bias, g1, g2 = bias_s[...], gain_s[...], gain_two[...]
    for f in range(n_f):
        line = jnp.concatenate(
            [
                bias[:, qk * f : qk * (f + 1)],
                bias[:, QW + KW + v * f : QW + KW + v * (f + 1)],
                g1[:, d_rows * f : d_rows * (f + 1)],
                jnp.zeros((1, 256 - qk - v - d_rows), F32),
                g2[:, d_rows * f : d_rows * (f + 1)],
                jnp.zeros((1, 768 - d_rows), F32),
            ],
            axis=1,
        )
        small_s[f] = jnp.broadcast_to(line, (8, 1024))
    core, y = meta[0] & 1, (meta[0] >> 1) & 1
    for f in range(n_f):
        x, z0, z1 = rel(meta, f)
        for yy in range(2):
            for c_to, to in ((0, rk_o), (1, rg_o)):
                at = pl.multiple_of((yy * 2 + (core ^ c_to)) * 256, 256)
                block = [w_s[d_rows * f : d_rows * (f + 1), pl.ds(at, 256)], small_s[f, :, pl.ds(at, 256)]]
                to[y ^ yy, x, z0, z1] = jnp.concatenate(block, axis=0).astype(BF)


def input_gradient_two(dq, own, other, source, mid, w, gains, out_o):
    kv = (own[...].astype(F32) + other[...].astype(F32)).astype(BF)
    first_grad = dot(dq[:, :QW], w[:, :QW], 1, 1) + dot(kv, w[:, QW:], 1, 1)
    scale_one, normed = norm_parts(source[...].astype(F32))
    turned(out_o, mid[...] + norm_back(first_grad, gains[0:1, :], scale_one, normed))


def place_gate(meta, near, far, out_o, parts=1, part=0):
    core = meta[0] & 1
    n = near.shape[2]
    for pieces, c_rel in ((near, 0), (far, 1)):
        for yy in range(2):
            at = pl.multiple_of(((yy * 2 + (core ^ c_rel)) * parts + part) * n, 128)
            out_o[:, pl.ds(at, n)] = pieces[yy].astype(F32)


def place_down(part_d, meta, p00, p10, p01, p11, out_o, wout_o):
    seq = meta[0]
    part_o = p00.shape[0] - part_d
    for piece, o in ((p00[...], 0), (p10[...], 2), (p01[...], 1), (p11[...], 3)):
        piece = piece.astype(F32)
        to = seq ^ o
        out_o[pl.ds(pl.multiple_of(to * part_d, 16), part_d), :] = piece[:part_d]

        @pl.when(to < 3)
        def _():
            wout_o[pl.ds(pl.multiple_of(to * part_o, 8), part_o), :] = piece[part_d:]


def place_qkv(qk, v, meta, p00, p10, p01, p11, w_o, bqk_o, bv_o, gains_o, all_s):
    n = p00.shape[1]
    for piece, o in ((p00, 0), (p10, 2), (p01, 1), (p11, 3)):
        all_s[:, pl.ds(pl.multiple_of((meta[0] ^ o) * n, 128), n)] = piece[...].astype(F32)
    d_rows = w_o.shape[0]
    w_o[:, :QW] = all_s[:d_rows, 2 * KW : 2 * KW + QW]
    w_o[:, QW:] = all_s[:d_rows, : 2 * KW]
    line = all_s[d_rows : d_rows + 1, :]
    bqk_o[...] = line[:, :qk]
    bv_o[...] = line[:, qk : qk + v]
    gains_o[0:1, :] = line[:, qk + v : qk + v + d_rows]
    gains_o[1:2, :] = line[:, 256 : 256 + d_rows]


def place_all(part_d, qk, v, meta, a_near, a_far, b_near, b_far, d0, d1, d2, d3, r0, r1, far,
              gate_o, down_o, wout_o, w_o, bqk_o, bv_o, gains_o, all_s):
    place_gate(meta, a_near, a_far, gate_o, 2, 0)
    place_gate(meta, b_near, b_far, gate_o, 2, 1)
    place_down(part_d, meta, d0, d1, d2, d3, down_o, wout_o)
    place_qkv(qk, v, meta, r0, r1, far.at[0], far.at[1], w_o, bqk_o, bv_o, gains_o, all_s)


class Net:
    def __init__(self, n_fsdp, n_seq):
        self.n_fsdp, self.n_seq = n_fsdp, n_seq
        self.total = n_fsdp * n_seq
        f, s = lax.axis_index("fsdp"), lax.axis_index("seq")
        self.index = f * n_seq + s
        self.seq_bits = [1 << b for b in range(n_seq.bit_length() - 1)]
        self.fsdp_bits = [n_seq << b for b in range(n_fsdp.bit_length() - 1)]

    def swap(self, value, mask):
        pairs = [(i, i ^ mask) for i in range(self.total)]
        return lax.ppermute(value, ("fsdp", "seq"), pairs)

    def bit(self, mask):
        return (self.index & mask) != 0

    def both(self, mine, mask, axis, other=None):
        other = self.swap(mine, mask) if other is None else other
        high = self.bit(mask)
        return jnp.stack([jnp.where(high, other, mine), jnp.where(high, mine, other)], axis=axis)

    def half(self, value, mask, axis):
        return lax.dynamic_index_in_dim(
            value, self.bit(mask).astype(jnp.int32), axis, keepdims=False
        )

    def add_half(self, value, mask, axis):
        mine = self.bit(mask).astype(jnp.int32)
        keep = lax.dynamic_index_in_dim(value, mine, axis, keepdims=False)
        give = lax.dynamic_index_in_dim(value, 1 - mine, axis, keepdims=False)
        got = self.swap(give, mask)
        return (keep.astype(F32) + got.astype(F32)).astype(value.dtype)

    def gather_fsdp(self, value):
        for step, mask in enumerate(reversed(self.fsdp_bits)):
            value = self.both(value, mask, step)
        return value

    def scatter_fsdp(self, value, first_axis=0):
        count = len(self.fsdp_bits)
        for step, mask in enumerate(self.fsdp_bits):
            value = self.add_half(value, mask, first_axis + count - 1 - step)
        return value


def on_device(
    hidden, w_qkv, b_qkv, w_out, w_gate_up, w_down, norm_gains, segment_ids, token_counts, cotangent,
    n_fsdp, n_seq,
):
    net = Net(n_fsdp, n_seq)
    micro, batch, length, width = hidden.shape
    full_length = length * n_seq
    tokens_micro = batch * n_fsdp * full_length
    scale = HEAD_DIM ** (-0.5)
    rows = micro * batch * length
    d_rows = w_qkv.shape[0]
    ff_rows = w_down.shape[0]
    units = w_gate_up.shape[1] // 2
    qkv_w = w_qkv.shape[1]
    core = net.seq_bits[0]
    f_lead = (2,) * len(net.fsdp_bits)

    ids = segment_ids.reshape(rows, 1).astype(BF)
    block = jnp.concatenate(
        [hidden.reshape(rows, width), jnp.broadcast_to(ids, (rows, 64))], axis=1
    )
    blocks = block[None]
    for mask in reversed(net.seq_bits):
        blocks = jnp.concatenate([blocks, net.swap(blocks, mask)], axis=0)
    order = [0]
    for mask in reversed(net.seq_bits):
        order = order + [o ^ mask for o in order]
    seq_index = lax.axis_index("seq")
    block_ids = [seq_index ^ o for o in order]

    pad_rows = -(d_rows + 1) % 16 + 1
    extra = jnp.zeros((pad_rows, qkv_w), BF)
    small = jnp.concatenate([b_qkv, norm_gains.reshape(-1)])
    extra = extra.at[0, : small.shape[0]].set(small)
    shard_a = jnp.concatenate([w_qkv, extra], axis=0).reshape(2, -1, qkv_w)
    got_a = net.gather_fsdp(net.half(shard_a, core, 0))
    full_a = net.both(got_a, core, len(f_lead)).reshape(n_fsdp, d_rows + pad_rows, qkv_w)
    wf_qkv = full_a[:, :d_rows].reshape(n_fsdp * d_rows, qkv_w)
    smalls = full_a[:, d_rows]
    n_bias = b_qkv.shape[0]
    bias = smalls[:, :n_bias].reshape(-1).astype(F32)
    gains = smalls[:, n_bias : n_bias + 2 * d_rows].reshape(n_fsdp, 2, d_rows).astype(F32)
    gain_one = gains[:, 0].reshape(-1)
    gain_two = gains[:, 1].reshape(-1)

    pad_b = -(d_rows + ff_rows) % 16
    shard_b = jnp.concatenate([w_out, w_down, jnp.zeros((pad_b, width), BF)], axis=0)
    shard_b = shard_b.reshape(2, -1, width)
    got_b = net.gather_fsdp(net.half(shard_b, core, 0))

    parts = n_seq
    shard_c = w_gate_up.reshape(d_rows, parts, -1)
    got_c = net.gather_fsdp(lax.dynamic_index_in_dim(shard_c, seq_index, 1, keepdims=False))
    full_b = net.both(got_b, core, len(f_lead)).reshape(n_fsdp, -1, width)
    wf_out = full_b[:, :d_rows].reshape(n_fsdp * d_rows, width)
    wf_down = full_b[:, d_rows : d_rows + ff_rows].reshape(n_fsdp * ff_rows, width)
    got_c = got_c.reshape(n_fsdp * d_rows, -1)
    for mask in reversed(net.seq_bits):
        got_c = net.both(got_c, mask, got_c.ndim - 1)
    wf_gate_up = got_c.reshape(n_fsdp * d_rows, 2 * units)

    places = np.arange(full_length, dtype=np.float32)
    speeds = np.power(ROPE_BASE, -2.0 * np.arange(HEAD_DIM // 2, dtype=np.float32) / HEAD_DIM)
    angles = places[:, None] * speeds.astype(np.float32)[None, :]
    cos_t = np.tile(np.cos(angles), (1, 4)).reshape(n_seq, length, 128)
    sin_t = np.concatenate([-np.sin(angles), np.sin(angles)] * 2, axis=1).reshape(n_seq, length, 128)
    cos_t, sin_t = jnp.asarray(cos_t, F32), jnp.asarray(sin_t, F32)
    seqs = micro * batch
    seg_all = blocks[..., width].reshape(n_seq, seqs, length).transpose(1, 0, 2)
    own_places = seq_index * length + jnp.arange(length, dtype=jnp.int32)
    key_places = jnp.stack(block_ids)[:, None] * length + jnp.arange(length, dtype=jnp.int32)
    allowed = (seg_all[:, 0, :, None] == seg_all.reshape(seqs, 1, -1)) & (
        own_places[None, :, None] >= key_places.reshape(1, 1, -1)
    )
    allowed = allowed.astype(F32)
    seq_scalar = seq_index.astype(jnp.int32).reshape(1)
    wq, wkv = wf_qkv[:, : QW + 64], wf_qkv[:, QW:]
    gain_one, gain_two = gain_one[None], gain_two[None]
    source = hidden.reshape(rows, width)
    n_all = n_seq * rows
    attended, q_s, k_s, v_s = call(
        functools.partial(attention_forward, order, length),
        [seq_scalar],
        [blocks, wq, wkv, bias[None, : QW + 64], bias[None, QW:], gain_one, cos_t, sin_t, allowed],
        [
            sds((rows, QW), BF),
            sds((seqs, KV_HEADS, GROUP * length, HEAD_DIM), BF),
            sds((seqs, KV_HEADS, full_length, HEAD_DIM), BF),
            sds((seqs, KV_HEADS, full_length, HEAD_DIM), BF),
        ],
        2 * n_all * width * 2 * KW + 2 * rows * width * QW + 4 * rows * full_length * QW,
    )

    weight = tokens_micro / token_counts.astype(F32)
    weight = jnp.repeat(weight, batch * length)[:, None]
    block_out, down_grad, gate_up_wgrad, middle_grad, out_wgrad, attended_grad, gain_two_grad = call(
        feed_forward,
        [],
        [attended, source, wf_out, wf_gate_up, wf_down, gain_two, cotangent.reshape(rows, width), weight],
        [
            sds((rows, width), BF),
            sds((units, width), BF),
            sds((width, 2 * units), BF),
            sds((rows, width), F32),
            sds((QW, width), BF),
            sds((rows, QW), BF),
            sds((1, width), F32),
        ],
        6 * rows * width * 3 * units + 6 * rows * width * QW,
    )
    block_out = block_out.reshape(hidden.shape)

    def seq_axes(value, axis, masks):
        for mask in masks:
            value = net.add_half(value, mask, axis)
        return value

    quarter = (2,) * len(net.seq_bits)
    n_f = len(f_lead)
    red_down = down_grad.reshape(f_lead + quarter + (ff_rows // n_seq, width))
    for step, mask in enumerate(net.seq_bits):
        red_down = net.add_half(red_down, mask, n_f + len(quarter) - 1 - step)
    red_down = net.scatter_fsdp(red_down)

    red_gate = gate_up_wgrad.reshape(f_lead + (d_rows,) + quarter + (2 * units // n_seq,))
    red_gate = net.add_half(red_gate, core, n_f + len(quarter))
    red_gate = net.add_half(red_gate, net.fsdp_bits[0], n_f - 1)
    for step, mask in enumerate(net.seq_bits[1:]):
        red_gate = net.add_half(red_gate, mask, n_f - 1 + len(quarter) - 1 - step)
    for step, mask in enumerate(net.fsdp_bits[1:]):
        red_gate = net.add_half(red_gate, mask, n_f - 2 - step)

    dq, dkv, qkv_wgrad, bias_grad, gain_one_grad = call(
        functools.partial(attention_backward, order, length),
        [seq_scalar],
        [blocks, wq, wkv, gain_one, cos_t, sin_t, allowed, q_s, k_s, v_s, attended_grad],
        [
            sds((rows, QW + 64), BF),
            sds((n_seq, rows, 2 * KW), BF),
            sds((width, qkv_w), BF),
            sds((1, qkv_w), F32),
            sds((1, width), F32),
        ],
        4 * n_all * width * 2 * KW + 4 * rows * width * QW + 10 * rows * full_length * QW,
    )
    kv_parts = [dkv[0]]
    for place, mask_bits in enumerate(order):
        if mask_bits:
            kv_parts.append(net.swap(dkv[place], mask_bits))
    (hidden_grad,) = call(
        input_gradient,
        [],
        [dq, *kv_parts, source, middle_grad, wq, wkv, gain_one],
        [sds((rows, width), F32)],
        2 * rows * width * qkv_w,
    )
    hidden_grad = hidden_grad.reshape(hidden.shape)
    bias_grad, gain_one_grad, gain_two_grad = bias_grad[0], gain_one_grad[0], gain_two_grad[0]

    qk_rows, v_rows = (QW + KW) // n_fsdp, KW // n_fsdp
    small_grads = jnp.concatenate(
        [
            bias_grad[: QW + KW].reshape(n_fsdp, qk_rows),
            bias_grad[QW + KW :].reshape(n_fsdp, v_rows),
            gain_one_grad.reshape(n_fsdp, d_rows),
            gain_two_grad.reshape(n_fsdp, d_rows),
        ],
        axis=1,
    ).astype(BF)
    wide = qkv_w + width
    small_pad = jnp.zeros((n_fsdp, pad_rows, wide), BF)
    small_pad = small_pad.at[:, 0, : small_grads.shape[1]].set(small_grads)
    rest = jnp.concatenate([qkv_wgrad, out_wgrad], axis=1)
    rest = jnp.concatenate([rest.reshape(n_fsdp, d_rows, wide), small_pad], axis=1)
    rest = rest.reshape(f_lead + (d_rows + pad_rows,) + quarter + (wide // n_seq,))
    for step, mask in enumerate(net.seq_bits):
        rest = net.add_half(rest, mask, n_f + 1 + len(quarter) - 1 - step)
    rest = net.scatter_fsdp(rest)

    def seq_back(value, axis):
        for step, mask in enumerate(reversed(net.seq_bits)):
            value = net.both(value, mask, axis + step)
        return value

    out_down = seq_back(red_down, 0).reshape(ff_rows, width).astype(F32)
    out_gate = seq_back(red_gate, 1).reshape(d_rows, 2 * units).astype(F32)
    out_rest = seq_back(rest, 1).reshape(d_rows + pad_rows, wide).astype(F32)
    line = out_rest[d_rows]
    edge = qk_rows + v_rows
    return (
        block_out,
        hidden_grad,
        out_rest[:d_rows, :qkv_w],
        line[:qk_rows],
        line[qk_rows:edge],
        out_rest[:d_rows, qkv_w:],
        out_gate,
        out_down,
        line[edge : edge + 2 * d_rows].reshape(2, d_rows),
    )


def after(value, *others):
    return lax.optimization_barrier((value, *others))[0]


def rope_tables(full_length, n_seq):
    places = np.arange(full_length, dtype=np.float32)
    speeds = np.power(ROPE_BASE, -2.0 * np.arange(HEAD_DIM // 2, dtype=np.float32) / HEAD_DIM)
    angles = places[:, None] * speeds.astype(np.float32)[None, :]
    cos_t = np.tile(np.cos(angles), (1, 4)).reshape(n_seq, -1, 128)
    sin_t = np.concatenate([-np.sin(angles), np.sin(angles)] * 2, axis=1).reshape(n_seq, -1, 128)
    return jnp.asarray(cos_t, F32), jnp.asarray(sin_t, F32)


def on_device_tiled(
    hidden, w_qkv, b_qkv, w_out, w_gate_up, w_down, norm_gains, segment_ids, token_counts, cotangent,
    n_fsdp, n_seq,
):
    net = Net(n_fsdp, n_seq)
    micro, batch, length, width = hidden.shape
    full_length = length * n_seq
    tokens_micro = batch * n_fsdp * full_length
    rows = micro * batch * length
    seqs = micro * batch
    d_rows, qkv_w = w_qkv.shape
    ff_rows = w_down.shape[0]
    units = w_gate_up.shape[1] // 2
    n_bias = b_qkv.shape[0]
    core, ybit = net.seq_bits
    xbit, znear, zfar = net.fsdp_bits
    order = [0, 2, 1, 3]
    seq_index = lax.axis_index("seq")
    meta = jnp.stack([seq_index, lax.axis_index("fsdp")]).astype(jnp.int32)
    source = hidden.reshape(rows, width)

    small = [w_qkv, b_qkv[None], norm_gains]
    a0 = pl.pallas_call(
        functools.partial(cut_qkv, core),
        out_shape=sds(((d_rows + 8) // 2, qkv_w), BF),
        in_specs=[pl.BlockSpec(memory_space=pltpu.SMEM)] + [pl.BlockSpec(memory_space=pltpu.HBM)] * 3,
        out_specs=pl.BlockSpec(memory_space=pltpu.VMEM),
        scratch_shapes=[
            *[pltpu.VMEM(v.shape, BF) for v in small],
            pltpu.VMEM((d_rows + 8, qkv_w), F32),
            pltpu.SemaphoreType.DMA((3,)),
        ],
        compiler_params=pltpu.CompilerParams(vmem_limit_bytes=52 * 1024 * 1024),
    )(meta, *small)
    a1 = net.both(a0, zfar, 0)

    ids = segment_ids.reshape(rows, 1).astype(BF)
    block = jnp.concatenate([source, jnp.broadcast_to(ids, (rows, 64))], axis=1)
    block = after(block, a0)
    block_y = net.swap(block, ybit)
    block_c = net.swap(block, core)

    quarter = 2 * units // n_seq
    gu0 = lax.dynamic_slice_in_dim(after(w_gate_up, a0), seq_index * quarter, quarter, axis=1)
    half_b = jnp.concatenate(
        [
            w_down.reshape(2, ff_rows // 2, width),
            jnp.concatenate([w_out, jnp.zeros((8, width), BF)], axis=0).reshape(2, -1, width),
        ],
        axis=1,
    )
    a2 = net.both(a1, znear, 0)
    a_x = net.swap(a2, xbit)
    a_c = net.swap(a2, core)
    gu1 = net.both(gu0, zfar, 0)
    gu2 = net.both(after(gu1, a2), znear, 0)
    block_yc = net.swap(block_y, core)
    a_xc = net.swap(a_x, core)
    gu_x = net.swap(gu2, xbit)
    gu_y = net.swap(gu2, ybit)
    gu_c = net.swap(gu2, core)
    b0 = net.half(after(half_b, a1), core, 0)
    b1 = net.both(b0, zfar, 0, after(net.swap(b0, zfar), a2))
    b_x = net.swap(b1, xbit)
    b_z = net.swap(after(b1, gu2), znear)
    b_c = net.swap(b1, core)
    a_xc = after(a_xc, gu2, b1)

    cos_t, sin_t = rope_tables(full_length, n_seq)
    block_ids = [seq_index ^ o for o in order]
    blocks = [block, block_y, block_c, block_yc]
    seg_all = jnp.stack([b[:, width].reshape(seqs, length) for b in blocks], axis=1)
    own_places = seq_index * length + jnp.arange(length, dtype=jnp.int32)
    key_places = jnp.stack(block_ids)[:, None] * length + jnp.arange(length, dtype=jnp.int32)
    allowed = (seg_all[:, 0, :, None] == seg_all.reshape(seqs, 1, -1)) & (
        own_places[None, :, None] >= key_places.reshape(1, 1, -1)
    )
    allowed = allowed.astype(F32)
    attended, q_s, k_s, v_s, wf, gains = call(
        functools.partial(first_forward, order, length, d_rows, n_bias),
        [meta],
        [*blocks, a2, a_x, a_c, a_xc, cos_t, sin_t, allowed],
        [
            sds((rows, QW), BF),
            sds((seqs, KV_HEADS, GROUP * length, HEAD_DIM), BF),
            sds((seqs, KV_HEADS, full_length, HEAD_DIM), BF),
            sds((seqs, KV_HEADS, full_length, HEAD_DIM), BF),
            sds((width, qkv_w), BF),
            sds((2, width), F32),
        ],
        1.2e10,
        [(n_fsdp * (d_rows + 8), qkv_w), (1, qkv_w)],
    )
    gu_y = after(gu_y, attended)
    gu_x, b_z, b_x = after(gu_x, gu_y), after(b_z, gu_y), after(b_x, gu_y)
    gu_xy = net.swap(gu_x, ybit)
    b_zx = net.swap(b_z, xbit)
    gu_yc = net.swap(gu_y, core)
    gu_xc = net.swap(gu_x, core)
    b_zc = net.swap(b_z, core)
    b_xc = net.swap(b_x, core)
    b_zxc = net.swap(b_zx, core)
    gu_xyc = net.swap(gu_xy, core)
    pieces = [b1, b_c, b_x, b_xc, b_z, b_zc, b_zx, b_zxc]
    pieces += [gu2, gu_c, gu_y, gu_yc, gu_x, gu_xc, gu_xy, gu_xyc]

    weight = tokens_micro / token_counts.astype(F32)
    weight = jnp.repeat(weight, batch * length)[:, None]
    lead = (2, 2, 2, 2)
    cot = cotangent.reshape(rows, width)
    gate_lead = lead + (d_rows, units // 4)
    block_out, a_keep, a_give, b_keep, b_give, down_keep, down_give, middle_grad, attended_grad, gain_two = call(
        functools.partial(feed_forward_pieces, d_rows, ff_rows),
        [meta],
        [attended, source, gains, cot, weight],
        [
            sds((seqs, width, length), BF),
            sds(gate_lead, BF),
            sds(gate_lead, BF),
            sds(gate_lead, BF),
            sds(gate_lead, BF),
            sds(lead + (ff_rows // 4 + d_rows // 3, width), BF),
            sds(lead + (ff_rows // 4 + d_rows // 3, width), BF),
            sds((rows, width), F32),
            sds((rows, QW), BF),
            sds((1, width), F32),
        ],
        1.4e10,
        [(units // 2, width), (n_fsdp, d_rows + d_rows // 3, width)],
        fetched=pieces,
        landing=[(2, 2, 2, 2) + b1.shape[1:], (2, 2, 2, 2, 2, d_rows, units // 2)],
    )
    block_out = block_out.reshape(micro, batch, width, length).swapaxes(2, 3)

    def add(keep, got):
        return (keep.astype(F32) + got.astype(F32)).astype(BF)

    def halves(keep, got):
        return add(keep[0], got[0]), add(keep[1], got[1])

    down_got = net.swap(down_give, core)
    a_got = net.swap(after(a_give, down_got), core)
    b_got = net.swap(after(b_give, down_got), core)
    a, a_give = halves(a_keep, a_got)
    a_got = net.swap(a_give, xbit)
    b, b_give = halves(b_keep, b_got)
    b_got = net.swap(b_give, znear)
    down, down_give = halves(down_keep, down_got)
    attended_grad = after(attended_grad, a_give, b_give, down_give)
    down_got = net.swap(down_give, ybit)

    dq, dkv_keep, dkv_give, rest_keep, rest_give = call(
        functools.partial(attention_backward_pieces, order, length, d_rows),
        [meta],
        [*blocks, wf, gains, cos_t, sin_t, allowed, q_s, k_s, v_s, attended_grad, gain_two],
        [
            sds((rows, QW + 64), BF),
            sds((2, rows, 2 * KW), BF),
            sds((2, rows, 2 * KW), BF),
            sds(lead + (d_rows + 8, 256), BF),
            sds(lead + (d_rows + 8, 256), BF),
        ],
        1.4e10,
        [(width, 1024), (1, qkv_w), (1, width), (n_fsdp, 8, 1024)],
        24,
    )
    b, b_give = halves(b, after(b_got, dq))
    a, a_give = halves(a, after(a_got, b_give))
    b_got = net.swap(b_give, zfar)
    a_got = net.swap(a_give, znear)
    rest, rest_give = halves(rest_keep, after(net.swap(rest_give, core), b_give, down_got))
    rest_got = net.swap(rest_give, ybit)
    down, down_give = halves(down, after(down_got, rest_give))
    down_got = net.swap(down_give, xbit)
    dkv, dkv_give = halves(dkv_keep, after(net.swap(dkv_give, core), down_give))
    dkv_got = net.swap(dkv_give, ybit)
    a, a_give = halves(a, after(a_got, dkv_give))
    a_got = net.swap(a_give, zfar)
    rest, rest_give = halves(rest, after(rest_got, a_give))
    rest_got = net.swap(rest_give, xbit)
    b, b_give = halves(b, after(b_got, rest_give))
    b_got = net.swap(b_give, xbit)
    down, down_give = halves(down, after(down_got, b_give))
    down_got = net.swap(down_give, znear)
    rest, rest_give = halves(rest, after(rest_got, down_give))
    rest_got = net.swap(rest_give, znear)
    (hidden_grad,) = call(
        input_gradient_two,
        [],
        [dq, dkv, after(dkv_got, rest_give), source, middle_grad, wf, gains],
        [sds((seqs, width, length), F32)],
        3e9,
        mib=16,
    )
    a_got = after(a_got, hidden_grad)
    hidden_grad = hidden_grad.reshape(micro, batch, width, length).swapaxes(2, 3)
    a = add(a, a_got)
    a_got = net.swap(a, ybit)
    b = add(b, after(b_got, a))
    b_got = net.swap(b, ybit)
    down, down_give = halves(down, after(down_got, b))
    down_got = net.swap(down_give, zfar)
    rest, rest_give = halves(rest, after(rest_got, down_give))
    rest_got = net.swap(rest_give, zfar)
    a = add(a, after(a_got, rest_give))
    a_far = net.swap(a, core)
    b = add(b, b_got)
    b_far = net.swap(b, core)
    down = add(down, after(down_got, a))
    down_y = net.swap(down, ybit)
    down_c = net.swap(after(down, down_y), core)
    rest = add(rest, after(rest_got, down))
    rest_y = net.swap(rest, ybit)
    down_yc = net.swap(after(down_y, rest_y), core)
    rest_far = net.swap(jnp.stack([rest, rest_y]), core)
    qk, v = (QW + KW) // n_fsdp, KW // n_fsdp
    out_gate, out_down, out_wout, out_qkv, b_qk, b_v, out_gains = call(
        functools.partial(place_all, ff_rows // 4, qk, v),
        [meta],
        [a, a_far, b, b_far, down, down_y, down_c, down_yc, rest, rest_y, rest_far],
        [
            sds((d_rows, 2 * units), F32),
            sds((ff_rows, width), F32),
            sds((d_rows, width), F32),
            sds((d_rows, qkv_w), F32),
            sds((1, qk), F32),
            sds((1, v), F32),
            sds((2, d_rows), F32),
        ],
        3e9,
        [(d_rows + 8, 1024)],
        16,
    )
    return (
        block_out,
        hidden_grad,
        out_qkv,
        b_qk.reshape(qk),
        b_v.reshape(v),
        out_wout,
        out_gate,
        out_down,
        out_gains,
    )


def solution(mesh):
    n_fsdp, n_seq = mesh.shape["fsdp"], mesh.shape["seq"]
    in_specs = (
        P(None, "fsdp", "seq", None),
        P("fsdp", None),
        P("fsdp"),
        P("fsdp", None),
        P("fsdp", None),
        P("fsdp", None),
        P(None, "fsdp"),
        P(None, "fsdp", "seq"),
        P(),
        P(None, "fsdp", "seq", None),
    )
    out_specs = (
        P(None, "fsdp", "seq", None),
        P(None, "fsdp", "seq", None),
        P("fsdp", None),
        P("fsdp"),
        P("fsdp"),
        P("fsdp", None),
        P("fsdp", None),
        P("fsdp", None),
        P(None, "fsdp"),
    )

    def local(*args):
        body = on_device_tiled if (n_fsdp, n_seq) == (8, 4) else on_device
        return body(*args, n_fsdp=n_fsdp, n_seq=n_seq)

    return jax.shard_map(local, mesh=mesh, in_specs=in_specs, out_specs=out_specs, check_vma=False)
```

```python
import functools

import jax
import jax.numpy as jnp
import numpy as np
from jax import lax
from jax.experimental import pallas as pl
from jax.experimental.pallas import tpu as pltpu
from jax.sharding import PartitionSpec as P

HEADS = 9
KV_HEADS = 3
HEAD_DIM = 64
GROUP = HEADS // KV_HEADS
QW = HEADS * HEAD_DIM
KW = KV_HEADS * HEAD_DIM
EPS = 1e-05
ROPE_BASE = 100000.0
MASKED = -1000000000.0
BF = jnp.bfloat16
F32 = jnp.float32


def dot(a, b, ca, cb):
    return lax.dot_general(a, b, (((ca,), (cb,)), ((), ())), preferred_element_type=F32)


def rotary(values, cosine, sine):
    half = values.shape[-1] // 2
    a, b = values[..., :half], values[..., half:]
    return jnp.concatenate([a * cosine - b * sine, b * cosine + a * sine], axis=-1)


def norm_parts(values):
    factor = lax.rsqrt(jnp.mean(values * values, axis=-1, keepdims=True) + EPS)
    return factor, values * factor


def norm_back(grad_in, gain, factor, normed):
    scaled = grad_in * gain
    return factor * (scaled - normed * jnp.mean(scaled * normed, axis=-1, keepdims=True))


def whole(*shape_dtypes):
    return [pl.BlockSpec(memory_space=pltpu.VMEM) for _ in shape_dtypes]


def call(kernel, scalars, arrays, outs, flops, scratch=(), mib=52, fetched=(), landing=()):
    specs = [pl.BlockSpec(memory_space=pltpu.SMEM)] * len(scalars) + whole(*arrays)
    specs += [pl.BlockSpec(memory_space=pltpu.HBM)] * len(fetched)
    arrays = [*arrays, *fetched]
    moved = sum(a.size * a.dtype.itemsize for a in arrays) + sum(
        int(np.prod(o.shape)) * o.dtype.itemsize for o in outs
    )
    return pl.pallas_call(
        kernel,
        out_shape=outs,
        in_specs=specs,
        out_specs=whole(*outs),
        scratch_shapes=[
            *[pltpu.VMEM(shape, F32) for shape in scratch],
            *[pltpu.VMEM(shape, BF) for shape in landing],
            *([pltpu.SemaphoreType.DMA((len(fetched),))] if fetched else []),
        ],
        compiler_params=pltpu.CompilerParams(vmem_limit_bytes=mib * 1024 * 1024),
        cost_estimate=pl.CostEstimate(flops=int(flops), bytes_accessed=moved, transcendentals=0),
    )(*scalars, *arrays)


def sds(shape, dtype):
    return jax.ShapeDtypeStruct(shape, dtype)


def turn(x, cosine, sine):
    tiles = []
    low = lax.broadcasted_iota(jnp.int32, (1, 128), 1) % HEAD_DIM < HEAD_DIM // 2
    for t in range(x.shape[1] // 128):
        part = x[:, 128 * t : 128 * t + 128]
        other = jnp.where(low, pltpu.roll(part, 96, 1), pltpu.roll(part, 32, 1))
        tiles.append(part * cosine + other * sine)
    return tiles


def turn_kv(x, cosine, sine):
    lane = lax.broadcasted_iota(jnp.int32, (1, 128), 1)
    first, second = turn(x[:, :256], cosine, sine)
    second = jnp.where(lane < KW - 128, second, x[:, 128:256])
    return jnp.concatenate([first, second, x[:, 256:]], axis=1)


def tables(seq, order, cos_ref, sin_ref):
    cosine = jnp.concatenate([cos_ref[seq ^ o] for o in order], axis=0)
    sine = jnp.concatenate([sin_ref[seq ^ o] for o in order], axis=0)
    return cosine, sine


def heads_to_rows(x, g):
    return jnp.concatenate(
        [x[:, HEAD_DIM * h : HEAD_DIM * (h + 1)] for h in range(GROUP * g, GROUP * (g + 1))], axis=0
    )


def rows_to_heads(parts, length):
    return jnp.concatenate(
        [p[length * r : length * (r + 1)] for p in parts for r in range(GROUP)], axis=1
    )


def attention_forward(order, length, seq_ref, blocks, wq, wkv, bq, bkv, gain, cos, sin, mask,
                      att_o, q_o, k_o, v_o):
    seq = seq_ref[0]
    cosine, sine = tables(seq, order, cos, sin)
    width = gain.shape[1]
    for b in range(blocks.shape[1] // length):
        x = blocks[:, b * length : (b + 1) * length, :width].astype(F32)
        x = x.reshape(len(order) * length, width)
        first = (norm_parts(x)[1] * gain[...]).astype(BF)
        kv = dot(first, wkv[...], 1, 0) + bkv[...]
        q = dot(first[:length], wq[...], 1, 0) + bq[...]
        q = jnp.concatenate(turn(q, cosine[:length], sine[:length]), axis=1).astype(BF)
        q = q * jnp.asarray(HEAD_DIM ** (-0.5), BF)
        kv = turn_kv(kv, cosine, sine).astype(BF)
        allowed = jnp.concatenate([mask[b]] * GROUP, axis=0) > 0.0
        parts = []
        for g in range(KV_HEADS):
            qg = heads_to_rows(q, g)
            kg = kv[:, HEAD_DIM * g : HEAD_DIM * (g + 1)]
            vg = kv[:, KW + HEAD_DIM * g : KW + HEAD_DIM * (g + 1)]
            q_o[b, g] = qg
            k_o[b, g] = kg
            v_o[b, g] = vg
            scores = jnp.where(allowed, dot(qg, kg, 1, 1), MASKED)
            top = jnp.max(scores, axis=-1, keepdims=True)
            e = jnp.exp(scores - top)
            total = jnp.sum(e, axis=-1, keepdims=True)
            probs = (e * (1.0 / total)).astype(BF)
            parts.append(dot(probs, vg, 1, 0))
        att_o[b * length : (b + 1) * length, :] = rows_to_heads(parts, length).astype(BF)


def feed_forward(attended, source, wo, wgu, wd, gain, cot, weight,
                 out_o, down_o, gu_o, mid_o, wout_o, attg_o, gain_o):
    units = wd.shape[0]
    step = units // 3
    att = attended[...]
    middle = source[...].astype(F32) + dot(att, wo[...], 1, 0)
    scale_two, normed = norm_parts(middle)
    g2 = gain[...]
    second = (normed * g2).astype(BF)
    out_grad = cot[...].astype(F32) * weight[...]
    feed_grad = out_grad.astype(BF)
    feed = None
    back = None
    for j in range(0, units, step):
        wg = wgu[:, j : j + step]
        wu = wgu[:, units + j : units + j + step]
        wdj = wd[j : j + step, :]
        gate = dot(second, wg, 1, 0)
        up = dot(second, wu, 1, 0)
        sig = jax.nn.sigmoid(gate)
        act = gate * sig
        product = (act * up).astype(BF)
        part = dot(product, wdj, 1, 0)
        feed = part if feed is None else feed + part
        down_o[j : j + step, :] = dot(product, feed_grad, 0, 0).astype(BF)
        pgrad = dot(feed_grad, wdj, 1, 1)
        ggrad = (pgrad * up * (sig * (1.0 + gate * (1.0 - sig)))).astype(BF)
        ugrad = (pgrad * act).astype(BF)
        gu_o[:, j : j + step] = dot(second, ggrad, 0, 0).astype(BF)
        gu_o[:, units + j : units + j + step] = dot(second, ugrad, 0, 0).astype(BF)
        part = dot(ggrad, wg, 1, 1) + dot(ugrad, wu, 1, 1)
        back = part if back is None else back + part
    out_o[...] = (middle + feed).astype(BF)
    gain_o[...] = jnp.sum(back * normed, axis=0, keepdims=True)
    middle_grad = out_grad + norm_back(back, g2, scale_two, normed)
    mid_o[...] = middle_grad
    branch = middle_grad.astype(BF)
    wout_o[...] = dot(att, branch, 0, 0).astype(BF)
    attg_o[...] = dot(branch, wo[...], 1, 1).astype(BF)


def attention_backward(order, length, seq_ref, blocks, wq, wkv, gain, cos, sin, mask, q_i, k_i, v_i,
                       attg, dq_o, dkv_o, wgrad_o, bias_o, gain_o):
    seq = seq_ref[0]
    cosine, sine = tables(seq, order, cos, sin)
    width = gain.shape[1]
    q_wgrad = kv_wgrad = bias_q = bias_kv = gain_sum = None
    for b in range(blocks.shape[1] // length):
        x = blocks[:, b * length : (b + 1) * length, :width].astype(F32)
        x = x.reshape(len(order) * length, width)
        normed = norm_parts(x)[1]
        first = (normed * gain[...]).astype(BF)
        allowed = jnp.concatenate([mask[b]] * GROUP, axis=0) > 0.0
        ag = attg[b * length : (b + 1) * length, :]
        dqs, dks, dvs = [], [], []
        for g in range(KV_HEADS):
            qg, kg, vg = q_i[b, g], k_i[b, g], v_i[b, g]
            agg = heads_to_rows(ag, g)
            scores = jnp.where(allowed, dot(qg, kg, 1, 1), MASKED)
            e = jnp.exp(scores - jnp.max(scores, axis=-1, keepdims=True))
            p = e * (1.0 / jnp.sum(e, axis=-1, keepdims=True))
            dvs.append(dot(p.astype(BF), agg, 0, 0))
            pg = dot(agg, vg, 1, 1)
            inner = jnp.sum(p * pg, axis=-1, keepdims=True)
            ds = (p * (pg - inner)).astype(BF)
            dqs.append(dot(ds, kg, 1, 0) * HEAD_DIM ** (-0.5))
            dks.append(dot(ds, qg, 0, 0))
        dq = rows_to_heads(dqs, length)
        dq = jnp.concatenate([dq, jnp.zeros((length, 64), F32)], axis=1)
        dq = jnp.concatenate(turn(dq, cosine[:length], -sine[:length]), axis=1).astype(BF)
        dkv = jnp.concatenate(dks + dvs, axis=1)
        dkv = turn_kv(dkv, cosine, -sine).astype(BF)
        dq_o[b * length : (b + 1) * length, :] = dq
        for r in range(len(order)):
            dkv_o[r, b * length : (b + 1) * length, :] = dkv[r * length : (r + 1) * length, :]
        wq_part = dot(first[:length], dq, 0, 0)
        wkv_part = dot(first, dkv, 0, 0)
        bq_part = jnp.sum(dq.astype(F32), axis=0, keepdims=True)
        bkv_part = jnp.sum(dkv.astype(F32), axis=0, keepdims=True)
        e_kv = dot(dkv, wkv[...], 1, 1) * normed
        e_q = dot(dq[:, :QW], wq[:, :QW], 1, 1) * normed[:length]
        g_part = jnp.sum(e_kv, axis=0, keepdims=True) + jnp.sum(e_q, axis=0, keepdims=True)
        if q_wgrad is None:
            q_wgrad, kv_wgrad, bias_q, bias_kv, gain_sum = wq_part, wkv_part, bq_part, bkv_part, g_part
        else:
            q_wgrad, kv_wgrad = q_wgrad + wq_part, kv_wgrad + wkv_part
            bias_q, bias_kv, gain_sum = bias_q + bq_part, bias_kv + bkv_part, gain_sum + g_part
    wgrad_o[...] = jnp.concatenate([q_wgrad[:, :QW], kv_wgrad], axis=1).astype(BF)
    bias_o[...] = jnp.concatenate([bias_q[:, :QW], bias_kv], axis=1)
    gain_o[...] = gain_sum


def input_gradient(dq, own, a, b, c, source, mid, wq, wkv, gain, out_o):
    kv = own[...].astype(F32) + a[...].astype(F32) + b[...].astype(F32) + c[...].astype(F32)
    first_grad = dot(dq[:, :QW], wq[:, :QW], 1, 1) + dot(kv.astype(BF), wkv[...], 1, 1)
    scale_one, normed = norm_parts(source[...].astype(F32))
    out_o[...] = mid[...] + norm_back(first_grad, gain[...], scale_one, normed)

def chosen(flag, a, b):
    return jnp.where(flag != 0, b, a)


class Blocks:
    def __init__(self, *refs):
        self.refs = refs
        self.shape = (len(refs),) + refs[0].shape

    def __getitem__(self, key):
        return jnp.stack([ref[key[1:]] for ref in self.refs])


def cut_qkv(core_bit, meta, w_hbm, bias_hbm, gains_hbm, out_o, w, bias, gains, all_s, sems):
    pairs = ((w_hbm, w), (bias_hbm, bias), (gains_hbm, gains))
    copies = [pltpu.make_async_copy(a, b, sems.at[i]) for i, (a, b) in enumerate(pairs)]
    for copy in copies:
        copy.start()
    for copy in copies:
        copy.wait()
    rows = w.shape[0]
    n = bias.shape[1]
    all_s[:rows, :] = w[...].astype(F32)
    all_s[rows:, :] = jnp.zeros((8, w.shape[1]), F32)
    all_s[rows : rows + 1, :n] = bias[...].astype(F32)
    for i in range(2):
        all_s[rows : rows + 1, n + rows * i : n + rows * (i + 1)] = gains[i : i + 1, :].astype(F32)
    half = out_o.shape[0]
    at = pl.multiple_of((meta[0] & core_bit) * half, 8)
    out_o[...] = all_s[pl.ds(at, half), :].astype(BF)


def first_forward(order, length, d_rows, n_bias, meta, b0, b1, b2, b3, a00, a10, a01, a11, cos, sin, mask,
                  att_o, q_o, k_o, v_o, w_o, gain_o, w_s, b_s):
    blocks = Blocks(b0, b1, b2, b3)
    core, x = meta[0] & 1, meta[1] & 1
    cut = a00.shape[2]
    for x_rel, c_rel, piece in ((0, 0, a00), (1, 0, a10), (0, 1, a01), (1, 1, a11)):
        for z0 in range(2):
            for z1 in range(2):
                at = (z1 * 4 + z0 * 2 + (x ^ x_rel)) * 2 * cut + (core ^ c_rel) * cut
                w_s[pl.ds(pl.multiple_of(at, 8), cut), :] = piece[z0, z1].astype(F32)
    n_f = w_s.shape[0] // (2 * cut)
    starts = [2 * cut * f for f in range(n_f)]
    w_o[...] = jnp.concatenate([w_s[at : at + d_rows, :] for at in starts], axis=0).astype(BF)
    lines = [w_s[at + d_rows : at + d_rows + 1, :] for at in starts]
    b_s[...] = jnp.concatenate([line[:, :n_bias] for line in lines], axis=1)
    for i in range(2):
        at = n_bias + d_rows * i
        gain_o[i : i + 1, :] = jnp.concatenate([line[:, at : at + d_rows] for line in lines], axis=1)
    wide = QW + 64
    attention_forward(order, length, meta, blocks, w_o[:, :wide], w_o[:, QW:], b_s[:, :wide], b_s[:, QW:],
                      gain_o[0:1, :], cos, sin, mask, att_o, q_o, k_o, v_o)


def turned(out, value):
    length = out.shape[2]
    for b in range(out.shape[0]):
        out[b] = value[length * b : length * (b + 1)].T.astype(out.dtype)


def rel(meta, f):
    r = f ^ meta[1]
    return r & 1, (r >> 1) & 1, (r >> 2) & 1


def fetch_pieces(meta, refs, b_s, g_s, sems):
    core, y, x, z0 = meta[0] & 1, (meta[0] >> 1) & 1, meta[1] & 1, (meta[1] >> 1) & 1
    copies = []
    for i in range(8):
        at = (z0 ^ (i >> 2), x ^ ((i >> 1) & 1), core ^ (i & 1))
        copies.append(pltpu.make_async_copy(refs[i], b_s.at[at], sems.at[i]))
    for i in range(8):
        at = (y ^ ((i >> 1) & 1), core ^ (i & 1), x ^ (i >> 2))
        copies.append(pltpu.make_async_copy(refs[8 + i], g_s.at[at], sems.at[8 + i]))
    for copy in copies:
        copy.start()
    return copies


def feed_forward_pieces(d_rows, ff_rows, meta, attended, source, gains, cot, weight, *refs):
    out_o, ak_o, ag_o, bk_o, bg_o, dk_o, dg_o, mid_o, attg_o, gain_o, down_s, wout_s, b_s, g_s, sems = refs[16:]
    copies = fetch_pieces(meta, refs, b_s, g_s, sems)
    core, y = meta[0] & 1, (meta[0] >> 1) & 1
    part_d = ff_rows // 4
    part_o = d_rows // 3
    cut = b_s.shape[4] - ff_rows // 2
    half = g_s.shape[-1] // 2
    for copy in copies[:8]:
        copy.wait()
    wo = []
    for f in range(8):
        for c in range(2):
            rows = b_s[(f >> 1) & 1, f & 1, c, f >> 2, ff_rows // 2 :, :].astype(F32)
            wo.append(rows if c == 0 else rows[: d_rows - cut])
    wo = jnp.concatenate(wo, axis=0).astype(BF)
    att = attended[...]
    middle = source[...].astype(F32) + dot(att, wo, 1, 0)
    scale_two, normed = norm_parts(middle)
    g2 = gains[1:2, :]
    second = (normed * g2).astype(BF)
    out_grad = cot[...].astype(F32) * weight[...]
    feed_grad = out_grad.astype(BF)
    for copy in copies[8:]:
        copy.wait()
    feed = back = None
    for c_rel in (1, 0):
        h = core ^ c_rel
        weights = []
        for yy in range(2):
            rows = [g_s[yy, h, f & 1, (f >> 1) & 1, f >> 2].astype(F32) for f in range(8)]
            weights.append(jnp.concatenate(rows, axis=0).astype(BF))
        wg, wu = weights
        wd = [b_s[i >> 1, i & 1, c, h, : ff_rows // 2, :] for i in range(4) for c in range(2)]
        wd = jnp.concatenate(wd, axis=0)
        gate = dot(second, wg, 1, 0)
        up = dot(second, wu, 1, 0)
        sig = jax.nn.sigmoid(gate)
        act = gate * sig
        product = (act * up).astype(BF)
        part = dot(product, wd, 1, 0)
        feed = part if feed is None else feed + part
        down_s[...] = dot(product, feed_grad, 0, 0)
        pgrad = dot(feed_grad, wd, 1, 1)
        ggrad = (pgrad * up * (sig * (1.0 + gate * (1.0 - sig)))).astype(BF)
        ugrad = (pgrad * act).astype(BF)
        part = dot(ggrad, wg, 1, 1) + dot(ugrad, wu, 1, 1)
        back = part if back is None else back + part
        for i in range(4):
            x, z0, z1 = rel(meta, 4 * h + i)
            for yy in range(2):
                for c_to, to in ((0, dk_o), (1, dg_o)):
                    at = pl.multiple_of(i * ff_rows + (yy * 2 + (core ^ c_to)) * part_d, 16)
                    to[y ^ yy, x, z0, z1, :part_d, :] = down_s[pl.ds(at, part_d), :].astype(BF)
        to_a, to_b = (ag_o, bg_o) if c_rel else (ak_o, bk_o)
        for yy, grad in ((0, ggrad), (1, ugrad)):
            wgrad = dot(second, grad, 0, 0)
            for f in range(8):
                x, z0, z1 = rel(meta, f)
                block = wgrad[d_rows * f : d_rows * (f + 1), :].astype(BF)
                to_a[x, z0, z1, yy] = block[:, :half]
                to_b[z0, z1, x, yy] = block[:, half:]
    turned(out_o, middle + feed)
    gain_o[...] = jnp.sum(back * normed, axis=0, keepdims=True)
    middle_grad = out_grad + norm_back(back, g2, scale_two, normed)
    mid_o[...] = middle_grad
    branch = middle_grad.astype(BF)
    attg_o[...] = dot(branch, wo, 1, 1).astype(BF)
    wout = dot(att, branch, 0, 0)
    for f in range(8):
        wout_s[f, :d_rows, :] = wout[d_rows * f : d_rows * (f + 1), :]
        wout_s[f, d_rows:, :] = jnp.zeros((part_o, wout.shape[1]), F32)
    for f in range(8):
        x, z0, z1 = rel(meta, f)
        for yy in range(2):
            for c_to, to in ((0, dk_o), (1, dg_o)):
                at = pl.multiple_of((yy * 2 + (core ^ c_to)) * part_o, 8)
                to[y ^ yy, x, z0, z1, part_d:, :] = wout_s[f, pl.ds(at, part_o), :].astype(BF)


def attention_backward_pieces(order, length, d_rows, meta, b0, b1, b2, b3, w, gains, cos, sin, mask, q_i, k_i, v_i,
                              attg, gain_two, dq_o, dk_o, dg_o, rk_o, rg_o, w_s, bias_s, gain_s, small_s):
    blocks = Blocks(b0, b1, b2, b3)
    half = len(order) // 2

    class Pieces:
        def __setitem__(self, key, value):
            ref = dk_o if key[0] < half else dg_o
            ref[(key[0] % half,) + key[1:]] = value

    class Wgrad:
        def __setitem__(self, key, value):
            w_s[:, : 2 * KW] = value[:, QW:].astype(F32)
            w_s[:, 2 * KW : 2 * KW + QW] = value[:, :QW].astype(F32)
            w_s[:, 2 * KW + QW :] = jnp.zeros((value.shape[0], 64), F32)

    wide = QW + 64
    attention_backward(order, length, meta, blocks, w[:, :wide], w[:, QW:], gains[0:1, :], cos, sin, mask,
                       q_i, k_i, v_i, attg, dq_o, Pieces(), Wgrad(), bias_s, gain_s)
    n_f = small_s.shape[0]
    qk, v = (QW + KW) // n_f, KW // n_f
    bias, g1, g2 = bias_s[...], gain_s[...], gain_two[...]
    for f in range(n_f):
        line = jnp.concatenate(
            [
                bias[:, qk * f : qk * (f + 1)],
                bias[:, QW + KW + v * f : QW + KW + v * (f + 1)],
                g1[:, d_rows * f : d_rows * (f + 1)],
                jnp.zeros((1, 256 - qk - v - d_rows), F32),
                g2[:, d_rows * f : d_rows * (f + 1)],
                jnp.zeros((1, 768 - d_rows), F32),
            ],
            axis=1,
        )
        small_s[f] = jnp.broadcast_to(line, (8, 1024))
    core, y = meta[0] & 1, (meta[0] >> 1) & 1
    for f in range(n_f):
        x, z0, z1 = rel(meta, f)
        for yy in range(2):
            for c_to, to in ((0, rk_o), (1, rg_o)):
                at = pl.multiple_of((yy * 2 + (core ^ c_to)) * 256, 256)
                block = [w_s[d_rows * f : d_rows * (f + 1), pl.ds(at, 256)], small_s[f, :, pl.ds(at, 256)]]
                to[y ^ yy, x, z0, z1] = jnp.concatenate(block, axis=0).astype(BF)


def input_gradient_two(dq, own, other, source, mid, w, gains, out_o):
    kv = (own[...].astype(F32) + other[...].astype(F32)).astype(BF)
    first_grad = dot(dq[:, :QW], w[:, :QW], 1, 1) + dot(kv, w[:, QW:], 1, 1)
    scale_one, normed = norm_parts(source[...].astype(F32))
    turned(out_o, mid[...] + norm_back(first_grad, gains[0:1, :], scale_one, normed))


def place_gate(meta, near, far, out_o, parts=1, part=0):
    core = meta[0] & 1
    n = near.shape[2]
    for pieces, c_rel in ((near, 0), (far, 1)):
        for yy in range(2):
            at = pl.multiple_of(((yy * 2 + (core ^ c_rel)) * parts + part) * n, 128)
            out_o[:, pl.ds(at, n)] = pieces[yy].astype(F32)


def place_down(part_d, meta, p00, p10, p01, p11, out_o, wout_o):
    seq = meta[0]
    part_o = p00.shape[0] - part_d
    for piece, o in ((p00[...], 0), (p10[...], 2), (p01[...], 1), (p11[...], 3)):
        piece = piece.astype(F32)
        to = seq ^ o
        out_o[pl.ds(pl.multiple_of(to * part_d, 16), part_d), :] = piece[:part_d]

        @pl.when(to < 3)
        def _():
            wout_o[pl.ds(pl.multiple_of(to * part_o, 8), part_o), :] = piece[part_d:]


def place_qkv(qk, v, meta, p00, p10, p01, p11, w_o, bqk_o, bv_o, gains_o, all_s):
    n = p00.shape[1]
    for piece, o in ((p00, 0), (p10, 2), (p01, 1), (p11, 3)):
        all_s[:, pl.ds(pl.multiple_of((meta[0] ^ o) * n, 128), n)] = piece[...].astype(F32)
    d_rows = w_o.shape[0]
    w_o[:, :QW] = all_s[:d_rows, 2 * KW : 2 * KW + QW]
    w_o[:, QW:] = all_s[:d_rows, : 2 * KW]
    line = all_s[d_rows : d_rows + 1, :]
    bqk_o[...] = line[:, :qk]
    bv_o[...] = line[:, qk : qk + v]
    gains_o[0:1, :] = line[:, qk + v : qk + v + d_rows]
    gains_o[1:2, :] = line[:, 256 : 256 + d_rows]


def place_all(part_d, qk, v, meta, a_near, a_far, b_near, b_far, d0, d1, d2, d3, r0, r1, far,
              gate_o, down_o, wout_o, w_o, bqk_o, bv_o, gains_o, all_s):
    place_gate(meta, a_near, a_far, gate_o, 2, 0)
    place_gate(meta, b_near, b_far, gate_o, 2, 1)
    place_down(part_d, meta, d0, d1, d2, d3, down_o, wout_o)
    place_qkv(qk, v, meta, r0, r1, far.at[0], far.at[1], w_o, bqk_o, bv_o, gains_o, all_s)


class Net:
    def __init__(self, n_fsdp, n_seq):
        self.n_fsdp, self.n_seq = n_fsdp, n_seq
        self.total = n_fsdp * n_seq
        f, s = lax.axis_index("fsdp"), lax.axis_index("seq")
        self.index = f * n_seq + s
        self.seq_bits = [1 << b for b in range(n_seq.bit_length() - 1)]
        self.fsdp_bits = [n_seq << b for b in range(n_fsdp.bit_length() - 1)]

    def swap(self, value, mask):
        pairs = [(i, i ^ mask) for i in range(self.total)]
        return lax.ppermute(value, ("fsdp", "seq"), pairs)

    def bit(self, mask):
        return (self.index & mask) != 0

    def both(self, mine, mask, axis, other=None):
        other = self.swap(mine, mask) if other is None else other
        high = self.bit(mask)
        return jnp.stack([jnp.where(high, other, mine), jnp.where(high, mine, other)], axis=axis)

    def half(self, value, mask, axis):
        return lax.dynamic_index_in_dim(
            value, self.bit(mask).astype(jnp.int32), axis, keepdims=False
        )

    def add_half(self, value, mask, axis):
        mine = self.bit(mask).astype(jnp.int32)
        keep = lax.dynamic_index_in_dim(value, mine, axis, keepdims=False)
        give = lax.dynamic_index_in_dim(value, 1 - mine, axis, keepdims=False)
        got = self.swap(give, mask)
        return (keep.astype(F32) + got.astype(F32)).astype(value.dtype)

    def gather_fsdp(self, value):
        for step, mask in enumerate(reversed(self.fsdp_bits)):
            value = self.both(value, mask, step)
        return value

    def scatter_fsdp(self, value, first_axis=0):
        count = len(self.fsdp_bits)
        for step, mask in enumerate(self.fsdp_bits):
            value = self.add_half(value, mask, first_axis + count - 1 - step)
        return value


def on_device(
    hidden, w_qkv, b_qkv, w_out, w_gate_up, w_down, norm_gains, segment_ids, token_counts, cotangent,
    n_fsdp, n_seq,
):
    net = Net(n_fsdp, n_seq)
    micro, batch, length, width = hidden.shape
    full_length = length * n_seq
    tokens_micro = batch * n_fsdp * full_length
    scale = HEAD_DIM ** (-0.5)
    rows = micro * batch * length
    d_rows = w_qkv.shape[0]
    ff_rows = w_down.shape[0]
    units = w_gate_up.shape[1] // 2
    qkv_w = w_qkv.shape[1]
    core = net.seq_bits[0]
    f_lead = (2,) * len(net.fsdp_bits)

    ids = segment_ids.reshape(rows, 1).astype(BF)
    block = jnp.concatenate(
        [hidden.reshape(rows, width), jnp.broadcast_to(ids, (rows, 64))], axis=1
    )
    blocks = block[None]
    for mask in reversed(net.seq_bits):
        blocks = jnp.concatenate([blocks, net.swap(blocks, mask)], axis=0)
    order = [0]
    for mask in reversed(net.seq_bits):
        order = order + [o ^ mask for o in order]
    seq_index = lax.axis_index("seq")
    block_ids = [seq_index ^ o for o in order]

    pad_rows = -(d_rows + 1) % 16 + 1
    extra = jnp.zeros((pad_rows, qkv_w), BF)
    small = jnp.concatenate([b_qkv, norm_gains.reshape(-1)])
    extra = extra.at[0, : small.shape[0]].set(small)
    shard_a = jnp.concatenate([w_qkv, extra], axis=0).reshape(2, -1, qkv_w)
    got_a = net.gather_fsdp(net.half(shard_a, core, 0))
    full_a = net.both(got_a, core, len(f_lead)).reshape(n_fsdp, d_rows + pad_rows, qkv_w)
    wf_qkv = full_a[:, :d_rows].reshape(n_fsdp * d_rows, qkv_w)
    smalls = full_a[:, d_rows]
    n_bias = b_qkv.shape[0]
    bias = smalls[:, :n_bias].reshape(-1).astype(F32)
    gains = smalls[:, n_bias : n_bias + 2 * d_rows].reshape(n_fsdp, 2, d_rows).astype(F32)
    gain_one = gains[:, 0].reshape(-1)
    gain_two = gains[:, 1].reshape(-1)

    pad_b = -(d_rows + ff_rows) % 16
    shard_b = jnp.concatenate([w_out, w_down, jnp.zeros((pad_b, width), BF)], axis=0)
    shard_b = shard_b.reshape(2, -1, width)
    got_b = net.gather_fsdp(net.half(shard_b, core, 0))

    parts = n_seq
    shard_c = w_gate_up.reshape(d_rows, parts, -1)
    got_c = net.gather_fsdp(lax.dynamic_index_in_dim(shard_c, seq_index, 1, keepdims=False))
    full_b = net.both(got_b, core, len(f_lead)).reshape(n_fsdp, -1, width)
    wf_out = full_b[:, :d_rows].reshape(n_fsdp * d_rows, width)
    wf_down = full_b[:, d_rows : d_rows + ff_rows].reshape(n_fsdp * ff_rows, width)
    got_c = got_c.reshape(n_fsdp * d_rows, -1)
    for mask in reversed(net.seq_bits):
        got_c = net.both(got_c, mask, got_c.ndim - 1)
    wf_gate_up = got_c.reshape(n_fsdp * d_rows, 2 * units)

    places = np.arange(full_length, dtype=np.float32)
    speeds = np.power(ROPE_BASE, -2.0 * np.arange(HEAD_DIM // 2, dtype=np.float32) / HEAD_DIM)
    angles = places[:, None] * speeds.astype(np.float32)[None, :]
    cos_t = np.tile(np.cos(angles), (1, 4)).reshape(n_seq, length, 128)
    sin_t = np.concatenate([-np.sin(angles), np.sin(angles)] * 2, axis=1).reshape(n_seq, length, 128)
    cos_t, sin_t = jnp.asarray(cos_t, F32), jnp.asarray(sin_t, F32)
    seqs = micro * batch
    seg_all = blocks[..., width].reshape(n_seq, seqs, length).transpose(1, 0, 2)
    own_places = seq_index * length + jnp.arange(length, dtype=jnp.int32)
    key_places = jnp.stack(block_ids)[:, None] * length + jnp.arange(length, dtype=jnp.int32)
    allowed = (seg_all[:, 0, :, None] == seg_all.reshape(seqs, 1, -1)) & (
        own_places[None, :, None] >= key_places.reshape(1, 1, -1)
    )
    allowed = allowed.astype(F32)
    seq_scalar = seq_index.astype(jnp.int32).reshape(1)
    wq, wkv = wf_qkv[:, : QW + 64], wf_qkv[:, QW:]
    gain_one, gain_two = gain_one[None], gain_two[None]
    source = hidden.reshape(rows, width)
    n_all = n_seq * rows
    attended, q_s, k_s, v_s = call(
        functools.partial(attention_forward, order, length),
        [seq_scalar],
        [blocks, wq, wkv, bias[None, : QW + 64], bias[None, QW:], gain_one, cos_t, sin_t, allowed],
        [
            sds((rows, QW), BF),
            sds((seqs, KV_HEADS, GROUP * length, HEAD_DIM), BF),
            sds((seqs, KV_HEADS, full_length, HEAD_DIM), BF),
            sds((seqs, KV_HEADS, full_length, HEAD_DIM), BF),
        ],
        2 * n_all * width * 2 * KW + 2 * rows * width * QW + 4 * rows * full_length * QW,
    )

    weight = tokens_micro / token_counts.astype(F32)
    weight = jnp.repeat(weight, batch * length)[:, None]
    block_out, down_grad, gate_up_wgrad, middle_grad, out_wgrad, attended_grad, gain_two_grad = call(
        feed_forward,
        [],
        [attended, source, wf_out, wf_gate_up, wf_down, gain_two, cotangent.reshape(rows, width), weight],
        [
            sds((rows, width), BF),
            sds((units, width), BF),
            sds((width, 2 * units), BF),
            sds((rows, width), F32),
            sds((QW, width), BF),
            sds((rows, QW), BF),
            sds((1, width), F32),
        ],
        6 * rows * width * 3 * units + 6 * rows * width * QW,
    )
    block_out = block_out.reshape(hidden.shape)

    def seq_axes(value, axis, masks):
        for mask in masks:
            value = net.add_half(value, mask, axis)
        return value

    quarter = (2,) * len(net.seq_bits)
    n_f = len(f_lead)
    red_down = down_grad.reshape(f_lead + quarter + (ff_rows // n_seq, width))
    for step, mask in enumerate(net.seq_bits):
        red_down = net.add_half(red_down, mask, n_f + len(quarter) - 1 - step)
    red_down = net.scatter_fsdp(red_down)

    red_gate = gate_up_wgrad.reshape(f_lead + (d_rows,) + quarter + (2 * units // n_seq,))
    red_gate = net.add_half(red_gate, core, n_f + len(quarter))
    red_gate = net.add_half(red_gate, net.fsdp_bits[0], n_f - 1)
    for step, mask in enumerate(net.seq_bits[1:]):
        red_gate = net.add_half(red_gate, mask, n_f - 1 + len(quarter) - 1 - step)
    for step, mask in enumerate(net.fsdp_bits[1:]):
        red_gate = net.add_half(red_gate, mask, n_f - 2 - step)

    dq, dkv, qkv_wgrad, bias_grad, gain_one_grad = call(
        functools.partial(attention_backward, order, length),
        [seq_scalar],
        [blocks, wq, wkv, gain_one, cos_t, sin_t, allowed, q_s, k_s, v_s, attended_grad],
        [
            sds((rows, QW + 64), BF),
            sds((n_seq, rows, 2 * KW), BF),
            sds((width, qkv_w), BF),
            sds((1, qkv_w), F32),
            sds((1, width), F32),
        ],
        4 * n_all * width * 2 * KW + 4 * rows * width * QW + 10 * rows * full_length * QW,
    )
    kv_parts = [dkv[0]]
    for place, mask_bits in enumerate(order):
        if mask_bits:
            kv_parts.append(net.swap(dkv[place], mask_bits))
    (hidden_grad,) = call(
        input_gradient,
        [],
        [dq, *kv_parts, source, middle_grad, wq, wkv, gain_one],
        [sds((rows, width), F32)],
        2 * rows * width * qkv_w,
    )
    hidden_grad = hidden_grad.reshape(hidden.shape)
    bias_grad, gain_one_grad, gain_two_grad = bias_grad[0], gain_one_grad[0], gain_two_grad[0]

    qk_rows, v_rows = (QW + KW) // n_fsdp, KW // n_fsdp
    small_grads = jnp.concatenate(
        [
            bias_grad[: QW + KW].reshape(n_fsdp, qk_rows),
            bias_grad[QW + KW :].reshape(n_fsdp, v_rows),
            gain_one_grad.reshape(n_fsdp, d_rows),
            gain_two_grad.reshape(n_fsdp, d_rows),
        ],
        axis=1,
    ).astype(BF)
    wide = qkv_w + width
    small_pad = jnp.zeros((n_fsdp, pad_rows, wide), BF)
    small_pad = small_pad.at[:, 0, : small_grads.shape[1]].set(small_grads)
    rest = jnp.concatenate([qkv_wgrad, out_wgrad], axis=1)
    rest = jnp.concatenate([rest.reshape(n_fsdp, d_rows, wide), small_pad], axis=1)
    rest = rest.reshape(f_lead + (d_rows + pad_rows,) + quarter + (wide // n_seq,))
    for step, mask in enumerate(net.seq_bits):
        rest = net.add_half(rest, mask, n_f + 1 + len(quarter) - 1 - step)
    rest = net.scatter_fsdp(rest)

    def seq_back(value, axis):
        for step, mask in enumerate(reversed(net.seq_bits)):
            value = net.both(value, mask, axis + step)
        return value

    out_down = seq_back(red_down, 0).reshape(ff_rows, width).astype(F32)
    out_gate = seq_back(red_gate, 1).reshape(d_rows, 2 * units).astype(F32)
    out_rest = seq_back(rest, 1).reshape(d_rows + pad_rows, wide).astype(F32)
    line = out_rest[d_rows]
    edge = qk_rows + v_rows
    return (
        block_out,
        hidden_grad,
        out_rest[:d_rows, :qkv_w],
        line[:qk_rows],
        line[qk_rows:edge],
        out_rest[:d_rows, qkv_w:],
        out_gate,
        out_down,
        line[edge : edge + 2 * d_rows].reshape(2, d_rows),
    )


def after(value, *others):
    return lax.optimization_barrier((value, *others))[0]


def rope_tables(full_length, n_seq):
    places = np.arange(full_length, dtype=np.float32)
    speeds = np.power(ROPE_BASE, -2.0 * np.arange(HEAD_DIM // 2, dtype=np.float32) / HEAD_DIM)
    angles = places[:, None] * speeds.astype(np.float32)[None, :]
    cos_t = np.tile(np.cos(angles), (1, 4)).reshape(n_seq, -1, 128)
    sin_t = np.concatenate([-np.sin(angles), np.sin(angles)] * 2, axis=1).reshape(n_seq, -1, 128)
    return jnp.asarray(cos_t, F32), jnp.asarray(sin_t, F32)


def on_device_tiled(
    hidden, w_qkv, b_qkv, w_out, w_gate_up, w_down, norm_gains, segment_ids, token_counts, cotangent,
    n_fsdp, n_seq,
):
    net = Net(n_fsdp, n_seq)
    micro, batch, length, width = hidden.shape
    full_length = length * n_seq
    tokens_micro = batch * n_fsdp * full_length
    rows = micro * batch * length
    seqs = micro * batch
    d_rows, qkv_w = w_qkv.shape
    ff_rows = w_down.shape[0]
    units = w_gate_up.shape[1] // 2
    n_bias = b_qkv.shape[0]
    core, ybit = net.seq_bits
    xbit, znear, zfar = net.fsdp_bits
    order = [0, 2, 1, 3]
    seq_index = lax.axis_index("seq")
    meta = jnp.stack([seq_index, lax.axis_index("fsdp")]).astype(jnp.int32)
    source = hidden.reshape(rows, width)

    small = [w_qkv, b_qkv[None], norm_gains]
    a0 = pl.pallas_call(
        functools.partial(cut_qkv, core),
        out_shape=sds(((d_rows + 8) // 2, qkv_w), BF),
        in_specs=[pl.BlockSpec(memory_space=pltpu.SMEM)] + [pl.BlockSpec(memory_space=pltpu.HBM)] * 3,
        out_specs=pl.BlockSpec(memory_space=pltpu.VMEM),
        scratch_shapes=[
            *[pltpu.VMEM(v.shape, BF) for v in small],
            pltpu.VMEM((d_rows + 8, qkv_w), F32),
            pltpu.SemaphoreType.DMA((3,)),
        ],
        compiler_params=pltpu.CompilerParams(vmem_limit_bytes=52 * 1024 * 1024),
    )(meta, *small)
    a1 = net.both(a0, zfar, 0)

    ids = segment_ids.reshape(rows, 1).astype(BF)
    block = jnp.concatenate([source, jnp.broadcast_to(ids, (rows, 64))], axis=1)
    block = after(block, a0)
    block_y = net.swap(block, ybit)
    block_c = net.swap(block, core)

    quarter = 2 * units // n_seq
    gu0 = lax.dynamic_slice_in_dim(after(w_gate_up, a0), seq_index * quarter, quarter, axis=1)
    half_b = jnp.concatenate(
        [
            w_down.reshape(2, ff_rows // 2, width),
            jnp.concatenate([w_out, jnp.zeros((8, width), BF)], axis=0).reshape(2, -1, width),
        ],
        axis=1,
    )
    a2 = net.both(a1, znear, 0)
    a_x = net.swap(a2, xbit)
    a_c = net.swap(a2, core)
    gu1 = net.both(gu0, zfar, 0)
    gu2 = net.both(after(gu1, a2), znear, 0)
    block_yc = net.swap(block_y, core)
    a_xc = net.swap(a_x, core)
    gu_x = net.swap(gu2, xbit)
    gu_y = net.swap(gu2, ybit)
    gu_c = net.swap(gu2, core)
    b0 = net.half(after(half_b, a1), core, 0)
    b1 = net.both(b0, zfar, 0, after(net.swap(b0, zfar), a2))
    b_x = net.swap(b1, xbit)
    b_z = net.swap(after(b1, gu2), znear)
    b_c = net.swap(b1, core)
    a_xc = after(a_xc, gu2, b1)

    cos_t, sin_t = rope_tables(full_length, n_seq)
    block_ids = [seq_index ^ o for o in order]
    blocks = [block, block_y, block_c, block_yc]
    seg_all = jnp.stack([b[:, width].reshape(seqs, length) for b in blocks], axis=1)
    own_places = seq_index * length + jnp.arange(length, dtype=jnp.int32)
    key_places = jnp.stack(block_ids)[:, None] * length + jnp.arange(length, dtype=jnp.int32)
    allowed = (seg_all[:, 0, :, None] == seg_all.reshape(seqs, 1, -1)) & (
        own_places[None, :, None] >= key_places.reshape(1, 1, -1)
    )
    allowed = allowed.astype(F32)
    attended, q_s, k_s, v_s, wf, gains = call(
        functools.partial(first_forward, order, length, d_rows, n_bias),
        [meta],
        [*blocks, a2, a_x, a_c, a_xc, cos_t, sin_t, allowed],
        [
            sds((rows, QW), BF),
            sds((seqs, KV_HEADS, GROUP * length, HEAD_DIM), BF),
            sds((seqs, KV_HEADS, full_length, HEAD_DIM), BF),
            sds((seqs, KV_HEADS, full_length, HEAD_DIM), BF),
            sds((width, qkv_w), BF),
            sds((2, width), F32),
        ],
        1.2e10,
        [(n_fsdp * (d_rows + 8), qkv_w), (1, qkv_w)],
    )
    gu_y = after(gu_y, attended)
    gu_x, b_z, b_x = after(gu_x, gu_y), after(b_z, gu_y), after(b_x, gu_y)
    gu_xy = net.swap(gu_x, ybit)
    b_zx = net.swap(b_z, xbit)
    gu_yc = net.swap(gu_y, core)
    gu_xc = net.swap(gu_x, core)
    b_zc = net.swap(b_z, core)
    b_xc = net.swap(b_x, core)
    b_zxc = net.swap(b_zx, core)
    gu_xyc = net.swap(gu_xy, core)
    pieces = [b1, b_c, b_x, b_xc, b_z, b_zc, b_zx, b_zxc]
    pieces += [gu2, gu_c, gu_y, gu_yc, gu_x, gu_xc, gu_xy, gu_xyc]

    weight = tokens_micro / token_counts.astype(F32)
    weight = jnp.repeat(weight, batch * length)[:, None]
    lead = (2, 2, 2, 2)
    cot = cotangent.reshape(rows, width)
    gate_lead = lead + (d_rows, units // 4)
    block_out, a_keep, a_give, b_keep, b_give, down_keep, down_give, middle_grad, attended_grad, gain_two = call(
        functools.partial(feed_forward_pieces, d_rows, ff_rows),
        [meta],
        [attended, source, gains, cot, weight],
        [
            sds((seqs, width, length), BF),
            sds(gate_lead, BF),
            sds(gate_lead, BF),
            sds(gate_lead, BF),
            sds(gate_lead, BF),
            sds(lead + (ff_rows // 4 + d_rows // 3, width), BF),
            sds(lead + (ff_rows // 4 + d_rows // 3, width), BF),
            sds((rows, width), F32),
            sds((rows, QW), BF),
            sds((1, width), F32),
        ],
        1.4e10,
        [(units // 2, width), (n_fsdp, d_rows + d_rows // 3, width)],
        fetched=pieces,
        landing=[(2, 2, 2, 2) + b1.shape[1:], (2, 2, 2, 2, 2, d_rows, units // 2)],
    )
    block_out = block_out.reshape(micro, batch, width, length).swapaxes(2, 3)

    def add(keep, got):
        return (keep.astype(F32) + got.astype(F32)).astype(BF)

    def halves(keep, got):
        return add(keep[0], got[0]), add(keep[1], got[1])

    down_got = net.swap(down_give, core)
    a_got = net.swap(after(a_give, down_got), core)
    b_got = net.swap(after(b_give, down_got), core)
    a_give, a_core = add(a_keep[1], a_got[1]), a_got
    b_give, b_core = add(b_keep[1], b_got[1]), b_got
    down_give, down_core = add(down_keep[1], down_got[1]), down_got
    a_got = net.swap(a_give, xbit)
    b_got = net.swap(b_give, znear)
    down_got = net.swap(down_give, ybit)
    attended_grad = after(attended_grad, a_give, b_give, down_give)

    dq, dkv_keep, dkv_give, rest_keep, rest_give = call(
        functools.partial(attention_backward_pieces, order, length, d_rows),
        [meta],
        [*blocks, wf, gains, cos_t, sin_t, allowed, q_s, k_s, v_s, attended_grad, gain_two],
        [
            sds((rows, QW + 64), BF),
            sds((2, rows, 2 * KW), BF),
            sds((2, rows, 2 * KW), BF),
            sds(lead + (d_rows + 8, 256), BF),
            sds(lead + (d_rows + 8, 256), BF),
        ],
        1.4e10,
        [(width, 1024), (1, qkv_w), (1, width), (n_fsdp, 8, 1024)],
        24,
    )
    a = add(a_keep[0], after(a_core, dq)[0])
    b = add(b_keep[0], after(b_core, dq)[0])
    down = add(down_keep[0], after(down_core, dq)[0])
    b, b_give = halves(b, after(b_got, dq))
    a, a_give = halves(a, after(a_got, b_give))
    b_got = net.swap(b_give, zfar)
    a_got = net.swap(a_give, znear)
    rest, rest_give = halves(rest_keep, after(net.swap(rest_give, core), b_give, down_got))
    rest_got = net.swap(rest_give, ybit)
    down, down_give = halves(down, after(down_got, rest_give))
    down_got = net.swap(down_give, xbit)
    dkv, dkv_give = halves(dkv_keep, after(net.swap(dkv_give, core), down_give))
    dkv_got = net.swap(dkv_give, ybit)
    a, a_give = halves(a, after(a_got, dkv_give))
    a_got = net.swap(a_give, zfar)
    rest, rest_give = halves(rest, after(rest_got, a_give))
    rest_got = net.swap(rest_give, xbit)
    b, b_give = halves(b, after(b_got, rest_give))
    b_got = net.swap(b_give, xbit)
    down, down_give = halves(down, after(down_got, b_give))
    down_got = net.swap(down_give, znear)
    rest, rest_give = halves(rest, after(rest_got, down_give))
    rest_got = net.swap(rest_give, znear)
    (hidden_grad,) = call(
        input_gradient_two,
        [],
        [dq, dkv, after(dkv_got, rest_give), source, middle_grad, wf, gains],
        [sds((seqs, width, length), F32)],
        3e9,
        mib=16,
    )
    a_got = after(a_got, hidden_grad)
    hidden_grad = hidden_grad.reshape(micro, batch, width, length).swapaxes(2, 3)
    a = add(a, a_got)
    a_got = net.swap(a, ybit)
    b = add(b, after(b_got, a))
    b_got = net.swap(b, ybit)
    down, down_give = halves(down, after(down_got, b))
    down_got = net.swap(down_give, zfar)
    rest, rest_give = halves(rest, after(rest_got, down_give))
    rest_got = net.swap(rest_give, zfar)
    a = add(a, after(a_got, rest_give))
    a_far = net.swap(a, core)
    b = add(b, b_got)
    b_far = net.swap(b, core)
    down = add(down, after(down_got, a))
    down_y = net.swap(down, ybit)
    down_c = net.swap(after(down, down_y), core)
    rest = add(rest, after(rest_got, down))
    rest_y = net.swap(rest, ybit)
    down_yc = net.swap(after(down_y, rest_y), core)
    rest_far = net.swap(jnp.stack([rest, rest_y]), core)
    qk, v = (QW + KW) // n_fsdp, KW // n_fsdp
    out_gate, out_down, out_wout, out_qkv, b_qk, b_v, out_gains = call(
        functools.partial(place_all, ff_rows // 4, qk, v),
        [meta],
        [a, a_far, b, b_far, down, down_y, down_c, down_yc, rest, rest_y, rest_far],
        [
            sds((d_rows, 2 * units), F32),
            sds((ff_rows, width), F32),
            sds((d_rows, width), F32),
            sds((d_rows, qkv_w), F32),
            sds((1, qk), F32),
            sds((1, v), F32),
            sds((2, d_rows), F32),
        ],
        3e9,
        [(d_rows + 8, 1024)],
        16,
    )
    return (
        block_out,
        hidden_grad,
        out_qkv,
        b_qk.reshape(qk),
        b_v.reshape(v),
        out_wout,
        out_gate,
        out_down,
        out_gains,
    )


def solution(mesh):
    n_fsdp, n_seq = mesh.shape["fsdp"], mesh.shape["seq"]
    in_specs = (
        P(None, "fsdp", "seq", None),
        P("fsdp", None),
        P("fsdp"),
        P("fsdp", None),
        P("fsdp", None),
        P("fsdp", None),
        P(None, "fsdp"),
        P(None, "fsdp", "seq"),
        P(),
        P(None, "fsdp", "seq", None),
    )
    out_specs = (
        P(None, "fsdp", "seq", None),
        P(None, "fsdp", "seq", None),
        P("fsdp", None),
        P("fsdp"),
        P("fsdp"),
        P("fsdp", None),
        P("fsdp", None),
        P("fsdp", None),
        P(None, "fsdp"),
    )

    def local(*args):
        body = on_device_tiled if (n_fsdp, n_seq) == (8, 4) else on_device
        return body(*args, n_fsdp=n_fsdp, n_seq=n_seq)

    return jax.shard_map(local, mesh=mesh, in_specs=in_specs, out_specs=out_specs, check_vma=False)
```

```python
import functools

import jax
import jax.numpy as jnp
import numpy as np
from jax import lax
from jax.experimental import pallas as pl
from jax.experimental.pallas import tpu as pltpu
from jax.sharding import PartitionSpec as P

HEADS = 9
KV_HEADS = 3
HEAD_DIM = 64
GROUP = HEADS // KV_HEADS
QW = HEADS * HEAD_DIM
KW = KV_HEADS * HEAD_DIM
EPS = 1e-05
ROPE_BASE = 100000.0
MASKED = -1000000000.0
BF = jnp.bfloat16
F32 = jnp.float32


def dot(a, b, ca, cb):
    return lax.dot_general(a, b, (((ca,), (cb,)), ((), ())), preferred_element_type=F32)


def rotary(values, cosine, sine):
    half = values.shape[-1] // 2
    a, b = values[..., :half], values[..., half:]
    return jnp.concatenate([a * cosine - b * sine, b * cosine + a * sine], axis=-1)


def norm_parts(values):
    factor = lax.rsqrt(jnp.mean(values * values, axis=-1, keepdims=True) + EPS)
    return factor, values * factor


def norm_back(grad_in, gain, factor, normed):
    scaled = grad_in * gain
    return factor * (scaled - normed * jnp.mean(scaled * normed, axis=-1, keepdims=True))


def whole(*shape_dtypes):
    return [pl.BlockSpec(memory_space=pltpu.VMEM) for _ in shape_dtypes]


def call(kernel, scalars, arrays, outs, flops, scratch=(), mib=52, fetched=(), landing=()):
    specs = [pl.BlockSpec(memory_space=pltpu.SMEM)] * len(scalars) + whole(*arrays)
    specs += [pl.BlockSpec(memory_space=pltpu.HBM)] * len(fetched)
    arrays = [*arrays, *fetched]
    moved = sum(a.size * a.dtype.itemsize for a in arrays) + sum(
        int(np.prod(o.shape)) * o.dtype.itemsize for o in outs
    )
    return pl.pallas_call(
        kernel,
        out_shape=outs,
        in_specs=specs,
        out_specs=whole(*outs),
        scratch_shapes=[
            *[pltpu.VMEM(shape, F32) for shape in scratch],
            *[pltpu.VMEM(shape, BF) for shape in landing],
            *([pltpu.SemaphoreType.DMA((len(fetched),))] if fetched else []),
        ],
        compiler_params=pltpu.CompilerParams(vmem_limit_bytes=mib * 1024 * 1024),
        cost_estimate=pl.CostEstimate(flops=int(flops), bytes_accessed=moved, transcendentals=0),
    )(*scalars, *arrays)


def sds(shape, dtype):
    return jax.ShapeDtypeStruct(shape, dtype)


def turn(x, cosine, sine):
    tiles = []
    low = lax.broadcasted_iota(jnp.int32, (1, 128), 1) % HEAD_DIM < HEAD_DIM // 2
    for t in range(x.shape[1] // 128):
        part = x[:, 128 * t : 128 * t + 128]
        other = jnp.where(low, pltpu.roll(part, 96, 1), pltpu.roll(part, 32, 1))
        tiles.append(part * cosine + other * sine)
    return tiles


def turn_kv(x, cosine, sine):
    lane = lax.broadcasted_iota(jnp.int32, (1, 128), 1)
    first, second = turn(x[:, :256], cosine, sine)
    second = jnp.where(lane < KW - 128, second, x[:, 128:256])
    return jnp.concatenate([first, second, x[:, 256:]], axis=1)


def tables(seq, order, cos_ref, sin_ref):
    cosine = jnp.concatenate([cos_ref[seq ^ o] for o in order], axis=0)
    sine = jnp.concatenate([sin_ref[seq ^ o] for o in order], axis=0)
    return cosine, sine


def heads_to_rows(x, g):
    return jnp.concatenate(
        [x[:, HEAD_DIM * h : HEAD_DIM * (h + 1)] for h in range(GROUP * g, GROUP * (g + 1))], axis=0
    )


def rows_to_heads(parts, length):
    return jnp.concatenate(
        [p[length * r : length * (r + 1)] for p in parts for r in range(GROUP)], axis=1
    )


def attention_forward(order, length, seq_ref, blocks, wq, wkv, bq, bkv, gain, cos, sin, mask,
                      att_o, q_o, k_o, v_o):
    seq = seq_ref[0]
    cosine, sine = tables(seq, order, cos, sin)
    width = gain.shape[1]
    for b in range(blocks.shape[1] // length):
        x = blocks[:, b * length : (b + 1) * length, :width].astype(F32)
        x = x.reshape(len(order) * length, width)
        first = (norm_parts(x)[1] * gain[...]).astype(BF)
        kv = dot(first, wkv[...], 1, 0) + bkv[...]
        q = dot(first[:length], wq[...], 1, 0) + bq[...]
        q = jnp.concatenate(turn(q, cosine[:length], sine[:length]), axis=1).astype(BF)
        q = q * jnp.asarray(HEAD_DIM ** (-0.5), BF)
        kv = turn_kv(kv, cosine, sine).astype(BF)
        allowed = jnp.concatenate([mask[b]] * GROUP, axis=0) > 0.0
        parts = []
        for g in range(KV_HEADS):
            qg = heads_to_rows(q, g)
            kg = kv[:, HEAD_DIM * g : HEAD_DIM * (g + 1)]
            vg = kv[:, KW + HEAD_DIM * g : KW + HEAD_DIM * (g + 1)]
            q_o[b, g] = qg
            k_o[b, g] = kg
            v_o[b, g] = vg
            scores = jnp.where(allowed, dot(qg, kg, 1, 1), MASKED)
            top = jnp.max(scores, axis=-1, keepdims=True)
            e = jnp.exp(scores - top)
            total = jnp.sum(e, axis=-1, keepdims=True)
            probs = (e * (1.0 / total)).astype(BF)
            parts.append(dot(probs, vg, 1, 0))
        att_o[b * length : (b + 1) * length, :] = rows_to_heads(parts, length).astype(BF)


def feed_forward(attended, source, wo, wgu, wd, gain, cot, weight,
                 out_o, down_o, gu_o, mid_o, wout_o, attg_o, gain_o):
    units = wd.shape[0]
    step = units // 3
    att = attended[...]
    middle = source[...].astype(F32) + dot(att, wo[...], 1, 0)
    scale_two, normed = norm_parts(middle)
    g2 = gain[...]
    second = (normed * g2).astype(BF)
    out_grad = cot[...].astype(F32) * weight[...]
    feed_grad = out_grad.astype(BF)
    feed = None
    back = None
    for j in range(0, units, step):
        wg = wgu[:, j : j + step]
        wu = wgu[:, units + j : units + j + step]
        wdj = wd[j : j + step, :]
        gate = dot(second, wg, 1, 0)
        up = dot(second, wu, 1, 0)
        sig = jax.nn.sigmoid(gate)
        act = gate * sig
        product = (act * up).astype(BF)
        part = dot(product, wdj, 1, 0)
        feed = part if feed is None else feed + part
        down_o[j : j + step, :] = dot(product, feed_grad, 0, 0).astype(BF)
        pgrad = dot(feed_grad, wdj, 1, 1)
        ggrad = (pgrad * up * (sig * (1.0 + gate * (1.0 - sig)))).astype(BF)
        ugrad = (pgrad * act).astype(BF)
        gu_o[:, j : j + step] = dot(second, ggrad, 0, 0).astype(BF)
        gu_o[:, units + j : units + j + step] = dot(second, ugrad, 0, 0).astype(BF)
        part = dot(ggrad, wg, 1, 1) + dot(ugrad, wu, 1, 1)
        back = part if back is None else back + part
    out_o[...] = (middle + feed).astype(BF)
    gain_o[...] = jnp.sum(back * normed, axis=0, keepdims=True)
    middle_grad = out_grad + norm_back(back, g2, scale_two, normed)
    mid_o[...] = middle_grad
    branch = middle_grad.astype(BF)
    wout_o[...] = dot(att, branch, 0, 0).astype(BF)
    attg_o[...] = dot(branch, wo[...], 1, 1).astype(BF)


def attention_backward(order, length, seq_ref, blocks, wq, wkv, gain, cos, sin, mask, q_i, k_i, v_i,
                       attg, dq_o, dkv_o, wgrad_o, bias_o, gain_o):
    seq = seq_ref[0]
    cosine, sine = tables(seq, order, cos, sin)
    width = gain.shape[1]
    q_wgrad = kv_wgrad = bias_q = bias_kv = gain_sum = None
    for b in range(blocks.shape[1] // length):
        x = blocks[:, b * length : (b + 1) * length, :width].astype(F32)
        x = x.reshape(len(order) * length, width)
        normed = norm_parts(x)[1]
        first = (normed * gain[...]).astype(BF)
        allowed = jnp.concatenate([mask[b]] * GROUP, axis=0) > 0.0
        ag = attg[b * length : (b + 1) * length, :]
        dqs, dks, dvs = [], [], []
        for g in range(KV_HEADS):
            qg, kg, vg = q_i[b, g], k_i[b, g], v_i[b, g]
            agg = heads_to_rows(ag, g)
            scores = jnp.where(allowed, dot(qg, kg, 1, 1), MASKED)
            e = jnp.exp(scores - jnp.max(scores, axis=-1, keepdims=True))
            p = e * (1.0 / jnp.sum(e, axis=-1, keepdims=True))
            dvs.append(dot(p.astype(BF), agg, 0, 0))
            pg = dot(agg, vg, 1, 1)
            inner = jnp.sum(p * pg, axis=-1, keepdims=True)
            ds = (p * (pg - inner)).astype(BF)
            dqs.append(dot(ds, kg, 1, 0) * HEAD_DIM ** (-0.5))
            dks.append(dot(ds, qg, 0, 0))
        dq = rows_to_heads(dqs, length)
        dq = jnp.concatenate([dq, jnp.zeros((length, 64), F32)], axis=1)
        dq = jnp.concatenate(turn(dq, cosine[:length], -sine[:length]), axis=1).astype(BF)
        dkv = jnp.concatenate(dks + dvs, axis=1)
        dkv = turn_kv(dkv, cosine, -sine).astype(BF)
        dq_o[b * length : (b + 1) * length, :] = dq
        for r in range(len(order)):
            dkv_o[r, b * length : (b + 1) * length, :] = dkv[r * length : (r + 1) * length, :]
        wq_part = dot(first[:length], dq, 0, 0)
        wkv_part = dot(first, dkv, 0, 0)
        bq_part = jnp.sum(dq.astype(F32), axis=0, keepdims=True)
        bkv_part = jnp.sum(dkv.astype(F32), axis=0, keepdims=True)
        e_kv = dot(dkv, wkv[...], 1, 1) * normed
        e_q = dot(dq[:, :QW], wq[:, :QW], 1, 1) * normed[:length]
        g_part = jnp.sum(e_kv, axis=0, keepdims=True) + jnp.sum(e_q, axis=0, keepdims=True)
        if q_wgrad is None:
            q_wgrad, kv_wgrad, bias_q, bias_kv, gain_sum = wq_part, wkv_part, bq_part, bkv_part, g_part
        else:
            q_wgrad, kv_wgrad = q_wgrad + wq_part, kv_wgrad + wkv_part
            bias_q, bias_kv, gain_sum = bias_q + bq_part, bias_kv + bkv_part, gain_sum + g_part
    wgrad_o[...] = jnp.concatenate([q_wgrad[:, :QW], kv_wgrad], axis=1).astype(BF)
    bias_o[...] = jnp.concatenate([bias_q[:, :QW], bias_kv], axis=1)
    gain_o[...] = gain_sum


def input_gradient(dq, own, a, b, c, source, mid, wq, wkv, gain, out_o):
    kv = own[...].astype(F32) + a[...].astype(F32) + b[...].astype(F32) + c[...].astype(F32)
    first_grad = dot(dq[:, :QW], wq[:, :QW], 1, 1) + dot(kv.astype(BF), wkv[...], 1, 1)
    scale_one, normed = norm_parts(source[...].astype(F32))
    out_o[...] = mid[...] + norm_back(first_grad, gain[...], scale_one, normed)

def chosen(flag, a, b):
    return jnp.where(flag != 0, b, a)


class Blocks:
    def __init__(self, *refs):
        self.refs = refs
        self.shape = (len(refs),) + refs[0].shape

    def __getitem__(self, key):
        return jnp.stack([ref[key[1:]] for ref in self.refs])


def cut_qkv(core_bit, meta, w_hbm, bias_hbm, gains_hbm, out_o, w, bias, gains, all_s, sems):
    pairs = ((w_hbm, w), (bias_hbm, bias), (gains_hbm, gains))
    copies = [pltpu.make_async_copy(a, b, sems.at[i]) for i, (a, b) in enumerate(pairs)]
    for copy in copies:
        copy.start()
    for copy in copies:
        copy.wait()
    rows = w.shape[0]
    n = bias.shape[1]
    all_s[:rows, :] = w[...].astype(F32)
    all_s[rows:, :] = jnp.zeros((8, w.shape[1]), F32)
    all_s[rows : rows + 1, :n] = bias[...].astype(F32)
    for i in range(2):
        all_s[rows : rows + 1, n + rows * i : n + rows * (i + 1)] = gains[i : i + 1, :].astype(F32)
    half = out_o.shape[0]
    at = pl.multiple_of((meta[0] & core_bit) * half, 8)
    out_o[...] = all_s[pl.ds(at, half), :].astype(BF)


def first_forward(order, length, d_rows, n_bias, meta, b0, b1, b2, b3, a00, a10, a01, a11, cos, sin, mask,
                  att_o, q_o, k_o, v_o, w_o, gain_o, w_s, b_s):
    blocks = Blocks(b0, b1, b2, b3)
    core, x = meta[0] & 1, meta[1] & 1
    cut = a00.shape[2]
    for x_rel, c_rel, piece in ((0, 0, a00), (1, 0, a10), (0, 1, a01), (1, 1, a11)):
        for z0 in range(2):
            for z1 in range(2):
                at = (z1 * 4 + z0 * 2 + (x ^ x_rel)) * 2 * cut + (core ^ c_rel) * cut
                w_s[pl.ds(pl.multiple_of(at, 8), cut), :] = piece[z0, z1].astype(F32)
    n_f = w_s.shape[0] // (2 * cut)
    starts = [2 * cut * f for f in range(n_f)]
    w_o[...] = jnp.concatenate([w_s[at : at + d_rows, :] for at in starts], axis=0).astype(BF)
    lines = [w_s[at + d_rows : at + d_rows + 1, :] for at in starts]
    b_s[...] = jnp.concatenate([line[:, :n_bias] for line in lines], axis=1)
    for i in range(2):
        at = n_bias + d_rows * i
        gain_o[i : i + 1, :] = jnp.concatenate([line[:, at : at + d_rows] for line in lines], axis=1)
    wide = QW + 64
    attention_forward(order, length, meta, blocks, w_o[:, :wide], w_o[:, QW:], b_s[:, :wide], b_s[:, QW:],
                      gain_o[0:1, :], cos, sin, mask, att_o, q_o, k_o, v_o)


def turned(out, value):
    length = out.shape[2]
    for b in range(out.shape[0]):
        out[b] = value[length * b : length * (b + 1)].T.astype(out.dtype)


def rel(meta, f):
    r = f ^ meta[1]
    return r & 1, (r >> 1) & 1, (r >> 2) & 1


def fetch_pieces(meta, refs, b_s, g_s, sems):
    core, y, x, z0 = meta[0] & 1, (meta[0] >> 1) & 1, meta[1] & 1, (meta[1] >> 1) & 1
    copies = []
    for i in range(8):
        at = (z0 ^ (i >> 2), x ^ ((i >> 1) & 1), core ^ (i & 1))
        copies.append(pltpu.make_async_copy(refs[i], b_s.at[at], sems.at[i]))
    for i in range(8):
        at = (y ^ ((i >> 1) & 1), core ^ (i & 1), x ^ (i >> 2))
        copies.append(pltpu.make_async_copy(refs[8 + i], g_s.at[at], sems.at[8 + i]))
    for copy in copies:
        copy.start()
    return copies


def feed_forward_pieces(d_rows, ff_rows, meta, attended, source, gains, cot, weight, *refs):
    out_o, ak_o, ag_o, bk_o, bg_o, dk_o, dg_o, mid_o, attg_o, gain_o, down_s, wout_s, b_s, g_s, sems = refs[16:]
    copies = fetch_pieces(meta, refs, b_s, g_s, sems)
    core, y = meta[0] & 1, (meta[0] >> 1) & 1
    part_d = ff_rows // 4
    part_o = d_rows // 3
    cut = b_s.shape[4] - ff_rows // 2
    half = g_s.shape[-1] // 2
    for copy in copies[:8]:
        copy.wait()
    wo = []
    for f in range(8):
        for c in range(2):
            rows = b_s[(f >> 1) & 1, f & 1, c, f >> 2, ff_rows // 2 :, :].astype(F32)
            wo.append(rows if c == 0 else rows[: d_rows - cut])
    wo = jnp.concatenate(wo, axis=0).astype(BF)
    att = attended[...]
    middle = source[...].astype(F32) + dot(att, wo, 1, 0)
    scale_two, normed = norm_parts(middle)
    g2 = gains[1:2, :]
    second = (normed * g2).astype(BF)
    out_grad = cot[...].astype(F32) * weight[...]
    feed_grad = out_grad.astype(BF)
    for copy in copies[8:]:
        copy.wait()
    feed = back = None
    for c_rel in (1, 0):
        h = core ^ c_rel
        weights = []
        for yy in range(2):
            rows = [g_s[yy, h, f & 1, (f >> 1) & 1, f >> 2].astype(F32) for f in range(8)]
            weights.append(jnp.concatenate(rows, axis=0).astype(BF))
        wg, wu = weights
        wd = [b_s[i >> 1, i & 1, c, h, : ff_rows // 2, :] for i in range(4) for c in range(2)]
        wd = jnp.concatenate(wd, axis=0)
        gate = dot(second, wg, 1, 0)
        up = dot(second, wu, 1, 0)
        sig = jax.nn.sigmoid(gate)
        act = gate * sig
        product = (act * up).astype(BF)
        part = dot(product, wd, 1, 0)
        feed = part if feed is None else feed + part
        down_s[...] = dot(product, feed_grad, 0, 0)
        pgrad = dot(feed_grad, wd, 1, 1)
        ggrad = (pgrad * up * (sig * (1.0 + gate * (1.0 - sig)))).astype(BF)
        ugrad = (pgrad * act).astype(BF)
        part = dot(ggrad, wg, 1, 1) + dot(ugrad, wu, 1, 1)
        back = part if back is None else back + part
        for i in range(4):
            x, z0, z1 = rel(meta, 4 * h + i)
            for yy in range(2):
                for c_to, to in ((0, dk_o), (1, dg_o)):
                    at = pl.multiple_of(i * ff_rows + (yy * 2 + (core ^ c_to)) * part_d, 16)
                    to[y ^ yy, x, z0, z1, :part_d, :] = down_s[pl.ds(at, part_d), :].astype(BF)
        to_a, to_b = (ag_o, bg_o) if c_rel else (ak_o, bk_o)
        for yy, grad in ((0, ggrad), (1, ugrad)):
            wgrad = dot(second, grad, 0, 0)
            for f in range(8):
                x, z0, z1 = rel(meta, f)
                block = wgrad[d_rows * f : d_rows * (f + 1), :].astype(BF)
                to_a[x, z0, z1, yy] = block[:, :half]
                to_b[z0, z1, x, yy] = block[:, half:]
    turned(out_o, middle + feed)
    gain_o[...] = jnp.sum(back * normed, axis=0, keepdims=True)
    middle_grad = out_grad + norm_back(back, g2, scale_two, normed)
    mid_o[...] = middle_grad
    branch = middle_grad.astype(BF)
    attg_o[...] = dot(branch, wo, 1, 1).astype(BF)
    wout = dot(att, branch, 0, 0)
    for f in range(8):
        wout_s[f, :d_rows, :] = wout[d_rows * f : d_rows * (f + 1), :]
        wout_s[f, d_rows:, :] = jnp.zeros((part_o, wout.shape[1]), F32)
    for f in range(8):
        x, z0, z1 = rel(meta, f)
        for yy in range(2):
            for c_to, to in ((0, dk_o), (1, dg_o)):
                at = pl.multiple_of((yy * 2 + (core ^ c_to)) * part_o, 8)
                to[y ^ yy, x, z0, z1, part_d:, :] = wout_s[f, pl.ds(at, part_o), :].astype(BF)


def attention_backward_pieces(order, length, d_rows, meta, b0, b1, b2, b3, w, gains, cos, sin, mask, q_i, k_i, v_i,
                              attg, gain_two, dq_o, dk_o, dg_o, rk_o, rg_o, w_s, bias_s, gain_s, small_s):
    blocks = Blocks(b0, b1, b2, b3)
    half = len(order) // 2

    class Pieces:
        def __setitem__(self, key, value):
            ref = dk_o if key[0] < half else dg_o
            ref[(key[0] % half,) + key[1:]] = value

    class Wgrad:
        def __setitem__(self, key, value):
            w_s[:, : 2 * KW] = value[:, QW:].astype(F32)
            w_s[:, 2 * KW : 2 * KW + QW] = value[:, :QW].astype(F32)
            w_s[:, 2 * KW + QW :] = jnp.zeros((value.shape[0], 64), F32)

    wide = QW + 64
    attention_backward(order, length, meta, blocks, w[:, :wide], w[:, QW:], gains[0:1, :], cos, sin, mask,
                       q_i, k_i, v_i, attg, dq_o, Pieces(), Wgrad(), bias_s, gain_s)
    n_f = small_s.shape[0]
    qk, v = (QW + KW) // n_f, KW // n_f
    bias, g1, g2 = bias_s[...], gain_s[...], gain_two[...]
    for f in range(n_f):
        line = jnp.concatenate(
            [
                bias[:, qk * f : qk * (f + 1)],
                bias[:, QW + KW + v * f : QW + KW + v * (f + 1)],
                g1[:, d_rows * f : d_rows * (f + 1)],
                jnp.zeros((1, 256 - qk - v - d_rows), F32),
                g2[:, d_rows * f : d_rows * (f + 1)],
                jnp.zeros((1, 768 - d_rows), F32),
            ],
            axis=1,
        )
        small_s[f] = jnp.broadcast_to(line, (8, 1024))
    core, y = meta[0] & 1, (meta[0] >> 1) & 1
    for f in range(n_f):
        x, z0, z1 = rel(meta, f)
        for yy in range(2):
            for c_to, to in ((0, rk_o), (1, rg_o)):
                at = pl.multiple_of((yy * 2 + (core ^ c_to)) * 256, 256)
                block = [w_s[d_rows * f : d_rows * (f + 1), pl.ds(at, 256)], small_s[f, :, pl.ds(at, 256)]]
                to[y ^ yy, x, z0, z1] = jnp.concatenate(block, axis=0).astype(BF)


def input_gradient_two(dq, own, other, source, mid, w, gains, out_o):
    kv = (own[...].astype(F32) + other[...].astype(F32)).astype(BF)
    first_grad = dot(dq[:, :QW], w[:, :QW], 1, 1) + dot(kv, w[:, QW:], 1, 1)
    scale_one, normed = norm_parts(source[...].astype(F32))
    turned(out_o, mid[...] + norm_back(first_grad, gains[0:1, :], scale_one, normed))


def place_gate(meta, near, far, out_o, parts=1, part=0):
    core = meta[0] & 1
    n = near.shape[2]
    for pieces, c_rel in ((near, 0), (far, 1)):
        for yy in range(2):
            at = pl.multiple_of(((yy * 2 + (core ^ c_rel)) * parts + part) * n, 128)
            out_o[:, pl.ds(at, n)] = pieces[yy].astype(F32)


def place_down(part_d, meta, p00, p10, p01, p11, out_o, wout_o):
    seq = meta[0]
    part_o = p00.shape[0] - part_d
    for piece, o in ((p00[...], 0), (p10[...], 2), (p01[...], 1), (p11[...], 3)):
        piece = piece.astype(F32)
        to = seq ^ o
        out_o[pl.ds(pl.multiple_of(to * part_d, 16), part_d), :] = piece[:part_d]

        @pl.when(to < 3)
        def _():
            wout_o[pl.ds(pl.multiple_of(to * part_o, 8), part_o), :] = piece[part_d:]


def place_qkv(qk, v, meta, p00, p10, p01, p11, w_o, bqk_o, bv_o, gains_o, all_s):
    n = p00.shape[1]
    for piece, o in ((p00, 0), (p10, 2), (p01, 1), (p11, 3)):
        all_s[:, pl.ds(pl.multiple_of((meta[0] ^ o) * n, 128), n)] = piece[...].astype(F32)
    d_rows = w_o.shape[0]
    w_o[:, :QW] = all_s[:d_rows, 2 * KW : 2 * KW + QW]
    w_o[:, QW:] = all_s[:d_rows, : 2 * KW]
    line = all_s[d_rows : d_rows + 1, :]
    bqk_o[...] = line[:, :qk]
    bv_o[...] = line[:, qk : qk + v]
    gains_o[0:1, :] = line[:, qk + v : qk + v + d_rows]
    gains_o[1:2, :] = line[:, 256 : 256 + d_rows]


def place_all(part_d, qk, v, meta, a_near, a_far, b_near, b_far, d0, d1, d2, d3, r0, r1, far,
              gate_o, down_o, wout_o, w_o, bqk_o, bv_o, gains_o, all_s):
    place_gate(meta, a_near, a_far, gate_o, 2, 0)
    place_gate(meta, b_near, b_far, gate_o, 2, 1)
    place_down(part_d, meta, d0, d1, d2, d3, down_o, wout_o)
    place_qkv(qk, v, meta, r0, r1, far.at[0], far.at[1], w_o, bqk_o, bv_o, gains_o, all_s)


class Net:
    def __init__(self, n_fsdp, n_seq):
        self.n_fsdp, self.n_seq = n_fsdp, n_seq
        self.total = n_fsdp * n_seq
        f, s = lax.axis_index("fsdp"), lax.axis_index("seq")
        self.index = f * n_seq + s
        self.seq_bits = [1 << b for b in range(n_seq.bit_length() - 1)]
        self.fsdp_bits = [n_seq << b for b in range(n_fsdp.bit_length() - 1)]

    def swap(self, value, mask):
        pairs = [(i, i ^ mask) for i in range(self.total)]
        return lax.ppermute(value, ("fsdp", "seq"), pairs)

    def bit(self, mask):
        return (self.index & mask) != 0

    def both(self, mine, mask, axis, other=None):
        other = self.swap(mine, mask) if other is None else other
        high = self.bit(mask)
        return jnp.stack([jnp.where(high, other, mine), jnp.where(high, mine, other)], axis=axis)

    def half(self, value, mask, axis):
        return lax.dynamic_index_in_dim(
            value, self.bit(mask).astype(jnp.int32), axis, keepdims=False
        )

    def add_half(self, value, mask, axis):
        mine = self.bit(mask).astype(jnp.int32)
        keep = lax.dynamic_index_in_dim(value, mine, axis, keepdims=False)
        give = lax.dynamic_index_in_dim(value, 1 - mine, axis, keepdims=False)
        got = self.swap(give, mask)
        return (keep.astype(F32) + got.astype(F32)).astype(value.dtype)

    def gather_fsdp(self, value):
        for step, mask in enumerate(reversed(self.fsdp_bits)):
            value = self.both(value, mask, step)
        return value

    def scatter_fsdp(self, value, first_axis=0):
        count = len(self.fsdp_bits)
        for step, mask in enumerate(self.fsdp_bits):
            value = self.add_half(value, mask, first_axis + count - 1 - step)
        return value


def on_device(
    hidden, w_qkv, b_qkv, w_out, w_gate_up, w_down, norm_gains, segment_ids, token_counts, cotangent,
    n_fsdp, n_seq,
):
    net = Net(n_fsdp, n_seq)
    micro, batch, length, width = hidden.shape
    full_length = length * n_seq
    tokens_micro = batch * n_fsdp * full_length
    scale = HEAD_DIM ** (-0.5)
    rows = micro * batch * length
    d_rows = w_qkv.shape[0]
    ff_rows = w_down.shape[0]
    units = w_gate_up.shape[1] // 2
    qkv_w = w_qkv.shape[1]
    core = net.seq_bits[0]
    f_lead = (2,) * len(net.fsdp_bits)

    ids = segment_ids.reshape(rows, 1).astype(BF)
    block = jnp.concatenate(
        [hidden.reshape(rows, width), jnp.broadcast_to(ids, (rows, 64))], axis=1
    )
    blocks = block[None]
    for mask in reversed(net.seq_bits):
        blocks = jnp.concatenate([blocks, net.swap(blocks, mask)], axis=0)
    order = [0]
    for mask in reversed(net.seq_bits):
        order = order + [o ^ mask for o in order]
    seq_index = lax.axis_index("seq")
    block_ids = [seq_index ^ o for o in order]

    pad_rows = -(d_rows + 1) % 16 + 1
    extra = jnp.zeros((pad_rows, qkv_w), BF)
    small = jnp.concatenate([b_qkv, norm_gains.reshape(-1)])
    extra = extra.at[0, : small.shape[0]].set(small)
    shard_a = jnp.concatenate([w_qkv, extra], axis=0).reshape(2, -1, qkv_w)
    got_a = net.gather_fsdp(net.half(shard_a, core, 0))
    full_a = net.both(got_a, core, len(f_lead)).reshape(n_fsdp, d_rows + pad_rows, qkv_w)
    wf_qkv = full_a[:, :d_rows].reshape(n_fsdp * d_rows, qkv_w)
    smalls = full_a[:, d_rows]
    n_bias = b_qkv.shape[0]
    bias = smalls[:, :n_bias].reshape(-1).astype(F32)
    gains = smalls[:, n_bias : n_bias + 2 * d_rows].reshape(n_fsdp, 2, d_rows).astype(F32)
    gain_one = gains[:, 0].reshape(-1)
    gain_two = gains[:, 1].reshape(-1)

    pad_b = -(d_rows + ff_rows) % 16
    shard_b = jnp.concatenate([w_out, w_down, jnp.zeros((pad_b, width), BF)], axis=0)
    shard_b = shard_b.reshape(2, -1, width)
    got_b = net.gather_fsdp(net.half(shard_b, core, 0))

    parts = n_seq
    shard_c = w_gate_up.reshape(d_rows, parts, -1)
    got_c = net.gather_fsdp(lax.dynamic_index_in_dim(shard_c, seq_index, 1, keepdims=False))
    full_b = net.both(got_b, core, len(f_lead)).reshape(n_fsdp, -1, width)
    wf_out = full_b[:, :d_rows].reshape(n_fsdp * d_rows, width)
    wf_down = full_b[:, d_rows : d_rows + ff_rows].reshape(n_fsdp * ff_rows, width)
    got_c = got_c.reshape(n_fsdp * d_rows, -1)
    for mask in reversed(net.seq_bits):
        got_c = net.both(got_c, mask, got_c.ndim - 1)
    wf_gate_up = got_c.reshape(n_fsdp * d_rows, 2 * units)

    places = np.arange(full_length, dtype=np.float32)
    speeds = np.power(ROPE_BASE, -2.0 * np.arange(HEAD_DIM // 2, dtype=np.float32) / HEAD_DIM)
    angles = places[:, None] * speeds.astype(np.float32)[None, :]
    cos_t = np.tile(np.cos(angles), (1, 4)).reshape(n_seq, length, 128)
    sin_t = np.concatenate([-np.sin(angles), np.sin(angles)] * 2, axis=1).reshape(n_seq, length, 128)
    cos_t, sin_t = jnp.asarray(cos_t, F32), jnp.asarray(sin_t, F32)
    seqs = micro * batch
    seg_all = blocks[..., width].reshape(n_seq, seqs, length).transpose(1, 0, 2)
    own_places = seq_index * length + jnp.arange(length, dtype=jnp.int32)
    key_places = jnp.stack(block_ids)[:, None] * length + jnp.arange(length, dtype=jnp.int32)
    allowed = (seg_all[:, 0, :, None] == seg_all.reshape(seqs, 1, -1)) & (
        own_places[None, :, None] >= key_places.reshape(1, 1, -1)
    )
    allowed = allowed.astype(F32)
    seq_scalar = seq_index.astype(jnp.int32).reshape(1)
    wq, wkv = wf_qkv[:, : QW + 64], wf_qkv[:, QW:]
    gain_one, gain_two = gain_one[None], gain_two[None]
    source = hidden.reshape(rows, width)
    n_all = n_seq * rows
    attended, q_s, k_s, v_s = call(
        functools.partial(attention_forward, order, length),
        [seq_scalar],
        [blocks, wq, wkv, bias[None, : QW + 64], bias[None, QW:], gain_one, cos_t, sin_t, allowed],
        [
            sds((rows, QW), BF),
            sds((seqs, KV_HEADS, GROUP * length, HEAD_DIM), BF),
            sds((seqs, KV_HEADS, full_length, HEAD_DIM), BF),
            sds((seqs, KV_HEADS, full_length, HEAD_DIM), BF),
        ],
        2 * n_all * width * 2 * KW + 2 * rows * width * QW + 4 * rows * full_length * QW,
    )

    weight = tokens_micro / token_counts.astype(F32)
    weight = jnp.repeat(weight, batch * length)[:, None]
    block_out, down_grad, gate_up_wgrad, middle_grad, out_wgrad, attended_grad, gain_two_grad = call(
        feed_forward,
        [],
        [attended, source, wf_out, wf_gate_up, wf_down, gain_two, cotangent.reshape(rows, width), weight],
        [
            sds((rows, width), BF),
            sds((units, width), BF),
            sds((width, 2 * units), BF),
            sds((rows, width), F32),
            sds((QW, width), BF),
            sds((rows, QW), BF),
            sds((1, width), F32),
        ],
        6 * rows * width * 3 * units + 6 * rows * width * QW,
    )
    block_out = block_out.reshape(hidden.shape)

    def seq_axes(value, axis, masks):
        for mask in masks:
            value = net.add_half(value, mask, axis)
        return value

    quarter = (2,) * len(net.seq_bits)
    n_f = len(f_lead)
    red_down = down_grad.reshape(f_lead + quarter + (ff_rows // n_seq, width))
    for step, mask in enumerate(net.seq_bits):
        red_down = net.add_half(red_down, mask, n_f + len(quarter) - 1 - step)
    red_down = net.scatter_fsdp(red_down)

    red_gate = gate_up_wgrad.reshape(f_lead + (d_rows,) + quarter + (2 * units // n_seq,))
    red_gate = net.add_half(red_gate, core, n_f + len(quarter))
    red_gate = net.add_half(red_gate, net.fsdp_bits[0], n_f - 1)
    for step, mask in enumerate(net.seq_bits[1:]):
        red_gate = net.add_half(red_gate, mask, n_f - 1 + len(quarter) - 1 - step)
    for step, mask in enumerate(net.fsdp_bits[1:]):
        red_gate = net.add_half(red_gate, mask, n_f - 2 - step)

    dq, dkv, qkv_wgrad, bias_grad, gain_one_grad = call(
        functools.partial(attention_backward, order, length),
        [seq_scalar],
        [blocks, wq, wkv, gain_one, cos_t, sin_t, allowed, q_s, k_s, v_s, attended_grad],
        [
            sds((rows, QW + 64), BF),
            sds((n_seq, rows, 2 * KW), BF),
            sds((width, qkv_w), BF),
            sds((1, qkv_w), F32),
            sds((1, width), F32),
        ],
        4 * n_all * width * 2 * KW + 4 * rows * width * QW + 10 * rows * full_length * QW,
    )
    kv_parts = [dkv[0]]
    for place, mask_bits in enumerate(order):
        if mask_bits:
            kv_parts.append(net.swap(dkv[place], mask_bits))
    (hidden_grad,) = call(
        input_gradient,
        [],
        [dq, *kv_parts, source, middle_grad, wq, wkv, gain_one],
        [sds((rows, width), F32)],
        2 * rows * width * qkv_w,
    )
    hidden_grad = hidden_grad.reshape(hidden.shape)
    bias_grad, gain_one_grad, gain_two_grad = bias_grad[0], gain_one_grad[0], gain_two_grad[0]

    qk_rows, v_rows = (QW + KW) // n_fsdp, KW // n_fsdp
    small_grads = jnp.concatenate(
        [
            bias_grad[: QW + KW].reshape(n_fsdp, qk_rows),
            bias_grad[QW + KW :].reshape(n_fsdp, v_rows),
            gain_one_grad.reshape(n_fsdp, d_rows),
            gain_two_grad.reshape(n_fsdp, d_rows),
        ],
        axis=1,
    ).astype(BF)
    wide = qkv_w + width
    small_pad = jnp.zeros((n_fsdp, pad_rows, wide), BF)
    small_pad = small_pad.at[:, 0, : small_grads.shape[1]].set(small_grads)
    rest = jnp.concatenate([qkv_wgrad, out_wgrad], axis=1)
    rest = jnp.concatenate([rest.reshape(n_fsdp, d_rows, wide), small_pad], axis=1)
    rest = rest.reshape(f_lead + (d_rows + pad_rows,) + quarter + (wide // n_seq,))
    for step, mask in enumerate(net.seq_bits):
        rest = net.add_half(rest, mask, n_f + 1 + len(quarter) - 1 - step)
    rest = net.scatter_fsdp(rest)

    def seq_back(value, axis):
        for step, mask in enumerate(reversed(net.seq_bits)):
            value = net.both(value, mask, axis + step)
        return value

    out_down = seq_back(red_down, 0).reshape(ff_rows, width).astype(F32)
    out_gate = seq_back(red_gate, 1).reshape(d_rows, 2 * units).astype(F32)
    out_rest = seq_back(rest, 1).reshape(d_rows + pad_rows, wide).astype(F32)
    line = out_rest[d_rows]
    edge = qk_rows + v_rows
    return (
        block_out,
        hidden_grad,
        out_rest[:d_rows, :qkv_w],
        line[:qk_rows],
        line[qk_rows:edge],
        out_rest[:d_rows, qkv_w:],
        out_gate,
        out_down,
        line[edge : edge + 2 * d_rows].reshape(2, d_rows),
    )


def after(value, *others):
    return lax.optimization_barrier((value, *others))[0]


def rope_tables(full_length, n_seq):
    places = np.arange(full_length, dtype=np.float32)
    speeds = np.power(ROPE_BASE, -2.0 * np.arange(HEAD_DIM // 2, dtype=np.float32) / HEAD_DIM)
    angles = places[:, None] * speeds.astype(np.float32)[None, :]
    cos_t = np.tile(np.cos(angles), (1, 4)).reshape(n_seq, -1, 128)
    sin_t = np.concatenate([-np.sin(angles), np.sin(angles)] * 2, axis=1).reshape(n_seq, -1, 128)
    return jnp.asarray(cos_t, F32), jnp.asarray(sin_t, F32)


def on_device_tiled(
    hidden, w_qkv, b_qkv, w_out, w_gate_up, w_down, norm_gains, segment_ids, token_counts, cotangent,
    n_fsdp, n_seq,
):
    net = Net(n_fsdp, n_seq)
    micro, batch, length, width = hidden.shape
    full_length = length * n_seq
    tokens_micro = batch * n_fsdp * full_length
    rows = micro * batch * length
    seqs = micro * batch
    d_rows, qkv_w = w_qkv.shape
    ff_rows = w_down.shape[0]
    units = w_gate_up.shape[1] // 2
    n_bias = b_qkv.shape[0]
    core, ybit = net.seq_bits
    xbit, znear, zfar = net.fsdp_bits
    order = [0, 2, 1, 3]
    seq_index = lax.axis_index("seq")
    meta = jnp.stack([seq_index, lax.axis_index("fsdp")]).astype(jnp.int32)
    source = hidden.reshape(rows, width)

    small = [w_qkv, b_qkv[None], norm_gains]
    a0 = pl.pallas_call(
        functools.partial(cut_qkv, core),
        out_shape=sds(((d_rows + 8) // 2, qkv_w), BF),
        in_specs=[pl.BlockSpec(memory_space=pltpu.SMEM)] + [pl.BlockSpec(memory_space=pltpu.HBM)] * 3,
        out_specs=pl.BlockSpec(memory_space=pltpu.VMEM),
        scratch_shapes=[
            *[pltpu.VMEM(v.shape, BF) for v in small],
            pltpu.VMEM((d_rows + 8, qkv_w), F32),
            pltpu.SemaphoreType.DMA((3,)),
        ],
        compiler_params=pltpu.CompilerParams(vmem_limit_bytes=52 * 1024 * 1024),
    )(meta, *small)
    a1 = net.both(a0, zfar, 0)

    ids = segment_ids.reshape(rows, 1).astype(BF)
    block = jnp.concatenate([source, jnp.broadcast_to(ids, (rows, 64))], axis=1)
    block = after(block, a0)
    block_y = net.swap(block, ybit)
    block_c = net.swap(block, core)

    quarter = 2 * units // n_seq
    gu0 = lax.dynamic_slice_in_dim(after(w_gate_up, a0), seq_index * quarter, quarter, axis=1)
    half_b = jnp.concatenate(
        [
            w_down.reshape(2, ff_rows // 2, width),
            jnp.concatenate([w_out, jnp.zeros((8, width), BF)], axis=0).reshape(2, -1, width),
        ],
        axis=1,
    )
    a2 = net.both(a1, znear, 0)
    a_x = net.swap(a2, xbit)
    a_c = net.swap(a2, core)
    gu1 = net.both(gu0, zfar, 0)
    gu2 = net.both(after(gu1, a2), znear, 0)
    block_yc = net.swap(block_y, core)
    a_xc = net.swap(a_x, core)
    gu_x = net.swap(gu2, xbit)
    gu_y = net.swap(gu2, ybit)
    gu_c = net.swap(gu2, core)
    b0 = net.half(after(half_b, a1), core, 0)
    b1 = net.both(b0, zfar, 0, after(net.swap(b0, zfar), a2))
    b_x = net.swap(b1, xbit)
    b_z = net.swap(after(b1, gu2), znear)
    b_c = net.swap(b1, core)
    a_xc = after(a_xc, gu2, b1)

    cos_t, sin_t = rope_tables(full_length, n_seq)
    block_ids = [seq_index ^ o for o in order]
    blocks = [block, block_y, block_c, block_yc]
    seg_all = jnp.stack([b[:, width].reshape(seqs, length) for b in blocks], axis=1)
    own_places = seq_index * length + jnp.arange(length, dtype=jnp.int32)
    key_places = jnp.stack(block_ids)[:, None] * length + jnp.arange(length, dtype=jnp.int32)
    allowed = (seg_all[:, 0, :, None] == seg_all.reshape(seqs, 1, -1)) & (
        own_places[None, :, None] >= key_places.reshape(1, 1, -1)
    )
    allowed = allowed.astype(F32)
    attended, q_s, k_s, v_s, wf, gains = call(
        functools.partial(first_forward, order, length, d_rows, n_bias),
        [meta],
        [*blocks, a2, a_x, a_c, a_xc, cos_t, sin_t, allowed],
        [
            sds((rows, QW), BF),
            sds((seqs, KV_HEADS, GROUP * length, HEAD_DIM), BF),
            sds((seqs, KV_HEADS, full_length, HEAD_DIM), BF),
            sds((seqs, KV_HEADS, full_length, HEAD_DIM), BF),
            sds((width, qkv_w), BF),
            sds((2, width), F32),
        ],
        1.2e10,
        [(n_fsdp * (d_rows + 8), qkv_w), (1, qkv_w)],
    )
    gu_y = after(gu_y, attended)
    gu_x, b_z, b_x = after(gu_x, gu_y), after(b_z, gu_y), after(b_x, gu_y)
    gu_xy = net.swap(gu_x, ybit)
    b_zx = net.swap(b_z, xbit)
    gu_yc = net.swap(gu_y, core)
    gu_xc = net.swap(gu_x, core)
    b_zc = net.swap(b_z, core)
    b_xc = net.swap(b_x, core)
    b_zxc = net.swap(b_zx, core)
    gu_xyc = net.swap(gu_xy, core)
    pieces = [b1, b_c, b_x, b_xc, b_z, b_zc, b_zx, b_zxc]
    pieces += [gu2, gu_c, gu_y, gu_yc, gu_x, gu_xc, gu_xy, gu_xyc]

    weight = tokens_micro / token_counts.astype(F32)
    weight = jnp.repeat(weight, batch * length)[:, None]
    lead = (2, 2, 2, 2)
    cot = cotangent.reshape(rows, width)
    gate_lead = lead + (d_rows, units // 4)
    block_out, a_keep, a_give, b_keep, b_give, down_keep, down_give, middle_grad, attended_grad, gain_two = call(
        functools.partial(feed_forward_pieces, d_rows, ff_rows),
        [meta],
        [attended, source, gains, cot, weight],
        [
            sds((seqs, width, length), BF),
            sds(gate_lead, BF),
            sds(gate_lead, BF),
            sds(gate_lead, BF),
            sds(gate_lead, BF),
            sds(lead + (ff_rows // 4 + d_rows // 3, width), BF),
            sds(lead + (ff_rows // 4 + d_rows // 3, width), BF),
            sds((rows, width), F32),
            sds((rows, QW), BF),
            sds((1, width), F32),
        ],
        1.4e10,
        [(units // 2, width), (n_fsdp, d_rows + d_rows // 3, width)],
        mib=36,
        fetched=pieces,
        landing=[(2, 2, 2, 2) + b1.shape[1:], (2, 2, 2, 2, 2, d_rows, units // 2)],
    )
    block_out = block_out.reshape(micro, batch, width, length).swapaxes(2, 3)

    def add(keep, got):
        return (keep.astype(F32) + got.astype(F32)).astype(BF)

    def halves(keep, got):
        return add(keep[0], got[0]), add(keep[1], got[1])

    down_got = net.swap(down_give, core)
    a_got = net.swap(after(a_give, down_got), core)
    b_got = net.swap(after(b_give, down_got), core)
    a, a_give = halves(a_keep, a_got)
    a_got = net.swap(a_give, xbit)
    b, b_give = halves(b_keep, b_got)
    b_got = net.swap(b_give, znear)
    down, down_give = halves(down_keep, down_got)
    attended_grad = after(attended_grad, a_give, b_give, down_give)
    down_got = net.swap(down_give, ybit)

    dq, dkv_keep, dkv_give, rest_keep, rest_give = call(
        functools.partial(attention_backward_pieces, order, length, d_rows),
        [meta],
        [*blocks, wf, gains, cos_t, sin_t, allowed, q_s, k_s, v_s, attended_grad, gain_two],
        [
            sds((rows, QW + 64), BF),
            sds((2, rows, 2 * KW), BF),
            sds((2, rows, 2 * KW), BF),
            sds(lead + (d_rows + 8, 256), BF),
            sds(lead + (d_rows + 8, 256), BF),
        ],
        1.4e10,
        [(width, 1024), (1, qkv_w), (1, width), (n_fsdp, 8, 1024)],
        24,
    )
    b, b_give = halves(b, after(b_got, dq))
    a, a_give = halves(a, after(a_got, b_give))
    b_got = net.swap(b_give, zfar)
    a_got = net.swap(a_give, znear)
    rest, rest_give = halves(rest_keep, after(net.swap(rest_give, core), b_give, down_got))
    rest_got = net.swap(rest_give, ybit)
    down, down_give = halves(down, after(down_got, rest_give))
    down_got = net.swap(down_give, xbit)
    dkv, dkv_give = halves(dkv_keep, after(net.swap(dkv_give, core), down_give))
    dkv_got = net.swap(dkv_give, ybit)
    a, a_give = halves(a, after(a_got, dkv_give))
    a_got = net.swap(a_give, zfar)
    rest, rest_give = halves(rest, after(rest_got, a_give))
    rest_got = net.swap(rest_give, xbit)
    b, b_give = halves(b, after(b_got, rest_give))
    b_got = net.swap(b_give, xbit)
    down, down_give = halves(down, after(down_got, b_give))
    down_got = net.swap(down_give, znear)
    rest, rest_give = halves(rest, after(rest_got, down_give))
    rest_got = net.swap(rest_give, znear)
    (hidden_grad,) = call(
        input_gradient_two,
        [],
        [dq, dkv, after(dkv_got, rest_give), source, middle_grad, wf, gains],
        [sds((seqs, width, length), F32)],
        3e9,
        mib=16,
    )
    a_got = after(a_got, hidden_grad)
    hidden_grad = hidden_grad.reshape(micro, batch, width, length).swapaxes(2, 3)
    a = add(a, a_got)
    a_got = net.swap(a, ybit)
    b = add(b, after(b_got, a))
    b_got = net.swap(b, ybit)
    down, down_give = halves(down, after(down_got, b))
    down_got = net.swap(down_give, zfar)
    rest, rest_give = halves(rest, after(rest_got, down_give))
    rest_got = net.swap(rest_give, zfar)
    a = add(a, after(a_got, rest_give))
    a_far = net.swap(a, core)
    b = add(b, b_got)
    b_far = net.swap(b, core)
    down = add(down, after(down_got, a))
    down_y = net.swap(down, ybit)
    down_c = net.swap(after(down, down_y), core)
    rest = add(rest, after(rest_got, down))
    rest_y = net.swap(rest, ybit)
    down_yc = net.swap(after(down_y, rest_y), core)
    rest_far = net.swap(jnp.stack([rest, rest_y]), core)
    qk, v = (QW + KW) // n_fsdp, KW // n_fsdp
    out_gate, out_down, out_wout, out_qkv, b_qk, b_v, out_gains = call(
        functools.partial(place_all, ff_rows // 4, qk, v),
        [meta],
        [a, a_far, b, b_far, down, down_y, down_c, down_yc, rest, rest_y, rest_far],
        [
            sds((d_rows, 2 * units), F32),
            sds((ff_rows, width), F32),
            sds((d_rows, width), F32),
            sds((d_rows, qkv_w), F32),
            sds((1, qk), F32),
            sds((1, v), F32),
            sds((2, d_rows), F32),
        ],
        3e9,
        [(d_rows + 8, 1024)],
        16,
    )
    return (
        block_out,
        hidden_grad,
        out_qkv,
        b_qk.reshape(qk),
        b_v.reshape(v),
        out_wout,
        out_gate,
        out_down,
        out_gains,
    )


def solution(mesh):
    n_fsdp, n_seq = mesh.shape["fsdp"], mesh.shape["seq"]
    in_specs = (
        P(None, "fsdp", "seq", None),
        P("fsdp", None),
        P("fsdp"),
        P("fsdp", None),
        P("fsdp", None),
        P("fsdp", None),
        P(None, "fsdp"),
        P(None, "fsdp", "seq"),
        P(),
        P(None, "fsdp", "seq", None),
    )
    out_specs = (
        P(None, "fsdp", "seq", None),
        P(None, "fsdp", "seq", None),
        P("fsdp", None),
        P("fsdp"),
        P("fsdp"),
        P("fsdp", None),
        P("fsdp", None),
        P("fsdp", None),
        P(None, "fsdp"),
    )

    def local(*args):
        body = on_device_tiled if (n_fsdp, n_seq) == (8, 4) else on_device
        return body(*args, n_fsdp=n_fsdp, n_seq=n_seq)

    return jax.shard_map(local, mesh=mesh, in_specs=in_specs, out_specs=out_specs, check_vma=False)
```
